32 devices in a mesh: traj: 4 (over z), tm: 8 (over y, x, core).
Axes of the slice: x: 2, y: 2, z: 4, core: 2. Of those that a mesh axis runs over, the one named last changes fastest.
Arguments:
- query_states: bfloat16 [8192, 768], P(('traj', 'tm')), parts along dimension 0, may hold values from -8 to 8
- key_states: bfloat16 [8192, 768], P(('traj', 'tm')), parts along dimension 0, may hold values from -8 to 8
- value_states: bfloat16 [8192, 768], P(('traj', 'tm')), parts along dimension 0, may hold values from -6 to 6
- grad_out: bfloat16 [8192, 768], P(('traj', 'tm')), parts along dimension 0, may hold values from -6 to 6
- camera_pose: int32 [64], P('traj'), parts along dimension 0, may hold values from 0 to 15
- pose_bias: float32 [6, 16, 16], replicated, may hold values from -2 to 2
- memory_index: int32 [32, 2], P(('traj', 'tm')), parts along dimension 0, may hold values from 0 to 3, all different within a row
- bank_frames: int32 [16], P('traj'), parts along dimension 0, may hold values from 0 to 15, as said below
Outputs:
- attended: bfloat16 [8192, 768], P(('traj', 'tm')), parts along dimension 0
- grad_query: bfloat16 [8192, 768], P(('traj', 'tm')), parts along dimension 0
- grad_key: bfloat16 [8192, 768], P(('traj', 'tm')), parts along dimension 0
- grad_value: bfloat16 [8192, 768], P(('traj', 'tm')), parts along dimension 0
The draws below stay inside these ranges and needn't reach their ends.
There are 4 independent parts, one for each index of `traj`. The reference program is written for one: setup_inputs(seed, part) draws one part's arguments, and reference() takes and returns one part's arrays. A program takes and returns all parts, laid end to end along the dimension named above; an argument that names none is the same for every part. Nothing has to cross between parts.
Inputs may be any that keep to these rules, and one draw needn't show every extreme that they name: `bank_frames`: 4 distinct frames; frame 0 and frame 16 - 1 are always among them. `memory_index`: each group names 2 different slots, and every slot is named by some group.
All inputs are finite; a program needn't handle non-finite values.
Results may differ from the reference program's by a relative error of at most 0.0085.
Values may be sent and summed in bfloat16 or wider, within the bound.
No kernel may reach another device: no remote copies, remote signals or barrier semaphores. Data moves between devices by JAX's collectives and lax.ppermute only.
A program may use at most 64 MiB of HBM per device.

```python
import math
import jax
import jax.numpy as jnp
from jax import lax

HEADS = 6
HDIM = 128
FT = 128
FR_DEV = 2
BANK = 4
MEM = 2
POSES = 16
HD = 768
GROUPS = 8
FRAMES = 16
TOKENS = 2048


def draw_query_states(key, part):
    key = jax.random.fold_in(key, 11)
    shape = (FRAMES * FT, HEADS * HDIM)
    base = jnp.clip(jax.random.normal(key, shape), -8.0, 8.0)
    return base.astype(jnp.bfloat16)


def draw_key_states(key, part):
    key = jax.random.fold_in(key, 17)
    shape = (FRAMES * FT, HEADS * HDIM)
    base = jnp.clip(jax.random.normal(key, shape), -8.0, 8.0)
    return base.astype(jnp.bfloat16)


def draw_bank_frames(key, part):
    key = jax.random.fold_in(key, 23)
    middle_key, order_key = jax.random.split(key)
    middle = jax.random.permutation(middle_key, FRAMES - 2)[:BANK - 2].astype(jnp.int32) + 1
    frames_all = jnp.concatenate([jnp.zeros((1,), jnp.int32), jnp.full((1,), FRAMES - 1, jnp.int32), middle])
    return frames_all[jax.random.permutation(order_key, BANK)].astype(jnp.int32)


def place_ends(drawn, rng, low, largest):
    index_at = [jax.random.randint(jax.random.fold_in(rng, axis), (), 0, length) for axis, length in enumerate(drawn.shape)]
    longest = drawn.shape.index(max(drawn.shape))
    neighbour = index_at[:longest] + [(index_at[longest] + 1) % drawn.shape[longest]] + index_at[longest + 1:]
    return drawn.at[tuple(index_at)].set(low).at[tuple(neighbour)].set(largest)


def block_scale(key, shape, shards, low, top_value):
    def one(dim, shards_of):
        draws = jax.random.uniform(jax.random.fold_in(jax.random.fold_in(key, 6), dim), (shards_of,), jnp.float32, low / len(shards), top_value / len(shards))
        return jnp.repeat(jnp.exp(draws), shape[dim] // shards_of).reshape((-1,) + (1,) * (len(shape) - dim - 1))

    factor_of = one(*shards[0])
    for cut in shards[1:]:
        factor_of = factor_of * one(*cut)
    return factor_of


def picks_of(key, rows, amount, top, lift):
    sequence = jax.random.permutation(jax.random.fold_in(key, 1), amount)
    pull = sequence
    for power in range(3):
        pull = pull * pull // amount
    pull = pull * lift // amount
    chance = jax.random.randint(jax.random.fold_in(key, 2), (rows, amount), 0, 4096) + pull
    sure = jax.random.permutation(jax.random.fold_in(key, 3), rows)[jnp.arange(amount) % rows]
    chance = jnp.where(jnp.arange(rows)[:, None] == sure[None, :], 1 << 14, chance)
    score = chance * amount + jnp.arange(amount)
    return lax.top_k(score.astype(jnp.int32), top)[1].astype(jnp.int32)


def normal_values(key, dims, deviation, limit, shards=(), kind=jnp.bfloat16):
    array = deviation * jax.random.normal(key, dims, jnp.float32)
    if shards:
        array = array * block_scale(key, dims, shards, -0.22, 0.18)
    return jnp.clip(array, -limit, limit).astype(kind)


def setup_inputs(seed: int = 0, part: int = 0) -> dict:
    key_list = jax.random.split(jax.random.key(seed), 9)
    part_keys = jax.random.split(jax.random.fold_in(key_list[8], part), 9)
    return {
        "query_states": draw_query_states(jax.random.fold_in(jax.random.fold_in(key_list[8], part), 71), part),
        "key_states": draw_key_states(jax.random.fold_in(jax.random.fold_in(key_list[8], part), 71), part),
        "value_states": normal_values(part_keys[2], (TOKENS, HD), 1.0, 6.0, ((0, 8),)),
        "grad_out": normal_values(part_keys[3], (TOKENS, HD), 1.0, 6.0, ((0, 8),)),
        "camera_pose": place_ends(jax.random.randint(part_keys[4], (FRAMES,), 0, POSES), jax.random.fold_in(part_keys[4], 1), 0, POSES - 1).astype(jnp.int32),
        "pose_bias": jnp.clip(jax.random.uniform(key_list[5], (HEADS, POSES, POSES), jnp.float32, -2.0, 2.0), -2.0, 2.0),
        "memory_index": picks_of(part_keys[6], GROUPS, BANK, MEM, 4096),
        "bank_frames": draw_bank_frames(jax.random.fold_in(jax.random.fold_in(key_list[8], part), 71), part),
    }


BLOCKED_LOGIT = -1e+30

def pose_table(pose_bias, query_pose, key_pose):
    pose_count = pose_bias.shape[1]
    pose_range = jnp.arange(pose_count, dtype=jnp.int32)
    left_hot = (query_pose[:, None] == pose_range[None, :]).astype(jnp.float32)
    right_hot = (key_pose[:, None] == pose_range[None, :]).astype(jnp.float32)
    return jnp.einsum('ap,hpr,br->hab', left_hot, pose_bias, right_hot, precision=lax.Precision.HIGHEST)

def attend(query_rows, key_rows, value_rows, cotangent, bias_rows, blocked):
    head_count = bias_rows.shape[0]
    query_frames = bias_rows.shape[1]
    key_frames = bias_rows.shape[2]
    query_count = query_rows.shape[0]
    key_count = key_rows.shape[0]
    head_depth = query_rows.shape[1] // head_count
    factor = 1.0 / math.sqrt(head_depth)
    query_heads = query_rows.reshape(query_count, head_count, head_depth).astype(jnp.float32)
    key_heads = key_rows.reshape(key_count, head_count, head_depth).astype(jnp.float32)
    value_heads = value_rows.reshape(key_count, head_count, head_depth).astype(jnp.float32)
    cotangent_heads = cotangent.reshape(query_count, head_count, head_depth).astype(jnp.float32)
    logits = jnp.einsum('qhd,khd->hqk', query_heads, key_heads) * factor
    logits = logits.reshape(head_count, query_frames, query_count // query_frames, key_frames, key_count // key_frames)
    logits = logits + bias_rows[:, :, None, :, None]
    logits = jnp.where(blocked[None, None, None, :, None], BLOCKED_LOGIT, logits)
    logits = logits.reshape(head_count, query_count, key_count)
    row_peak = lax.optimization_barrier(jnp.max(logits, axis=-1, keepdims=True))
    shifted_exp = jnp.exp(logits - row_peak)
    row_total = lax.optimization_barrier(jnp.sum(shifted_exp, axis=-1, keepdims=True))
    probs_all = shifted_exp / row_total
    weights = lax.optimization_barrier(probs_all.astype(jnp.bfloat16)).astype(jnp.float32)
    attended = jnp.einsum('hqk,khd->qhd', weights, value_heads).reshape(query_count, -1).astype(jnp.bfloat16)
    slope_grad = jnp.einsum('qhd,khd->hqk', cotangent_heads, value_heads)
    spread = lax.optimization_barrier(jnp.sum(probs_all * slope_grad, axis=-1, keepdims=True))
    logit_grad = lax.optimization_barrier((probs_all * (slope_grad - spread)).astype(jnp.bfloat16)).astype(jnp.float32)
    grad_query = (jnp.einsum('hqk,khd->qhd', logit_grad, key_heads) * factor).reshape(query_count, -1).astype(jnp.bfloat16)
    key_grad = (jnp.einsum('hqk,qhd->khd', logit_grad, query_heads) * factor).reshape(key_count, -1)
    value_grad = jnp.einsum('hqk,qhd->khd', weights, cotangent_heads).reshape(key_count, -1)
    return (attended, grad_query, key_grad, value_grad)

def reference(query_states, key_states, value_states, grad_out, camera_pose, pose_bias, memory_index, bank_frames):
    width = query_states.shape[1]
    group_rows = FR_DEV * FT
    query_framed = query_states.reshape(FRAMES, FT, width)
    key_framed = key_states.reshape(FRAMES, FT, width)
    value_framed = value_states.reshape(FRAMES, FT, width)
    cotangent_framed = grad_out.reshape(FRAMES, FT, width)
    slot_range = jnp.arange(BANK, dtype=jnp.int32)
    frame_range = jnp.arange(FR_DEV, dtype=jnp.int32)
    key_slots = jnp.arange(2 * FR_DEV + MEM, dtype=jnp.int32)

    def bank_part(select, grads):
        framed = grads.reshape(MEM, FT, width)
        summed = lax.optimization_barrier(jnp.sum(jnp.where(select[:, :, None, None], framed[:, None], 0.0), axis=0))
        return lax.optimization_barrier(summed.astype(jnp.bfloat16)).astype(jnp.float32)

    def per_group(running, group_index):
        own_ids = group_index * FR_DEV + frame_range
        prev_ids = jnp.maximum(own_ids - FR_DEV, 0)
        chosen = memory_index[group_index]
        mem_ids = bank_frames[chosen]
        key_ids = jnp.concatenate([prev_ids, own_ids, mem_ids])
        bias_rows = pose_table(pose_bias, camera_pose[own_ids], camera_pose[key_ids])
        blocked = (key_slots < FR_DEV) & (group_index == 0)
        attended, grad_query, key_grad, value_grad = attend(query_framed[own_ids].reshape(group_rows, width), key_framed[key_ids].reshape(-1, width), value_framed[key_ids].reshape(-1, width), cotangent_framed[own_ids].reshape(group_rows, width), bias_rows, blocked)
        select = chosen[:, None] == slot_range[None, :]
        running = (running[0] + bank_part(select, key_grad[2 * group_rows:]), running[1] + bank_part(select, value_grad[2 * group_rows:]))
        return (running, (attended, grad_query, key_grad[:group_rows], value_grad[:group_rows], key_grad[group_rows:2 * group_rows], value_grad[group_rows:2 * group_rows]))
    empty = jnp.zeros((BANK, FT, width), jnp.float32)
    banked, stacked = lax.scan(per_group, (empty, empty), jnp.arange(GROUPS, dtype=jnp.int32))
    attended, grad_query, prev_key, prev_value, own_key, own_value = stacked

    def combine(own_part, prev_part, bank_sum):
        shifted_back = jnp.concatenate([prev_part[1:], jnp.zeros_like(prev_part[:1])], axis=0)
        summed_grad = (own_part + shifted_back).reshape(FRAMES, FT, width)
        summed_grad = summed_grad.at[bank_frames].add(bank_sum)
        return summed_grad.reshape(FRAMES * FT, width).astype(jnp.bfloat16)
    return (attended.reshape(-1, width), grad_query.reshape(-1, width), combine(own_key, prev_key, banked[0]), combine(own_value, prev_value, banked[1]))
```

```python
import functools
import math

import jax
import jax.numpy as jnp
from jax import lax
from jax.experimental import pallas as pl
from jax.experimental.pallas import tpu as pltpu
from jax.sharding import PartitionSpec as P

FR_DEV = 2
MEM = 2

BLOCKED_LOGIT = -1e30
LOG2E = math.log2(math.e)

SMEM = pl.BlockSpec(memory_space=pltpu.SMEM)
VMEM = pl.BlockSpec(memory_space=pltpu.VMEM)
PARAMS = pltpu.CompilerParams(vmem_limit_bytes=32 * 1024 * 1024)


def swap(block, bit, peers):
    return lax.ppermute(block, "tm", [(i, i ^ bit) for i in range(peers)])


def passed_along(block, by, peers):
    pairs = [(i, i + by) for i in range(peers) if 0 <= i + by < peers]
    return lax.ppermute(block, "tm", pairs)


def dyn_frames(bank_ref, slots, last_frame):
    found = [jnp.int32(0)] * (slots - 2)
    seen = jnp.int32(0)
    for slot in range(slots):
        frame = bank_ref[slot]
        free = jnp.logical_and(frame != 0, frame != last_frame)
        for j in range(slots - 2):
            found[j] = jnp.where(jnp.logical_and(free, seen == j), frame, found[j])
        seen = seen + free.astype(jnp.int32)
    return found


def place_of(frame, dyns, last_frame):
    place = jnp.where(frame == 0, len(dyns), len(dyns) + 1)
    for j, dyn in enumerate(dyns):
        place = jnp.where(frame == dyn, j, place)
    return place


def choose(out, take_first, first, second):
    @pl.when(take_first)
    def _():
        out[...] = first[...]

    @pl.when(jnp.logical_not(take_first))
    def _():
        out[...] = second[...]


def has_end(me, done, peers):
    return jnp.logical_or((me & ~done) == 0, (me | done) == peers - 1)


def has_dyn(me, frame, done):
    return ((me ^ (frame // FR_DEV)) & ~done) == 0


def pack_kernel(peers, bank_ref, key_ref, value_ref, keep_ref, send_ref):
    me = lax.axis_index("tm")
    slots = bank_ref.shape[0]
    frame_len = key_ref.shape[0] // FR_DEV
    last_frame = peers * FR_DEV - 1
    dyns = dyn_frames(bank_ref, slots, last_frame)
    even = (me & 1) == 0
    rows = [(dyn % FR_DEV) for dyn in dyns] + [jnp.where(me == peers - 1, FR_DEV - 1, 0)]
    for j, row in enumerate(rows):
        part = pl.ds(pl.multiple_of(row * frame_len, frame_len), frame_len)
        choose(keep_ref.at[j], even, key_ref.at[part], value_ref.at[part])
        choose(send_ref.at[j], even, value_ref.at[part], key_ref.at[part])


def split_kernel(peers, bank_ref, mine_ref, got_ref, low_ref, high_ref):
    me = lax.axis_index("tm")
    slots = bank_ref.shape[0]
    half = mine_ref.shape[1] // 2
    dyns = dyn_frames(bank_ref, slots, peers * FR_DEV - 1)
    flags = [has_dyn(me, dyn, 0) for dyn in dyns] + [has_end(me, 0, peers)]
    for j, flag in enumerate(flags):
        for out, start in ((low_ref, 0), (high_ref, half)):
            part = pl.ds(start, half)
            choose(out.at[j], flag, mine_ref.at[j, part], got_ref.at[j, part])


def step_kernel(peers, low_done, high_done, bank_ref, low_mine, low_got, high_mine, high_got, low_ref, high_ref):
    me = lax.axis_index("tm")
    slots = bank_ref.shape[0]
    dyns = dyn_frames(bank_ref, slots, peers * FR_DEV - 1)
    for out, mine, got, done in (
        (low_ref, low_mine, low_got, low_done),
        (high_ref, high_mine, high_got, high_done),
    ):
        flags = [has_dyn(me, dyn, done) for dyn in dyns] + [has_end(me, done, peers)]
        for j, flag in enumerate(flags):
            choose(out.at[j], flag, mine.at[j], got.at[j])


def pick_kernel(
    peers,
    low_bit,
    high_bit,
    bank_ref,
    index_ref,
    other_index_ref,
    low_mine,
    low_got,
    high_mine,
    high_got,
    own_ref,
    other_ref,
):
    me = lax.axis_index("tm")
    slots = bank_ref.shape[0]
    half = low_mine.shape[1]
    last_frame = peers * FR_DEV - 1
    dyns = dyn_frames(bank_ref, slots, last_frame)
    for out, chosen in ((own_ref, index_ref), (other_ref, other_index_ref)):
        for m in range(MEM):
            frame = bank_ref[chosen[0, m]]
            place = place_of(frame, dyns, last_frame)
            source = jnp.minimum(place, len(dyns))
            for start, mine, got, bit in (
                (0, low_mine, low_got, low_bit),
                (half, high_mine, high_got, high_bit),
            ):
                upper = (me & bit) != 0
                done = (peers - 1) & ~bit
                local = jnp.where(frame == 0, jnp.logical_not(upper), upper)
                for j, dyn in enumerate(dyns):
                    local = jnp.where(frame == dyn, has_dyn(me, dyn, done), local)
                choose(out.at[m, pl.ds(start, half)], local, mine.at[source], got.at[source])


def attend_kernel(
    peers,
    pose_ref,
    bias_ref,
    index_ref,
    bank_ref,
    query_ref,
    cotangent_ref,
    prev_key_ref,
    prev_value_ref,
    key_ref,
    value_ref,
    mem_mine_ref,
    mem_got_ref,
    attended_ref,
    grad_query_ref,
    back_ref,
    own_ref,
    mem_same_ref,
    mem_other_ref,
):
    me = lax.axis_index("tm")
    row_count, columns = query_ref.shape
    frame_len = row_count // FR_DEV
    depth = 128
    factor = 1.0 / math.sqrt(depth)
    even = (me & 1) == 0
    own_ids = [me * FR_DEV + j for j in range(FR_DEV)]
    prev_ids = [jnp.maximum(own - FR_DEV, 0) for own in own_ids]
    mem_ids = [bank_ref[index_ref[0, m]] for m in range(MEM)]
    query_poses = [pose_ref[f] for f in own_ids]
    lane_frame = lax.broadcasted_iota(jnp.int32, (1, row_count), 1) // frame_len
    blocked = me == 0
    f32 = jnp.float32

    def dot(a, b, contract):
        return lax.dot_general(a, b, ((contract[:1], contract[1:]), ((), ())), preferred_element_type=f32)

    for local in range(columns // depth):
        head = pl.program_id(0) * (columns // depth) + local
        cols = pl.ds(local * depth, depth)
        query = query_ref[:, cols]
        cotangent = cotangent_ref[:, cols]
        mine = mem_mine_ref[:, :, cols].reshape(MEM * frame_len, depth)
        got = mem_got_ref[:, :, cols].reshape(MEM * frame_len, depth)
        keys = [prev_key_ref[:, cols], key_ref[:, cols], jnp.where(even, mine, got)]
        values = [prev_value_ref[:, cols], value_ref[:, cols], jnp.where(even, got, mine)]
        logits = []
        peak = None
        for piece, ids in enumerate((prev_ids, own_ids, mem_ids)):
            raw = dot(keys[piece], query, (1, 1)) * (factor * LOG2E)
            rows = []
            for j, frame in enumerate(ids):
                key_pose = pose_ref[frame]
                bias = jnp.zeros((1, row_count), f32)
                for a, query_pose in enumerate(query_poses):
                    value = bias_ref[head, query_pose, key_pose] * LOG2E
                    if piece == 0:
                        value = jnp.where(blocked, BLOCKED_LOGIT, value)
                    bias = jnp.where(lane_frame == a, value, bias)
                rows.append(raw[j * frame_len : (j + 1) * frame_len] + bias)
            block = jnp.concatenate(rows, axis=0)
            logits.append(block)
            block_peak = jnp.max(block, axis=0, keepdims=True)
            peak = block_peak if peak is None else jnp.maximum(peak, block_peak)
        exps = [jnp.exp2(block - peak) for block in logits]
        total = sum(jnp.sum(block, axis=0, keepdims=True) for block in exps)
        inverse = 1.0 / total
        probs = [block * inverse for block in exps]
        weights = [block.astype(jnp.bfloat16) for block in probs]
        slopes = [dot(value, cotangent, (1, 1)) for value in values]
        spread = sum(jnp.sum(p * s, axis=0, keepdims=True) for p, s in zip(probs, slopes))
        dlogits = [(p * (s - spread)).astype(jnp.bfloat16) for p, s in zip(probs, slopes)]
        attended = sum(dot(value, w, (0, 0)) for value, w in zip(values, weights))
        attended_ref[:, cols] = attended.T.astype(jnp.bfloat16)
        grad_query = sum(dot(key, d, (0, 0)) for key, d in zip(keys, dlogits)) * factor
        grad_query_ref[:, cols] = grad_query.T.astype(jnp.bfloat16)
        key_terms = [dot(d, query, (1, 0)) * factor for d in dlogits]
        value_terms = [dot(w, cotangent, (1, 0)) for w in weights]
        back_ref[0, :, cols] = key_terms[0].astype(jnp.bfloat16)
        back_ref[1, :, cols] = value_terms[0].astype(jnp.bfloat16)
        own_ref[0, :, cols] = key_terms[1]
        own_ref[1, :, cols] = value_terms[1]
        shape = (MEM, frame_len, depth)
        key_part = key_terms[2].astype(jnp.bfloat16).reshape(shape)
        value_part = value_terms[2].astype(jnp.bfloat16).reshape(shape)
        mem_same_ref[:, :, cols] = jnp.where(even, key_part, value_part)
        mem_other_ref[:, :, cols] = jnp.where(even, value_part, key_part)


def sum_kernel(
    peers,
    low_bit,
    high_bit,
    bank_ref,
    index_ref,
    other_index_ref,
    mine_ref,
    got_ref,
    low_keep,
    low_send,
    high_keep,
    high_send,
):
    me = lax.axis_index("tm")
    slots = bank_ref.shape[0]
    half = mine_ref.shape[1] // 2
    last_frame = peers * FR_DEV - 1
    dyns = dyn_frames(bank_ref, slots, last_frame)
    named = [(bank_ref[index_ref[0, m]], mine_ref, m) for m in range(MEM)]
    named += [(bank_ref[other_index_ref[0, m]], got_ref, m) for m in range(MEM)]
    for start, keep, send, bit in ((0, low_keep, low_send, low_bit), (half, high_keep, high_send, high_bit)):
        upper = (me & bit) != 0
        near = jnp.where(upper, last_frame, 0)
        far = jnp.where(upper, 0, last_frame)
        part = pl.ds(start, half)
        terms = [ref[m, part].astype(jnp.float32) for _, ref, m in named]

        def total(frame):
            return sum(jnp.where(name == frame, term, 0.0) for (name, _, _), term in zip(named, terms))

        for j, dyn in enumerate(dyns):
            value = total(dyn)
            keep[j] = value
            send[j] = value.astype(jnp.bfloat16)
        keep[len(dyns)] = total(near)
        send[len(dyns)] = total(far).astype(jnp.bfloat16)


def add_kernel(low_keep, low_got, high_keep, high_got, low_out, low_send, high_out, high_send):
    for keep, got, out, send in ((low_keep, low_got, low_out, low_send), (high_keep, high_got, high_out, high_send)):
        value = keep[...] + got[...].astype(jnp.float32)
        out[...] = value
        send[...] = value.astype(jnp.bfloat16)


def owned_kernel(peers, bank_ref, low_keep, low_got, high_keep, high_got, mine_ref, other_ref):
    me = lax.axis_index("tm")
    slots = bank_ref.shape[0]
    half = low_keep.shape[1]
    last_frame = peers * FR_DEV - 1
    dyns = dyn_frames(bank_ref, slots, last_frame)
    for start, keep, got in ((0, low_keep, low_got), (half, high_keep, high_got)):
        part = pl.ds(start, half)
        for out, group in ((mine_ref, me), (other_ref, me ^ 1)):
            for j in range(FR_DEV):
                frame = group * FR_DEV + j
                named = jnp.logical_or(frame == 0, frame == last_frame)
                place = jnp.int32(len(dyns))
                for d, dyn in enumerate(dyns):
                    named = jnp.logical_or(named, frame == dyn)
                    place = jnp.where(frame == dyn, d, place)

                @pl.when(named)
                def _(out=out, j=j, place=place):
                    value = keep[place] + got[place].astype(jnp.float32)
                    out[j, part] = value.astype(out.dtype)

                @pl.when(jnp.logical_not(named))
                def _(out=out, j=j):
                    out[j, part] = jnp.zeros((half, out.shape[2]), out.dtype)


def final_kernel(own_ref, back_ref, mine_ref, got_ref, grad_key_ref, grad_value_ref):
    even = (lax.axis_index("tm") & 1) == 0
    shape = grad_key_ref.shape
    mine = mine_ref[...].reshape(shape)
    got = got_ref[...].astype(jnp.float32).reshape(shape)
    key_sum = own_ref[0] + back_ref[0].astype(jnp.float32) + jnp.where(even, mine, got)
    value_sum = own_ref[1] + back_ref[1].astype(jnp.float32) + jnp.where(even, got, mine)
    grad_key_ref[...] = key_sum.astype(jnp.bfloat16)
    grad_value_ref[...] = value_sum.astype(jnp.bfloat16)


def body(
    query_states,
    key_states,
    value_states,
    grad_out,
    camera_pose,
    pose_bias,
    memory_index,
    bank_frames,
):
    row_count, width = query_states.shape
    frame_len = row_count // FR_DEV
    half = frame_len // 2
    slots = bank_frames.shape[0]
    peers = lax.axis_size("tm")
    bits = [1 << i for i in range(1, peers.bit_length() - 1)]
    kept = slots - 1
    bf16, f32 = jnp.bfloat16, jnp.float32

    def shape(dtype, *dims):
        return jax.ShapeDtypeStruct(dims, dtype)

    def call(kernel, outs, scalars, arrays):
        return pl.pallas_call(
            kernel,
            out_shape=outs,
            in_specs=[SMEM] * len(scalars) + [VMEM] * len(arrays),
            out_specs=[VMEM] * len(outs),
            compiler_params=PARAMS,
        )(*scalars, *arrays)

    prev_keys = passed_along(key_states, 1, peers)
    prev_values = passed_along(value_states, 1, peers)
    other_index = swap(memory_index, 1, peers)
    frames = shape(bf16, kept, frame_len, width)
    halves = shape(bf16, kept, half, width)
    sums = shape(f32, kept, half, width)
    keep, send = call(functools.partial(pack_kernel, peers), [frames] * 2, [bank_frames], [key_states, value_states])
    got = swap(send, 1, peers)
    low, high = call(functools.partial(split_kernel, peers), [halves] * 2, [bank_frames], [keep, got])
    low_done = high_done = 1
    for step, (low_bit, high_bit) in enumerate(zip(bits, bits[::-1])):
        low_got = swap(low, low_bit, peers)
        high_got = swap(high, high_bit, peers)
        if step + 1 < len(bits):
            low, high = call(
                functools.partial(step_kernel, peers, low_done, high_done),
                [halves] * 2,
                [bank_frames],
                [low, low_got, high, high_got],
            )
        low_done |= low_bit
        high_done |= high_bit
    chosen = shape(bf16, MEM, frame_len, width)
    mem_mine, mem_send = call(
        functools.partial(pick_kernel, peers, bits[-1], bits[0]),
        [chosen] * 2,
        [bank_frames, memory_index, other_index],
        [low, low_got, high, high_got],
    )
    mem_got = swap(mem_send, 1, peers)

    columns = 256
    rows_spec = pl.BlockSpec((row_count, columns), lambda i: (0, i))
    pair_spec = pl.BlockSpec((2, row_count, columns), lambda i: (0, 0, i))
    mem_spec = pl.BlockSpec((MEM, frame_len, columns), lambda i: (0, 0, i))
    attended, grad_query, back, own, mem_same, mem_other = pl.pallas_call(
        functools.partial(attend_kernel, peers),
        grid=(width // columns,),
        out_shape=[
            shape(bf16, row_count, width),
            shape(bf16, row_count, width),
            shape(bf16, 2, row_count, width),
            shape(f32, 2, row_count, width),
            chosen,
            chosen,
        ],
        in_specs=[SMEM] * 4 + [rows_spec] * 6 + [mem_spec] * 2,
        out_specs=[rows_spec] * 2 + [pair_spec] * 2 + [mem_spec] * 2,
        compiler_params=PARAMS,
    )(
        camera_pose,
        pose_bias,
        memory_index,
        bank_frames,
        query_states,
        grad_out,
        prev_keys,
        prev_values,
        key_states,
        value_states,
        mem_mine,
        mem_got,
    )
    same_got = swap(mem_other, 1, peers)
    back_got = passed_along(back, -1, peers)
    low_keep, low_send, high_keep, high_send = call(
        functools.partial(sum_kernel, peers, bits[-1], bits[0]),
        [sums, halves] * 2,
        [bank_frames, memory_index, other_index],
        [mem_same, same_got],
    )
    for step, (low_bit, high_bit) in enumerate(zip(bits[::-1], bits)):
        low_got = swap(low_send, low_bit, peers)
        high_got = swap(high_send, high_bit, peers)
        if step + 1 < len(bits):
            low_keep, low_send, high_keep, high_send = call(
                add_kernel, [sums, halves] * 2, [], [low_keep, low_got, high_keep, high_got]
            )
    owned_mine, owned_send = call(
        functools.partial(owned_kernel, peers),
        [shape(f32, FR_DEV, frame_len, width), shape(bf16, FR_DEV, frame_len, width)],
        [bank_frames],
        [low_keep, low_got, high_keep, high_got],
    )
    owned_got = swap(owned_send, 1, peers)
    grad_key, grad_value = call(
        final_kernel, [shape(bf16, row_count, width)] * 2, [], [own, back_got, owned_mine, owned_got]
    )
    return (attended, grad_query, grad_key, grad_value)


def solution(mesh):
    rows = P(("traj", "tm"), None)
    in_specs = (rows, rows, rows, rows, P("traj"), P(), rows, P("traj"))
    return jax.shard_map(body, mesh=mesh, in_specs=in_specs, out_specs=(rows,) * 4, check_vma=False)
```

```python
import functools
import math

import jax
import jax.numpy as jnp
from jax import lax
from jax.experimental import pallas as pl
from jax.experimental.pallas import tpu as pltpu
from jax.sharding import PartitionSpec as P

FR_DEV = 2
MEM = 2
DEPTH = 128

BLOCKED_LOGIT = -1e30
LOG2E = math.log2(math.e)
FACTOR = 1.0 / math.sqrt(DEPTH)

SMEM = pl.BlockSpec(memory_space=pltpu.SMEM)
VMEM = pl.BlockSpec(memory_space=pltpu.VMEM)
ANY = pl.BlockSpec(memory_space=pl.ANY)
VMEM_LIMIT = 32 * 1024 * 1024
BF16, F32 = jnp.bfloat16, jnp.float32


def shape(dtype, *dims):
    return jax.ShapeDtypeStruct(dims, dtype)


def call(kernel, outs, arrays, scalars=(), after=(), flops=0, name=None):
    count = len(scalars) + len(arrays)

    def run(*refs):
        kernel(*refs[:count], *refs[count + len(after) :])

    return pl.pallas_call(
        run,
        out_shape=outs,
        in_specs=[SMEM] * len(scalars) + [VMEM] * len(arrays) + [ANY] * len(after),
        out_specs=[VMEM] * len(outs),
        compiler_params=pltpu.CompilerParams(vmem_limit_bytes=VMEM_LIMIT),
        cost_estimate=pl.CostEstimate(flops=flops, bytes_accessed=0, transcendentals=0) if flops else None,
        name=name,
    )(*scalars, *arrays, *after)


def swap(block, bit, peers):
    return lax.ppermute(block, "tm", [(i, i ^ bit) for i in range(peers)])


def shift(block, by, start, peers):
    pairs = [(i, i + by) for i in range(start, peers, 2) if 0 <= i + by < peers]
    return lax.ppermute(block, "tm", pairs)


def read_table(table_ref, row):
    return jnp.max(table_ref[row : row + 1, :])


def dyn_frames(bank, last_frame):
    found = [jnp.int32(0)] * (len(bank) - 2)
    seen = jnp.int32(0)
    for frame in bank:
        free = jnp.logical_and(frame != 0, frame != last_frame)
        for j in range(len(found)):
            found[j] = jnp.where(jnp.logical_and(free, seen == j), frame, found[j])
        seen = seen + free.astype(jnp.int32)
    return found


def choose(out, take_first, first, second):
    @pl.when(take_first)
    def _():
        out[...] = first[...]

    @pl.when(jnp.logical_not(take_first))
    def _():
        out[...] = second[...]


def has_end(me, done, peers):
    return jnp.logical_or((me & ~done) == 0, (me | done) == peers - 1)


def has_dyn(me, frame, done):
    return ((me ^ (frame // FR_DEV)) & ~done) == 0


def table_kernel(peers, bank_ref, index_ref, pose_ref, bias_ref, table_ref, rows_ref):
    me = lax.axis_index("tm")
    slots = bank_ref.shape[0]
    heads, _, row_count = rows_ref.shape
    lanes = table_ref.shape[1]
    mem_ids = [bank_ref[index_ref[0, m]] for m in range(MEM)]
    for row, value in enumerate([bank_ref[slot] for slot in range(slots)] + mem_ids):
        table_ref[row : row + 1, :] = jnp.full((1, lanes), value, jnp.int32)
    own_ids = [me * FR_DEV + j for j in range(FR_DEV)]
    prev_ids = [jnp.maximum(own - FR_DEV, 0) for own in own_ids]
    query_poses = [pose_ref[frame] for frame in own_ids]
    key_poses = [pose_ref[frame] for frame in prev_ids + own_ids + mem_ids]
    frame_of = lax.broadcasted_iota(jnp.int32, (1, row_count), 1) // (row_count // FR_DEV)
    for head in range(heads):
        for j, key_pose in enumerate(key_poses):
            row = jnp.zeros((1, row_count), F32)
            for a, query_pose in enumerate(query_poses):
                value = bias_ref[head, query_pose, key_pose] * LOG2E
                if j < FR_DEV:
                    value = jnp.where(me == 0, BLOCKED_LOGIT, value)
                row = jnp.where(frame_of == a, value, row)
            rows_ref[head, j : j + 1, :] = row


def split_kernel(peers, slots, table_ref, key_ref, value_ref, pair_key_ref, pair_value_ref, low_ref, high_ref):
    me = lax.axis_index("tm")
    frame_len = key_ref.shape[0] // FR_DEV
    half = frame_len // 2
    dyns = dyn_frames([read_table(table_ref, slot) for slot in range(slots)], peers * FR_DEV - 1)
    even = (me & 1) == 0
    places = [(has_dyn(me, dyn, 0), dyn % FR_DEV) for dyn in dyns]
    places.append((has_end(me, 0, peers), jnp.where(me < peers // 2, 0, FR_DEV - 1)))
    for j, (local, frame) in enumerate(places):
        for source, taken in (
            (key_ref, jnp.logical_and(even, local)),
            (value_ref, jnp.logical_and(jnp.logical_not(even), local)),
            (pair_key_ref, jnp.logical_and(even, jnp.logical_not(local))),
            (pair_value_ref, jnp.logical_not(jnp.logical_or(even, local))),
        ):

            @pl.when(taken)
            def _(source=source, j=j, frame=frame):
                start = pl.multiple_of(frame * frame_len, frame_len)
                low_ref[j] = source[pl.ds(start, half)]
                high_ref[j] = source[pl.ds(start + half, half)]


def step_kernel(peers, slots, done, table_ref, mine_ref, got_ref, out_ref):
    me = lax.axis_index("tm")
    dyns = dyn_frames([read_table(table_ref, slot) for slot in range(slots)], peers * FR_DEV - 1)
    flags = [has_dyn(me, dyn, done) for dyn in dyns] + [has_end(me, done, peers)]
    for j, flag in enumerate(flags):
        choose(out_ref.at[j], flag, mine_ref.at[j], got_ref.at[j])


def pick_kernel(
    peers, slots, low_bit, high_bit, table_ref, pair_table_ref, low_mine, low_got, high_mine, high_got, own_ref, pair_ref
):
    me = lax.axis_index("tm")
    half = low_mine.shape[1]
    dyns = dyn_frames([read_table(table_ref, slot) for slot in range(slots)], peers * FR_DEV - 1)
    for out, table in ((own_ref, table_ref), (pair_ref, pair_table_ref)):
        for m in range(MEM):
            frame = read_table(table, slots + m)
            source = jnp.int32(len(dyns))
            for j, dyn in enumerate(dyns):
                source = jnp.where(frame == dyn, j, source)
            for start, mine, got, bit in ((0, low_mine, low_got, low_bit), (half, high_mine, high_got, high_bit)):
                upper = (me & bit) != 0
                local = jnp.where(frame == 0, jnp.logical_not(upper), upper)
                for dyn in dyns:
                    local = jnp.where(frame == dyn, has_dyn(me, dyn, (peers - 1) & ~bit), local)
                choose(out.at[m, pl.ds(start, half)], local, mine.at[source], got.at[source])


def dot(a, b, left, right):
    return lax.dot_general(a, b, (((left,), (right,)), ((), ())), preferred_element_type=F32)


def logits_of(keys, query, rows_ref, head, piece):
    frame_len = query.shape[0] // FR_DEV
    raw = dot(keys, query, 1, 1) * (FACTOR * LOG2E)
    parts = []
    for j in range(FR_DEV):
        row = piece * FR_DEV + j
        parts.append(raw[j * frame_len : (j + 1) * frame_len] + rows_ref[head, row : row + 1, :])
    return jnp.concatenate(parts, axis=0)


def stats_kernel(rows_ref, query_ref, cotangent_ref, prev_key_ref, prev_value_ref, key_ref, value_ref, stats_ref):
    for head in range(query_ref.shape[1] // DEPTH):
        cols = pl.ds(head * DEPTH, DEPTH)
        query, cotangent = query_ref[:, cols], cotangent_ref[:, cols]
        logits = [
            logits_of(keys[:, cols], query, rows_ref, head, piece) for piece, keys in enumerate((prev_key_ref, key_ref))
        ]
        peak = functools.reduce(jnp.maximum, [jnp.max(block, axis=0, keepdims=True) for block in logits])
        exps = [jnp.exp2(block - peak) for block in logits]
        slopes = [dot(values[:, cols], cotangent, 1, 1) for values in (prev_value_ref, value_ref)]
        stats_ref[head, 0:1, :] = peak
        stats_ref[head, 1:2, :] = sum(jnp.sum(e, axis=0, keepdims=True) for e in exps)
        stats_ref[head, 2:3, :] = sum(jnp.sum(e * s, axis=0, keepdims=True) for e, s in zip(exps, slopes))


def memory_kernel(
    rows_ref, part_ref, query_ref, cotangent_ref, mine_ref, got_ref, stats_ref, mem_same_ref, mem_other_ref
):
    even = (lax.axis_index("tm") & 1) == 0
    frame_len = mine_ref.shape[1]
    for head in range(query_ref.shape[1] // DEPTH):
        cols = pl.ds(head * DEPTH, DEPTH)
        query, cotangent = query_ref[:, cols], cotangent_ref[:, cols]
        mine = mine_ref[:, :, cols].reshape(MEM * frame_len, DEPTH)
        got = got_ref[:, :, cols].reshape(MEM * frame_len, DEPTH)
        keys, values = jnp.where(even, mine, got), jnp.where(even, got, mine)
        logits = logits_of(keys, query, rows_ref, head, 2)
        part_peak = part_ref[head, 0:1, :]
        peak = jnp.maximum(part_peak, jnp.max(logits, axis=0, keepdims=True))
        exps = jnp.exp2(logits - peak)
        slopes = dot(values, cotangent, 1, 1)
        scale = jnp.exp2(part_peak - peak)
        total = part_ref[head, 1:2, :] * scale + jnp.sum(exps, axis=0, keepdims=True)
        inverse = 1.0 / total
        spread = (part_ref[head, 2:3, :] * scale + jnp.sum(exps * slopes, axis=0, keepdims=True)) * inverse
        stats_ref[head, 0:1, :] = peak
        stats_ref[head, 1:2, :] = inverse
        stats_ref[head, 2:3, :] = spread
        probs = exps * inverse
        dlogits = (probs * (slopes - spread)).astype(BF16)
        key_part = (dot(dlogits, query, 1, 0) * FACTOR).astype(BF16).reshape(MEM, frame_len, DEPTH)
        value_part = dot(probs.astype(BF16), cotangent, 1, 0).astype(BF16).reshape(MEM, frame_len, DEPTH)
        mem_same_ref[:, :, cols] = jnp.where(even, key_part, value_part)
        mem_other_ref[:, :, cols] = jnp.where(even, value_part, key_part)


def probs_of(keys, values, query, cotangent, rows_ref, stats_ref, head, piece):
    logits = logits_of(keys, query, rows_ref, head, piece)
    probs = jnp.exp2(logits - stats_ref[head, 0:1, :]) * stats_ref[head, 1:2, :]
    dlogits = probs * (dot(values, cotangent, 1, 1) - stats_ref[head, 2:3, :])
    return probs.astype(BF16), dlogits.astype(BF16)


def back_kernel(rows_ref, stats_ref, query_ref, cotangent_ref, prev_key_ref, prev_value_ref, back_ref):
    for head in range(query_ref.shape[1] // DEPTH):
        cols = pl.ds(head * DEPTH, DEPTH)
        query, cotangent = query_ref[:, cols], cotangent_ref[:, cols]
        weights, dlogits = probs_of(
            prev_key_ref[:, cols], prev_value_ref[:, cols], query, cotangent, rows_ref, stats_ref, head, 0
        )
        back_ref[0, :, cols] = (dot(dlogits, query, 1, 0) * FACTOR).astype(BF16)
        back_ref[1, :, cols] = dot(weights, cotangent, 1, 0).astype(BF16)


def rest_kernel(
    rows_ref,
    stats_ref,
    query_ref,
    cotangent_ref,
    prev_key_ref,
    prev_value_ref,
    key_ref,
    value_ref,
    mine_ref,
    got_ref,
    attended_ref,
    grad_query_ref,
    own_ref,
):
    even = (lax.axis_index("tm") & 1) == 0
    frame_len = mine_ref.shape[1]
    for head in range(query_ref.shape[1] // DEPTH):
        cols = pl.ds(head * DEPTH, DEPTH)
        query, cotangent = query_ref[:, cols], cotangent_ref[:, cols]
        mine = mine_ref[:, :, cols].reshape(MEM * frame_len, DEPTH)
        got = got_ref[:, :, cols].reshape(MEM * frame_len, DEPTH)
        pieces = (
            (prev_key_ref[:, cols], prev_value_ref[:, cols]),
            (key_ref[:, cols], value_ref[:, cols]),
            (jnp.where(even, mine, got), jnp.where(even, got, mine)),
        )
        attended = grad_query = 0.0
        for piece, (keys, values) in enumerate(pieces):
            weights, dlogits = probs_of(keys, values, query, cotangent, rows_ref, stats_ref, head, piece)
            attended += dot(values, weights, 0, 0)
            grad_query += dot(keys, dlogits, 0, 0)
            if piece == 1:
                own_ref[0, :, cols] = dot(dlogits, query, 1, 0) * FACTOR
                own_ref[1, :, cols] = dot(weights, cotangent, 1, 0)
        attended_ref[:, cols] = attended.T.astype(BF16)
        grad_query_ref[:, cols] = (grad_query * FACTOR).T.astype(BF16)


def sum_kernel(
    peers,
    slots,
    low_bit,
    high_bit,
    table_ref,
    pair_table_ref,
    mine_ref,
    got_ref,
    low_keep,
    low_send,
    high_keep,
    high_send,
):
    me = lax.axis_index("tm")
    half = mine_ref.shape[1] // 2
    last_frame = peers * FR_DEV - 1
    dyns = dyn_frames([read_table(table_ref, slot) for slot in range(slots)], last_frame)
    named = [(read_table(table_ref, slots + m), mine_ref, m) for m in range(MEM)]
    named += [(read_table(pair_table_ref, slots + m), got_ref, m) for m in range(MEM)]
    for start, keep, send, bit in ((0, low_keep, low_send, low_bit), (half, high_keep, high_send, high_bit)):
        upper = (me & bit) != 0
        near = jnp.where(upper, last_frame, 0)
        far = jnp.where(upper, 0, last_frame)
        part = pl.ds(start, half)
        terms = [ref[m, part].astype(F32) for _, ref, m in named]

        def total(frame):
            return sum(jnp.where(name == frame, term, 0.0) for (name, _, _), term in zip(named, terms))

        for j, dyn in enumerate(dyns):
            value = total(dyn)
            keep[j] = value
            send[j] = value.astype(BF16)
        keep[len(dyns)] = total(near)
        send[len(dyns)] = total(far).astype(BF16)


def add_kernel(keep_ref, got_ref, out_ref, send_ref):
    value = keep_ref[...] + got_ref[...].astype(F32)
    out_ref[...] = value
    send_ref[...] = value.astype(BF16)


def owned_kernel(peers, slots, table_ref, low_keep, low_got, high_keep, high_got, mine_ref, pair_ref):
    me = lax.axis_index("tm")
    half = low_keep.shape[1]
    last_frame = peers * FR_DEV - 1
    dyns = dyn_frames([read_table(table_ref, slot) for slot in range(slots)], last_frame)
    for start, keep, got in ((0, low_keep, low_got), (half, high_keep, high_got)):
        part = pl.ds(start, half)
        for out, group in ((mine_ref, me), (pair_ref, me ^ 1)):
            for j in range(FR_DEV):
                frame = group * FR_DEV + j
                named = jnp.logical_or(frame == 0, frame == last_frame)
                place = jnp.int32(len(dyns))
                for d, dyn in enumerate(dyns):
                    named = jnp.logical_or(named, frame == dyn)
                    place = jnp.where(frame == dyn, d, place)

                @pl.when(named)
                def _(out=out, j=j, place=place, keep=keep, got=got, part=part):
                    value = keep[place] + got[place].astype(F32)
                    out[j, part] = value.astype(out.dtype)

                @pl.when(jnp.logical_not(named))
                def _(out=out, j=j, part=part):
                    out[j, part] = jnp.zeros((half, out.shape[2]), out.dtype)


def final_kernel(own_ref, back_inner_ref, back_outer_ref, mine_ref, got_ref, grad_key_ref, grad_value_ref):
    even = (lax.axis_index("tm") & 1) == 0
    rows = grad_key_ref.shape
    mine = mine_ref[...].reshape(rows)
    got = got_ref[...].astype(F32).reshape(rows)
    back = jnp.where(even, back_inner_ref[...], back_outer_ref[...]).astype(F32)
    grad_key_ref[...] = (own_ref[0] + back[0] + jnp.where(even, mine, got)).astype(BF16)
    grad_value_ref[...] = (own_ref[1] + back[1] + jnp.where(even, got, mine)).astype(BF16)


def body(
    query_states,
    key_states,
    value_states,
    grad_out,
    camera_pose,
    pose_bias,
    memory_index,
    bank_frames,
):
    row_count, width = query_states.shape
    frame_len = row_count // FR_DEV
    half = frame_len // 2
    heads = pose_bias.shape[0]
    slots = bank_frames.shape[0]
    kept = slots - 1
    peers = lax.axis_size("tm")
    bits = [1 << i for i in range(1, peers.bit_length() - 1)]
    even = (lax.axis_index("tm") & 1) == 0
    piece_flops = 2 * row_count * row_count * width

    outer_keys = shift(key_states, 1, 1, peers)
    outer_values = shift(value_states, 1, 1, peers)
    pair_values = shift(value_states, 1, 0, peers)
    pair_keys = shift(key_states, -1, 1, peers)
    inner_keys = shift(key_states, 1, 0, peers)

    table_rows = -(-(slots + MEM) // 8) * 8
    bias_rows = -(-(2 * FR_DEV + MEM) // 8) * 8
    table, rows = call(
        functools.partial(table_kernel, peers),
        [shape(jnp.int32, table_rows, 128), shape(F32, heads, bias_rows, row_count)],
        [],
        scalars=[bank_frames, memory_index, camera_pose, pose_bias],
        name="table",
    )
    pair_table = swap(table, 1, peers)
    halves = shape(BF16, kept, half, width)
    sums = shape(F32, kept, half, width)
    low, high = call(
        functools.partial(split_kernel, peers, slots),
        [halves] * 2,
        [table, key_states, value_states, pair_keys, pair_values],
        name="split",
    )
    low_done = high_done = 1
    low_got = swap(low, bits[0], peers)
    high_got = swap(high, bits[-1], peers)
    prev_keys = jnp.where(even, outer_keys, inner_keys)
    prev_values = jnp.where(even, outer_values, pair_values)
    stats = shape(F32, heads, 8, row_count)
    (part,) = call(
        stats_kernel,
        [stats],
        [rows, query_states, grad_out, prev_keys, prev_values, key_states, value_states],
        flops=4 * piece_flops,
        name="stats",
    )
    for step in range(1, len(bits)):
        low_done |= bits[step - 1]
        high_done |= bits[-step]
        (high,) = call(
            functools.partial(step_kernel, peers, slots, high_done & ~bits[-step]),
            [halves],
            [table, high, high_got],
            name="step_high",
        )
        high_got = swap(high, bits[-step - 1], peers)
        (low,) = call(
            functools.partial(step_kernel, peers, slots, low_done & ~bits[step - 1]),
            [halves],
            [table, low, low_got],
            name="step_low",
        )
        low_got = swap(low, bits[step], peers)
    chosen = shape(BF16, MEM, frame_len, width)
    mem_mine, mem_send = call(
        functools.partial(pick_kernel, peers, slots, bits[-1], bits[0]),
        [chosen] * 2,
        [table, pair_table, low, low_got, high, high_got],
        after=[part],
        name="pick",
    )
    mem_got = swap(mem_send, 1, peers)

    stats_all, mem_same, mem_other = call(
        memory_kernel,
        [stats, chosen, chosen],
        [rows, part, query_states, grad_out, mem_mine, mem_got],
        flops=4 * piece_flops,
        name="memory",
    )
    same_got = swap(mem_other, 1, peers)
    (back,) = call(
        back_kernel,
        [shape(BF16, 2, row_count, width)],
        [rows, stats_all, query_states, grad_out, prev_keys, prev_values],
        flops=4 * piece_flops,
        name="back",
    )
    back_outer = shift(back, -1, 2, peers)
    back_inner = shift(back, -1, 1, peers)
    low_keep, low_send, high_keep, high_send = call(
        functools.partial(sum_kernel, peers, slots, bits[-1], bits[0]),
        [sums, halves] * 2,
        [table, pair_table, mem_same, same_got],
        after=[back],
        name="sum",
    )
    low_got = swap(low_send, bits[-1], peers)
    high_got = swap(high_send, bits[0], peers)
    attended, grad_query, own = call(
        rest_kernel,
        [shape(BF16, row_count, width)] * 2 + [shape(F32, 2, row_count, width)],
        [
            rows,
            stats_all,
            query_states,
            grad_out,
            prev_keys,
            prev_values,
            key_states,
            value_states,
            mem_mine,
            mem_got,
        ],
        flops=14 * piece_flops,
        name="rest",
    )
    for step in range(1, len(bits)):
        low_keep, low_send = call(add_kernel, [sums, halves], [low_keep, low_got], name="add_low")
        low_got = swap(low_send, bits[-step - 1], peers)
        high_keep, high_send = call(add_kernel, [sums, halves], [high_keep, high_got], name="add_high")
        high_got = swap(high_send, bits[step], peers)
    owned = shape(F32, FR_DEV, frame_len, width)
    owned_mine, owned_send = call(
        functools.partial(owned_kernel, peers, slots),
        [owned, shape(BF16, FR_DEV, frame_len, width)],
        [table, low_keep, low_got, high_keep, high_got],
        after=[own],
        name="owned",
    )
    owned_got = swap(owned_send, 1, peers)
    grad_key, grad_value = call(
        final_kernel,
        [shape(BF16, row_count, width)] * 2,
        [own, back_inner, back_outer, owned_mine, owned_got],
        name="final",
    )
    return (attended, grad_query, grad_key, grad_value)


def solution(mesh):
    rows = P(("traj", "tm"), None)
    in_specs = (rows, rows, rows, rows, P("traj"), P(), rows, P("traj"))
    return jax.shard_map(body, mesh=mesh, in_specs=in_specs, out_specs=(rows,) * 4, check_vma=False)
```

```python
import functools
import math

import jax
import jax.numpy as jnp
from jax import lax
from jax.experimental import pallas as pl
from jax.experimental.pallas import tpu as pltpu
from jax.sharding import PartitionSpec as P

FR_DEV = 2
MEM = 2
DEPTH = 128
TAIL = 16

BLOCKED_LOGIT = -1e30
LOG2E = math.log2(math.e)
FACTOR = 1.0 / math.sqrt(DEPTH)

SMEM = pl.BlockSpec(memory_space=pltpu.SMEM)
VMEM = pl.BlockSpec(memory_space=pltpu.VMEM)
ANY = pl.BlockSpec(memory_space=pl.ANY)
VMEM_LIMIT = 32 * 1024 * 1024
BF16, F32 = jnp.bfloat16, jnp.float32


def shape(dtype, *dims):
    return jax.ShapeDtypeStruct(dims, dtype)


def call(kernel, outs, arrays, scalars=(), after=(), flops=0, name=None):
    count = len(scalars) + len(arrays)

    def run(*refs):
        kernel(*refs[:count], *refs[count + len(after) :])

    return pl.pallas_call(
        run,
        out_shape=outs,
        in_specs=[SMEM] * len(scalars) + [VMEM] * len(arrays) + [ANY] * len(after),
        out_specs=[VMEM] * len(outs),
        compiler_params=pltpu.CompilerParams(vmem_limit_bytes=VMEM_LIMIT),
        cost_estimate=pl.CostEstimate(flops=flops, bytes_accessed=0, transcendentals=0) if flops else None,
        name=name,
    )(*scalars, *arrays, *after)


def swap(block, even_bit, odd_bit, peers):
    return lax.ppermute(block, "tm", [(i, i ^ (odd_bit if i & 1 else even_bit)) for i in range(peers)])


def shift(block, by, start, peers):
    pairs = [(i, i + by) for i in range(start, peers, 2) if 0 <= i + by < peers]
    return lax.ppermute(block, "tm", pairs)


def lane_value(row, lane):
    lanes = lax.broadcasted_iota(jnp.int32, row.shape, 1)
    return jnp.max(jnp.where(lanes == lane, row, 0))


def bank_of(bank_ref):
    row = bank_ref[...]
    return [lane_value(row, slot) for slot in range(row.shape[1])]


def own_picks(bank_ref, index_ref):
    return [lane_value(bank_ref[...], lane_value(index_ref[...], m)) for m in range(MEM)]


def pair_picks(bank_ref, pair_ref):
    start = pair_ref.shape[0] - TAIL
    picks = []
    for m in range(MEM):
        slot = jnp.max(pair_ref[start : start + TAIL, m * DEPTH : (m + 1) * DEPTH].astype(F32)).astype(jnp.int32)
        picks.append(lane_value(bank_ref[...], slot))
    return picks


def dyn_frames(bank, last_frame):
    found = [jnp.int32(0)] * (len(bank) - 2)
    seen = jnp.int32(0)
    for frame in bank:
        free = jnp.logical_and(frame != 0, frame != last_frame)
        for j in range(len(found)):
            found[j] = jnp.where(jnp.logical_and(free, seen == j), frame, found[j])
        seen = seen + free.astype(jnp.int32)
    return found


def place_of(frame, dyns):
    place = jnp.int32(len(dyns))
    for j, dyn in enumerate(dyns):
        place = jnp.where(frame == dyn, j, place)
    return place


def choose(out, take_first, first, second):
    @pl.when(take_first)
    def _():
        out[...] = first[...]

    @pl.when(jnp.logical_not(take_first))
    def _():
        out[...] = second[...]


def has_end(me, done, peers):
    return jnp.logical_or((me & ~done) == 0, (me | done) == peers - 1)


def has_dyn(me, frame, done):
    return ((me ^ (frame // FR_DEV)) & ~done) == 0


def by_role(me, even_value, odd_value):
    return jnp.where((me & 1) == 0, even_value, odd_value)


def join_kernel(index_ref, key_ref, value_ref, joined_ref, index_buf, sems):
    rows = key_ref.shape[0]
    copies = [
        pltpu.make_async_copy(index_ref, index_buf, sems.at[0]),
        pltpu.make_async_copy(key_ref, joined_ref.at[pl.ds(0, rows)], sems.at[1]),
        pltpu.make_async_copy(value_ref, joined_ref.at[pl.ds(rows, rows)], sems.at[2]),
    ]
    for copy in copies:
        copy.start()
    copies[0].wait()
    width = joined_ref.shape[1]
    lane = lax.broadcasted_iota(jnp.int32, (TAIL, width), 1) // DEPTH
    tail = jnp.zeros((TAIL, width), jnp.int32)
    for m in range(MEM):
        tail = jnp.where(lane == m, index_buf[0:1, m : m + 1], tail)
    joined_ref[2 * rows : 2 * rows + TAIL, :] = tail.astype(F32).astype(BF16)
    copies[1].wait()
    copies[2].wait()


def bias_kernel(bank_ref, index_ref, pose_ref, bias_ref, rows_ref):
    me = lax.axis_index("tm")
    heads, _, row_count = rows_ref.shape
    mem_ids = [bank_ref[0, index_ref[0, m]] for m in range(MEM)]
    own_ids = [me * FR_DEV + j for j in range(FR_DEV)]
    prev_ids = [jnp.maximum(own - FR_DEV, 0) for own in own_ids]
    query_poses = [pose_ref[frame] for frame in own_ids]
    key_poses = [pose_ref[frame] for frame in prev_ids + own_ids + mem_ids]
    frame_of = lax.broadcasted_iota(jnp.int32, (1, row_count), 1) // (row_count // FR_DEV)
    for head in range(heads):
        for j, key_pose in enumerate(key_poses):
            row = jnp.zeros((1, row_count), F32)
            for a, query_pose in enumerate(query_poses):
                value = bias_ref[head, query_pose, key_pose] * LOG2E
                if j < FR_DEV:
                    value = jnp.where(me == 0, BLOCKED_LOGIT, value)
                row = jnp.where(frame_of == a, value, row)
            rows_ref[head, j : j + 1, :] = row


def split_kernel(peers, bank_ref, mine_ref, pair_ref, out_ref):
    me = lax.axis_index("tm")
    frame_len = out_ref.shape[1]
    dyns = dyn_frames(bank_of(bank_ref), peers * FR_DEV - 1)
    places = [(has_dyn(me, dyn, 0), dyn % FR_DEV) for dyn in dyns]
    places.append((has_end(me, 0, peers), jnp.where(me < peers // 2, 0, FR_DEV - 1)))
    for j, (local, frame) in enumerate(places):
        start = pl.multiple_of(((me & 1) * FR_DEV + frame) * frame_len, frame_len)
        part = pl.ds(start, frame_len)
        choose(out_ref.at[j], local, mine_ref.at[part], pair_ref.at[part])


def step_kernel(peers, even_done, odd_done, bank_ref, mine_ref, got_ref, out_ref):
    me = lax.axis_index("tm")
    done = by_role(me, even_done, odd_done)
    dyns = dyn_frames(bank_of(bank_ref), peers * FR_DEV - 1)
    flags = [has_dyn(me, dyn, done) for dyn in dyns] + [has_end(me, done, peers)]
    for j, flag in enumerate(flags):
        choose(out_ref.at[j], flag, mine_ref.at[j], got_ref.at[j])


def pick_kernel(peers, even_bit, odd_bit, bank_ref, index_ref, pair_ref, mine_ref, got_ref, own_out, pair_out):
    me = lax.axis_index("tm")
    bit = by_role(me, even_bit, odd_bit)
    upper = (me & bit) != 0
    dyns = dyn_frames(bank_of(bank_ref), peers * FR_DEV - 1)
    for out, frames in ((own_out, own_picks(bank_ref, index_ref)), (pair_out, pair_picks(bank_ref, pair_ref))):
        for m, frame in enumerate(frames):
            source = place_of(frame, dyns)
            local = jnp.where(frame == 0, jnp.logical_not(upper), upper)
            local = jnp.where(source < len(dyns), has_dyn(me, frame, (peers - 1) & ~bit), local)
            choose(out.at[m], local, mine_ref.at[source], got_ref.at[source])


def dot(a, b, left, right):
    return lax.dot_general(a, b, (((left,), (right,)), ((), ())), preferred_element_type=F32)


def logits_of(keys, query, rows_ref, head, piece):
    frame_len = query.shape[0] // FR_DEV
    raw = dot(keys, query, 1, 1) * (FACTOR * LOG2E)
    parts = []
    for j in range(FR_DEV):
        row = piece * FR_DEV + j
        parts.append(raw[j * frame_len : (j + 1) * frame_len] + rows_ref[head, row : row + 1, :])
    return jnp.concatenate(parts, axis=0)


def joined_parts(joined_ref, cols):
    rows = (joined_ref.shape[0] - TAIL) // 2
    return joined_ref[0:rows, cols], joined_ref[rows : 2 * rows, cols]


def stats_kernel(rows_ref, query_ref, cotangent_ref, prev_ref, own_ref, stats_ref):
    for head in range(query_ref.shape[1] // DEPTH):
        cols = pl.ds(head * DEPTH, DEPTH)
        query, cotangent = query_ref[:, cols], cotangent_ref[:, cols]
        pieces = [joined_parts(ref, cols) for ref in (prev_ref, own_ref)]
        logits = [logits_of(keys, query, rows_ref, head, piece) for piece, (keys, _) in enumerate(pieces)]
        peak = functools.reduce(jnp.maximum, [jnp.max(block, axis=0, keepdims=True) for block in logits])
        exps = [jnp.exp2(block - peak) for block in logits]
        slopes = [dot(values, cotangent, 1, 1) for _, values in pieces]
        stats_ref[head, 0:1, :] = peak
        stats_ref[head, 1:2, :] = sum(jnp.sum(e, axis=0, keepdims=True) for e in exps)
        stats_ref[head, 2:3, :] = sum(jnp.sum(e * s, axis=0, keepdims=True) for e, s in zip(exps, slopes))


def memory_kernel(
    rows_ref, part_ref, query_ref, cotangent_ref, mine_ref, got_ref, stats_ref, mem_same_ref, mem_other_ref
):
    even = (lax.axis_index("tm") & 1) == 0
    frame_len = mine_ref.shape[1]
    for head in range(query_ref.shape[1] // DEPTH):
        cols = pl.ds(head * DEPTH, DEPTH)
        query, cotangent = query_ref[:, cols], cotangent_ref[:, cols]
        mine = mine_ref[:, :, cols].reshape(MEM * frame_len, DEPTH)
        got = got_ref[:, :, cols].reshape(MEM * frame_len, DEPTH)
        keys, values = jnp.where(even, mine, got), jnp.where(even, got, mine)
        logits = logits_of(keys, query, rows_ref, head, 2)
        part_peak = part_ref[head, 0:1, :]
        peak = jnp.maximum(part_peak, jnp.max(logits, axis=0, keepdims=True))
        exps = jnp.exp2(logits - peak)
        slopes = dot(values, cotangent, 1, 1)
        scale = jnp.exp2(part_peak - peak)
        total = part_ref[head, 1:2, :] * scale + jnp.sum(exps, axis=0, keepdims=True)
        inverse = 1.0 / total
        spread = (part_ref[head, 2:3, :] * scale + jnp.sum(exps * slopes, axis=0, keepdims=True)) * inverse
        stats_ref[head, 0:1, :] = peak
        stats_ref[head, 1:2, :] = inverse
        stats_ref[head, 2:3, :] = spread
        probs = exps * inverse
        dlogits = (probs * (slopes - spread)).astype(BF16)
        key_part = (dot(dlogits, query, 1, 0) * FACTOR).astype(BF16).reshape(MEM, frame_len, DEPTH)
        value_part = dot(probs.astype(BF16), cotangent, 1, 0).astype(BF16).reshape(MEM, frame_len, DEPTH)
        mem_same_ref[:, :, cols] = jnp.where(even, key_part, value_part)
        mem_other_ref[:, :, cols] = jnp.where(even, value_part, key_part)


def probs_of(keys, values, query, cotangent, rows_ref, stats_ref, head, piece):
    logits = logits_of(keys, query, rows_ref, head, piece)
    probs = jnp.exp2(logits - stats_ref[head, 0:1, :]) * stats_ref[head, 1:2, :]
    dlogits = probs * (dot(values, cotangent, 1, 1) - stats_ref[head, 2:3, :])
    return probs.astype(BF16), dlogits.astype(BF16)


def back_kernel(rows_ref, stats_ref, query_ref, cotangent_ref, prev_ref, back_ref):
    for head in range(query_ref.shape[1] // DEPTH):
        cols = pl.ds(head * DEPTH, DEPTH)
        query, cotangent = query_ref[:, cols], cotangent_ref[:, cols]
        keys, values = joined_parts(prev_ref, cols)
        weights, dlogits = probs_of(keys, values, query, cotangent, rows_ref, stats_ref, head, 0)
        back_ref[0, :, cols] = (dot(dlogits, query, 1, 0) * FACTOR).astype(BF16)
        back_ref[1, :, cols] = dot(weights, cotangent, 1, 0).astype(BF16)


def rest_kernel(
    rows_ref,
    stats_ref,
    query_ref,
    cotangent_ref,
    prev_ref,
    joined_ref,
    mine_ref,
    got_ref,
    attended_ref,
    grad_query_ref,
    own_ref,
):
    even = (lax.axis_index("tm") & 1) == 0
    frame_len = mine_ref.shape[1]
    for head in range(query_ref.shape[1] // DEPTH):
        cols = pl.ds(head * DEPTH, DEPTH)
        query, cotangent = query_ref[:, cols], cotangent_ref[:, cols]
        mine = mine_ref[:, :, cols].reshape(MEM * frame_len, DEPTH)
        got = got_ref[:, :, cols].reshape(MEM * frame_len, DEPTH)
        pieces = (
            joined_parts(prev_ref, cols),
            joined_parts(joined_ref, cols),
            (jnp.where(even, mine, got), jnp.where(even, got, mine)),
        )
        attended = grad_query = 0.0
        for piece, (keys, values) in enumerate(pieces):
            weights, dlogits = probs_of(keys, values, query, cotangent, rows_ref, stats_ref, head, piece)
            attended += dot(values, weights, 0, 0)
            grad_query += dot(keys, dlogits, 0, 0)
            if piece == 1:
                own_ref[0, :, cols] = dot(dlogits, query, 1, 0) * FACTOR
                own_ref[1, :, cols] = dot(weights, cotangent, 1, 0)
        attended_ref[:, cols] = attended.T.astype(BF16)
        grad_query_ref[:, cols] = (grad_query * FACTOR).T.astype(BF16)


def sum_kernel(
    peers, even_bit, odd_bit, bank_ref, index_ref, pair_ref, mine_ref, got_ref, keep_ref, send_ref
):
    me = lax.axis_index("tm")
    last_frame = peers * FR_DEV - 1
    dyns = dyn_frames(bank_of(bank_ref), last_frame)
    named = [(frame, mine_ref, m) for m, frame in enumerate(own_picks(bank_ref, index_ref))]
    named += [(frame, got_ref, m) for m, frame in enumerate(pair_picks(bank_ref, pair_ref))]
    upper = (me & by_role(me, even_bit, odd_bit)) != 0
    near = jnp.where(upper, last_frame, 0)
    far = jnp.where(upper, 0, last_frame)
    terms = [ref[m].astype(F32) for _, ref, m in named]

    def total(frame):
        return sum(jnp.where(name == frame, term, 0.0) for (name, _, _), term in zip(named, terms))

    for j, dyn in enumerate(dyns):
        value = total(dyn)
        keep_ref[j] = value
        send_ref[j] = value.astype(BF16)
    keep_ref[len(dyns)] = total(near)
    send_ref[len(dyns)] = total(far).astype(BF16)


def add_kernel(keep_ref, got_ref, out_ref, send_ref):
    value = keep_ref[...] + got_ref[...].astype(F32)
    out_ref[...] = value
    send_ref[...] = value.astype(BF16)


def owned_kernel(peers, bank_ref, keep_ref, got_ref, mine_ref, pair_ref):
    me = lax.axis_index("tm")
    last_frame = peers * FR_DEV - 1
    dyns = dyn_frames(bank_of(bank_ref), last_frame)
    for out, group in ((mine_ref, me), (pair_ref, me ^ 1)):
        for j in range(FR_DEV):
            frame = group * FR_DEV + j
            place = place_of(frame, dyns)
            named = jnp.logical_or(place < len(dyns), jnp.logical_or(frame == 0, frame == last_frame))

            @pl.when(named)
            def _(out=out, j=j, place=place):
                value = keep_ref[place] + got_ref[place].astype(F32)
                out[j] = value.astype(out.dtype)

            @pl.when(jnp.logical_not(named))
            def _(out=out, j=j):
                out[j] = jnp.zeros(out.shape[1:], out.dtype)


def final_kernel(own_ref, back_inner_ref, back_outer_ref, mine_ref, got_ref, grad_key_ref, grad_value_ref):
    even = (lax.axis_index("tm") & 1) == 0
    rows = grad_key_ref.shape
    mine = mine_ref[...].reshape(rows)
    got = got_ref[...].astype(F32).reshape(rows)
    back = jnp.where(even, back_inner_ref[...], back_outer_ref[...]).astype(F32)
    grad_key_ref[...] = (own_ref[0] + back[0] + jnp.where(even, mine, got)).astype(BF16)
    grad_value_ref[...] = (own_ref[1] + back[1] + jnp.where(even, got, mine)).astype(BF16)


def body(
    query_states,
    key_states,
    value_states,
    grad_out,
    camera_pose,
    pose_bias,
    memory_index,
    bank_frames,
):
    row_count, width = query_states.shape
    frame_len = row_count // FR_DEV
    heads = pose_bias.shape[0]
    slots = bank_frames.shape[0]
    peers = lax.axis_size("tm")
    bits = [1 << i for i in range(1, peers.bit_length() - 1)]
    turns = list(zip(bits, bits[::-1]))
    even = (lax.axis_index("tm") & 1) == 0
    piece_flops = 2 * row_count * row_count * width
    bank_frames = bank_frames.reshape(1, slots)
    last_bits = turns[-1]

    joined_rows = 2 * row_count + TAIL
    joined = pl.pallas_call(
        join_kernel,
        out_shape=shape(BF16, joined_rows, width),
        in_specs=[pl.BlockSpec(memory_space=pltpu.HBM)] * 3,
        out_specs=VMEM,
        scratch_shapes=[pltpu.VMEM(memory_index.shape, jnp.int32), pltpu.SemaphoreType.DMA((3,))],
        compiler_params=pltpu.CompilerParams(vmem_limit_bytes=VMEM_LIMIT),
        name="join",
    )(*(pltpu.with_memory_space_constraint(x, pltpu.HBM) for x in (memory_index, key_states, value_states)))
    outer = shift(joined, 1, 1, peers)
    pair = swap(joined, 1, 1, peers)

    bias_rows = -(-(2 * FR_DEV + MEM) // 8) * 8
    (rows,) = call(
        bias_kernel,
        [shape(F32, heads, bias_rows, row_count)],
        [],
        scalars=[bank_frames, memory_index, camera_pose, pose_bias],
        flops=piece_flops,
        name="bias",
    )
    held = shape(BF16, slots - 1, frame_len, width)
    sums = shape(F32, slots - 1, frame_len, width)
    (mine,) = call(functools.partial(split_kernel, peers), [held], [bank_frames, joined, pair], name="split")
    prev = jnp.where(even, outer, pair)
    stats = shape(F32, heads, 8, row_count)
    (part,) = call(
        stats_kernel, [stats], [rows, query_states, grad_out, prev, joined], flops=4 * piece_flops, name="stats"
    )
    even_done = odd_done = 1
    for step, (even_bit, odd_bit) in enumerate(turns):
        got = swap(mine, even_bit, odd_bit, peers)
        if step + 1 < len(turns):
            kernel = functools.partial(step_kernel, peers, even_done, odd_done)
            (mine,) = call(kernel, [held], [bank_frames, mine, got], after=[outer], name="step")
        even_done |= even_bit
        odd_done |= odd_bit
    chosen = shape(BF16, MEM, frame_len, width)
    mem_mine, mem_send = call(
        functools.partial(pick_kernel, peers, *last_bits),
        [chosen] * 2,
        [bank_frames, memory_index, pair, mine, got],
        after=[part],
        name="pick",
    )
    mem_got = swap(mem_send, 1, 1, peers)

    stats_all, mem_same, mem_other = call(
        memory_kernel,
        [stats, chosen, chosen],
        [rows, part, query_states, grad_out, mem_mine, mem_got],
        flops=4 * piece_flops,
        name="memory",
    )
    same_got = swap(mem_other, 1, 1, peers)
    (back,) = call(
        back_kernel,
        [shape(BF16, 2, row_count, width)],
        [rows, stats_all, query_states, grad_out, prev],
        flops=4 * piece_flops,
        name="back",
    )
    back_outer = shift(back, -1, 2, peers)
    back_inner = shift(back, -1, 1, peers)
    keep, send = call(
        functools.partial(sum_kernel, peers, *last_bits),
        [sums, held],
        [bank_frames, memory_index, pair, mem_same, same_got],
        after=[back],
        name="sum",
    )
    attended, grad_query, own = call(
        rest_kernel,
        [shape(BF16, row_count, width)] * 2 + [shape(F32, 2, row_count, width)],
        [rows, stats_all, query_states, grad_out, prev, joined, mem_mine, mem_got],
        flops=14 * piece_flops,
        name="rest",
    )
    for step, (even_bit, odd_bit) in enumerate(turns[::-1]):
        got = swap(send, even_bit, odd_bit, peers)
        if step + 1 < len(turns):
            keep, send = call(add_kernel, [sums, held], [keep, got], after=[back_outer, own], name="add")
    owned = shape(F32, FR_DEV, frame_len, width)
    owned_mine, owned_send = call(
        functools.partial(owned_kernel, peers),
        [owned, shape(BF16, FR_DEV, frame_len, width)],
        [bank_frames, keep, got],
        name="owned",
    )
    owned_got = swap(owned_send, 1, 1, peers)
    grad_key, grad_value = call(
        final_kernel,
        [shape(BF16, row_count, width)] * 2,
        [own, back_inner, back_outer, owned_mine, owned_got],
        name="final",
    )
    return (attended, grad_query, grad_key, grad_value)


def solution(mesh):
    rows = P(("traj", "tm"), None)
    in_specs = (rows, rows, rows, rows, P("traj"), P(), rows, P("traj"))
    return jax.shard_map(body, mesh=mesh, in_specs=in_specs, out_specs=(rows,) * 4, check_vma=False)
```

```python
import functools
import math

import jax
import jax.numpy as jnp
from jax import lax
from jax.experimental import pallas as pl
from jax.experimental.pallas import tpu as pltpu
from jax.sharding import PartitionSpec as P

FR_DEV = 2
MEM = 2
DEPTH = 128
TAIL = 16

BLOCKED_LOGIT = -1e30
LOG2E = math.log2(math.e)
FACTOR = 1.0 / math.sqrt(DEPTH)

SMEM = pl.BlockSpec(memory_space=pltpu.SMEM)
VMEM = pl.BlockSpec(memory_space=pltpu.VMEM)
ANY = pl.BlockSpec(memory_space=pl.ANY)
HIDING = 200
VMEM_LIMIT = 32 * 1024 * 1024
BF16, F32 = jnp.bfloat16, jnp.float32


def shape(dtype, *dims):
    return jax.ShapeDtypeStruct(dims, dtype)


def call(kernel, outs, arrays, scalars=(), after=(), flops=0, name=None):
    count = len(scalars) + len(arrays)

    def run(*refs):
        kernel(*refs[:count], *refs[count + len(after) :])

    return pl.pallas_call(
        run,
        out_shape=outs,
        in_specs=[SMEM] * len(scalars) + [VMEM] * len(arrays) + [ANY] * len(after),
        out_specs=[VMEM] * len(outs),
        compiler_params=pltpu.CompilerParams(vmem_limit_bytes=VMEM_LIMIT),
        cost_estimate=pl.CostEstimate(flops=flops, bytes_accessed=0, transcendentals=0) if flops else None,
        name=name,
    )(*scalars, *arrays, *after)


def swap(block, even_bit, odd_bit, peers):
    return lax.ppermute(block, "tm", [(i, i ^ (odd_bit if i & 1 else even_bit)) for i in range(peers)])


def shift(block, by, start, peers):
    pairs = [(i, i + by) for i in range(start, peers, 2) if 0 <= i + by < peers]
    return lax.ppermute(block, "tm", pairs)


def lane_value(row, lane):
    lanes = lax.broadcasted_iota(jnp.int32, row.shape, 1)
    return jnp.max(jnp.where(lanes == lane, row, 0))


def bank_of(bank_ref):
    row = bank_ref[...]
    return [lane_value(row, slot) for slot in range(row.shape[1])]


def dyn_frames(bank, last_frame):
    found = [jnp.int32(0)] * (len(bank) - 2)
    seen = jnp.int32(0)
    for frame in bank:
        free = jnp.logical_and(frame != 0, frame != last_frame)
        for j in range(len(found)):
            found[j] = jnp.where(jnp.logical_and(free, seen == j), frame, found[j])
        seen = seen + free.astype(jnp.int32)
    return found


def place_of(frame, dyns):
    place = jnp.int32(len(dyns))
    for j, dyn in enumerate(dyns):
        place = jnp.where(frame == dyn, j, place)
    return place


def choose(out, take_first, first, second):
    @pl.when(take_first)
    def _():
        out[...] = first[...]

    @pl.when(jnp.logical_not(take_first))
    def _():
        out[...] = second[...]


def has_end(me, done, peers):
    return jnp.logical_or((me & ~done) == 0, (me | done) == peers - 1)


def has_dyn(me, frame, done):
    return ((me ^ (frame // FR_DEV)) & ~done) == 0


def by_role(me, even_value, odd_value):
    return jnp.where((me & 1) == 0, even_value, odd_value)


def join_kernel(index_ref, key_ref, value_ref, joined_ref, index_buf, sems):
    rows = key_ref.shape[0]
    copies = [
        pltpu.make_async_copy(index_ref, index_buf, sems.at[0]),
        pltpu.make_async_copy(key_ref, joined_ref.at[pl.ds(0, rows)], sems.at[1]),
        pltpu.make_async_copy(value_ref, joined_ref.at[pl.ds(rows, rows)], sems.at[2]),
    ]
    for copy in copies:
        copy.start()
    copies[0].wait()
    width = joined_ref.shape[1]
    lane = lax.broadcasted_iota(jnp.int32, (TAIL, width), 1) // DEPTH
    tail = jnp.zeros((TAIL, width), jnp.int32)
    for m in range(MEM):
        tail = jnp.where(lane == m, index_buf[0:1, m : m + 1], tail)
    joined_ref[2 * rows : 2 * rows + TAIL, :] = tail.astype(F32).astype(BF16)
    copies[1].wait()
    copies[2].wait()


def join_queries_kernel(query_ref, cotangent_ref, joined_ref, sems):
    rows = query_ref.shape[0]
    copies = [
        pltpu.make_async_copy(ref, joined_ref.at[pl.ds(j * rows, rows)], sems.at[j])
        for j, ref in enumerate((query_ref, cotangent_ref))
    ]
    for copy in copies:
        copy.start()
    for copy in copies:
        copy.wait()


def pack(fields, width):
    code = jnp.int32(0)
    for j, field in enumerate(fields):
        code = code | (field.astype(jnp.int32) << (j * width))
    return code


def field(code, j, width):
    return (code >> (j * width)) & ((1 << width) - 1)


def code_of(codes_ref, row):
    return jnp.max(codes_ref[row : row + 1, :])


PICK, SUM, OWNED = range(3)
PLACE_BITS = 4


def plan_kernel(peers, last_bits, bank_ref, index_ref, pose_ref, bias_ref, pair_ref, rows_ref, codes_ref):
    me = lax.axis_index("tm")
    last_frame = peers * FR_DEV - 1
    heads, _, row_count = rows_ref.shape
    bank = [bank_ref[0, slot] for slot in range(bank_ref.shape[1])]
    tail = pair_ref.shape[0] - TAIL
    pair_ids = []
    for m in range(MEM):
        slot = jnp.max(pair_ref[tail : tail + TAIL, m * DEPTH : (m + 1) * DEPTH].astype(F32)).astype(jnp.int32)
        pair_ids.append(bank_ref[0, slot])
    mem_ids = [bank_ref[0, index_ref[0, m]] for m in range(MEM)]

    own_ids = [me * FR_DEV + j for j in range(FR_DEV)]
    prev_ids = [jnp.maximum(own - FR_DEV, 0) for own in own_ids]
    next_ids = [jnp.minimum(own + FR_DEV, last_frame) for own in own_ids]
    key_ids = prev_ids + own_ids + mem_ids + own_ids
    poses = [[pose_ref[frame] for frame in ids] for ids in (own_ids, next_ids, key_ids)]
    frame_of = lax.broadcasted_iota(jnp.int32, (1, row_count), 1) // (row_count // FR_DEV)
    for head in range(heads):
        for j, key_pose in enumerate(poses[2]):
            row = jnp.zeros((1, row_count), F32)
            for a, query_pose in enumerate(poses[1] if j >= 2 * FR_DEV + MEM else poses[0]):
                value = bias_ref[head, query_pose, key_pose] * LOG2E
                if j < FR_DEV:
                    value = jnp.where(me == 0, BLOCKED_LOGIT, value)
                row = jnp.where(frame_of == a, value, row)
            rows_ref[head, j : j + 1, :] = row

    dyns = dyn_frames(bank, last_frame)
    bit = by_role(me, *last_bits)
    upper = (me & bit) != 0
    picks = []
    for frame in mem_ids + pair_ids:
        source = place_of(frame, dyns)
        local = jnp.where(frame == 0, jnp.logical_not(upper), upper)
        local = jnp.where(source < len(dyns), has_dyn(me, frame, (peers - 1) & ~bit), local)
        picks.append(source * 2 + local.astype(jnp.int32))
    places = dyns + [jnp.where(upper, last_frame, 0), jnp.where(upper, 0, last_frame)]
    terms = [name == frame for frame in places for name in mem_ids + pair_ids]
    owned = []
    for group in (me, me ^ 1):
        for j in range(FR_DEV):
            frame = group * FR_DEV + j
            place = place_of(frame, dyns)
            named = jnp.logical_or(place < len(dyns), jnp.logical_or(frame == 0, frame == last_frame))
            owned.append(place * 2 + named.astype(jnp.int32))
    lanes = codes_ref.shape[1]
    for row, code in ((PICK, pack(picks, PLACE_BITS)), (SUM, pack(terms, 1)), (OWNED, pack(owned, PLACE_BITS))):
        codes_ref[row : row + 1, :] = jnp.full((1, lanes), code, jnp.int32)


def split_kernel(peers, bank_ref, mine_ref, pair_ref, out_ref):
    me = lax.axis_index("tm")
    frame_len = out_ref.shape[1]
    dyns = dyn_frames(bank_of(bank_ref), peers * FR_DEV - 1)
    places = [(has_dyn(me, dyn, 0), dyn % FR_DEV) for dyn in dyns]
    places.append((has_end(me, 0, peers), jnp.where(me < peers // 2, 0, FR_DEV - 1)))
    for j, (local, frame) in enumerate(places):
        start = pl.multiple_of(((me & 1) * FR_DEV + frame) * frame_len, frame_len)
        part = pl.ds(start, frame_len)
        choose(out_ref.at[j], local, mine_ref.at[part], pair_ref.at[part])


def step_kernel(peers, even_done, odd_done, bank_ref, mine_ref, got_ref, out_ref):
    me = lax.axis_index("tm")
    done = by_role(me, even_done, odd_done)
    dyns = dyn_frames(bank_of(bank_ref), peers * FR_DEV - 1)
    flags = [has_dyn(me, dyn, done) for dyn in dyns] + [has_end(me, done, peers)]
    for j, flag in enumerate(flags):
        choose(out_ref.at[j], flag, mine_ref.at[j], got_ref.at[j])


def pick_kernel(codes_ref, mine_ref, got_ref, own_out, pair_out):
    code = code_of(codes_ref, PICK)
    for o, out in enumerate((own_out, pair_out)):
        for m in range(MEM):
            pick = field(code, o * MEM + m, PLACE_BITS)
            source = pick >> 1
            choose(out.at[m], (pick & 1) != 0, mine_ref.at[source], got_ref.at[source])


def dot(a, b, left, right):
    return lax.dot_general(a, b, (((left,), (right,)), ((), ())), preferred_element_type=F32)


def logits_of(keys, query, rows_ref, head, piece):
    frame_len = query.shape[0] // FR_DEV
    raw = dot(keys, query, 1, 1) * (FACTOR * LOG2E)
    parts = []
    for j in range(FR_DEV):
        row = piece * FR_DEV + j
        parts.append(raw[j * frame_len : (j + 1) * frame_len] + rows_ref[head, row : row + 1, :])
    return jnp.concatenate(parts, axis=0)


def joined_parts(joined_ref, cols):
    rows = joined_ref.shape[0] // 2 // DEPTH * DEPTH
    return joined_ref[0:rows, cols], joined_ref[rows : 2 * rows, cols]


def prev_parts(outer_ref, pair_ref, cols):
    even = (lax.axis_index("tm") & 1) == 0
    parts = zip(joined_parts(outer_ref, cols), joined_parts(pair_ref, cols))
    return tuple(jnp.where(even, outer, pair) for outer, pair in parts)


def stats_kernel(rows_ref, queries_ref, outer_ref, pair_ref, own_ref, stats_ref):
    for head in range(queries_ref.shape[1] // DEPTH):
        cols = pl.ds(head * DEPTH, DEPTH)
        query, cotangent = joined_parts(queries_ref, cols)
        pieces = [prev_parts(outer_ref, pair_ref, cols), joined_parts(own_ref, cols)]
        logits = [logits_of(keys, query, rows_ref, head, piece) for piece, (keys, _) in enumerate(pieces)]
        peak = functools.reduce(jnp.maximum, [jnp.max(block, axis=0, keepdims=True) for block in logits])
        exps = [jnp.exp2(block - peak) for block in logits]
        slopes = [dot(values, cotangent, 1, 1) for _, values in pieces]
        stats_ref[head, 0:1, :] = peak
        stats_ref[head, 1:2, :] = sum(jnp.sum(e, axis=0, keepdims=True) for e in exps)
        stats_ref[head, 2:3, :] = sum(jnp.sum(e * s, axis=0, keepdims=True) for e, s in zip(exps, slopes))


def memory_kernel(rows_ref, part_ref, queries_ref, mine_ref, got_ref, stats_ref, mem_same_ref, mem_other_ref):
    even = (lax.axis_index("tm") & 1) == 0
    frame_len = mine_ref.shape[1]
    for head in range(queries_ref.shape[1] // DEPTH):
        cols = pl.ds(head * DEPTH, DEPTH)
        query, cotangent = joined_parts(queries_ref, cols)
        mine = mine_ref[:, :, cols].reshape(MEM * frame_len, DEPTH)
        got = got_ref[:, :, cols].reshape(MEM * frame_len, DEPTH)
        keys, values = jnp.where(even, mine, got), jnp.where(even, got, mine)
        logits = logits_of(keys, query, rows_ref, head, 2)
        part_peak = part_ref[head, 0:1, :]
        peak = jnp.maximum(part_peak, jnp.max(logits, axis=0, keepdims=True))
        exps = jnp.exp2(logits - peak)
        slopes = dot(values, cotangent, 1, 1)
        scale = jnp.exp2(part_peak - peak)
        total = part_ref[head, 1:2, :] * scale + jnp.sum(exps, axis=0, keepdims=True)
        inverse = 1.0 / total
        spread = (part_ref[head, 2:3, :] * scale + jnp.sum(exps * slopes, axis=0, keepdims=True)) * inverse
        stats_ref[head, 0:1, :] = peak
        stats_ref[head, 1:2, :] = inverse
        stats_ref[head, 2:3, :] = spread
        probs = exps * inverse
        dlogits = (probs * (slopes - spread)).astype(BF16)
        key_part = (dot(dlogits, query, 1, 0) * FACTOR).astype(BF16).reshape(MEM, frame_len, DEPTH)
        value_part = dot(probs.astype(BF16), cotangent, 1, 0).astype(BF16).reshape(MEM, frame_len, DEPTH)
        mem_same_ref[:, :, cols] = jnp.where(even, key_part, value_part)
        mem_other_ref[:, :, cols] = jnp.where(even, value_part, key_part)


def probs_of(keys, values, query, cotangent, rows_ref, stats_ref, head, piece):
    logits = logits_of(keys, query, rows_ref, head, piece)
    probs = jnp.exp2(logits - stats_ref[head, 0:1, :]) * stats_ref[head, 1:2, :]
    dlogits = probs * (dot(values, cotangent, 1, 1) - stats_ref[head, 2:3, :])
    return probs.astype(BF16), dlogits.astype(BF16)


def next_kernel(rows_ref, stats_ref, queries_ref, own_ref, next_ref):
    for head in range(queries_ref.shape[1] // DEPTH):
        cols = pl.ds(head * DEPTH, DEPTH)
        query, cotangent = joined_parts(queries_ref, cols)
        keys, values = joined_parts(own_ref, cols)
        weights, dlogits = probs_of(keys, values, query, cotangent, rows_ref, stats_ref, head, 3)
        next_ref[0, :, cols] = dot(dlogits, query, 1, 0) * FACTOR
        next_ref[1, :, cols] = dot(weights, cotangent, 1, 0)


def rest_kernel(
    rows_ref,
    stats_ref,
    queries_ref,
    outer_ref,
    pair_ref,
    joined_ref,
    mine_ref,
    got_ref,
    next_ref,
    attended_ref,
    grad_query_ref,
    own_ref,
):
    even = (lax.axis_index("tm") & 1) == 0
    frame_len = mine_ref.shape[1]
    for head in range(queries_ref.shape[1] // DEPTH):
        cols = pl.ds(head * DEPTH, DEPTH)
        query, cotangent = joined_parts(queries_ref, cols)
        mine = mine_ref[:, :, cols].reshape(MEM * frame_len, DEPTH)
        got = got_ref[:, :, cols].reshape(MEM * frame_len, DEPTH)
        pieces = (
            prev_parts(outer_ref, pair_ref, cols),
            joined_parts(joined_ref, cols),
            (jnp.where(even, mine, got), jnp.where(even, got, mine)),
        )
        attended = grad_query = 0.0
        for piece, (keys, values) in enumerate(pieces):
            weights, dlogits = probs_of(keys, values, query, cotangent, rows_ref, stats_ref, head, piece)
            attended += dot(values, weights, 0, 0)
            grad_query += dot(keys, dlogits, 0, 0)
            if piece == 1:
                own_ref[0, :, cols] = dot(dlogits, query, 1, 0) * FACTOR + next_ref[0, :, cols]
                own_ref[1, :, cols] = dot(weights, cotangent, 1, 0) + next_ref[1, :, cols]
        attended_ref[:, cols] = attended.T.astype(BF16)
        grad_query_ref[:, cols] = (grad_query * FACTOR).T.astype(BF16)


def sum_kernel(codes_ref, mine_ref, got_ref, keep_ref, send_ref):
    code = code_of(codes_ref, SUM)
    kept = keep_ref.shape[0]
    terms = [ref[m].astype(F32) for ref in (mine_ref, got_ref) for m in range(MEM)]
    for place in range(kept + 1):
        value = sum(
            jnp.where(field(code, place * len(terms) + t, 1) != 0, term, 0.0) for t, term in enumerate(terms)
        )
        if place < kept:
            keep_ref[place] = value
        if place != kept - 1:
            send_ref[min(place, kept - 1)] = value.astype(BF16)


def add_kernel(keep_ref, got_ref, out_ref, send_ref):
    value = keep_ref[...] + got_ref[...].astype(F32)
    out_ref[...] = value
    send_ref[...] = value.astype(BF16)


def owned_kernel(codes_ref, keep_ref, got_ref, mine_ref, pair_ref):
    code = code_of(codes_ref, OWNED)
    for o, out in enumerate((mine_ref, pair_ref)):
        for j in range(FR_DEV):
            owned = field(code, o * FR_DEV + j, PLACE_BITS)
            place = owned >> 1
            named = (owned & 1) != 0

            @pl.when(named)
            def _(out=out, j=j, place=place):
                value = keep_ref[place] + got_ref[place].astype(F32)
                out[j] = value.astype(out.dtype)

            @pl.when(jnp.logical_not(named))
            def _(out=out, j=j):
                out[j] = jnp.zeros(out.shape[1:], out.dtype)


def final_kernel(own_ref, mine_ref, got_ref, grad_key_ref, grad_value_ref):
    even = (lax.axis_index("tm") & 1) == 0
    rows = grad_key_ref.shape
    mine = mine_ref[...].reshape(rows)
    got = got_ref[...].astype(F32).reshape(rows)
    grad_key_ref[...] = (own_ref[0] + jnp.where(even, mine, got)).astype(BF16)
    grad_value_ref[...] = (own_ref[1] + jnp.where(even, got, mine)).astype(BF16)


def body(
    query_states,
    key_states,
    value_states,
    grad_out,
    camera_pose,
    pose_bias,
    memory_index,
    bank_frames,
):
    row_count, width = query_states.shape
    frame_len = row_count // FR_DEV
    heads = pose_bias.shape[0]
    slots = bank_frames.shape[0]
    peers = lax.axis_size("tm")
    bits = [1 << i for i in range(1, peers.bit_length() - 1)]
    turns = list(zip(bits, bits[::-1]))
    piece_flops = 2 * row_count * row_count * width
    bank_frames = bank_frames.reshape(1, slots)
    last_bits = turns[-1]

    def join(kernel, rows, arrays, scratch, name):
        return pl.pallas_call(
            kernel,
            out_shape=shape(BF16, rows, width),
            in_specs=[pl.BlockSpec(memory_space=pltpu.HBM)] * len(arrays),
            out_specs=VMEM,
            scratch_shapes=[*scratch, pltpu.SemaphoreType.DMA((len(arrays),))],
            compiler_params=pltpu.CompilerParams(vmem_limit_bytes=VMEM_LIMIT),
            name=name,
        )(*(pltpu.with_memory_space_constraint(array, pltpu.HBM) for array in arrays))

    joined = join(
        join_kernel,
        2 * row_count + TAIL,
        [memory_index, key_states, value_states],
        [pltpu.VMEM(memory_index.shape, jnp.int32)],
        "join",
    )
    outer = shift(joined, 1, 1, peers)
    pair = swap(joined, 1, 1, peers)
    queries = join(join_queries_kernel, 2 * row_count, [query_states, grad_out], [], "join_queries")
    next_queries = lax.ppermute(queries, "tm", [(i, i - 1) for i in range(1, peers)])

    bias_rows = -(-(3 * FR_DEV + MEM) // 8) * 8
    rows, codes = call(
        functools.partial(plan_kernel, peers, last_bits),
        [shape(F32, heads, bias_rows, row_count), shape(jnp.int32, 8, 128)],
        [pair],
        scalars=[bank_frames, memory_index, camera_pose, pose_bias],
        flops=piece_flops,
        name="plan",
    )
    held = shape(BF16, slots - 1, frame_len, width)
    sums = shape(F32, slots - 1, frame_len, width)
    (mine,) = call(functools.partial(split_kernel, peers), [held], [bank_frames, joined, pair], name="split")
    stats = shape(F32, heads, 8, row_count)
    (part,) = call(stats_kernel, [stats], [rows, queries, outer, pair, joined], flops=HIDING * piece_flops, name="stats")
    even_done = odd_done = 1
    for step, (even_bit, odd_bit) in enumerate(turns):
        got = swap(mine, even_bit, odd_bit, peers)
        if step + 1 < len(turns):
            kernel = functools.partial(step_kernel, peers, even_done, odd_done)
            (mine,) = call(kernel, [held], [bank_frames, mine, got], name="step")
        even_done |= even_bit
        odd_done |= odd_bit
    chosen = shape(BF16, MEM, frame_len, width)
    mem_mine, mem_send = call(pick_kernel, [chosen] * 2, [codes, mine, got], after=[part], name="pick")
    mem_got = swap(mem_send, 1, 1, peers)

    stats_all, mem_same, mem_other = call(
        memory_kernel,
        [stats, chosen, chosen],
        [rows, part, queries, mem_mine, mem_got],
        flops=4 * piece_flops,
        name="memory",
    )
    same_got = swap(mem_other, 1, 1, peers)
    next_stats = lax.ppermute(stats_all, "tm", [(i, i - 1) for i in range(1, peers)])
    keep, send = call(sum_kernel, [sums, held], [codes, mem_same, same_got], name="sum")
    pair_sums = shape(F32, 2, row_count, width)
    (from_next,) = call(
        next_kernel,
        [pair_sums],
        [rows, next_stats, next_queries, joined],
        flops=HIDING * piece_flops,
        name="next",
    )
    attended, grad_query, own = call(
        rest_kernel,
        [shape(BF16, row_count, width)] * 2 + [pair_sums],
        [rows, stats_all, queries, outer, pair, joined, mem_mine, mem_got, from_next],
        flops=HIDING * piece_flops,
        name="rest",
    )
    for step, (even_bit, odd_bit) in enumerate(turns[::-1]):
        got = swap(send, even_bit, odd_bit, peers)
        if step + 1 < len(turns):
            keep, send = call(add_kernel, [sums, held], [keep, got], after=[from_next], name="add")
    owned = shape(F32, FR_DEV, frame_len, width)
    owned_mine, owned_send = call(
        owned_kernel,
        [owned, shape(BF16, FR_DEV, frame_len, width)],
        [codes, keep, got],
        after=[own],
        name="owned",
    )
    owned_got = swap(owned_send, 1, 1, peers)
    grad_key, grad_value = call(
        final_kernel, [shape(BF16, row_count, width)] * 2, [own, owned_mine, owned_got], name="final"
    )
    return (attended, grad_query, grad_key, grad_value)


def solution(mesh):
    rows = P(("traj", "tm"), None)
    in_specs = (rows, rows, rows, rows, P("traj"), P(), rows, P("traj"))
    return jax.shard_map(body, mesh=mesh, in_specs=in_specs, out_specs=(rows,) * 4, check_vma=False)
```

```python
import functools
import math

import jax
import jax.numpy as jnp
from jax import lax
from jax.experimental import pallas as pl
from jax.experimental.pallas import tpu as pltpu
from jax.sharding import PartitionSpec as P

FR_DEV = 2
MEM = 2
DEPTH = 128
TAIL = 16

BLOCKED_LOGIT = -1e30
LOG2E = math.log2(math.e)
FACTOR = 1.0 / math.sqrt(DEPTH)

SMEM = pl.BlockSpec(memory_space=pltpu.SMEM)
VMEM = pl.BlockSpec(memory_space=pltpu.VMEM)
ANY = pl.BlockSpec(memory_space=pl.ANY)
HIDING = 200
VMEM_LIMIT = 32 * 1024 * 1024
BF16, F32 = jnp.bfloat16, jnp.float32


def shape(dtype, *dims):
    return jax.ShapeDtypeStruct(dims, dtype)


def call(kernel, outs, arrays, scalars=(), after=(), flops=0, name=None):
    count = len(scalars) + len(arrays)

    def run(*refs):
        kernel(*refs[:count], *refs[count + len(after) :])

    return pl.pallas_call(
        run,
        out_shape=outs,
        in_specs=[SMEM] * len(scalars) + [VMEM] * len(arrays) + [ANY] * len(after),
        out_specs=[VMEM] * len(outs),
        compiler_params=pltpu.CompilerParams(vmem_limit_bytes=VMEM_LIMIT),
        cost_estimate=pl.CostEstimate(flops=flops, bytes_accessed=0, transcendentals=0) if flops else None,
        name=name,
    )(*scalars, *arrays, *after)


def swap(block, even_bit, odd_bit, peers):
    return lax.ppermute(block, "tm", [(i, i ^ (odd_bit if i & 1 else even_bit)) for i in range(peers)])


def shift(block, by, start, peers):
    pairs = [(i, i + by) for i in range(start, peers, 2) if 0 <= i + by < peers]
    return lax.ppermute(block, "tm", pairs)


def lane_value(row, lane):
    lanes = lax.broadcasted_iota(jnp.int32, row.shape, 1)
    return jnp.max(jnp.where(lanes == lane, row, 0))


def bank_of(bank_ref):
    row = bank_ref[...]
    return [lane_value(row, slot) for slot in range(row.shape[1])]


def dyn_frames(bank, last_frame):
    found = [jnp.int32(0)] * (len(bank) - 2)
    seen = jnp.int32(0)
    for frame in bank:
        free = jnp.logical_and(frame != 0, frame != last_frame)
        for j in range(len(found)):
            found[j] = jnp.where(jnp.logical_and(free, seen == j), frame, found[j])
        seen = seen + free.astype(jnp.int32)
    return found


def place_of(frame, dyns):
    place = jnp.int32(len(dyns))
    for j, dyn in enumerate(dyns):
        place = jnp.where(frame == dyn, j, place)
    return place


def choose(out, take_first, first, second):
    @pl.when(take_first)
    def _():
        out[...] = first[...]

    @pl.when(jnp.logical_not(take_first))
    def _():
        out[...] = second[...]


def has_end(me, done, peers):
    return jnp.logical_or((me & ~done) == 0, (me | done) == peers - 1)


def has_dyn(me, frame, done):
    return ((me ^ (frame // FR_DEV)) & ~done) == 0


def by_role(me, even_value, odd_value):
    return jnp.where((me & 1) == 0, even_value, odd_value)


def join_kernel(index_ref, key_ref, value_ref, joined_ref, index_buf, sems):
    rows = key_ref.shape[0]
    copies = [
        pltpu.make_async_copy(index_ref, index_buf, sems.at[0]),
        pltpu.make_async_copy(key_ref, joined_ref.at[pl.ds(0, rows)], sems.at[1]),
        pltpu.make_async_copy(value_ref, joined_ref.at[pl.ds(rows, rows)], sems.at[2]),
    ]
    for copy in copies:
        copy.start()
    copies[0].wait()
    width = joined_ref.shape[1]
    lane = lax.broadcasted_iota(jnp.int32, (TAIL, width), 1) // DEPTH
    tail = jnp.zeros((TAIL, width), jnp.int32)
    for m in range(MEM):
        tail = jnp.where(lane == m, index_buf[0:1, m : m + 1], tail)
    joined_ref[2 * rows : 2 * rows + TAIL, :] = tail.astype(F32).astype(BF16)
    copies[1].wait()
    copies[2].wait()


def join_queries_kernel(query_ref, cotangent_ref, joined_ref, sems):
    rows = query_ref.shape[0]
    copies = [
        pltpu.make_async_copy(ref, joined_ref.at[pl.ds(j * rows, rows)], sems.at[j])
        for j, ref in enumerate((query_ref, cotangent_ref))
    ]
    for copy in copies:
        copy.start()
    for copy in copies:
        copy.wait()


def pack(fields, width):
    code = jnp.int32(0)
    for j, field in enumerate(fields):
        code = code | (field.astype(jnp.int32) << (j * width))
    return code


def field(code, j, width):
    return (code >> (j * width)) & ((1 << width) - 1)


def code_of(codes_ref, row):
    return jnp.max(codes_ref[row : row + 1, :])


PICK, SUM, OWNED = range(3)
PLACE_BITS = 4


def plan_kernel(peers, last_bits, bank_ref, index_ref, pose_ref, bias_ref, pair_ref, rows_ref, codes_ref):
    me = lax.axis_index("tm")
    last_frame = peers * FR_DEV - 1
    heads, _, row_count = rows_ref.shape
    bank = [bank_ref[0, slot] for slot in range(bank_ref.shape[1])]
    tail = pair_ref.shape[0] - TAIL
    pair_ids = []
    for m in range(MEM):
        slot = jnp.max(pair_ref[tail : tail + TAIL, m * DEPTH : (m + 1) * DEPTH].astype(F32)).astype(jnp.int32)
        pair_ids.append(bank_ref[0, slot])
    mem_ids = [bank_ref[0, index_ref[0, m]] for m in range(MEM)]

    own_ids = [me * FR_DEV + j for j in range(FR_DEV)]
    prev_ids = [jnp.maximum(own - FR_DEV, 0) for own in own_ids]
    next_ids = [jnp.minimum(own + FR_DEV, last_frame) for own in own_ids]
    key_ids = prev_ids + own_ids + mem_ids + own_ids
    poses = [[pose_ref[frame] for frame in ids] for ids in (own_ids, next_ids, key_ids)]
    frame_of = lax.broadcasted_iota(jnp.int32, (1, row_count), 1) // (row_count // FR_DEV)
    for head in range(heads):
        for j, key_pose in enumerate(poses[2]):
            row = jnp.zeros((1, row_count), F32)
            for a, query_pose in enumerate(poses[1] if j >= 2 * FR_DEV + MEM else poses[0]):
                value = bias_ref[head, query_pose, key_pose] * LOG2E
                if j < FR_DEV:
                    value = jnp.where(me == 0, BLOCKED_LOGIT, value)
                row = jnp.where(frame_of == a, value, row)
            rows_ref[head, j : j + 1, :] = row

    dyns = dyn_frames(bank, last_frame)
    bit = by_role(me, *last_bits)
    upper = (me & bit) != 0
    picks = []
    for frame in mem_ids + pair_ids:
        source = place_of(frame, dyns)
        local = jnp.where(frame == 0, jnp.logical_not(upper), upper)
        local = jnp.where(source < len(dyns), has_dyn(me, frame, (peers - 1) & ~bit), local)
        picks.append(source * 2 + local.astype(jnp.int32))
    places = dyns + [jnp.where(upper, last_frame, 0), jnp.where(upper, 0, last_frame)]
    terms = [name == frame for frame in places for name in mem_ids + pair_ids]
    owned = []
    for group in (me, me ^ 1):
        for j in range(FR_DEV):
            frame = group * FR_DEV + j
            place = place_of(frame, dyns)
            named = jnp.logical_or(place < len(dyns), jnp.logical_or(frame == 0, frame == last_frame))
            owned.append(place * 2 + named.astype(jnp.int32))
    lanes = codes_ref.shape[1]
    for row, code in ((PICK, pack(picks, PLACE_BITS)), (SUM, pack(terms, 1)), (OWNED, pack(owned, PLACE_BITS))):
        codes_ref[row : row + 1, :] = jnp.full((1, lanes), code, jnp.int32)


def split_kernel(peers, bank_ref, mine_ref, pair_ref, out_ref):
    me = lax.axis_index("tm")
    frame_len = out_ref.shape[1]
    dyns = dyn_frames(bank_of(bank_ref), peers * FR_DEV - 1)
    places = [(has_dyn(me, dyn, 0), dyn % FR_DEV) for dyn in dyns]
    places.append((has_end(me, 0, peers), jnp.where(me < peers // 2, 0, FR_DEV - 1)))
    for j, (local, frame) in enumerate(places):
        start = pl.multiple_of(((me & 1) * FR_DEV + frame) * frame_len, frame_len)
        part = pl.ds(start, frame_len)
        choose(out_ref.at[j], local, mine_ref.at[part], pair_ref.at[part])


def step_kernel(peers, even_done, odd_done, bank_ref, mine_ref, got_ref, out_ref):
    me = lax.axis_index("tm")
    done = by_role(me, even_done, odd_done)
    dyns = dyn_frames(bank_of(bank_ref), peers * FR_DEV - 1)
    flags = [has_dyn(me, dyn, done) for dyn in dyns] + [has_end(me, done, peers)]
    for j, flag in enumerate(flags):
        choose(out_ref.at[j], flag, mine_ref.at[j], got_ref.at[j])


def pick_kernel(codes_ref, mine_ref, got_ref, own_out, pair_out):
    code = code_of(codes_ref, PICK)
    for o, out in enumerate((own_out, pair_out)):
        for m in range(MEM):
            pick = field(code, o * MEM + m, PLACE_BITS)
            source = pick >> 1
            choose(out.at[m], (pick & 1) != 0, mine_ref.at[source], got_ref.at[source])


def dot(a, b, left, right):
    return lax.dot_general(a, b, (((left,), (right,)), ((), ())), preferred_element_type=F32)


def logits_of(keys, query, rows_ref, head, piece):
    frame_len = query.shape[0] // FR_DEV
    raw = dot(keys, query, 1, 1) * (FACTOR * LOG2E)
    parts = []
    for j in range(FR_DEV):
        row = piece * FR_DEV + j
        parts.append(raw[j * frame_len : (j + 1) * frame_len] + rows_ref[head, row : row + 1, :])
    return jnp.concatenate(parts, axis=0)


def joined_parts(joined_ref, cols):
    rows = joined_ref.shape[0] // 2 // DEPTH * DEPTH
    return joined_ref[0:rows, cols], joined_ref[rows : 2 * rows, cols]


def prev_parts(outer_refs, pair_ref, cols):
    even = (lax.axis_index("tm") & 1) == 0
    parts = zip(outer_refs, joined_parts(pair_ref, cols))
    return tuple(jnp.where(even, outer[:, cols], pair) for outer, pair in parts)


def stats_kernel(rows_ref, queries_ref, outer_key_ref, outer_value_ref, pair_ref, own_ref, stats_ref):
    for head in range(queries_ref.shape[1] // DEPTH):
        cols = pl.ds(head * DEPTH, DEPTH)
        query, cotangent = joined_parts(queries_ref, cols)
        pieces = [prev_parts((outer_key_ref, outer_value_ref), pair_ref, cols), joined_parts(own_ref, cols)]
        logits = [logits_of(keys, query, rows_ref, head, piece) for piece, (keys, _) in enumerate(pieces)]
        peak = functools.reduce(jnp.maximum, [jnp.max(block, axis=0, keepdims=True) for block in logits])
        exps = [jnp.exp2(block - peak) for block in logits]
        slopes = [dot(values, cotangent, 1, 1) for _, values in pieces]
        stats_ref[head, 0:1, :] = peak
        stats_ref[head, 1:2, :] = sum(jnp.sum(e, axis=0, keepdims=True) for e in exps)
        stats_ref[head, 2:3, :] = sum(jnp.sum(e * s, axis=0, keepdims=True) for e, s in zip(exps, slopes))


def memory_kernel(rows_ref, part_ref, queries_ref, mine_ref, got_ref, stats_ref, mem_same_ref, mem_other_ref):
    even = (lax.axis_index("tm") & 1) == 0
    frame_len = mine_ref.shape[1]
    heads = queries_ref.shape[1] // DEPTH

    def products(head):
        cols = pl.ds(head * DEPTH, DEPTH)
        query, cotangent = joined_parts(queries_ref, cols)
        mine = mine_ref[:, :, cols].reshape(MEM * frame_len, DEPTH)
        got = got_ref[:, :, cols].reshape(MEM * frame_len, DEPTH)
        keys, values = jnp.where(even, mine, got), jnp.where(even, got, mine)
        return logits_of(keys, query, rows_ref, head, 2), dot(values, cotangent, 1, 1)

    def rounded(head, logits, slopes):
        part_peak = part_ref[head, 0:1, :]
        peak = jnp.maximum(part_peak, jnp.max(logits, axis=0, keepdims=True))
        exps = jnp.exp2(logits - peak)
        scale = jnp.exp2(part_peak - peak)
        total = part_ref[head, 1:2, :] * scale + jnp.sum(exps, axis=0, keepdims=True)
        inverse = 1.0 / total
        spread = (part_ref[head, 2:3, :] * scale + jnp.sum(exps * slopes, axis=0, keepdims=True)) * inverse
        stats_ref[head, 0:1, :] = peak
        stats_ref[head, 1:2, :] = inverse
        stats_ref[head, 2:3, :] = spread
        probs = exps * inverse
        return probs.astype(BF16), (probs * (slopes - spread)).astype(BF16)

    def store(head, weights, dlogits):
        cols = pl.ds(head * DEPTH, DEPTH)
        query, cotangent = joined_parts(queries_ref, cols)
        key_part = (dot(dlogits, query, 1, 0) * FACTOR).astype(BF16).reshape(MEM, frame_len, DEPTH)
        value_part = dot(weights, cotangent, 1, 0).astype(BF16).reshape(MEM, frame_len, DEPTH)
        mem_same_ref[:, :, cols] = jnp.where(even, key_part, value_part)
        mem_other_ref[:, :, cols] = jnp.where(even, value_part, key_part)

    ahead = products(0)
    behind = None
    for head in range(heads):
        now = ahead
        if head + 1 < heads:
            ahead = products(head + 1)
        if behind is not None:
            store(head - 1, *behind)
        behind = rounded(head, *now)
    store(heads - 1, *behind)


def probs_of(keys, values, query, cotangent, rows_ref, stats_ref, head, piece):
    logits = logits_of(keys, query, rows_ref, head, piece)
    probs = jnp.exp2(logits - stats_ref[head, 0:1, :]) * stats_ref[head, 1:2, :]
    dlogits = probs * (dot(values, cotangent, 1, 1) - stats_ref[head, 2:3, :])
    return probs.astype(BF16), dlogits.astype(BF16)


def next_kernel(rows_ref, stats_ref, queries_ref, own_ref, term_ref, sum_ref):
    for head in range(queries_ref.shape[1] // DEPTH):
        cols = pl.ds(head * DEPTH, DEPTH)
        query, cotangent = joined_parts(queries_ref, cols)
        keys, values = joined_parts(own_ref, cols)
        weights, dlogits = probs_of(keys, values, query, cotangent, rows_ref, stats_ref, head, 3)
        sum_ref[0, :, cols] = term_ref[0, :, cols] + dot(dlogits, query, 1, 0) * FACTOR
        sum_ref[1, :, cols] = term_ref[1, :, cols] + dot(weights, cotangent, 1, 0)


def rest_kernel(
    rows_ref,
    stats_ref,
    queries_ref,
    outer_key_ref,
    outer_value_ref,
    pair_ref,
    joined_ref,
    mine_ref,
    got_ref,
    attended_ref,
    grad_query_ref,
    own_ref,
    stats_out_ref,
):
    even = (lax.axis_index("tm") & 1) == 0
    frame_len = mine_ref.shape[1]
    stats_out_ref[...] = stats_ref[...]
    for head in range(queries_ref.shape[1] // DEPTH):
        cols = pl.ds(head * DEPTH, DEPTH)
        query, cotangent = joined_parts(queries_ref, cols)
        mine = mine_ref[:, :, cols].reshape(MEM * frame_len, DEPTH)
        got = got_ref[:, :, cols].reshape(MEM * frame_len, DEPTH)
        pieces = (
            prev_parts((outer_key_ref, outer_value_ref), pair_ref, cols),
            joined_parts(joined_ref, cols),
            (jnp.where(even, mine, got), jnp.where(even, got, mine)),
        )
        attended = grad_query = 0.0
        for piece, (keys, values) in enumerate(pieces):
            weights, dlogits = probs_of(keys, values, query, cotangent, rows_ref, stats_ref, head, piece)
            attended += dot(values, weights, 0, 0)
            grad_query += dot(keys, dlogits, 0, 0)
            if piece == 1:
                own_ref[0, :, cols] = dot(dlogits, query, 1, 0) * FACTOR
                own_ref[1, :, cols] = dot(weights, cotangent, 1, 0)
        attended_ref[:, cols] = attended.T.astype(BF16)
        grad_query_ref[:, cols] = (grad_query * FACTOR).T.astype(BF16)


def sum_kernel(codes_ref, mine_ref, got_ref, keep_ref, send_ref):
    code = code_of(codes_ref, SUM)
    kept = keep_ref.shape[0]
    terms = [ref[m].astype(F32) for ref in (mine_ref, got_ref) for m in range(MEM)]
    for place in range(kept + 1):
        value = sum(
            jnp.where(field(code, place * len(terms) + t, 1) != 0, term, 0.0) for t, term in enumerate(terms)
        )
        if place < kept:
            keep_ref[place] = value
        if place != kept - 1:
            send_ref[min(place, kept - 1)] = value.astype(BF16)


def add_kernel(keep_ref, got_ref, out_ref, send_ref):
    value = keep_ref[...] + got_ref[...].astype(F32)
    out_ref[...] = value
    send_ref[...] = value.astype(BF16)


def mark_kernel(mark_ref):
    mark_ref[...] = jnp.zeros(mark_ref.shape, F32)


def owned_kernel(codes_ref, keep_ref, got_ref, mine_ref, pair_ref):
    code = code_of(codes_ref, OWNED)
    for o, out in enumerate((mine_ref, pair_ref)):
        for j in range(FR_DEV):
            owned = field(code, o * FR_DEV + j, PLACE_BITS)
            place = owned >> 1
            named = (owned & 1) != 0

            @pl.when(named)
            def _(out=out, j=j, place=place):
                value = keep_ref[place] + got_ref[place].astype(F32)
                out[j] = value.astype(out.dtype)

            @pl.when(jnp.logical_not(named))
            def _(out=out, j=j):
                out[j] = jnp.zeros(out.shape[1:], out.dtype)


def final_kernel(own_ref, mine_ref, got_ref, grad_key_ref, grad_value_ref):
    even = (lax.axis_index("tm") & 1) == 0
    rows = grad_key_ref.shape
    mine = mine_ref[...].reshape(rows)
    got = got_ref[...].astype(F32).reshape(rows)
    grad_key_ref[...] = (own_ref[0] + jnp.where(even, mine, got)).astype(BF16)
    grad_value_ref[...] = (own_ref[1] + jnp.where(even, got, mine)).astype(BF16)


def body(
    query_states,
    key_states,
    value_states,
    grad_out,
    camera_pose,
    pose_bias,
    memory_index,
    bank_frames,
):
    row_count, width = query_states.shape
    frame_len = row_count // FR_DEV
    heads = pose_bias.shape[0]
    slots = bank_frames.shape[0]
    peers = lax.axis_size("tm")
    bits = [1 << i for i in range(1, peers.bit_length() - 1)]
    turns = list(zip(bits, bits[::-1]))
    piece_flops = 2 * row_count * row_count * width
    bank_frames = bank_frames.reshape(1, slots)
    last_bits = turns[-1]

    def join(kernel, rows, arrays, scratch, name):
        return pl.pallas_call(
            kernel,
            out_shape=shape(BF16, rows, width),
            in_specs=[pl.BlockSpec(memory_space=pltpu.HBM)] * len(arrays),
            out_specs=VMEM,
            scratch_shapes=[*scratch, pltpu.SemaphoreType.DMA((len(arrays),))],
            compiler_params=pltpu.CompilerParams(vmem_limit_bytes=VMEM_LIMIT),
            name=name,
        )(*(pltpu.with_memory_space_constraint(array, pltpu.HBM) for array in arrays))

    joined = join(
        join_kernel,
        2 * row_count + TAIL,
        [memory_index, key_states, value_states],
        [pltpu.VMEM(memory_index.shape, jnp.int32)],
        "join",
    )
    outer_keys = shift(key_states, 1, 1, peers)
    outer_values = shift(value_states, 1, 1, peers)
    pair = swap(joined, 1, 1, peers)
    queries = join(join_queries_kernel, 2 * row_count, [query_states, grad_out], [], "join_queries")
    next_queries = lax.ppermute(queries, "tm", [(i, i - 1) for i in range(1, peers)])

    bias_rows = -(-(3 * FR_DEV + MEM) // 8) * 8
    rows, codes = call(
        functools.partial(plan_kernel, peers, last_bits),
        [shape(F32, heads, bias_rows, row_count), shape(jnp.int32, 8, 128)],
        [pair],
        scalars=[bank_frames, memory_index, camera_pose, pose_bias],
        after=[outer_keys],
        flops=HIDING * piece_flops,
        name="plan",
    )
    held = shape(BF16, slots - 1, frame_len, width)
    sums = shape(F32, slots - 1, frame_len, width)
    (mine,) = call(functools.partial(split_kernel, peers), [held], [bank_frames, joined, pair], name="split")
    stats = shape(F32, heads, 8, row_count)
    (part,) = call(stats_kernel, [stats], [rows, queries, outer_keys, outer_values, pair, joined], name="stats")
    even_done = odd_done = 1
    for step, (even_bit, odd_bit) in enumerate(turns):
        got = swap(mine, even_bit, odd_bit, peers)
        if step + 1 < len(turns):
            kernel = functools.partial(step_kernel, peers, even_done, odd_done)
            (mine,) = call(kernel, [held], [bank_frames, mine, got], after=[codes], name="step")
        even_done |= even_bit
        odd_done |= odd_bit
    chosen = shape(BF16, MEM, frame_len, width)
    mem_mine, mem_send = call(pick_kernel, [chosen] * 2, [codes, mine, got], after=[part], name="pick")
    mem_got = swap(mem_send, 1, 1, peers)

    stats_all, mem_same, mem_other = call(
        memory_kernel,
        [stats, chosen, chosen],
        [rows, part, queries, mem_mine, mem_got],
        flops=HIDING * piece_flops,
        name="memory",
    )
    same_got = swap(mem_other, 1, 1, peers)
    keep, send = call(sum_kernel, [sums, held], [codes, mem_same, same_got], name="sum")
    pair_sums = shape(F32, 2, row_count, width)
    attended, grad_query, own_terms, stats_sent = call(
        rest_kernel,
        [shape(BF16, row_count, width)] * 2 + [pair_sums, stats],
        [rows, stats_all, queries, outer_keys, outer_values, pair, joined, mem_mine, mem_got],
        after=[send],
        name="rest",
    )
    next_stats = lax.ppermute(stats_sent, "tm", [(i, i - 1) for i in range(1, peers)])
    (arrived,) = call(
        mark_kernel,
        [shape(F32, 8, 128)],
        [],
        after=[own_terms, next_queries],
        flops=HIDING * piece_flops,
        name="arrived",
    )
    (own,) = call(
        next_kernel,
        [pair_sums],
        [rows, next_stats, next_queries, joined, own_terms],
        flops=HIDING * piece_flops,
        name="next",
    )
    for step, (even_bit, odd_bit) in enumerate(turns[::-1]):
        got = swap(send, even_bit, odd_bit, peers)
        if step + 1 < len(turns):
            keep, send = call(add_kernel, [sums, held], [keep, got], after=[arrived], name="add")
    owned = shape(F32, FR_DEV, frame_len, width)
    owned_mine, owned_send = call(
        owned_kernel,
        [owned, shape(BF16, FR_DEV, frame_len, width)],
        [codes, keep, got],
        after=[own],
        name="owned",
    )
    owned_got = swap(owned_send, 1, 1, peers)
    grad_key, grad_value = call(
        final_kernel, [shape(BF16, row_count, width)] * 2, [own, owned_mine, owned_got], name="final"
    )
    return (attended, grad_query, grad_key, grad_value)


def solution(mesh):
    rows = P(("traj", "tm"), None)
    in_specs = (rows, rows, rows, rows, P("traj"), P(), rows, P("traj"))
    return jax.shard_map(body, mesh=mesh, in_specs=in_specs, out_specs=(rows,) * 4, check_vma=False)
```

```python
import functools
import math

import jax
import jax.numpy as jnp
from jax import lax
from jax.experimental import pallas as pl
from jax.experimental.pallas import tpu as pltpu
from jax.sharding import PartitionSpec as P

FR_DEV = 2
MEM = 2
DEPTH = 128
TAIL = 16

BLOCKED_LOGIT = -1e30
LOG2E = math.log2(math.e)
FACTOR = 1.0 / math.sqrt(DEPTH)

SMEM = pl.BlockSpec(memory_space=pltpu.SMEM)
VMEM = pl.BlockSpec(memory_space=pltpu.VMEM)
ANY = pl.BlockSpec(memory_space=pl.ANY)
HIDING = 200
VMEM_LIMIT = 32 * 1024 * 1024
BF16, F32 = jnp.bfloat16, jnp.float32


def shape(dtype, *dims):
    return jax.ShapeDtypeStruct(dims, dtype)


def call(kernel, outs, arrays, scalars=(), after=(), flops=0, name=None):
    count = len(scalars) + len(arrays)

    def run(*refs):
        kernel(*refs[:count], *refs[count + len(after) :])

    return pl.pallas_call(
        run,
        out_shape=outs,
        in_specs=[SMEM] * len(scalars) + [VMEM] * len(arrays) + [ANY] * len(after),
        out_specs=[VMEM] * len(outs),
        compiler_params=pltpu.CompilerParams(vmem_limit_bytes=VMEM_LIMIT),
        cost_estimate=pl.CostEstimate(flops=flops, bytes_accessed=0, transcendentals=0) if flops else None,
        name=name,
    )(*scalars, *arrays, *after)


def swap(block, even_bit, odd_bit, peers):
    return lax.ppermute(block, "tm", [(i, i ^ (odd_bit if i & 1 else even_bit)) for i in range(peers)])


def shift(block, by, start, peers):
    pairs = [(i, i + by) for i in range(start, peers, 2) if 0 <= i + by < peers]
    return lax.ppermute(block, "tm", pairs)


def lane_value(row, lane):
    lanes = lax.broadcasted_iota(jnp.int32, row.shape, 1)
    return jnp.max(jnp.where(lanes == lane, row, 0))


def bank_of(bank_ref):
    row = bank_ref[...]
    return [lane_value(row, slot) for slot in range(row.shape[1])]


def dyn_frames(bank, last_frame):
    found = [jnp.int32(0)] * (len(bank) - 2)
    seen = jnp.int32(0)
    for frame in bank:
        free = jnp.logical_and(frame != 0, frame != last_frame)
        for j in range(len(found)):
            found[j] = jnp.where(jnp.logical_and(free, seen == j), frame, found[j])
        seen = seen + free.astype(jnp.int32)
    return found


def place_of(frame, dyns):
    place = jnp.int32(len(dyns))
    for j, dyn in enumerate(dyns):
        place = jnp.where(frame == dyn, j, place)
    return place


def choose(out, take_first, first, second):
    @pl.when(take_first)
    def _():
        out[...] = first[...]

    @pl.when(jnp.logical_not(take_first))
    def _():
        out[...] = second[...]


def has_end(me, done, peers):
    return jnp.logical_or((me & ~done) == 0, (me | done) == peers - 1)


def has_dyn(me, frame, done):
    return ((me ^ (frame // FR_DEV)) & ~done) == 0


def by_role(me, even_value, odd_value):
    return jnp.where((me & 1) == 0, even_value, odd_value)


def join_kernel(index_ref, key_ref, value_ref, joined_ref, index_buf, sems):
    rows = key_ref.shape[0]
    copies = [
        pltpu.make_async_copy(index_ref, index_buf, sems.at[0]),
        pltpu.make_async_copy(key_ref, joined_ref.at[pl.ds(0, rows)], sems.at[1]),
        pltpu.make_async_copy(value_ref, joined_ref.at[pl.ds(rows, rows)], sems.at[2]),
    ]
    for copy in copies:
        copy.start()
    copies[0].wait()
    width = joined_ref.shape[1]
    lane = lax.broadcasted_iota(jnp.int32, (TAIL, width), 1) // DEPTH
    tail = jnp.zeros((TAIL, width), jnp.int32)
    for m in range(MEM):
        tail = jnp.where(lane == m, index_buf[0:1, m : m + 1], tail)
    joined_ref[2 * rows : 2 * rows + TAIL, :] = tail.astype(F32).astype(BF16)
    copies[1].wait()
    copies[2].wait()


def join_queries_kernel(query_ref, cotangent_ref, joined_ref, sems):
    rows = query_ref.shape[0]
    copies = [
        pltpu.make_async_copy(ref, joined_ref.at[pl.ds(j * rows, rows)], sems.at[j])
        for j, ref in enumerate((query_ref, cotangent_ref))
    ]
    for copy in copies:
        copy.start()
    for copy in copies:
        copy.wait()


def pack(fields, width):
    code = jnp.int32(0)
    for j, field in enumerate(fields):
        code = code | (field.astype(jnp.int32) << (j * width))
    return code


def field(code, j, width):
    return (code >> (j * width)) & ((1 << width) - 1)


def code_of(codes_ref, row):
    return jnp.max(codes_ref[row : row + 1, :])


PICK, SUM, OWNED = range(3)
PLACE_BITS = 4
PREV, OWN, MEMORY, NEXT, PAIR = range(5)


def plan_kernel(peers, last_bits, bank_ref, index_ref, pose_ref, bias_ref, pair_ref, rows_ref, codes_ref):
    me = lax.axis_index("tm")
    last_frame = peers * FR_DEV - 1
    heads, _, row_count = rows_ref.shape
    bank = [bank_ref[0, slot] for slot in range(bank_ref.shape[1])]
    tail = pair_ref.shape[0] - TAIL
    pair_ids = []
    for m in range(MEM):
        slot = jnp.max(pair_ref[tail : tail + TAIL, m * DEPTH : (m + 1) * DEPTH].astype(F32)).astype(jnp.int32)
        pair_ids.append(bank_ref[0, slot])
    mem_ids = [bank_ref[0, index_ref[0, m]] for m in range(MEM)]

    own_ids = [me * FR_DEV + j for j in range(FR_DEV)]
    prev_ids = [jnp.maximum(own - FR_DEV, 0) for own in own_ids]
    next_ids = [jnp.minimum(own + FR_DEV, last_frame) for own in own_ids]
    pair_own_ids = [(me ^ 1) * FR_DEV + j for j in range(FR_DEV)]
    pieces = ((prev_ids, own_ids), (own_ids, own_ids), (mem_ids, own_ids), (own_ids, next_ids), (pair_ids, pair_own_ids))
    poses = [([pose_ref[f] for f in key_ids], [pose_ref[f] for f in query_ids]) for key_ids, query_ids in pieces]
    frame_of = lax.broadcasted_iota(jnp.int32, (1, row_count), 1) // (row_count // FR_DEV)
    for head in range(heads):
        for piece, (key_poses, query_poses) in enumerate(poses):
            for j, key_pose in enumerate(key_poses):
                row = jnp.zeros((1, row_count), F32)
                for a, query_pose in enumerate(query_poses):
                    value = bias_ref[head, query_pose, key_pose] * LOG2E
                    if piece == PREV:
                        value = jnp.where(me == 0, BLOCKED_LOGIT, value)
                    row = jnp.where(frame_of == a, value, row)
                rows_ref[head, piece * FR_DEV + j : piece * FR_DEV + j + 1, :] = row

    dyns = dyn_frames(bank, last_frame)
    bit = by_role(me, *last_bits)
    upper = (me & bit) != 0
    picks = []
    for frame in mem_ids + pair_ids:
        source = place_of(frame, dyns)
        local = jnp.where(frame == 0, jnp.logical_not(upper), upper)
        local = jnp.where(source < len(dyns), has_dyn(me, frame, (peers - 1) & ~bit), local)
        picks.append(source * 2 + local.astype(jnp.int32))
    far = jnp.where(upper, 0, last_frame)
    sums = [jnp.where(frame == far, len(dyns) + 1, place_of(frame, dyns)) for frame in mem_ids + pair_ids]
    owned = []
    for group in (me, me ^ 1):
        for j in range(FR_DEV):
            frame = group * FR_DEV + j
            place = place_of(frame, dyns)
            named = jnp.logical_or(place < len(dyns), jnp.logical_or(frame == 0, frame == last_frame))
            owned.append(place * 2 + named.astype(jnp.int32))
    lanes = codes_ref.shape[1]
    for row, code in ((PICK, pack(picks, PLACE_BITS)), (SUM, pack(sums, PLACE_BITS)), (OWNED, pack(owned, PLACE_BITS))):
        codes_ref[row : row + 1, :] = jnp.full((1, lanes), code, jnp.int32)


def split_kernel(peers, bank_ref, mine_ref, pair_ref, out_ref):
    me = lax.axis_index("tm")
    frame_len, half_width = out_ref.shape[2:]
    dyns = dyn_frames(bank_of(bank_ref), peers * FR_DEV - 1)
    places = [(has_dyn(me, dyn, 0), dyn % FR_DEV) for dyn in dyns]
    places.append((has_end(me, 0, peers), jnp.where(me < peers // 2, 0, FR_DEV - 1)))
    for j, (local, frame) in enumerate(places):
        for role in range(2):
            for source, taken in ((mine_ref, local), (pair_ref, jnp.logical_not(local))):

                @pl.when(jnp.logical_and((me & 1) == role, taken))
                def _(source=source, j=j, frame=frame, role=role):
                    for kind in range(2):
                        start = pl.multiple_of((kind * FR_DEV + frame) * frame_len, frame_len)
                        out_ref[j, kind] = source[pl.ds(start, frame_len), role * half_width : (role + 1) * half_width]


def step_kernel(peers, even_done, odd_done, bank_ref, mine_ref, got_ref, out_ref):
    me = lax.axis_index("tm")
    done = by_role(me, even_done, odd_done)
    dyns = dyn_frames(bank_of(bank_ref), peers * FR_DEV - 1)
    flags = [has_dyn(me, dyn, done) for dyn in dyns] + [has_end(me, done, peers)]
    for j, flag in enumerate(flags):
        choose(out_ref.at[j], flag, mine_ref.at[j], got_ref.at[j])


def pick_kernel(codes_ref, mine_ref, got_ref, own_out, pair_out):
    code = code_of(codes_ref, PICK)
    for o, out in enumerate((own_out, pair_out)):
        for m in range(MEM):
            pick = field(code, o * MEM + m, PLACE_BITS)
            source = pick >> 1
            choose(out.at[m], (pick & 1) != 0, mine_ref.at[source], got_ref.at[source])


def dot(a, b, left, right):
    return lax.dot_general(a, b, (((left,), (right,)), ((), ())), preferred_element_type=F32)


def logits_of(keys, query, rows_ref, head, piece):
    frame_len = query.shape[0] // FR_DEV
    raw = dot(keys, query, 1, 1) * (FACTOR * LOG2E)
    parts = []
    for j in range(FR_DEV):
        row = piece * FR_DEV + j
        parts.append(raw[j * frame_len : (j + 1) * frame_len] + rows_ref[head, row : row + 1, :])
    return jnp.concatenate(parts, axis=0)


def joined_parts(joined_ref, cols):
    rows = joined_ref.shape[0] // 2 // DEPTH * DEPTH
    return joined_ref[0:rows, cols], joined_ref[rows : 2 * rows, cols]


def head_cols(head):
    return pl.ds(head * DEPTH, DEPTH)


def part_of(logits, slopes):
    peak = jnp.max(logits, axis=0, keepdims=True)
    exps = jnp.exp2(logits - peak)
    return peak, jnp.sum(exps, axis=0, keepdims=True), jnp.sum(exps * slopes, axis=0, keepdims=True)


def merged(left, right):
    peak = jnp.maximum(left[0], right[0])
    scales = [jnp.exp2(part[0] - peak) for part in (left, right)]
    return peak, *(left[j] * scales[0] + right[j] * scales[1] for j in (1, 2))


def load_part(ref, head):
    return tuple(ref[head, j : j + 1, :] for j in range(3))


def store_part(ref, head, part):
    for j, row in enumerate(part):
        ref[head, j : j + 1, :] = row


def ahead_kernel(rows_ref, next_queries_ref, own_ref, part_ref):
    heads = part_ref.shape[0]
    for local in range(heads):
        query, cotangent = joined_parts(next_queries_ref, head_cols(local))
        keys, values = joined_parts(own_ref, head_cols(heads + local))
        logits = logits_of(keys, query, rows_ref, heads + local, NEXT)
        store_part(part_ref, local, part_of(logits, dot(values, cotangent, 1, 1)))


def stats_kernel(rows_ref, queries_ref, outer_ref, pair_ref, own_ref, ahead_ref, part_ref, keys_out, queries_out):
    me = lax.axis_index("tm")
    even = (me & 1) == 0
    heads = queries_ref.shape[1] // DEPTH
    half = heads // 2
    rows = queries_ref.shape[0]
    half_width = half * DEPTH
    keys_out[...] = own_ref[0:rows, half_width : 2 * half_width]
    queries_out[...] = queries_ref[:, 0:half_width]

    def products(head):
        query, cotangent = joined_parts(queries_ref, head_cols(head))
        prev = joined_parts(pair_ref, head_cols(head))
        if head < half:
            outer = joined_parts(outer_ref, head_cols(head))
            prev = [jnp.where(even, there, here) for there, here in zip(outer, prev)]
        own = joined_parts(own_ref, head_cols(head))
        return [
            (logits_of(keys, query, rows_ref, head, piece), dot(values, cotangent, 1, 1))
            for piece, (keys, values) in ((PREV, prev), (OWN, own))
        ]

    ahead = products(0)
    for head in range(heads):
        now = ahead
        if head + 1 < heads:
            ahead = products(head + 1)
        prev, own = (part_of(*piece) for piece in now)
        if head >= half:
            there = load_part(ahead_ref, head - half)
            there = (jnp.where(me == 0, BLOCKED_LOGIT, there[0]), *there[1:])
            prev = tuple(jnp.where(even, a, b) for a, b in zip(there, prev))
        store_part(part_ref, head, merged(prev, own))


def rounded(part, logits, slopes):
    peak, total, spread = merged(part, part_of(logits, slopes))
    inverse = 1.0 / total
    stats = peak, inverse, spread * inverse
    return stats, *weights_of(stats, logits, slopes)


def weights_of(stats, logits, slopes):
    peak, inverse, spread = stats
    probs = jnp.exp2(logits - peak) * inverse
    return probs.astype(BF16), (probs * (slopes - spread)).astype(BF16)


def memory_kernel(
    codes_ref, rows_ref, part_ref, pair_part_ref, own_queries, pair_queries, own_mem, pair_mem, keep_ref, send_ref
):
    role = lax.axis_index("tm") & 1
    code = code_of(codes_ref, SUM)
    frame_len, half_width = own_mem.shape[2:]
    half = half_width // DEPTH
    groups = ((own_queries, own_mem, part_ref, MEMORY), (pair_queries, pair_mem, pair_part_ref, PAIR))
    work = [(g, local) for local in range(half) for g in range(len(groups))]
    keep_ref[...] = jnp.zeros(keep_ref.shape, F32)

    def products(g, local):
        queries, mem, _, piece = groups[g]
        query, cotangent = joined_parts(queries, head_cols(local))
        keys, values = (mem[:, kind, :, head_cols(local)].reshape(MEM * frame_len, DEPTH) for kind in range(2))
        return logits_of(keys, query, rows_ref, role * half + local, piece), dot(values, cotangent, 1, 1)

    def add(g, local, _, weights, dlogits):
        query, cotangent = joined_parts(groups[g][0], head_cols(local))
        terms = (dot(dlogits, query, 1, 0) * FACTOR, dot(weights, cotangent, 1, 0))
        for m in range(MEM):
            place = field(code, g * MEM + m, PLACE_BITS)
            for kind, term in enumerate(terms):
                part = term[m * frame_len : (m + 1) * frame_len].astype(BF16).astype(F32)
                keep_ref[place, kind, :, head_cols(local)] += part

    ahead = products(*work[0])
    behind = None
    for j, (g, local) in enumerate(work):
        now = ahead
        if j + 1 < len(work):
            ahead = products(*work[j + 1])
        if behind is not None:
            add(*work[j - 1], *behind)
        behind = rounded(load_part(groups[g][2], role * half + local), *now)
    add(*work[-1], *behind)
    kept = send_ref.shape[0]
    for place in range(kept):
        send_ref[place] = keep_ref[place if place + 1 < kept else kept].astype(BF16)


def next_kernel(
    rows_ref, stats_ref, pair_queries, outer_first, outer_second, own_ref, term_ref, sum_ref
):
    even = (lax.axis_index("tm") & 1) == 0
    heads = pair_queries.shape[1] // DEPTH
    half = heads // 2

    def operands(head):
        outer = joined_parts((outer_first, outer_second)[head // half], head_cols(head % half))
        return [jnp.where(even, a, b) for a, b in zip(joined_parts(pair_queries, head_cols(head)), outer)]

    def products(head):
        query, cotangent = operands(head)
        keys, values = joined_parts(own_ref, head_cols(head))
        return logits_of(keys, query, rows_ref, head, NEXT), dot(values, cotangent, 1, 1)

    ahead = products(0)
    for head in range(heads):
        now = ahead
        if head + 1 < heads:
            ahead = products(head + 1)
        weights, dlogits = weights_of(load_part(stats_ref, head), *now)
        query, cotangent = operands(head)
        cols = head_cols(head)
        sum_ref[0, :, cols] = term_ref[0, :, cols] + dot(dlogits, query, 1, 0) * FACTOR
        sum_ref[1, :, cols] = term_ref[1, :, cols] + dot(weights, cotangent, 1, 0)


def rest_kernel(
    rows_ref,
    part_ref,
    queries_ref,
    outer_first,
    outer_second,
    pair_ref,
    own_ref,
    own_mem,
    other_mem,
    attended_ref,
    grad_query_ref,
    term_ref,
    stats_ref,
):
    role = lax.axis_index("tm") & 1
    frame_len, half_width = own_mem.shape[2:]
    heads = queries_ref.shape[1] // DEPTH
    half = half_width // DEPTH

    def pieces(head):
        cols = head_cols(head % half)
        outer = joined_parts((outer_first, outer_second)[head // half], cols)
        prev = [jnp.where(role == 0, a, b) for a, b in zip(outer, joined_parts(pair_ref, head_cols(head)))]
        memory = [
            jnp.where(role == head // half, own_mem[:, kind, :, cols], other_mem[:, kind, :, cols]).reshape(
                MEM * frame_len, DEPTH
            )
            for kind in range(2)
        ]
        return (PREV, prev), (OWN, joined_parts(own_ref, head_cols(head))), (MEMORY, memory)

    def products(head):
        query, cotangent = joined_parts(queries_ref, head_cols(head))
        return [
            (logits_of(keys, query, rows_ref, head, piece), dot(values, cotangent, 1, 1))
            for piece, (keys, values) in pieces(head)
        ]

    ahead = products(0)
    for head in range(heads):
        now = ahead
        if head + 1 < heads:
            ahead = products(head + 1)
        cols = head_cols(head)
        query, cotangent = joined_parts(queries_ref, cols)
        stats, *last = rounded(load_part(part_ref, head), *now[-1])
        store_part(stats_ref, head, stats)
        rounds = [weights_of(stats, *now[PREV]), weights_of(stats, *now[OWN]), last]
        attended = grad_query = 0.0
        for (piece, (keys, values)), (weights, dlogits) in zip(pieces(head), rounds):
            attended += dot(values, weights, 0, 0)
            grad_query += dot(keys, dlogits, 0, 0)
            if piece == OWN:
                term_ref[0, :, cols] = dot(dlogits, query, 1, 0) * FACTOR
                term_ref[1, :, cols] = dot(weights, cotangent, 1, 0)
        attended_ref[:, cols] = attended.T.astype(BF16)
        grad_query_ref[:, cols] = (grad_query * FACTOR).T.astype(BF16)


def add_kernel(keep_ref, got_ref, out_ref, send_ref):
    value = keep_ref[0 : got_ref.shape[0]] + got_ref[...].astype(F32)
    out_ref[...] = value
    send_ref[...] = value.astype(BF16)


def owned_kernel(codes_ref, keep_ref, got_ref, mine_ref, pair_ref):
    code = code_of(codes_ref, OWNED)
    for o, out in enumerate((mine_ref, pair_ref)):
        for j in range(FR_DEV):
            owned = field(code, o * FR_DEV + j, PLACE_BITS)
            place = owned >> 1
            named = (owned & 1) != 0

            @pl.when(named)
            def _(out=out, j=j, place=place):
                value = keep_ref[place] + got_ref[place].astype(F32)
                out[j] = value.astype(out.dtype)

            @pl.when(jnp.logical_not(named))
            def _(out=out, j=j):
                out[j] = jnp.zeros(out.shape[1:], out.dtype)


def final_kernel(own_ref, mine_ref, got_ref, grad_key_ref, grad_value_ref):
    role = lax.axis_index("tm") & 1
    frame_len, half_width = mine_ref.shape[2:]
    for kind, out in enumerate((grad_key_ref, grad_value_ref)):
        for j in range(FR_DEV):
            rows = pl.ds(j * frame_len, frame_len)
            for half in range(2):
                cols = pl.ds(half * half_width, half_width)
                bank = jnp.where(role == half, mine_ref[j, kind], got_ref[j, kind].astype(F32))
                out[rows, cols] = (own_ref[kind, rows, cols] + bank).astype(BF16)


def body(
    query_states,
    key_states,
    value_states,
    grad_out,
    camera_pose,
    pose_bias,
    memory_index,
    bank_frames,
):
    row_count, width = query_states.shape
    frame_len = row_count // FR_DEV
    heads = pose_bias.shape[0]
    slots = bank_frames.shape[0]
    peers = lax.axis_size("tm")
    bits = [1 << i for i in range(1, peers.bit_length() - 1)]
    turns = list(zip(bits, bits[::-1]))
    even = (lax.axis_index("tm") & 1) == 0
    piece_flops = 2 * row_count * row_count * width
    bank_frames = bank_frames.reshape(1, slots)
    last_bits = turns[-1]

    def join(kernel, rows, arrays, scratch, name, after=()):
        def run(*refs):
            kernel(*refs[: len(arrays)], *refs[len(arrays) + len(after) :])

        return pl.pallas_call(
            run,
            out_shape=shape(BF16, rows, width),
            in_specs=[pl.BlockSpec(memory_space=pltpu.HBM)] * len(arrays) + [ANY] * len(after),
            out_specs=VMEM,
            scratch_shapes=[*scratch, pltpu.SemaphoreType.DMA((len(arrays),))],
            compiler_params=pltpu.CompilerParams(vmem_limit_bytes=VMEM_LIMIT),
            name=name,
        )(*(pltpu.with_memory_space_constraint(array, pltpu.HBM) for array in arrays), *after)

    joined = join(
        join_kernel,
        2 * row_count + TAIL,
        [memory_index, key_states, value_states],
        [pltpu.VMEM(memory_index.shape, jnp.int32)],
        "join",
    )
    half_width = width // 2
    first, second = slice(0, half_width), slice(half_width, width)
    outer_first = shift(joined[: 2 * row_count, first], 1, 1, peers)
    pair = swap(joined, 1, 1, peers)
    held = shape(BF16, slots - 1, 2, frame_len, half_width)
    sums = shape(F32, slots - 1, 2, frame_len, half_width)
    (mine,) = call(functools.partial(split_kernel, peers), [held], [bank_frames, joined, pair], name="split")
    queries = join(join_queries_kernel, 2 * row_count, [query_states, grad_out], [], "join_queries", after=[mine])
    pair_queries = swap(queries, 1, 1, peers)
    next_second = shift(queries[:, second], -1, 2, peers)
    own_half = jnp.where(even, queries[:, first], queries[:, second])
    pair_half = jnp.where(even, pair_queries[:, first], pair_queries[:, second])

    bias_rows = -(-(5 * FR_DEV) // 8) * 8
    rows, codes = call(
        functools.partial(plan_kernel, peers, last_bits),
        [shape(F32, heads, bias_rows, row_count), shape(jnp.int32, 8, 128)],
        [pair],
        scalars=[bank_frames, memory_index, camera_pose, pose_bias],
        after=[outer_first],
        flops=HIDING * piece_flops,
        name="plan",
    )
    even_done = odd_done = 1
    for step, (even_bit, odd_bit) in enumerate(turns):
        got = swap(mine, even_bit, odd_bit, peers)
        if step + 1 < len(turns):
            kernel = functools.partial(step_kernel, peers, even_done, odd_done)
            after = [codes, pair_queries, next_second]
            (mine,) = call(kernel, [held], [bank_frames, mine, got], after=after, name="step")
        even_done |= even_bit
        odd_done |= odd_bit

    stats = shape(F32, heads, 8, row_count)
    half_joined = shape(BF16, 2 * row_count, half_width)
    (ahead,) = call(ahead_kernel, [shape(F32, heads // 2, 8, row_count)], [rows, next_second, joined], name="ahead")
    ahead = shift(ahead, 1, 1, peers)
    part, keys_out, queries_out = call(
        stats_kernel,
        [stats, half_joined, half_joined],
        [rows, queries, outer_first, pair, joined, ahead],
        name="stats",
    )
    pair_part = swap(part, 1, 1, peers)
    outer_second = shift(keys_out, 1, 1, peers)
    next_first = shift(queries_out, -1, 2, peers)
    chosen = shape(BF16, MEM, 2, frame_len, half_width)
    own_mem, pair_mem = call(pick_kernel, [chosen] * 2, [codes, mine, got], name="pick")
    keep, send = call(
        memory_kernel,
        [shape(F32, slots, 2, frame_len, half_width), held],
        [codes, rows, part, pair_part, own_half, pair_half, own_mem, pair_mem],
        flops=HIDING * piece_flops,
        name="memory",
    )
    other_mem = swap(pair_mem, 1, 1, peers)
    pair_sums = shape(F32, 2, row_count, width)
    attended, grad_query, own_terms, stats_all = call(
        rest_kernel,
        [shape(BF16, row_count, width)] * 2 + [pair_sums, stats],
        [rows, part, queries, outer_first, outer_second, pair, joined, own_mem, other_mem],
        after=[send, next_first],
        flops=HIDING * piece_flops,
        name="rest",
    )
    next_stats = lax.ppermute(stats_all, "tm", [(i, i - 1) for i in range(1, peers)])
    (own,) = call(
        next_kernel,
        [pair_sums],
        [rows, next_stats, pair_queries, next_first, next_second, joined, own_terms],
        flops=HIDING * piece_flops,
        name="next",
    )
    for step, (even_bit, odd_bit) in enumerate(turns[::-1]):
        got = swap(send, even_bit, odd_bit, peers)
        if step + 1 < len(turns):
            keep, send = call(add_kernel, [sums, held], [keep, got], after=[own_terms], name="add")
    owned_mine, owned_send = call(
        owned_kernel,
        [shape(F32, FR_DEV, 2, frame_len, half_width), shape(BF16, FR_DEV, 2, frame_len, half_width)],
        [codes, keep, got],
        after=[own],
        name="owned",
    )
    owned_got = swap(owned_send, 1, 1, peers)
    grad_key, grad_value = call(
        final_kernel, [shape(BF16, row_count, width)] * 2, [own, owned_mine, owned_got], name="final"
    )
    return (attended, grad_query, grad_key, grad_value)


def solution(mesh):
    rows = P(("traj", "tm"), None)
    in_specs = (rows, rows, rows, rows, P("traj"), P(), rows, P("traj"))
    return jax.shard_map(body, mesh=mesh, in_specs=in_specs, out_specs=(rows,) * 4, check_vma=False)
```

```python
import functools
import math

import jax
import jax.numpy as jnp
from jax import lax
from jax.experimental import pallas as pl
from jax.experimental.pallas import tpu as pltpu
from jax.sharding import PartitionSpec as P

FR_DEV = 2
MEM = 2
DEPTH = 128
TAIL = 16

BLOCKED_LOGIT = -1e30
LOG2E = math.log2(math.e)
FACTOR = 1.0 / math.sqrt(DEPTH)

SMEM = pl.BlockSpec(memory_space=pltpu.SMEM)
VMEM = pl.BlockSpec(memory_space=pltpu.VMEM)
ANY = pl.BlockSpec(memory_space=pl.ANY)
HIDING = 200
VMEM_LIMIT = 32 * 1024 * 1024
BF16, F32 = jnp.bfloat16, jnp.float32


def shape(dtype, *dims):
    return jax.ShapeDtypeStruct(dims, dtype)


def call(kernel, outs, arrays, scalars=(), after=(), flops=0, name=None):
    count = len(scalars) + len(arrays)

    def run(*refs):
        kernel(*refs[:count], *refs[count + len(after) :])

    return pl.pallas_call(
        run,
        out_shape=outs,
        in_specs=[SMEM] * len(scalars) + [VMEM] * len(arrays) + [ANY] * len(after),
        out_specs=[VMEM] * len(outs),
        compiler_params=pltpu.CompilerParams(vmem_limit_bytes=VMEM_LIMIT),
        cost_estimate=pl.CostEstimate(flops=flops, bytes_accessed=0, transcendentals=0) if flops else None,
        name=name,
    )(*scalars, *arrays, *after)


def swap(block, even_bit, odd_bit, peers):
    return lax.ppermute(block, "tm", [(i, i ^ (odd_bit if i & 1 else even_bit)) for i in range(peers)])


def shift(block, by, start, peers):
    pairs = [(i, i + by) for i in range(start, peers, 2) if 0 <= i + by < peers]
    return lax.ppermute(block, "tm", pairs)


def lane_value(row, lane):
    lanes = lax.broadcasted_iota(jnp.int32, row.shape, 1)
    return jnp.max(jnp.where(lanes == lane, row, 0))


def bank_of(bank_ref):
    row = bank_ref[...]
    return [lane_value(row, slot) for slot in range(row.shape[1])]


def dyn_frames(bank, last_frame):
    found = [jnp.int32(0)] * (len(bank) - 2)
    seen = jnp.int32(0)
    for frame in bank:
        free = jnp.logical_and(frame != 0, frame != last_frame)
        for j in range(len(found)):
            found[j] = jnp.where(jnp.logical_and(free, seen == j), frame, found[j])
        seen = seen + free.astype(jnp.int32)
    return found


def place_of(frame, dyns):
    place = jnp.int32(len(dyns))
    for j, dyn in enumerate(dyns):
        place = jnp.where(frame == dyn, j, place)
    return place


def choose(out, take_first, first, second):
    @pl.when(take_first)
    def _():
        out[...] = first[...]

    @pl.when(jnp.logical_not(take_first))
    def _():
        out[...] = second[...]


def has_end(me, done, peers):
    return jnp.logical_or((me & ~done) == 0, (me | done) == peers - 1)


def has_dyn(me, frame, done):
    return ((me ^ (frame // FR_DEV)) & ~done) == 0


def by_role(me, even_value, odd_value):
    return jnp.where((me & 1) == 0, even_value, odd_value)


def join_kernel(index_ref, key_ref, value_ref, joined_ref, index_buf, sems):
    rows = key_ref.shape[0]
    copies = [
        pltpu.make_async_copy(index_ref, index_buf, sems.at[0]),
        pltpu.make_async_copy(key_ref, joined_ref.at[pl.ds(0, rows)], sems.at[1]),
        pltpu.make_async_copy(value_ref, joined_ref.at[pl.ds(rows, rows)], sems.at[2]),
    ]
    for copy in copies:
        copy.start()
    copies[0].wait()
    width = joined_ref.shape[1]
    lane = lax.broadcasted_iota(jnp.int32, (TAIL, width), 1) // DEPTH
    tail = jnp.zeros((TAIL, width), jnp.int32)
    for m in range(MEM):
        tail = jnp.where(lane == m, index_buf[0:1, m : m + 1], tail)
    joined_ref[2 * rows : 2 * rows + TAIL, :] = tail.astype(F32).astype(BF16)
    copies[1].wait()
    copies[2].wait()


def join_queries_kernel(query_ref, cotangent_ref, joined_ref, sems):
    rows = query_ref.shape[0]
    copies = [
        pltpu.make_async_copy(ref, joined_ref.at[pl.ds(j * rows, rows)], sems.at[j])
        for j, ref in enumerate((query_ref, cotangent_ref))
    ]
    for copy in copies:
        copy.start()
    for copy in copies:
        copy.wait()


def pack(fields, width):
    code = jnp.int32(0)
    for j, field in enumerate(fields):
        code = code | (field.astype(jnp.int32) << (j * width))
    return code


def field(code, j, width):
    return (code >> (j * width)) & ((1 << width) - 1)


def code_of(codes_ref, row):
    return jnp.max(codes_ref[row : row + 1, :])


PICK, SUM, OWNED = range(3)
PLACE_BITS = 4


def plan_kernel(
    peers, last_bits, bank_ref, index_ref, pose_ref, bias_ref, pair_ref, joined_ref, rows_ref, codes_ref, values_out
):
    me = lax.axis_index("tm")
    last_frame = peers * FR_DEV - 1
    heads, _, row_count = rows_ref.shape
    values_out[...] = joined_ref[row_count : 2 * row_count, :]
    bank = [bank_ref[0, slot] for slot in range(bank_ref.shape[1])]
    tail = pair_ref.shape[0] - TAIL
    pair_ids = []
    for m in range(MEM):
        slot = jnp.max(pair_ref[tail : tail + TAIL, m * DEPTH : (m + 1) * DEPTH].astype(F32)).astype(jnp.int32)
        pair_ids.append(bank_ref[0, slot])
    mem_ids = [bank_ref[0, index_ref[0, m]] for m in range(MEM)]

    own_ids = [me * FR_DEV + j for j in range(FR_DEV)]
    prev_ids = [jnp.maximum(own - FR_DEV, 0) for own in own_ids]
    next_ids = [jnp.minimum(own + FR_DEV, last_frame) for own in own_ids]
    key_ids = prev_ids + own_ids + mem_ids + own_ids
    poses = [[pose_ref[frame] for frame in ids] for ids in (own_ids, next_ids, key_ids)]
    frame_of = lax.broadcasted_iota(jnp.int32, (1, row_count), 1) // (row_count // FR_DEV)
    for head in range(heads):
        for j, key_pose in enumerate(poses[2]):
            row = jnp.zeros((1, row_count), F32)
            for a, query_pose in enumerate(poses[1] if j >= 2 * FR_DEV + MEM else poses[0]):
                value = bias_ref[head, query_pose, key_pose] * LOG2E
                if j < FR_DEV:
                    value = jnp.where(me == 0, BLOCKED_LOGIT, value)
                row = jnp.where(frame_of == a, value, row)
            rows_ref[head, j : j + 1, :] = row

    dyns = dyn_frames(bank, last_frame)
    bit = by_role(me, *last_bits)
    upper = (me & bit) != 0
    picks = []
    for frame in mem_ids + pair_ids:
        source = place_of(frame, dyns)
        local = jnp.where(frame == 0, jnp.logical_not(upper), upper)
        local = jnp.where(source < len(dyns), has_dyn(me, frame, (peers - 1) & ~bit), local)
        picks.append(source * 2 + local.astype(jnp.int32))
    places = dyns + [jnp.where(upper, last_frame, 0), jnp.where(upper, 0, last_frame)]
    terms = [name == frame for frame in places for name in mem_ids + pair_ids]
    owned = []
    for group in (me, me ^ 1):
        for j in range(FR_DEV):
            frame = group * FR_DEV + j
            place = place_of(frame, dyns)
            named = jnp.logical_or(place < len(dyns), jnp.logical_or(frame == 0, frame == last_frame))
            owned.append(place * 2 + named.astype(jnp.int32))
    lanes = codes_ref.shape[1]
    for row, code in ((PICK, pack(picks, PLACE_BITS)), (SUM, pack(terms, 1)), (OWNED, pack(owned, PLACE_BITS))):
        codes_ref[row : row + 1, :] = jnp.full((1, lanes), code, jnp.int32)


def split_kernel(peers, bank_ref, mine_ref, pair_ref, out_ref):
    me = lax.axis_index("tm")
    frame_len = out_ref.shape[1]
    dyns = dyn_frames(bank_of(bank_ref), peers * FR_DEV - 1)
    places = [(has_dyn(me, dyn, 0), dyn % FR_DEV) for dyn in dyns]
    places.append((has_end(me, 0, peers), jnp.where(me < peers // 2, 0, FR_DEV - 1)))
    for j, (local, frame) in enumerate(places):
        start = pl.multiple_of(((me & 1) * FR_DEV + frame) * frame_len, frame_len)
        part = pl.ds(start, frame_len)
        choose(out_ref.at[j], local, mine_ref.at[part], pair_ref.at[part])


def step_kernel(peers, even_done, odd_done, bank_ref, mine_ref, got_ref, out_ref):
    me = lax.axis_index("tm")
    done = by_role(me, even_done, odd_done)
    dyns = dyn_frames(bank_of(bank_ref), peers * FR_DEV - 1)
    flags = [has_dyn(me, dyn, done) for dyn in dyns] + [has_end(me, done, peers)]
    for j, flag in enumerate(flags):
        choose(out_ref.at[j], flag, mine_ref.at[j], got_ref.at[j])


def pick_kernel(codes_ref, mine_ref, got_ref, own_out, pair_out):
    code = code_of(codes_ref, PICK)
    for o, out in enumerate((own_out, pair_out)):
        for m in range(MEM):
            pick = field(code, o * MEM + m, PLACE_BITS)
            source = pick >> 1
            choose(out.at[m], (pick & 1) != 0, mine_ref.at[source], got_ref.at[source])


def dot(a, b, left, right):
    return lax.dot_general(a, b, (((left,), (right,)), ((), ())), preferred_element_type=F32)


def logits_of(keys, query, rows_ref, head, piece):
    frame_len = query.shape[0] // FR_DEV
    raw = dot(keys, query, 1, 1) * (FACTOR * LOG2E)
    parts = []
    for j in range(FR_DEV):
        row = piece * FR_DEV + j
        parts.append(raw[j * frame_len : (j + 1) * frame_len] + rows_ref[head, row : row + 1, :])
    return jnp.concatenate(parts, axis=0)


def joined_parts(joined_ref, cols):
    rows = joined_ref.shape[0] // 2 // DEPTH * DEPTH
    return joined_ref[0:rows, cols], joined_ref[rows : 2 * rows, cols]


def prev_parts(outer_refs, pair_ref, cols):
    even = (lax.axis_index("tm") & 1) == 0
    parts = zip(outer_refs, joined_parts(pair_ref, cols))
    return tuple(jnp.where(even, outer[:, cols], pair) for outer, pair in parts)


def stats_kernel(rows_ref, queries_ref, outer_key_ref, outer_value_ref, pair_ref, own_ref, stats_ref, queries_out):
    queries_out[...] = queries_ref[...]
    for head in range(queries_ref.shape[1] // DEPTH):
        cols = pl.ds(head * DEPTH, DEPTH)
        query, cotangent = joined_parts(queries_ref, cols)
        pieces = [prev_parts((outer_key_ref, outer_value_ref), pair_ref, cols), joined_parts(own_ref, cols)]
        logits = [logits_of(keys, query, rows_ref, head, piece) for piece, (keys, _) in enumerate(pieces)]
        peak = functools.reduce(jnp.maximum, [jnp.max(block, axis=0, keepdims=True) for block in logits])
        exps = [jnp.exp2(block - peak) for block in logits]
        slopes = [dot(values, cotangent, 1, 1) for _, values in pieces]
        stats_ref[head, 0:1, :] = peak
        stats_ref[head, 1:2, :] = sum(jnp.sum(e, axis=0, keepdims=True) for e in exps)
        stats_ref[head, 2:3, :] = sum(jnp.sum(e * s, axis=0, keepdims=True) for e, s in zip(exps, slopes))


def memory_kernel(rows_ref, part_ref, queries_ref, mine_ref, got_ref, stats_ref, mem_same_ref, mem_other_ref):
    even = (lax.axis_index("tm") & 1) == 0
    frame_len = mine_ref.shape[1]
    heads = queries_ref.shape[1] // DEPTH

    def products(head):
        cols = pl.ds(head * DEPTH, DEPTH)
        query, cotangent = joined_parts(queries_ref, cols)
        mine = mine_ref[:, :, cols].reshape(MEM * frame_len, DEPTH)
        got = got_ref[:, :, cols].reshape(MEM * frame_len, DEPTH)
        keys, values = jnp.where(even, mine, got), jnp.where(even, got, mine)
        return logits_of(keys, query, rows_ref, head, 2), dot(values, cotangent, 1, 1)

    def rounded(head, logits, slopes):
        part_peak = part_ref[head, 0:1, :]
        peak = jnp.maximum(part_peak, jnp.max(logits, axis=0, keepdims=True))
        exps = jnp.exp2(logits - peak)
        scale = jnp.exp2(part_peak - peak)
        total = part_ref[head, 1:2, :] * scale + jnp.sum(exps, axis=0, keepdims=True)
        inverse = 1.0 / total
        spread = (part_ref[head, 2:3, :] * scale + jnp.sum(exps * slopes, axis=0, keepdims=True)) * inverse
        stats_ref[head, 0:1, :] = peak
        stats_ref[head, 1:2, :] = inverse
        stats_ref[head, 2:3, :] = spread
        probs = exps * inverse
        return probs.astype(BF16), (probs * (slopes - spread)).astype(BF16)

    def store(head, weights, dlogits):
        cols = pl.ds(head * DEPTH, DEPTH)
        query, cotangent = joined_parts(queries_ref, cols)
        key_part = (dot(dlogits, query, 1, 0) * FACTOR).astype(BF16).reshape(MEM, frame_len, DEPTH)
        value_part = dot(weights, cotangent, 1, 0).astype(BF16).reshape(MEM, frame_len, DEPTH)
        mem_same_ref[:, :, cols] = jnp.where(even, key_part, value_part)
        mem_other_ref[:, :, cols] = jnp.where(even, value_part, key_part)

    ahead = products(0)
    behind = None
    for head in range(heads):
        now = ahead
        if head + 1 < heads:
            ahead = products(head + 1)
        if behind is not None:
            store(head - 1, *behind)
        behind = rounded(head, *now)
    store(heads - 1, *behind)


def probs_of(keys, values, query, cotangent, rows_ref, stats_ref, head, piece):
    logits = logits_of(keys, query, rows_ref, head, piece)
    probs = jnp.exp2(logits - stats_ref[head, 0:1, :]) * stats_ref[head, 1:2, :]
    dlogits = probs * (dot(values, cotangent, 1, 1) - stats_ref[head, 2:3, :])
    return probs.astype(BF16), dlogits.astype(BF16)


def next_kernel(rows_ref, stats_ref, queries_ref, own_ref, term_ref, sum_ref):
    for head in range(queries_ref.shape[1] // DEPTH):
        cols = pl.ds(head * DEPTH, DEPTH)
        query, cotangent = joined_parts(queries_ref, cols)
        keys, values = joined_parts(own_ref, cols)
        weights, dlogits = probs_of(keys, values, query, cotangent, rows_ref, stats_ref, head, 3)
        sum_ref[0, :, cols] = term_ref[0, :, cols] + dot(dlogits, query, 1, 0) * FACTOR
        sum_ref[1, :, cols] = term_ref[1, :, cols] + dot(weights, cotangent, 1, 0)


def rest_kernel(
    rows_ref,
    stats_ref,
    queries_ref,
    outer_key_ref,
    outer_value_ref,
    pair_ref,
    joined_ref,
    mine_ref,
    got_ref,
    attended_ref,
    grad_query_ref,
    own_ref,
    stats_out_ref,
):
    even = (lax.axis_index("tm") & 1) == 0
    frame_len = mine_ref.shape[1]
    stats_out_ref[...] = stats_ref[...]
    for head in range(queries_ref.shape[1] // DEPTH):
        cols = pl.ds(head * DEPTH, DEPTH)
        query, cotangent = joined_parts(queries_ref, cols)
        mine = mine_ref[:, :, cols].reshape(MEM * frame_len, DEPTH)
        got = got_ref[:, :, cols].reshape(MEM * frame_len, DEPTH)
        pieces = (
            prev_parts((outer_key_ref, outer_value_ref), pair_ref, cols),
            joined_parts(joined_ref, cols),
            (jnp.where(even, mine, got), jnp.where(even, got, mine)),
        )
        attended = grad_query = 0.0
        for piece, (keys, values) in enumerate(pieces):
            weights, dlogits = probs_of(keys, values, query, cotangent, rows_ref, stats_ref, head, piece)
            attended += dot(values, weights, 0, 0)
            grad_query += dot(keys, dlogits, 0, 0)
            if piece == 1:
                own_ref[0, :, cols] = dot(dlogits, query, 1, 0) * FACTOR
                own_ref[1, :, cols] = dot(weights, cotangent, 1, 0)
        attended_ref[:, cols] = attended.T.astype(BF16)
        grad_query_ref[:, cols] = (grad_query * FACTOR).T.astype(BF16)


def sum_kernel(codes_ref, mine_ref, got_ref, keep_ref, send_ref):
    code = code_of(codes_ref, SUM)
    kept = keep_ref.shape[0]
    terms = [ref[m].astype(F32) for ref in (mine_ref, got_ref) for m in range(MEM)]
    for place in range(kept + 1):
        value = sum(
            jnp.where(field(code, place * len(terms) + t, 1) != 0, term, 0.0) for t, term in enumerate(terms)
        )
        if place < kept:
            keep_ref[place] = value
        if place != kept - 1:
            send_ref[min(place, kept - 1)] = value.astype(BF16)


def add_kernel(keep_ref, got_ref, out_ref, send_ref):
    value = keep_ref[...] + got_ref[...].astype(F32)
    out_ref[...] = value
    send_ref[...] = value.astype(BF16)


def mark_kernel(mark_ref):
    mark_ref[...] = jnp.zeros(mark_ref.shape, F32)


def owned_kernel(codes_ref, keep_ref, got_ref, mine_ref, pair_ref):
    code = code_of(codes_ref, OWNED)
    for o, out in enumerate((mine_ref, pair_ref)):
        for j in range(FR_DEV):
            owned = field(code, o * FR_DEV + j, PLACE_BITS)
            place = owned >> 1
            named = (owned & 1) != 0

            @pl.when(named)
            def _(out=out, j=j, place=place):
                value = keep_ref[place] + got_ref[place].astype(F32)
                out[j] = value.astype(out.dtype)

            @pl.when(jnp.logical_not(named))
            def _(out=out, j=j):
                out[j] = jnp.zeros(out.shape[1:], out.dtype)


def final_kernel(own_ref, mine_ref, got_ref, grad_key_ref, grad_value_ref):
    even = (lax.axis_index("tm") & 1) == 0
    rows = grad_key_ref.shape
    mine = mine_ref[...].reshape(rows)
    got = got_ref[...].astype(F32).reshape(rows)
    grad_key_ref[...] = (own_ref[0] + jnp.where(even, mine, got)).astype(BF16)
    grad_value_ref[...] = (own_ref[1] + jnp.where(even, got, mine)).astype(BF16)


def body(
    query_states,
    key_states,
    value_states,
    grad_out,
    camera_pose,
    pose_bias,
    memory_index,
    bank_frames,
):
    row_count, width = query_states.shape
    frame_len = row_count // FR_DEV
    heads = pose_bias.shape[0]
    slots = bank_frames.shape[0]
    peers = lax.axis_size("tm")
    bits = [1 << i for i in range(1, peers.bit_length() - 1)]
    turns = list(zip(bits, bits[::-1]))
    piece_flops = 2 * row_count * row_count * width
    bank_frames = bank_frames.reshape(1, slots)
    last_bits = turns[-1]

    def join(kernel, rows, arrays, scratch, name):
        return pl.pallas_call(
            kernel,
            out_shape=shape(BF16, rows, width),
            in_specs=[pl.BlockSpec(memory_space=pltpu.HBM)] * len(arrays),
            out_specs=VMEM,
            scratch_shapes=[*scratch, pltpu.SemaphoreType.DMA((len(arrays),))],
            compiler_params=pltpu.CompilerParams(vmem_limit_bytes=VMEM_LIMIT),
            name=name,
        )(*(pltpu.with_memory_space_constraint(array, pltpu.HBM) for array in arrays))

    joined = join(
        join_kernel,
        2 * row_count + TAIL,
        [memory_index, key_states, value_states],
        [pltpu.VMEM(memory_index.shape, jnp.int32)],
        "join",
    )
    outer_keys = shift(key_states, 1, 1, peers)
    pair = swap(joined, 1, 1, peers)
    queries = join(join_queries_kernel, 2 * row_count, [query_states, grad_out], [], "join_queries")

    bias_rows = -(-(3 * FR_DEV + MEM) // 8) * 8
    rows, codes, values_out = call(
        functools.partial(plan_kernel, peers, last_bits),
        [shape(F32, heads, bias_rows, row_count), shape(jnp.int32, 8, 128), shape(BF16, row_count, width)],
        [pair, joined],
        scalars=[bank_frames, memory_index, camera_pose, pose_bias],
        after=[outer_keys],
        flops=HIDING * piece_flops,
        name="plan",
    )
    outer_values = shift(values_out, 1, 1, peers)
    held = shape(BF16, slots - 1, frame_len, width)
    sums = shape(F32, slots - 1, frame_len, width)
    (mine,) = call(functools.partial(split_kernel, peers), [held], [bank_frames, joined, pair], name="split")
    stats = shape(F32, heads, 8, row_count)
    part, queries_out = call(
        stats_kernel,
        [stats, shape(BF16, 2 * row_count, width)],
        [rows, queries, outer_keys, outer_values, pair, joined], flops=HIDING * piece_flops, name="stats")
    next_queries = lax.ppermute(queries_out, "tm", [(i, i - 1) for i in range(1, peers)])
    even_done = odd_done = 1
    for step, (even_bit, odd_bit) in enumerate(turns):
        got = swap(mine, even_bit, odd_bit, peers)
        if step + 1 < len(turns):
            kernel = functools.partial(step_kernel, peers, even_done, odd_done)
            (mine,) = call(kernel, [held], [bank_frames, mine, got], after=[codes], name="step")
        even_done |= even_bit
        odd_done |= odd_bit
    chosen = shape(BF16, MEM, frame_len, width)
    mem_mine, mem_send = call(pick_kernel, [chosen] * 2, [codes, mine, got], after=[part], flops=HIDING * piece_flops, name="pick")
    mem_got = swap(mem_send, 1, 1, peers)

    stats_all, mem_same, mem_other = call(
        memory_kernel,
        [stats, chosen, chosen],
        [rows, part, queries, mem_mine, mem_got],
        name="memory",
    )
    same_got = swap(mem_other, 1, 1, peers)
    (arrived,) = call(
        mark_kernel,
        [shape(F32, 8, 128)],
        [],
        after=[next_queries],
        flops=HIDING * piece_flops,
        name="arrived",
    )
    keep, send = call(sum_kernel, [sums, held], [codes, mem_same, same_got], after=[arrived], name="sum")
    pair_sums = shape(F32, 2, row_count, width)
    attended, grad_query, own_terms, stats_sent = call(
        rest_kernel,
        [shape(BF16, row_count, width)] * 2 + [pair_sums, stats],
        [rows, stats_all, queries, outer_keys, outer_values, pair, joined, mem_mine, mem_got],
        after=[send],
        name="rest",
    )
    next_stats = lax.ppermute(stats_sent, "tm", [(i, i - 1) for i in range(1, peers)])
    (own,) = call(
        next_kernel,
        [pair_sums],
        [rows, next_stats, next_queries, joined, own_terms],
        flops=HIDING * piece_flops,
        name="next",
    )
    for step, (even_bit, odd_bit) in enumerate(turns[::-1]):
        got = swap(send, even_bit, odd_bit, peers)
        if step + 1 < len(turns):
            keep, send = call(add_kernel, [sums, held], [keep, got], after=[own_terms], name="add")
    owned = shape(F32, FR_DEV, frame_len, width)
    owned_mine, owned_send = call(
        owned_kernel,
        [owned, shape(BF16, FR_DEV, frame_len, width)],
        [codes, keep, got],
        after=[own],
        name="owned",
    )
    owned_got = swap(owned_send, 1, 1, peers)
    grad_key, grad_value = call(
        final_kernel, [shape(BF16, row_count, width)] * 2, [own, owned_mine, owned_got], name="final"
    )
    return (attended, grad_query, grad_key, grad_value)


def solution(mesh):
    rows = P(("traj", "tm"), None)
    in_specs = (rows, rows, rows, rows, P("traj"), P(), rows, P("traj"))
    return jax.shard_map(body, mesh=mesh, in_specs=in_specs, out_specs=(rows,) * 4, check_vma=False)
```

```python
import functools
import math

import jax
import jax.numpy as jnp
from jax import lax
from jax.experimental import pallas as pl
from jax.experimental.pallas import tpu as pltpu
from jax.sharding import PartitionSpec as P

FR_DEV = 2
MEM = 2
DEPTH = 128
TAIL = 16

BLOCKED_LOGIT = -1e30
LOG2E = math.log2(math.e)
FACTOR = 1.0 / math.sqrt(DEPTH)

SMEM = pl.BlockSpec(memory_space=pltpu.SMEM)
VMEM = pl.BlockSpec(memory_space=pltpu.VMEM)
ANY = pl.BlockSpec(memory_space=pl.ANY)
HIDING = 200
VMEM_LIMIT = 32 * 1024 * 1024
BF16, F32 = jnp.bfloat16, jnp.float32


def shape(dtype, *dims):
    return jax.ShapeDtypeStruct(dims, dtype)


def call(kernel, outs, arrays, scalars=(), after=(), flops=0, name=None):
    count = len(scalars) + len(arrays)

    def run(*refs):
        kernel(*refs[:count], *refs[count + len(after) :])

    return pl.pallas_call(
        run,
        out_shape=outs,
        in_specs=[SMEM] * len(scalars) + [VMEM] * len(arrays) + [ANY] * len(after),
        out_specs=[VMEM] * len(outs),
        compiler_params=pltpu.CompilerParams(vmem_limit_bytes=VMEM_LIMIT),
        cost_estimate=pl.CostEstimate(flops=flops, bytes_accessed=0, transcendentals=0) if flops else None,
        name=name,
    )(*scalars, *arrays, *after)


def swap(block, even_bit, odd_bit, peers):
    return lax.ppermute(block, "tm", [(i, i ^ (odd_bit if i & 1 else even_bit)) for i in range(peers)])


def shift(block, by, start, peers):
    pairs = [(i, i + by) for i in range(start, peers, 2) if 0 <= i + by < peers]
    return lax.ppermute(block, "tm", pairs)


def lane_value(row, lane):
    lanes = lax.broadcasted_iota(jnp.int32, row.shape, 1)
    return jnp.max(jnp.where(lanes == lane, row, 0))


def bank_of(bank_ref):
    row = bank_ref[...]
    return [lane_value(row, slot) for slot in range(row.shape[1])]


def dyn_frames(bank, last_frame):
    found = [jnp.int32(0)] * (len(bank) - 2)
    seen = jnp.int32(0)
    for frame in bank:
        free = jnp.logical_and(frame != 0, frame != last_frame)
        for j in range(len(found)):
            found[j] = jnp.where(jnp.logical_and(free, seen == j), frame, found[j])
        seen = seen + free.astype(jnp.int32)
    return found


def place_of(frame, dyns):
    place = jnp.int32(len(dyns))
    for j, dyn in enumerate(dyns):
        place = jnp.where(frame == dyn, j, place)
    return place


def choose(out, take_first, first, second):
    @pl.when(take_first)
    def _():
        out[...] = first[...]

    @pl.when(jnp.logical_not(take_first))
    def _():
        out[...] = second[...]


def has_end(me, done, peers):
    return jnp.logical_or((me & ~done) == 0, (me | done) == peers - 1)


def has_dyn(me, frame, done):
    return ((me ^ (frame // FR_DEV)) & ~done) == 0


def by_role(me, even_value, odd_value):
    return jnp.where((me & 1) == 0, even_value, odd_value)


def join_kernel(index_ref, key_ref, value_ref, joined_ref, index_buf, sems):
    rows = key_ref.shape[0]
    copies = [
        pltpu.make_async_copy(index_ref, index_buf, sems.at[0]),
        pltpu.make_async_copy(key_ref, joined_ref.at[pl.ds(0, rows)], sems.at[1]),
        pltpu.make_async_copy(value_ref, joined_ref.at[pl.ds(rows, rows)], sems.at[2]),
    ]
    for copy in copies:
        copy.start()
    copies[0].wait()
    width = joined_ref.shape[1]
    lane = lax.broadcasted_iota(jnp.int32, (TAIL, width), 1) // DEPTH
    tail = jnp.zeros((TAIL, width), jnp.int32)
    for m in range(MEM):
        tail = jnp.where(lane == m, index_buf[0:1, m : m + 1], tail)
    joined_ref[2 * rows : 2 * rows + TAIL, :] = tail.astype(F32).astype(BF16)
    copies[1].wait()
    copies[2].wait()


def join_queries_kernel(query_ref, cotangent_ref, joined_ref, sems):
    rows = query_ref.shape[0]
    copies = [
        pltpu.make_async_copy(ref, joined_ref.at[pl.ds(j * rows, rows)], sems.at[j])
        for j, ref in enumerate((query_ref, cotangent_ref))
    ]
    for copy in copies:
        copy.start()
    for copy in copies:
        copy.wait()


def pack(fields, width):
    code = jnp.int32(0)
    for j, field in enumerate(fields):
        code = code | (field.astype(jnp.int32) << (j * width))
    return code


def field(code, j, width):
    return (code >> (j * width)) & ((1 << width) - 1)


def code_of(codes_ref, row):
    return jnp.max(codes_ref[row : row + 1, :])


PICK, SUM, OWNED = range(3)
PLACE_BITS = 4
PREV, OWN, MEMORY, NEXT, PAIR = range(5)


def plan_kernel(
    peers, last_bits, bank_ref, index_ref, pose_ref, bias_ref, pair_ref, joined_ref, rows_ref, codes_ref, values_out
):
    me = lax.axis_index("tm")
    last_frame = peers * FR_DEV - 1
    heads, _, row_count = rows_ref.shape
    values_out[...] = joined_ref[row_count : 2 * row_count, :]
    bank = [bank_ref[0, slot] for slot in range(bank_ref.shape[1])]
    tail = pair_ref.shape[0] - TAIL
    pair_ids = []
    for m in range(MEM):
        slot = jnp.max(pair_ref[tail : tail + TAIL, m * DEPTH : (m + 1) * DEPTH].astype(F32)).astype(jnp.int32)
        pair_ids.append(bank_ref[0, slot])
    mem_ids = [bank_ref[0, index_ref[0, m]] for m in range(MEM)]

    own_ids = [me * FR_DEV + j for j in range(FR_DEV)]
    prev_ids = [jnp.maximum(own - FR_DEV, 0) for own in own_ids]
    next_ids = [jnp.minimum(own + FR_DEV, last_frame) for own in own_ids]
    pair_own_ids = [(me ^ 1) * FR_DEV + j for j in range(FR_DEV)]
    pieces = ((prev_ids, own_ids), (own_ids, own_ids), (mem_ids, own_ids), (own_ids, next_ids), (pair_ids, pair_own_ids))
    poses = [([pose_ref[f] for f in key_ids], [pose_ref[f] for f in query_ids]) for key_ids, query_ids in pieces]
    frame_of = lax.broadcasted_iota(jnp.int32, (1, row_count), 1) // (row_count // FR_DEV)
    for head in range(heads):
        for piece, (key_poses, query_poses) in enumerate(poses):
            for j, key_pose in enumerate(key_poses):
                row = jnp.zeros((1, row_count), F32)
                for a, query_pose in enumerate(query_poses):
                    value = bias_ref[head, query_pose, key_pose] * LOG2E
                    if piece == PREV:
                        value = jnp.where(me == 0, BLOCKED_LOGIT, value)
                    row = jnp.where(frame_of == a, value, row)
                rows_ref[head, piece * FR_DEV + j : piece * FR_DEV + j + 1, :] = row

    dyns = dyn_frames(bank, last_frame)
    bit = by_role(me, *last_bits)
    upper = (me & bit) != 0
    picks = []
    for frame in mem_ids + pair_ids:
        source = place_of(frame, dyns)
        local = jnp.where(frame == 0, jnp.logical_not(upper), upper)
        local = jnp.where(source < len(dyns), has_dyn(me, frame, (peers - 1) & ~bit), local)
        picks.append(source * 2 + local.astype(jnp.int32))
    far = jnp.where(upper, 0, last_frame)
    sums = [jnp.where(frame == far, len(dyns) + 1, place_of(frame, dyns)) for frame in mem_ids + pair_ids]
    owned = []
    for group in (me, me ^ 1):
        for j in range(FR_DEV):
            frame = group * FR_DEV + j
            place = place_of(frame, dyns)
            named = jnp.logical_or(place < len(dyns), jnp.logical_or(frame == 0, frame == last_frame))
            owned.append(place * 2 + named.astype(jnp.int32))
    lanes = codes_ref.shape[1]
    for row, code in ((PICK, pack(picks, PLACE_BITS)), (SUM, pack(sums, PLACE_BITS)), (OWNED, pack(owned, PLACE_BITS))):
        codes_ref[row : row + 1, :] = jnp.full((1, lanes), code, jnp.int32)


def split_kernel(peers, bank_ref, mine_ref, pair_ref, out_ref):
    me = lax.axis_index("tm")
    frame_len, half_width = out_ref.shape[2:]
    dyns = dyn_frames(bank_of(bank_ref), peers * FR_DEV - 1)
    places = [(has_dyn(me, dyn, 0), dyn % FR_DEV) for dyn in dyns]
    places.append((has_end(me, 0, peers), jnp.where(me < peers // 2, 0, FR_DEV - 1)))
    for j, (local, frame) in enumerate(places):
        for role in range(2):
            for source, taken in ((mine_ref, local), (pair_ref, jnp.logical_not(local))):

                @pl.when(jnp.logical_and((me & 1) == role, taken))
                def _(source=source, j=j, frame=frame, role=role):
                    for kind in range(2):
                        start = pl.multiple_of((kind * FR_DEV + frame) * frame_len, frame_len)
                        out_ref[j, kind] = source[pl.ds(start, frame_len), role * half_width : (role + 1) * half_width]


def step_kernel(peers, even_done, odd_done, bank_ref, mine_ref, got_ref, out_ref):
    me = lax.axis_index("tm")
    done = by_role(me, even_done, odd_done)
    dyns = dyn_frames(bank_of(bank_ref), peers * FR_DEV - 1)
    flags = [has_dyn(me, dyn, done) for dyn in dyns] + [has_end(me, done, peers)]
    for j, flag in enumerate(flags):
        choose(out_ref.at[j], flag, mine_ref.at[j], got_ref.at[j])


def pick_kernel(codes_ref, mine_ref, got_ref, own_out, pair_out):
    code = code_of(codes_ref, PICK)
    for o, out in enumerate((own_out, pair_out)):
        for m in range(MEM):
            pick = field(code, o * MEM + m, PLACE_BITS)
            source = pick >> 1
            choose(out.at[m], (pick & 1) != 0, mine_ref.at[source], got_ref.at[source])


def dot(a, b, left, right):
    return lax.dot_general(a, b, (((left,), (right,)), ((), ())), preferred_element_type=F32)


def logits_of(keys, query, rows_ref, head, piece):
    frame_len = query.shape[0] // FR_DEV
    raw = dot(keys, query, 1, 1) * (FACTOR * LOG2E)
    parts = []
    for j in range(FR_DEV):
        row = piece * FR_DEV + j
        parts.append(raw[j * frame_len : (j + 1) * frame_len] + rows_ref[head, row : row + 1, :])
    return jnp.concatenate(parts, axis=0)


def joined_parts(joined_ref, cols):
    rows = joined_ref.shape[0] // 2 // DEPTH * DEPTH
    return joined_ref[0:rows, cols], joined_ref[rows : 2 * rows, cols]


def head_cols(head):
    return pl.ds(head * DEPTH, DEPTH)


def part_of(logits, slopes):
    peak = jnp.max(logits, axis=0, keepdims=True)
    exps = jnp.exp2(logits - peak)
    return peak, jnp.sum(exps, axis=0, keepdims=True), jnp.sum(exps * slopes, axis=0, keepdims=True)


def merged(left, right):
    peak = jnp.maximum(left[0], right[0])
    scales = [jnp.exp2(part[0] - peak) for part in (left, right)]
    return peak, *(left[j] * scales[0] + right[j] * scales[1] for j in (1, 2))


def load_part(ref, head):
    return tuple(ref[head, j : j + 1, :] for j in range(3))


def store_part(ref, head, part):
    for j, row in enumerate(part):
        ref[head, j : j + 1, :] = row


def prev_parts(outer_refs, pair_ref, cols):
    even = (lax.axis_index("tm") & 1) == 0
    parts = zip(outer_refs, joined_parts(pair_ref, cols))
    return tuple(jnp.where(even, outer[:, cols], pair) for outer, pair in parts)


def stats_kernel(rows_ref, queries_ref, outer_keys, outer_values, pair_ref, own_ref, part_ref, queries_out):
    heads = queries_ref.shape[1] // DEPTH
    queries_out[...] = queries_ref[...]

    def products(head):
        cols = head_cols(head)
        query, cotangent = joined_parts(queries_ref, cols)
        pieces = ((PREV, prev_parts((outer_keys, outer_values), pair_ref, cols)), (OWN, joined_parts(own_ref, cols)))
        return [
            (logits_of(keys, query, rows_ref, head, piece), dot(values, cotangent, 1, 1))
            for piece, (keys, values) in pieces
        ]

    ahead = products(0)
    for head in range(heads):
        now = ahead
        if head + 1 < heads:
            ahead = products(head + 1)
        store_part(part_ref, head, merged(*(part_of(*piece) for piece in now)))


def rounded(part, logits, slopes):
    peak, total, spread = merged(part, part_of(logits, slopes))
    inverse = 1.0 / total
    stats = peak, inverse, spread * inverse
    return stats, *weights_of(stats, logits, slopes)


def weights_of(stats, logits, slopes):
    peak, inverse, spread = stats
    probs = jnp.exp2(logits - peak) * inverse
    return probs.astype(BF16), (probs * (slopes - spread)).astype(BF16)


def memory_kernel(
    codes_ref, rows_ref, part_ref, pair_part_ref, own_queries, pair_queries, own_mem, pair_mem, keep_ref, send_ref
):
    role = lax.axis_index("tm") & 1
    code = code_of(codes_ref, SUM)
    frame_len, half_width = own_mem.shape[2:]
    half = half_width // DEPTH
    groups = ((own_queries, own_mem, part_ref, MEMORY), (pair_queries, pair_mem, pair_part_ref, PAIR))
    work = [(g, local) for local in range(half) for g in range(len(groups))]
    keep_ref[...] = jnp.zeros(keep_ref.shape, F32)

    def products(g, local):
        queries, mem, _, piece = groups[g]
        query, cotangent = joined_parts(queries, head_cols(local))
        keys, values = (mem[:, kind, :, head_cols(local)].reshape(MEM * frame_len, DEPTH) for kind in range(2))
        return logits_of(keys, query, rows_ref, role * half + local, piece), dot(values, cotangent, 1, 1)

    def add(g, local, _, weights, dlogits):
        query, cotangent = joined_parts(groups[g][0], head_cols(local))
        terms = (dot(dlogits, query, 1, 0) * FACTOR, dot(weights, cotangent, 1, 0))
        for m in range(MEM):
            place = field(code, g * MEM + m, PLACE_BITS)
            for kind, term in enumerate(terms):
                part = term[m * frame_len : (m + 1) * frame_len].astype(BF16).astype(F32)
                keep_ref[place, kind, :, head_cols(local)] += part

    ahead = products(*work[0])
    behind = None
    for j, (g, local) in enumerate(work):
        now = ahead
        if j + 1 < len(work):
            ahead = products(*work[j + 1])
        if behind is not None:
            add(*work[j - 1], *behind)
        behind = rounded(load_part(groups[g][2], role * half + local), *now)
    add(*work[-1], *behind)
    kept = send_ref.shape[0]
    for place in range(kept):
        send_ref[place] = keep_ref[place if place + 1 < kept else kept].astype(BF16)


def next_kernel(rows_ref, stats_ref, pair_queries, outer_queries, own_ref, term_ref, sum_ref):
    even = (lax.axis_index("tm") & 1) == 0
    heads = pair_queries.shape[1] // DEPTH

    def operands(head):
        cols = head_cols(head)
        return [jnp.where(even, a, b) for a, b in zip(joined_parts(pair_queries, cols), joined_parts(outer_queries, cols))]

    def products(head):
        query, cotangent = operands(head)
        keys, values = joined_parts(own_ref, head_cols(head))
        return logits_of(keys, query, rows_ref, head, NEXT), dot(values, cotangent, 1, 1)

    ahead = products(0)
    for head in range(heads):
        now = ahead
        if head + 1 < heads:
            ahead = products(head + 1)
        weights, dlogits = weights_of(load_part(stats_ref, head), *now)
        query, cotangent = operands(head)
        cols = head_cols(head)
        sum_ref[0, :, cols] = term_ref[0, :, cols] + dot(dlogits, query, 1, 0) * FACTOR
        sum_ref[1, :, cols] = term_ref[1, :, cols] + dot(weights, cotangent, 1, 0)


def rest_kernel(
    rows_ref,
    part_ref,
    queries_ref,
    outer_keys,
    outer_values,
    pair_ref,
    own_ref,
    own_mem,
    other_mem,
    attended_ref,
    grad_query_ref,
    term_ref,
    stats_ref,
):
    role = lax.axis_index("tm") & 1
    frame_len, half_width = own_mem.shape[2:]
    heads = queries_ref.shape[1] // DEPTH
    half = half_width // DEPTH

    def pieces(head):
        cols = head_cols(head % half)
        prev = prev_parts((outer_keys, outer_values), pair_ref, head_cols(head))
        memory = [
            jnp.where(role == head // half, own_mem[:, kind, :, cols], other_mem[:, kind, :, cols]).reshape(
                MEM * frame_len, DEPTH
            )
            for kind in range(2)
        ]
        return (PREV, prev), (OWN, joined_parts(own_ref, head_cols(head))), (MEMORY, memory)

    def products(head):
        query, cotangent = joined_parts(queries_ref, head_cols(head))
        return [
            (logits_of(keys, query, rows_ref, head, piece), dot(values, cotangent, 1, 1))
            for piece, (keys, values) in pieces(head)
        ]

    ahead = products(0)
    for head in range(heads):
        now = ahead
        if head + 1 < heads:
            ahead = products(head + 1)
        cols = head_cols(head)
        query, cotangent = joined_parts(queries_ref, cols)
        stats, *last = rounded(load_part(part_ref, head), *now[-1])
        store_part(stats_ref, head, stats)
        rounds = [weights_of(stats, *now[PREV]), weights_of(stats, *now[OWN]), last]
        attended = grad_query = 0.0
        for (piece, (keys, values)), (weights, dlogits) in zip(pieces(head), rounds):
            attended += dot(values, weights, 0, 0)
            grad_query += dot(keys, dlogits, 0, 0)
            if piece == OWN:
                term_ref[0, :, cols] = dot(dlogits, query, 1, 0) * FACTOR
                term_ref[1, :, cols] = dot(weights, cotangent, 1, 0)
        attended_ref[:, cols] = attended.T.astype(BF16)
        grad_query_ref[:, cols] = (grad_query * FACTOR).T.astype(BF16)


def add_kernel(keep_ref, got_ref, out_ref, send_ref):
    value = keep_ref[0 : got_ref.shape[0]] + got_ref[...].astype(F32)
    out_ref[...] = value
    send_ref[...] = value.astype(BF16)


def owned_kernel(codes_ref, keep_ref, got_ref, mine_ref, pair_ref):
    code = code_of(codes_ref, OWNED)
    for o, out in enumerate((mine_ref, pair_ref)):
        for j in range(FR_DEV):
            owned = field(code, o * FR_DEV + j, PLACE_BITS)
            place = owned >> 1
            named = (owned & 1) != 0

            @pl.when(named)
            def _(out=out, j=j, place=place):
                value = keep_ref[place] + got_ref[place].astype(F32)
                out[j] = value.astype(out.dtype)

            @pl.when(jnp.logical_not(named))
            def _(out=out, j=j):
                out[j] = jnp.zeros(out.shape[1:], out.dtype)


def final_kernel(own_ref, mine_ref, got_ref, grad_key_ref, grad_value_ref):
    role = lax.axis_index("tm") & 1
    frame_len, half_width = mine_ref.shape[2:]
    for kind, out in enumerate((grad_key_ref, grad_value_ref)):
        for j in range(FR_DEV):
            rows = pl.ds(j * frame_len, frame_len)
            for half in range(2):
                cols = pl.ds(half * half_width, half_width)
                bank = jnp.where(role == half, mine_ref[j, kind], got_ref[j, kind].astype(F32))
                out[rows, cols] = (own_ref[kind, rows, cols] + bank).astype(BF16)


def body(
    query_states,
    key_states,
    value_states,
    grad_out,
    camera_pose,
    pose_bias,
    memory_index,
    bank_frames,
):
    row_count, width = query_states.shape
    frame_len = row_count // FR_DEV
    heads = pose_bias.shape[0]
    slots = bank_frames.shape[0]
    peers = lax.axis_size("tm")
    bits = [1 << i for i in range(1, peers.bit_length() - 1)]
    turns = list(zip(bits, bits[::-1]))
    even = (lax.axis_index("tm") & 1) == 0
    piece_flops = 2 * row_count * row_count * width
    bank_frames = bank_frames.reshape(1, slots)
    last_bits = turns[-1]

    def join(kernel, rows, arrays, scratch, name, after=()):
        def run(*refs):
            kernel(*refs[: len(arrays)], *refs[len(arrays) + len(after) :])

        return pl.pallas_call(
            run,
            out_shape=shape(BF16, rows, width),
            in_specs=[pl.BlockSpec(memory_space=pltpu.HBM)] * len(arrays) + [ANY] * len(after),
            out_specs=VMEM,
            scratch_shapes=[*scratch, pltpu.SemaphoreType.DMA((len(arrays),))],
            compiler_params=pltpu.CompilerParams(vmem_limit_bytes=VMEM_LIMIT),
            name=name,
        )(*(pltpu.with_memory_space_constraint(array, pltpu.HBM) for array in arrays), *after)

    joined = join(
        join_kernel,
        2 * row_count + TAIL,
        [memory_index, key_states, value_states],
        [pltpu.VMEM(memory_index.shape, jnp.int32)],
        "join",
    )
    half_width = width // 2
    first, second = slice(0, half_width), slice(half_width, width)
    outer_keys = shift(key_states, 1, 1, peers)
    pair = swap(joined, 1, 1, peers)
    held = shape(BF16, slots - 1, 2, frame_len, half_width)
    sums = shape(F32, slots - 1, 2, frame_len, half_width)
    (mine,) = call(functools.partial(split_kernel, peers), [held], [bank_frames, joined, pair], name="split")
    queries = join(join_queries_kernel, 2 * row_count, [query_states, grad_out], [], "join_queries", after=[mine])
    pair_queries = swap(queries, 1, 1, peers)
    own_half = jnp.where(even, queries[:, first], queries[:, second])
    pair_half = jnp.where(even, pair_queries[:, first], pair_queries[:, second])

    bias_rows = -(-(5 * FR_DEV) // 8) * 8
    rows, codes, values_out = call(
        functools.partial(plan_kernel, peers, last_bits),
        [shape(F32, heads, bias_rows, row_count), shape(jnp.int32, 8, 128), shape(BF16, row_count, width)],
        [pair, joined],
        scalars=[bank_frames, memory_index, camera_pose, pose_bias],
        after=[outer_keys],
        flops=HIDING * piece_flops,
        name="plan",
    )
    outer_values = shift(values_out, 1, 1, peers)
    even_done = odd_done = 1
    for step, (even_bit, odd_bit) in enumerate(turns):
        got = swap(mine, even_bit, odd_bit, peers)
        if step + 1 < len(turns):
            kernel = functools.partial(step_kernel, peers, even_done, odd_done)
            after = [codes, pair_queries]
            (mine,) = call(kernel, [held], [bank_frames, mine, got], after=after, name="step")
        even_done |= even_bit
        odd_done |= odd_bit

    stats = shape(F32, heads, 8, row_count)
    part, queries_out = call(
        stats_kernel,
        [stats, shape(BF16, 2 * row_count, width)],
        [rows, queries, outer_keys, outer_values, pair, joined],
        flops=HIDING * piece_flops,
        name="stats",
    )
    pair_part = swap(part, 1, 1, peers)
    next_queries = shift(queries_out, -1, 2, peers)
    chosen = shape(BF16, MEM, 2, frame_len, half_width)
    own_mem, pair_mem = call(pick_kernel, [chosen] * 2, [codes, mine, got], name="pick")
    keep, send = call(
        memory_kernel,
        [shape(F32, slots, 2, frame_len, half_width), held],
        [codes, rows, part, pair_part, own_half, pair_half, own_mem, pair_mem],
        flops=HIDING * piece_flops,
        name="memory",
    )
    other_mem = swap(pair_mem, 1, 1, peers)
    pair_sums = shape(F32, 2, row_count, width)
    attended, grad_query, own_terms, stats_all = call(
        rest_kernel,
        [shape(BF16, row_count, width)] * 2 + [pair_sums, stats],
        [rows, part, queries, outer_keys, outer_values, pair, joined, own_mem, other_mem],
        after=[send],
        flops=HIDING * piece_flops,
        name="rest",
    )
    next_stats = lax.ppermute(stats_all, "tm", [(i, i - 1) for i in range(1, peers)])
    (own,) = call(
        next_kernel,
        [pair_sums],
        [rows, next_stats, pair_queries, next_queries, joined, own_terms],
        flops=HIDING * piece_flops,
        name="next",
    )
    for step, (even_bit, odd_bit) in enumerate(turns[::-1]):
        got = swap(send, even_bit, odd_bit, peers)
        if step + 1 < len(turns):
            keep, send = call(add_kernel, [sums, held], [keep, got], after=[own_terms], name="add")
    owned_mine, owned_send = call(
        owned_kernel,
        [shape(F32, FR_DEV, 2, frame_len, half_width), shape(BF16, FR_DEV, 2, frame_len, half_width)],
        [codes, keep, got],
        after=[own],
        name="owned",
    )
    owned_got = swap(owned_send, 1, 1, peers)
    grad_key, grad_value = call(
        final_kernel, [shape(BF16, row_count, width)] * 2, [own, owned_mine, owned_got], name="final"
    )
    return (attended, grad_query, grad_key, grad_value)


def solution(mesh):
    rows = P(("traj", "tm"), None)
    in_specs = (rows, rows, rows, rows, P("traj"), P(), rows, P("traj"))
    return jax.shard_map(body, mesh=mesh, in_specs=in_specs, out_specs=(rows,) * 4, check_vma=False)
```

```python
import functools
import math

import jax
import jax.numpy as jnp
from jax import lax
from jax.experimental import pallas as pl
from jax.experimental.pallas import tpu as pltpu
from jax.sharding import PartitionSpec as P

FR_DEV = 2
MEM = 2
DEPTH = 128
TAIL = 16

BLOCKED_LOGIT = -1e30
LOG2E = math.log2(math.e)
FACTOR = 1.0 / math.sqrt(DEPTH)

SMEM = pl.BlockSpec(memory_space=pltpu.SMEM)
VMEM = pl.BlockSpec(memory_space=pltpu.VMEM)
ANY = pl.BlockSpec(memory_space=pl.ANY)
HIDING = 200
VMEM_LIMIT = 16 * 1024 * 1024
BF16, F32 = jnp.bfloat16, jnp.float32


def shape(dtype, *dims):
    return jax.ShapeDtypeStruct(dims, dtype)


def call(kernel, outs, arrays, scalars=(), after=(), flops=0, name=None):
    count = len(scalars) + len(arrays)

    def run(*refs):
        kernel(*refs[:count], *refs[count + len(after) :])

    return pl.pallas_call(
        run,
        out_shape=outs,
        in_specs=[SMEM] * len(scalars) + [VMEM] * len(arrays) + [ANY] * len(after),
        out_specs=[VMEM] * len(outs),
        compiler_params=pltpu.CompilerParams(vmem_limit_bytes=VMEM_LIMIT),
        cost_estimate=pl.CostEstimate(flops=flops, bytes_accessed=0, transcendentals=0) if flops else None,
        name=name,
    )(*scalars, *arrays, *after)


def swap(block, even_bit, odd_bit, peers):
    return lax.ppermute(block, "tm", [(i, i ^ (odd_bit if i & 1 else even_bit)) for i in range(peers)])


def shift(block, by, start, peers):
    pairs = [(i, i + by) for i in range(start, peers, 2) if 0 <= i + by < peers]
    return lax.ppermute(block, "tm", pairs)


def relays_of(by, start, peers):
    pairs = [(i, i + by) for i in range(start, peers, 2) if 0 <= i + by < peers]
    return {(i, j): i ^ 4 for i, j in pairs if peers == 8 and (i ^ j) >> 1 == 3}


def shift_first(block, by, start, peers):
    relays = relays_of(by, start, peers)
    pairs = [(i, i + by) for i in range(start, peers, 2) if 0 <= i + by < peers]
    return lax.ppermute(block, "tm", [(i, relays.get((i, j), j)) for i, j in pairs])


def shift_second(block, by, start, peers):
    pairs = [(relay, j) for (_, j), relay in relays_of(by, start, peers).items()]
    return lax.ppermute(block, "tm", pairs) if pairs else block


def through_relay(by, start, peers):
    me = lax.axis_index("tm")
    return functools.reduce(jnp.logical_or, [me == j for _, j in relays_of(by, start, peers)], me < 0)


def lane_value(row, lane):
    lanes = lax.broadcasted_iota(jnp.int32, row.shape, 1)
    return jnp.max(jnp.where(lanes == lane, row, 0))


def bank_of(bank_ref):
    row = bank_ref[...]
    return [lane_value(row, slot) for slot in range(row.shape[1])]


def dyn_frames(bank, last_frame):
    found = [jnp.int32(0)] * (len(bank) - 2)
    seen = jnp.int32(0)
    for frame in bank:
        free = jnp.logical_and(frame != 0, frame != last_frame)
        for j in range(len(found)):
            found[j] = jnp.where(jnp.logical_and(free, seen == j), frame, found[j])
        seen = seen + free.astype(jnp.int32)
    return found


def place_of(frame, dyns):
    place = jnp.int32(len(dyns))
    for j, dyn in enumerate(dyns):
        place = jnp.where(frame == dyn, j, place)
    return place


def choose(out, take_first, first, second):
    @pl.when(take_first)
    def _():
        out[...] = first[...]

    @pl.when(jnp.logical_not(take_first))
    def _():
        out[...] = second[...]


def has_end(me, done, peers):
    return jnp.logical_or((me & ~done) == 0, (me | done) == peers - 1)


def has_dyn(me, frame, done):
    return ((me ^ (frame // FR_DEV)) & ~done) == 0


def by_role(me, even_value, odd_value):
    return jnp.where((me & 1) == 0, even_value, odd_value)


def join_kernel(index_ref, key_ref, value_ref, joined_ref, index_buf, sems):
    rows = key_ref.shape[0]
    copies = [
        pltpu.make_async_copy(index_ref, index_buf, sems.at[0]),
        pltpu.make_async_copy(key_ref, joined_ref.at[pl.ds(0, rows)], sems.at[1]),
        pltpu.make_async_copy(value_ref, joined_ref.at[pl.ds(rows, rows)], sems.at[2]),
    ]
    for copy in copies:
        copy.start()
    copies[0].wait()
    width = joined_ref.shape[1]
    lane = lax.broadcasted_iota(jnp.int32, (TAIL, width), 1) // DEPTH
    tail = jnp.zeros((TAIL, width), jnp.int32)
    for m in range(MEM):
        tail = jnp.where(lane == m, index_buf[0:1, m : m + 1], tail)
    joined_ref[2 * rows : 2 * rows + TAIL, :] = tail.astype(F32).astype(BF16)
    copies[1].wait()
    copies[2].wait()


def join_queries_kernel(query_ref, cotangent_ref, joined_ref, sems):
    rows = query_ref.shape[0]
    copies = [
        pltpu.make_async_copy(ref, joined_ref.at[pl.ds(j * rows, rows)], sems.at[j])
        for j, ref in enumerate((query_ref, cotangent_ref))
    ]
    for copy in copies:
        copy.start()
    for copy in copies:
        copy.wait()


def pack(fields, width):
    code = jnp.int32(0)
    for j, field in enumerate(fields):
        code = code | (field.astype(jnp.int32) << (j * width))
    return code


def field(code, j, width):
    return (code >> (j * width)) & ((1 << width) - 1)


def code_of(codes_ref, row):
    return jnp.max(codes_ref[row : row + 1, :])


PICK, SUM, OWNED = range(3)
PLACE_BITS = 4
PREV, OWN, MEMORY, NEXT, PAIR = range(5)


def plan_kernel(
    peers,
    last_bits,
    bank_ref,
    index_ref,
    pose_ref,
    bias_ref,
    pair_ref,
    joined_ref,
    direct_keys,
    rows_ref,
    codes_ref,
    values_out,
    keys_out,
):
    me = lax.axis_index("tm")
    last_frame = peers * FR_DEV - 1
    heads, _, row_count = rows_ref.shape
    values_out[...] = joined_ref[row_count : 2 * row_count, :]
    keys_out[...] = direct_keys[...]
    bank = [bank_ref[0, slot] for slot in range(bank_ref.shape[1])]
    tail = pair_ref.shape[0] - TAIL
    pair_ids = []
    for m in range(MEM):
        slot = jnp.max(pair_ref[tail : tail + TAIL, m * DEPTH : (m + 1) * DEPTH].astype(F32)).astype(jnp.int32)
        pair_ids.append(bank_ref[0, slot])
    mem_ids = [bank_ref[0, index_ref[0, m]] for m in range(MEM)]

    own_ids = [me * FR_DEV + j for j in range(FR_DEV)]
    prev_ids = [jnp.maximum(own - FR_DEV, 0) for own in own_ids]
    next_ids = [jnp.minimum(own + FR_DEV, last_frame) for own in own_ids]
    pair_own_ids = [(me ^ 1) * FR_DEV + j for j in range(FR_DEV)]
    pieces = ((prev_ids, own_ids), (own_ids, own_ids), (mem_ids, own_ids), (own_ids, next_ids), (pair_ids, pair_own_ids))
    poses = [([pose_ref[f] for f in key_ids], [pose_ref[f] for f in query_ids]) for key_ids, query_ids in pieces]
    frame_of = lax.broadcasted_iota(jnp.int32, (1, row_count), 1) // (row_count // FR_DEV)
    for head in range(heads):
        for piece, (key_poses, query_poses) in enumerate(poses):
            for j, key_pose in enumerate(key_poses):
                row = jnp.zeros((1, row_count), F32)
                for a, query_pose in enumerate(query_poses):
                    value = bias_ref[head, query_pose, key_pose] * LOG2E
                    if piece == PREV:
                        value = jnp.where(me == 0, BLOCKED_LOGIT, value)
                    row = jnp.where(frame_of == a, value, row)
                rows_ref[head, piece * FR_DEV + j : piece * FR_DEV + j + 1, :] = row

    dyns = dyn_frames(bank, last_frame)
    bit = by_role(me, *last_bits)
    upper = (me & bit) != 0
    picks = []
    for frame in mem_ids + pair_ids:
        source = place_of(frame, dyns)
        local = jnp.where(frame == 0, jnp.logical_not(upper), upper)
        local = jnp.where(source < len(dyns), has_dyn(me, frame, (peers - 1) & ~bit), local)
        picks.append(source * 2 + local.astype(jnp.int32))
    far = jnp.where(upper, 0, last_frame)
    sums = [jnp.where(frame == far, len(dyns) + 1, place_of(frame, dyns)) for frame in mem_ids + pair_ids]
    owned = []
    for group in (me, me ^ 1):
        for j in range(FR_DEV):
            frame = group * FR_DEV + j
            place = place_of(frame, dyns)
            named = jnp.logical_or(place < len(dyns), jnp.logical_or(frame == 0, frame == last_frame))
            owned.append(place * 2 + named.astype(jnp.int32))
    lanes = codes_ref.shape[1]
    for row, code in ((PICK, pack(picks, PLACE_BITS)), (SUM, pack(sums, PLACE_BITS)), (OWNED, pack(owned, PLACE_BITS))):
        codes_ref[row : row + 1, :] = jnp.full((1, lanes), code, jnp.int32)


def split_kernel(peers, bank_ref, mine_ref, pair_ref, out_ref):
    me = lax.axis_index("tm")
    frame_len, half_width = out_ref.shape[2:]
    dyns = dyn_frames(bank_of(bank_ref), peers * FR_DEV - 1)
    places = [(has_dyn(me, dyn, 0), dyn % FR_DEV) for dyn in dyns]
    places.append((has_end(me, 0, peers), jnp.where(me < peers // 2, 0, FR_DEV - 1)))
    for j, (local, frame) in enumerate(places):
        for role in range(2):
            for source, taken in ((mine_ref, local), (pair_ref, jnp.logical_not(local))):

                @pl.when(jnp.logical_and((me & 1) == role, taken))
                def _(source=source, j=j, frame=frame, role=role):
                    for kind in range(2):
                        start = pl.multiple_of((kind * FR_DEV + frame) * frame_len, frame_len)
                        out_ref[j, kind] = source[pl.ds(start, frame_len), role * half_width : (role + 1) * half_width]


def step_kernel(peers, even_done, odd_done, bank_ref, mine_ref, got_ref, out_ref):
    me = lax.axis_index("tm")
    done = by_role(me, even_done, odd_done)
    dyns = dyn_frames(bank_of(bank_ref), peers * FR_DEV - 1)
    flags = [has_dyn(me, dyn, done) for dyn in dyns] + [has_end(me, done, peers)]
    for j, flag in enumerate(flags):
        choose(out_ref.at[j], flag, mine_ref.at[j], got_ref.at[j])


def pick_kernel(codes_ref, mine_ref, got_ref, own_out, pair_out):
    code = code_of(codes_ref, PICK)
    for o, out in enumerate((own_out, pair_out)):
        for m in range(MEM):
            pick = field(code, o * MEM + m, PLACE_BITS)
            source = pick >> 1
            choose(out.at[m], (pick & 1) != 0, mine_ref.at[source], got_ref.at[source])


def dot(a, b, left, right):
    return lax.dot_general(a, b, (((left,), (right,)), ((), ())), preferred_element_type=F32)


def logits_of(keys, query, rows_ref, head, piece):
    frame_len = query.shape[0] // FR_DEV
    raw = dot(keys, query, 1, 1) * (FACTOR * LOG2E)
    parts = []
    for j in range(FR_DEV):
        row = piece * FR_DEV + j
        parts.append(raw[j * frame_len : (j + 1) * frame_len] + rows_ref[head, row : row + 1, :])
    return jnp.concatenate(parts, axis=0)


def joined_parts(joined_ref, cols):
    rows = joined_ref.shape[0] // 2 // DEPTH * DEPTH
    return joined_ref[0:rows, cols], joined_ref[rows : 2 * rows, cols]


def head_cols(head):
    return pl.ds(head * DEPTH, DEPTH)


def part_of(logits, slopes):
    peak = jnp.max(logits, axis=0, keepdims=True)
    exps = jnp.exp2(logits - peak)
    return peak, jnp.sum(exps, axis=0, keepdims=True), jnp.sum(exps * slopes, axis=0, keepdims=True)


def merged(left, right):
    peak = jnp.maximum(left[0], right[0])
    scales = [jnp.exp2(part[0] - peak) for part in (left, right)]
    return peak, *(left[j] * scales[0] + right[j] * scales[1] for j in (1, 2))


def load_part(ref, head):
    return tuple(ref[head, j : j + 1, :] for j in range(3))


def store_part(ref, head, part):
    for j, row in enumerate(part):
        ref[head, j : j + 1, :] = row


def prev_parts(peers, direct_keys, relayed_keys, outer_values, pair_ref, cols):
    even = (lax.axis_index("tm") & 1) == 0
    keys = jnp.where(through_relay(1, 1, peers), relayed_keys[:, cols], direct_keys[:, cols])
    parts = zip((keys, outer_values[:, cols]), joined_parts(pair_ref, cols))
    return tuple(jnp.where(even, outer, pair) for outer, pair in parts)


def stats_kernel(
    peers,
    rows_ref,
    queries_ref,
    direct_keys,
    relayed_keys,
    outer_values,
    pair_ref,
    own_ref,
    part_ref,
    queries_out,
    cotangent_out,
):
    heads = queries_ref.shape[1] // DEPTH
    rows = queries_out.shape[0]
    queries_out[...] = queries_ref[0:rows]
    cotangent_out[...] = queries_ref[rows : 2 * rows]

    def products(head):
        cols = head_cols(head)
        query, cotangent = joined_parts(queries_ref, cols)
        pieces = ((PREV, prev_parts(peers, direct_keys, relayed_keys, outer_values, pair_ref, cols)), (OWN, joined_parts(own_ref, cols)))
        return [
            (logits_of(keys, query, rows_ref, head, piece), dot(values, cotangent, 1, 1))
            for piece, (keys, values) in pieces
        ]

    ahead = products(0)
    for head in range(heads):
        now = ahead
        if head + 1 < heads:
            ahead = products(head + 1)
        store_part(part_ref, head, merged(*(part_of(*piece) for piece in now)))


def rounded(part, logits, slopes):
    peak, total, spread = merged(part, part_of(logits, slopes))
    inverse = 1.0 / total
    stats = peak, inverse, spread * inverse
    return stats, *weights_of(stats, logits, slopes)


def weights_of(stats, logits, slopes):
    peak, inverse, spread = stats
    probs = jnp.exp2(logits - peak) * inverse
    return probs.astype(BF16), (probs * (slopes - spread)).astype(BF16)


def memory_kernel(
    codes_ref, rows_ref, part_ref, pair_part_ref, own_queries, pair_queries, own_mem, pair_mem, keep_ref, send_ref
):
    role = lax.axis_index("tm") & 1
    code = code_of(codes_ref, SUM)
    frame_len, half_width = own_mem.shape[2:]
    half = half_width // DEPTH
    groups = ((own_queries, own_mem, part_ref, MEMORY), (pair_queries, pair_mem, pair_part_ref, PAIR))
    work = [(g, local) for local in range(half) for g in range(len(groups))]
    keep_ref[...] = jnp.zeros(keep_ref.shape, F32)

    def products(g, local):
        queries, mem, _, piece = groups[g]
        query, cotangent = joined_parts(queries, head_cols(local))
        keys, values = (mem[:, kind, :, head_cols(local)].reshape(MEM * frame_len, DEPTH) for kind in range(2))
        return logits_of(keys, query, rows_ref, role * half + local, piece), dot(values, cotangent, 1, 1)

    def add(g, local, _, weights, dlogits):
        query, cotangent = joined_parts(groups[g][0], head_cols(local))
        terms = (dot(dlogits, query, 1, 0) * FACTOR, dot(weights, cotangent, 1, 0))
        for m in range(MEM):
            place = field(code, g * MEM + m, PLACE_BITS)
            for kind, term in enumerate(terms):
                part = term[m * frame_len : (m + 1) * frame_len].astype(BF16).astype(F32)
                keep_ref[place, kind, :, head_cols(local)] += part

    ahead = products(*work[0])
    behind = None
    for j, (g, local) in enumerate(work):
        now = ahead
        if j + 1 < len(work):
            ahead = products(*work[j + 1])
        if behind is not None:
            add(*work[j - 1], *behind)
        behind = rounded(load_part(groups[g][2], role * half + local), *now)
    add(*work[-1], *behind)
    kept = send_ref.shape[0]
    for place in range(kept):
        send_ref[place] = keep_ref[place if place + 1 < kept else kept].astype(BF16)


def next_kernel(
    peers,
    rows_ref,
    stats_ref,
    pair_queries,
    outer_queries,
    direct_cotangent,
    relayed_cotangent,
    own_ref,
    term_ref,
    sum_ref,
):
    even = (lax.axis_index("tm") & 1) == 0
    relayed = through_relay(-1, 2, peers)
    heads = pair_queries.shape[1] // DEPTH

    def operands(head):
        cols = head_cols(head)
        cotangent = jnp.where(relayed, relayed_cotangent[:, cols], direct_cotangent[:, cols])
        outer = outer_queries[:, cols], cotangent
        return [jnp.where(even, a, b) for a, b in zip(joined_parts(pair_queries, cols), outer)]

    def products(head):
        query, cotangent = operands(head)
        keys, values = joined_parts(own_ref, head_cols(head))
        return logits_of(keys, query, rows_ref, head, NEXT), dot(values, cotangent, 1, 1)

    ahead = products(0)
    for head in range(heads):
        now = ahead
        if head + 1 < heads:
            ahead = products(head + 1)
        weights, dlogits = weights_of(load_part(stats_ref, head), *now)
        query, cotangent = operands(head)
        cols = head_cols(head)
        sum_ref[0, :, cols] = term_ref[0, :, cols] + dot(dlogits, query, 1, 0) * FACTOR
        sum_ref[1, :, cols] = term_ref[1, :, cols] + dot(weights, cotangent, 1, 0)


def rest_kernel(
    peers,
    rows_ref,
    part_ref,
    queries_ref,
    direct_keys,
    relayed_keys,
    outer_values,
    pair_ref,
    own_ref,
    own_mem,
    other_mem,
    passed_ref,
    attended_ref,
    grad_query_ref,
    term_ref,
    stats_ref,
    passed_out,
):
    role = lax.axis_index("tm") & 1
    frame_len, half_width = own_mem.shape[2:]
    heads = queries_ref.shape[1] // DEPTH
    half = half_width // DEPTH
    passed_out[...] = passed_ref[...]

    def pieces(head):
        cols = head_cols(head % half)
        prev = prev_parts(peers, direct_keys, relayed_keys, outer_values, pair_ref, head_cols(head))
        memory = [
            jnp.where(role == head // half, own_mem[:, kind, :, cols], other_mem[:, kind, :, cols]).reshape(
                MEM * frame_len, DEPTH
            )
            for kind in range(2)
        ]
        return (PREV, prev), (OWN, joined_parts(own_ref, head_cols(head))), (MEMORY, memory)

    def products(head):
        query, cotangent = joined_parts(queries_ref, head_cols(head))
        return [
            (logits_of(keys, query, rows_ref, head, piece), dot(values, cotangent, 1, 1))
            for piece, (keys, values) in pieces(head)
        ]

    ahead = products(0)
    for head in range(heads):
        now = ahead
        if head + 1 < heads:
            ahead = products(head + 1)
        cols = head_cols(head)
        query, cotangent = joined_parts(queries_ref, cols)
        stats, *last = rounded(load_part(part_ref, head), *now[-1])
        store_part(stats_ref, head, stats)
        rounds = [weights_of(stats, *now[PREV]), weights_of(stats, *now[OWN]), last]
        attended = grad_query = 0.0
        for (piece, (keys, values)), (weights, dlogits) in zip(pieces(head), rounds):
            attended += dot(values, weights, 0, 0)
            grad_query += dot(keys, dlogits, 0, 0)
            if piece == OWN:
                term_ref[0, :, cols] = dot(dlogits, query, 1, 0) * FACTOR
                term_ref[1, :, cols] = dot(weights, cotangent, 1, 0)
        attended_ref[:, cols] = attended.T.astype(BF16)
        grad_query_ref[:, cols] = (grad_query * FACTOR).T.astype(BF16)


def add_kernel(keep_ref, got_ref, out_ref, send_ref):
    value = keep_ref[0 : got_ref.shape[0]] + got_ref[...].astype(F32)
    out_ref[...] = value
    send_ref[...] = value.astype(BF16)


def owned_kernel(codes_ref, keep_ref, got_ref, mine_ref, pair_ref):
    code = code_of(codes_ref, OWNED)
    for o, out in enumerate((mine_ref, pair_ref)):
        for j in range(FR_DEV):
            owned = field(code, o * FR_DEV + j, PLACE_BITS)
            place = owned >> 1
            named = (owned & 1) != 0

            @pl.when(named)
            def _(out=out, j=j, place=place):
                value = keep_ref[place] + got_ref[place].astype(F32)
                out[j] = value.astype(out.dtype)

            @pl.when(jnp.logical_not(named))
            def _(out=out, j=j):
                out[j] = jnp.zeros(out.shape[1:], out.dtype)


def final_kernel(own_ref, mine_ref, got_ref, grad_key_ref, grad_value_ref):
    role = lax.axis_index("tm") & 1
    frame_len, half_width = mine_ref.shape[2:]
    for kind, out in enumerate((grad_key_ref, grad_value_ref)):
        for j in range(FR_DEV):
            rows = pl.ds(j * frame_len, frame_len)
            for half in range(2):
                cols = pl.ds(half * half_width, half_width)
                bank = jnp.where(role == half, mine_ref[j, kind], got_ref[j, kind].astype(F32))
                out[rows, cols] = (own_ref[kind, rows, cols] + bank).astype(BF16)


def body(
    query_states,
    key_states,
    value_states,
    grad_out,
    camera_pose,
    pose_bias,
    memory_index,
    bank_frames,
):
    row_count, width = query_states.shape
    frame_len = row_count // FR_DEV
    heads = pose_bias.shape[0]
    slots = bank_frames.shape[0]
    peers = lax.axis_size("tm")
    bits = [1 << i for i in range(1, peers.bit_length() - 1)]
    turns = list(zip(bits, bits[::-1]))
    even = (lax.axis_index("tm") & 1) == 0
    piece_flops = 2 * row_count * row_count * width
    bank_frames = bank_frames.reshape(1, slots)
    last_bits = turns[-1]

    def join(kernel, rows, arrays, scratch, name, after=()):
        def run(*refs):
            kernel(*refs[: len(arrays)], *refs[len(arrays) + len(after) :])

        return pl.pallas_call(
            run,
            out_shape=shape(BF16, rows, width),
            in_specs=[pl.BlockSpec(memory_space=pltpu.HBM)] * len(arrays) + [ANY] * len(after),
            out_specs=VMEM,
            scratch_shapes=[*scratch, pltpu.SemaphoreType.DMA((len(arrays),))],
            compiler_params=pltpu.CompilerParams(vmem_limit_bytes=VMEM_LIMIT),
            name=name,
        )(*(pltpu.with_memory_space_constraint(array, pltpu.HBM) for array in arrays), *after)

    joined = join(
        join_kernel,
        2 * row_count + TAIL,
        [memory_index, key_states, value_states],
        [pltpu.VMEM(memory_index.shape, jnp.int32)],
        "join",
    )
    half_width = width // 2
    first, second = slice(0, half_width), slice(half_width, width)
    direct_keys = shift_first(key_states, 1, 1, peers)
    pair = swap(joined, 1, 1, peers)
    held = shape(BF16, slots - 1, 2, frame_len, half_width)
    sums = shape(F32, slots - 1, 2, frame_len, half_width)
    (mine,) = call(functools.partial(split_kernel, peers), [held], [bank_frames, joined, pair], name="split")
    queries = join(join_queries_kernel, 2 * row_count, [query_states, grad_out], [], "join_queries", after=[mine])
    pair_queries = swap(queries, 1, 1, peers)
    own_half = jnp.where(even, queries[:, first], queries[:, second])
    pair_half = jnp.where(even, pair_queries[:, first], pair_queries[:, second])

    bias_rows = -(-(5 * FR_DEV) // 8) * 8
    rows, codes, values_out, keys_out = call(
        functools.partial(plan_kernel, peers, last_bits),
        [shape(F32, heads, bias_rows, row_count), shape(jnp.int32, 8, 128)] + [shape(BF16, row_count, width)] * 2,
        [pair, joined, direct_keys],
        scalars=[bank_frames, memory_index, camera_pose, pose_bias],
        flops=HIDING * piece_flops,
        name="plan",
    )
    outer = [direct_keys, shift_second(keys_out, 1, 1, peers), shift(values_out, 1, 1, peers)]
    even_done = odd_done = 1
    for step, (even_bit, odd_bit) in enumerate(turns):
        got = swap(mine, even_bit, odd_bit, peers)
        if step + 1 < len(turns):
            kernel = functools.partial(step_kernel, peers, even_done, odd_done)
            after = [codes, pair_queries]
            (mine,) = call(kernel, [held], [bank_frames, mine, got], after=after, name="step")
        even_done |= even_bit
        odd_done |= odd_bit

    stats = shape(F32, heads, 8, row_count)
    part, queries_out, cotangent_out = call(
        functools.partial(stats_kernel, peers),
        [stats] + [shape(BF16, row_count, width)] * 2,
        [rows, queries, *outer, pair, joined],
        flops=HIDING * piece_flops,
        name="stats",
    )
    pair_part = swap(part, 1, 1, peers)
    next_queries = shift(queries_out, -1, 2, peers)
    direct_cotangent = shift_first(cotangent_out, -1, 2, peers)
    chosen = shape(BF16, MEM, 2, frame_len, half_width)
    own_mem, pair_mem = call(pick_kernel, [chosen] * 2, [codes, mine, got], name="pick")
    keep, send = call(
        memory_kernel,
        [shape(F32, slots, 2, frame_len, half_width), held],
        [codes, rows, part, pair_part, own_half, pair_half, own_mem, pair_mem],
        flops=HIDING * piece_flops,
        name="memory",
    )
    other_mem = swap(pair_mem, 1, 1, peers)
    pair_sums = shape(F32, 2, row_count, width)
    attended, grad_query, own_terms, stats_all, passed_on = call(
        functools.partial(rest_kernel, peers),
        [shape(BF16, row_count, width)] * 2 + [pair_sums, stats, shape(BF16, row_count, width)],
        [rows, part, queries, *outer, pair, joined, own_mem, other_mem, direct_cotangent],
        after=[send],
        flops=HIDING * piece_flops,
        name="rest",
    )
    next_stats = lax.ppermute(stats_all, "tm", [(i, i - 1) for i in range(1, peers)])
    relayed_cotangent = shift_second(passed_on, -1, 2, peers)
    (own,) = call(
        functools.partial(next_kernel, peers),
        [pair_sums],
        [rows, next_stats, pair_queries, next_queries, direct_cotangent, relayed_cotangent, joined, own_terms],
        flops=HIDING * piece_flops,
        name="next",
    )
    for step, (even_bit, odd_bit) in enumerate(turns[::-1]):
        got = swap(send, even_bit, odd_bit, peers)
        if step + 1 < len(turns):
            keep, send = call(add_kernel, [sums, held], [keep, got], after=[own_terms], name="add")
    owned_mine, owned_send = call(
        owned_kernel,
        [shape(F32, FR_DEV, 2, frame_len, half_width), shape(BF16, FR_DEV, 2, frame_len, half_width)],
        [codes, keep, got],
        after=[own],
        name="owned",
    )
    owned_got = swap(owned_send, 1, 1, peers)
    grad_key, grad_value = call(
        final_kernel, [shape(BF16, row_count, width)] * 2, [own, owned_mine, owned_got], name="final"
    )
    return (attended, grad_query, grad_key, grad_value)


def solution(mesh):
    rows = P(("traj", "tm"), None)
    in_specs = (rows, rows, rows, rows, P("traj"), P(), rows, P("traj"))
    return jax.shard_map(body, mesh=mesh, in_specs=in_specs, out_specs=(rows,) * 4, check_vma=False)
```

```python
import functools
import math

import jax
import jax.numpy as jnp
from jax import lax
from jax.experimental import pallas as pl
from jax.experimental.pallas import tpu as pltpu
from jax.sharding import PartitionSpec as P

FR_DEV = 2
MEM = 2
DEPTH = 128
TAIL = 16

BLOCKED_LOGIT = -1e30
LOG2E = math.log2(math.e)
FACTOR = 1.0 / math.sqrt(DEPTH)

SMEM = pl.BlockSpec(memory_space=pltpu.SMEM)
VMEM = pl.BlockSpec(memory_space=pltpu.VMEM)
ANY = pl.BlockSpec(memory_space=pl.ANY)
HIDING = 200
VMEM_LIMIT = 16 * 1024 * 1024
BF16, F32 = jnp.bfloat16, jnp.float32


def shape(dtype, *dims):
    return jax.ShapeDtypeStruct(dims, dtype)


def call(kernel, outs, arrays, scalars=(), after=(), flops=0, name=None):
    count = len(scalars) + len(arrays)

    def run(*refs):
        kernel(*refs[:count], *refs[count + len(after) :])

    return pl.pallas_call(
        run,
        out_shape=outs,
        in_specs=[SMEM] * len(scalars) + [VMEM] * len(arrays) + [ANY] * len(after),
        out_specs=[VMEM] * len(outs),
        compiler_params=pltpu.CompilerParams(vmem_limit_bytes=VMEM_LIMIT),
        cost_estimate=pl.CostEstimate(flops=flops, bytes_accessed=0, transcendentals=0) if flops else None,
        name=name,
    )(*scalars, *arrays, *after)


def swap(block, even_bit, odd_bit, peers):
    return lax.ppermute(block, "tm", [(i, i ^ (odd_bit if i & 1 else even_bit)) for i in range(peers)])


def shift(block, by, start, peers):
    pairs = [(i, i + by) for i in range(start, peers, 2) if 0 <= i + by < peers]
    return lax.ppermute(block, "tm", pairs)


def relays_of(by, start, peers):
    pairs = [(i, i + by) for i in range(start, peers, 2) if 0 <= i + by < peers]
    return {(i, j): i ^ 4 for i, j in pairs if peers == 8 and (i ^ j) >> 1 == 3}


def shift_first(block, by, start, peers):
    relays = relays_of(by, start, peers)
    pairs = [(i, i + by) for i in range(start, peers, 2) if 0 <= i + by < peers]
    return lax.ppermute(block, "tm", [(i, relays.get((i, j), j)) for i, j in pairs])


def shift_second(block, by, start, peers):
    pairs = [(relay, j) for (_, j), relay in relays_of(by, start, peers).items()]
    return lax.ppermute(block, "tm", pairs) if pairs else block


def through_relay(by, start, peers):
    me = lax.axis_index("tm")
    return functools.reduce(jnp.logical_or, [me == j for _, j in relays_of(by, start, peers)], me < 0)


def lane_value(row, lane):
    lanes = lax.broadcasted_iota(jnp.int32, row.shape, 1)
    return jnp.max(jnp.where(lanes == lane, row, 0))


def bank_of(bank_ref):
    row = bank_ref[...]
    return [lane_value(row, slot) for slot in range(row.shape[1])]


def dyn_frames(bank, last_frame):
    found = [jnp.int32(0)] * (len(bank) - 2)
    seen = jnp.int32(0)
    for frame in bank:
        free = jnp.logical_and(frame != 0, frame != last_frame)
        for j in range(len(found)):
            found[j] = jnp.where(jnp.logical_and(free, seen == j), frame, found[j])
        seen = seen + free.astype(jnp.int32)
    return found


def place_of(frame, dyns):
    place = jnp.int32(len(dyns))
    for j, dyn in enumerate(dyns):
        place = jnp.where(frame == dyn, j, place)
    return place


def choose(out, take_first, first, second):
    @pl.when(take_first)
    def _():
        out[...] = first[...]

    @pl.when(jnp.logical_not(take_first))
    def _():
        out[...] = second[...]


def has_end(me, done, peers):
    return jnp.logical_or((me & ~done) == 0, (me | done) == peers - 1)


def has_dyn(me, frame, done):
    return ((me ^ (frame // FR_DEV)) & ~done) == 0


def by_role(me, even_value, odd_value):
    return jnp.where((me & 1) == 0, even_value, odd_value)


def join_kernel(index_ref, key_ref, value_ref, joined_ref, index_buf, sems):
    rows = key_ref.shape[0]
    copies = [
        pltpu.make_async_copy(index_ref, index_buf, sems.at[0]),
        pltpu.make_async_copy(key_ref, joined_ref.at[pl.ds(0, rows)], sems.at[1]),
        pltpu.make_async_copy(value_ref, joined_ref.at[pl.ds(rows, rows)], sems.at[2]),
    ]
    for copy in copies:
        copy.start()
    copies[0].wait()
    width = joined_ref.shape[1]
    lane = lax.broadcasted_iota(jnp.int32, (TAIL, width), 1) // DEPTH
    tail = jnp.zeros((TAIL, width), jnp.int32)
    for m in range(MEM):
        tail = jnp.where(lane == m, index_buf[0:1, m : m + 1], tail)
    joined_ref[2 * rows : 2 * rows + TAIL, :] = tail.astype(F32).astype(BF16)
    copies[1].wait()
    copies[2].wait()


def join_queries_kernel(query_ref, cotangent_ref, joined_ref, sems):
    rows = query_ref.shape[0]
    copies = [
        pltpu.make_async_copy(ref, joined_ref.at[pl.ds(j * rows, rows)], sems.at[j])
        for j, ref in enumerate((query_ref, cotangent_ref))
    ]
    for copy in copies:
        copy.start()
    for copy in copies:
        copy.wait()


def pack(fields, width):
    code = jnp.int32(0)
    for j, field in enumerate(fields):
        code = code | (field.astype(jnp.int32) << (j * width))
    return code


def field(code, j, width):
    return (code >> (j * width)) & ((1 << width) - 1)


def code_of(codes_ref, row):
    return jnp.max(codes_ref[row : row + 1, :])


PICK, SUM, OWNED = range(3)
PLACE_BITS = 4
PREV, OWN, MEMORY, NEXT, PAIR = range(5)


def plan_kernel(
    peers,
    last_bits,
    bank_ref,
    index_ref,
    pose_ref,
    bias_ref,
    pair_ref,
    joined_ref,
    direct_keys,
    rows_ref,
    codes_ref,
    values_out,
    keys_out,
):
    me = lax.axis_index("tm")
    last_frame = peers * FR_DEV - 1
    heads, _, row_count = rows_ref.shape
    values_out[...] = joined_ref[row_count : 2 * row_count, :]
    keys_out[...] = direct_keys[...]
    bank = [bank_ref[0, slot] for slot in range(bank_ref.shape[1])]
    tail = pair_ref.shape[0] - TAIL
    pair_ids = []
    for m in range(MEM):
        slot = jnp.max(pair_ref[tail : tail + TAIL, m * DEPTH : (m + 1) * DEPTH].astype(F32)).astype(jnp.int32)
        pair_ids.append(bank_ref[0, slot])
    mem_ids = [bank_ref[0, index_ref[0, m]] for m in range(MEM)]

    own_ids = [me * FR_DEV + j for j in range(FR_DEV)]
    prev_ids = [jnp.maximum(own - FR_DEV, 0) for own in own_ids]
    next_ids = [jnp.minimum(own + FR_DEV, last_frame) for own in own_ids]
    pair_own_ids = [(me ^ 1) * FR_DEV + j for j in range(FR_DEV)]
    pieces = ((prev_ids, own_ids), (own_ids, own_ids), (mem_ids, own_ids), (own_ids, next_ids), (pair_ids, pair_own_ids))
    poses = [([pose_ref[f] for f in key_ids], [pose_ref[f] for f in query_ids]) for key_ids, query_ids in pieces]
    frame_of = lax.broadcasted_iota(jnp.int32, (1, row_count), 1) // (row_count // FR_DEV)
    for head in range(heads):
        for piece, (key_poses, query_poses) in enumerate(poses):
            for j, key_pose in enumerate(key_poses):
                row = jnp.zeros((1, row_count), F32)
                for a, query_pose in enumerate(query_poses):
                    value = bias_ref[head, query_pose, key_pose] * LOG2E
                    if piece == PREV:
                        value = jnp.where(me == 0, BLOCKED_LOGIT, value)
                    row = jnp.where(frame_of == a, value, row)
                rows_ref[head, piece * FR_DEV + j : piece * FR_DEV + j + 1, :] = row

    dyns = dyn_frames(bank, last_frame)
    bit = by_role(me, *last_bits)
    upper = (me & bit) != 0
    picks = []
    for frame in mem_ids + pair_ids:
        source = place_of(frame, dyns)
        local = jnp.where(frame == 0, jnp.logical_not(upper), upper)
        local = jnp.where(source < len(dyns), has_dyn(me, frame, (peers - 1) & ~bit), local)
        picks.append(source * 2 + local.astype(jnp.int32))
    far = jnp.where(upper, 0, last_frame)
    sums = [jnp.where(frame == far, len(dyns) + 1, place_of(frame, dyns)) for frame in mem_ids + pair_ids]
    owned = []
    for group in (me, me ^ 1):
        for j in range(FR_DEV):
            frame = group * FR_DEV + j
            place = place_of(frame, dyns)
            named = jnp.logical_or(place < len(dyns), jnp.logical_or(frame == 0, frame == last_frame))
            owned.append(place * 2 + named.astype(jnp.int32))
    lanes = codes_ref.shape[1]
    for row, code in ((PICK, pack(picks, PLACE_BITS)), (SUM, pack(sums, PLACE_BITS)), (OWNED, pack(owned, PLACE_BITS))):
        codes_ref[row : row + 1, :] = jnp.full((1, lanes), code, jnp.int32)


def split_kernel(peers, bank_ref, mine_ref, pair_ref, out_ref):
    me = lax.axis_index("tm")
    frame_len, half_width = out_ref.shape[2:]
    dyns = dyn_frames(bank_of(bank_ref), peers * FR_DEV - 1)
    places = [(has_dyn(me, dyn, 0), dyn % FR_DEV) for dyn in dyns]
    places.append((has_end(me, 0, peers), jnp.where(me < peers // 2, 0, FR_DEV - 1)))
    for j, (local, frame) in enumerate(places):
        for role in range(2):
            for source, taken in ((mine_ref, local), (pair_ref, jnp.logical_not(local))):

                @pl.when(jnp.logical_and((me & 1) == role, taken))
                def _(source=source, j=j, frame=frame, role=role):
                    for kind in range(2):
                        start = pl.multiple_of((kind * FR_DEV + frame) * frame_len, frame_len)
                        out_ref[j, kind] = source[pl.ds(start, frame_len), role * half_width : (role + 1) * half_width]


def step_kernel(peers, even_done, odd_done, bank_ref, mine_ref, got_ref, out_ref):
    me = lax.axis_index("tm")
    done = by_role(me, even_done, odd_done)
    dyns = dyn_frames(bank_of(bank_ref), peers * FR_DEV - 1)
    flags = [has_dyn(me, dyn, done) for dyn in dyns] + [has_end(me, done, peers)]
    for j, flag in enumerate(flags):
        choose(out_ref.at[j], flag, mine_ref.at[j], got_ref.at[j])


def pick_kernel(codes_ref, mine_ref, got_ref, own_out, pair_out):
    code = code_of(codes_ref, PICK)
    for o, out in enumerate((own_out, pair_out)):
        for m in range(MEM):
            pick = field(code, o * MEM + m, PLACE_BITS)
            source = pick >> 1
            choose(out.at[m], (pick & 1) != 0, mine_ref.at[source], got_ref.at[source])


def dot(a, b, left, right):
    return lax.dot_general(a, b, (((left,), (right,)), ((), ())), preferred_element_type=F32)


def logits_of(keys, query, rows_ref, head, piece):
    frame_len = query.shape[0] // FR_DEV
    raw = dot(keys, query, 1, 1) * (FACTOR * LOG2E)
    parts = []
    for j in range(FR_DEV):
        row = piece * FR_DEV + j
        parts.append(raw[j * frame_len : (j + 1) * frame_len] + rows_ref[head, row : row + 1, :])
    return jnp.concatenate(parts, axis=0)


def joined_parts(joined_ref, cols):
    rows = joined_ref.shape[0] // 2 // DEPTH * DEPTH
    return joined_ref[0:rows, cols], joined_ref[rows : 2 * rows, cols]


def head_cols(head):
    return pl.ds(head * DEPTH, DEPTH)


def part_of(logits, slopes):
    peak = jnp.max(logits, axis=0, keepdims=True)
    exps = jnp.exp2(logits - peak)
    return peak, jnp.sum(exps, axis=0, keepdims=True), jnp.sum(exps * slopes, axis=0, keepdims=True)


def merged(left, right):
    peak = jnp.maximum(left[0], right[0])
    scales = [jnp.exp2(part[0] - peak) for part in (left, right)]
    return peak, *(left[j] * scales[0] + right[j] * scales[1] for j in (1, 2))


def load_part(ref, head):
    return tuple(ref[head, j : j + 1, :] for j in range(3))


def store_part(ref, head, part):
    for j, row in enumerate(part):
        ref[head, j : j + 1, :] = row


def prev_parts(peers, direct_keys, relayed_keys, outer_values, pair_ref, cols):
    even = (lax.axis_index("tm") & 1) == 0
    keys = jnp.where(through_relay(1, 1, peers), relayed_keys[:, cols], direct_keys[:, cols])
    parts = zip((keys, outer_values[:, cols]), joined_parts(pair_ref, cols))
    return tuple(jnp.where(even, outer, pair) for outer, pair in parts)


def stats_kernel(
    peers,
    rows_ref,
    queries_ref,
    direct_keys,
    relayed_keys,
    outer_values,
    pair_ref,
    own_ref,
    part_ref,
    queries_out,
    cotangent_out,
):
    heads = queries_ref.shape[1] // DEPTH
    rows = queries_out.shape[0]
    queries_out[...] = queries_ref[0:rows]
    cotangent_out[...] = queries_ref[rows : 2 * rows]

    def products(head):
        cols = head_cols(head)
        query, cotangent = joined_parts(queries_ref, cols)
        pieces = ((PREV, prev_parts(peers, direct_keys, relayed_keys, outer_values, pair_ref, cols)), (OWN, joined_parts(own_ref, cols)))
        return [
            (logits_of(keys, query, rows_ref, head, piece), dot(values, cotangent, 1, 1))
            for piece, (keys, values) in pieces
        ]

    ahead = products(0)
    for head in range(heads):
        now = ahead
        if head + 1 < heads:
            ahead = products(head + 1)
        store_part(part_ref, head, merged(*(part_of(*piece) for piece in now)))


def rounded(part, logits, slopes):
    peak, total, spread = merged(part, part_of(logits, slopes))
    inverse = 1.0 / total
    stats = peak, inverse, spread * inverse
    return stats, *weights_of(stats, logits, slopes)


def weights_of(stats, logits, slopes):
    peak, inverse, spread = stats
    probs = jnp.exp2(logits - peak) * inverse
    return probs.astype(BF16), (probs * (slopes - spread)).astype(BF16)


def memory_kernel(
    codes_ref, rows_ref, part_ref, pair_part_ref, own_queries, pair_queries, own_mem, pair_mem, keep_ref, send_ref
):
    role = lax.axis_index("tm") & 1
    code = code_of(codes_ref, SUM)
    frame_len, half_width = own_mem.shape[2:]
    half = half_width // DEPTH
    groups = ((own_queries, own_mem, part_ref, MEMORY), (pair_queries, pair_mem, pair_part_ref, PAIR))
    work = [(g, local) for local in range(half) for g in range(len(groups))]
    keep_ref[...] = jnp.zeros(keep_ref.shape, F32)

    def operands(g, local):
        cols = pl.ds(pl.multiple_of((role * half + local) * DEPTH, DEPTH), DEPTH)
        return joined_parts(groups[g][0], cols)

    def products(g, local):
        _, mem, _, piece = groups[g]
        query, cotangent = operands(g, local)
        keys, values = (mem[:, kind, :, head_cols(local)].reshape(MEM * frame_len, DEPTH) for kind in range(2))
        return logits_of(keys, query, rows_ref, role * half + local, piece), dot(values, cotangent, 1, 1)

    def add(g, local, _, weights, dlogits):
        query, cotangent = operands(g, local)
        terms = (dot(dlogits, query, 1, 0) * FACTOR, dot(weights, cotangent, 1, 0))
        for m in range(MEM):
            place = field(code, g * MEM + m, PLACE_BITS)
            for kind, term in enumerate(terms):
                part = term[m * frame_len : (m + 1) * frame_len].astype(BF16).astype(F32)
                keep_ref[place, kind, :, head_cols(local)] += part

    ahead = products(*work[0])
    behind = None
    for j, (g, local) in enumerate(work):
        now = ahead
        if j + 1 < len(work):
            ahead = products(*work[j + 1])
        if behind is not None:
            add(*work[j - 1], *behind)
        behind = rounded(load_part(groups[g][2], role * half + local), *now)
    add(*work[-1], *behind)
    kept = send_ref.shape[0]
    for place in range(kept):
        send_ref[place] = keep_ref[place if place + 1 < kept else kept].astype(BF16)


def next_kernel(
    peers,
    rows_ref,
    stats_ref,
    pair_queries,
    outer_queries,
    direct_cotangent,
    relayed_cotangent,
    own_ref,
    term_ref,
    sum_ref,
):
    even = (lax.axis_index("tm") & 1) == 0
    relayed = through_relay(-1, 2, peers)
    heads = pair_queries.shape[1] // DEPTH

    def operands(head):
        cols = head_cols(head)
        cotangent = jnp.where(relayed, relayed_cotangent[:, cols], direct_cotangent[:, cols])
        outer = outer_queries[:, cols], cotangent
        return [jnp.where(even, a, b) for a, b in zip(joined_parts(pair_queries, cols), outer)]

    def products(head):
        query, cotangent = operands(head)
        keys, values = joined_parts(own_ref, head_cols(head))
        return logits_of(keys, query, rows_ref, head, NEXT), dot(values, cotangent, 1, 1)

    ahead = products(0)
    for head in range(heads):
        now = ahead
        if head + 1 < heads:
            ahead = products(head + 1)
        weights, dlogits = weights_of(load_part(stats_ref, head), *now)
        query, cotangent = operands(head)
        cols = head_cols(head)
        sum_ref[0, :, cols] = term_ref[0, :, cols] + dot(dlogits, query, 1, 0) * FACTOR
        sum_ref[1, :, cols] = term_ref[1, :, cols] + dot(weights, cotangent, 1, 0)


def rest_kernel(
    peers,
    rows_ref,
    part_ref,
    queries_ref,
    direct_keys,
    relayed_keys,
    outer_values,
    pair_ref,
    own_ref,
    own_mem,
    other_mem,
    attended_ref,
    grad_query_ref,
    term_ref,
    stats_ref,
):
    role = lax.axis_index("tm") & 1
    frame_len, half_width = own_mem.shape[2:]
    heads = queries_ref.shape[1] // DEPTH
    half = half_width // DEPTH

    def pieces(head):
        cols = head_cols(head % half)
        prev = prev_parts(peers, direct_keys, relayed_keys, outer_values, pair_ref, head_cols(head))
        memory = [
            jnp.where(role == head // half, own_mem[:, kind, :, cols], other_mem[:, kind, :, cols]).reshape(
                MEM * frame_len, DEPTH
            )
            for kind in range(2)
        ]
        return (PREV, prev), (OWN, joined_parts(own_ref, head_cols(head))), (MEMORY, memory)

    def products(head):
        query, cotangent = joined_parts(queries_ref, head_cols(head))
        return [
            (logits_of(keys, query, rows_ref, head, piece), dot(values, cotangent, 1, 1))
            for piece, (keys, values) in pieces(head)
        ]

    ahead = products(0)
    for head in range(heads):
        now = ahead
        if head + 1 < heads:
            ahead = products(head + 1)
        cols = head_cols(head)
        query, cotangent = joined_parts(queries_ref, cols)
        stats, *last = rounded(load_part(part_ref, head), *now[-1])
        store_part(stats_ref, head, stats)
        rounds = [weights_of(stats, *now[PREV]), weights_of(stats, *now[OWN]), last]
        attended = grad_query = 0.0
        for (piece, (keys, values)), (weights, dlogits) in zip(pieces(head), rounds):
            attended += dot(values, weights, 0, 0)
            grad_query += dot(keys, dlogits, 0, 0)
            if piece == OWN:
                term_ref[0, :, cols] = dot(dlogits, query, 1, 0) * FACTOR
                term_ref[1, :, cols] = dot(weights, cotangent, 1, 0)
        attended_ref[:, cols] = attended.T.astype(BF16)
        grad_query_ref[:, cols] = (grad_query * FACTOR).T.astype(BF16)


def add_kernel(keep_ref, got_ref, *refs):
    passed = len(refs) // 2 - 1
    for source, out in zip(refs[:passed], refs[passed + 2 :]):
        out[...] = source[...]
    out_ref, send_ref = refs[passed : passed + 2]
    value = keep_ref[0 : got_ref.shape[0]] + got_ref[...].astype(F32)
    out_ref[...] = value
    send_ref[...] = value.astype(BF16)


def owned_kernel(codes_ref, keep_ref, got_ref, mine_ref, pair_ref):
    code = code_of(codes_ref, OWNED)
    for o, out in enumerate((mine_ref, pair_ref)):
        for j in range(FR_DEV):
            owned = field(code, o * FR_DEV + j, PLACE_BITS)
            place = owned >> 1
            named = (owned & 1) != 0

            @pl.when(named)
            def _(out=out, j=j, place=place):
                value = keep_ref[place] + got_ref[place].astype(F32)
                out[j] = value.astype(out.dtype)

            @pl.when(jnp.logical_not(named))
            def _(out=out, j=j):
                out[j] = jnp.zeros(out.shape[1:], out.dtype)


def final_kernel(own_ref, mine_ref, got_ref, grad_key_ref, grad_value_ref):
    role = lax.axis_index("tm") & 1
    frame_len, half_width = mine_ref.shape[2:]
    for kind, out in enumerate((grad_key_ref, grad_value_ref)):
        for j in range(FR_DEV):
            rows = pl.ds(j * frame_len, frame_len)
            for half in range(2):
                cols = pl.ds(half * half_width, half_width)
                bank = jnp.where(role == half, mine_ref[j, kind], got_ref[j, kind].astype(F32))
                out[rows, cols] = (own_ref[kind, rows, cols] + bank).astype(BF16)


def body(
    query_states,
    key_states,
    value_states,
    grad_out,
    camera_pose,
    pose_bias,
    memory_index,
    bank_frames,
):
    row_count, width = query_states.shape
    frame_len = row_count // FR_DEV
    heads = pose_bias.shape[0]
    slots = bank_frames.shape[0]
    peers = lax.axis_size("tm")
    bits = [1 << i for i in range(1, peers.bit_length() - 1)]
    turns = list(zip(bits, bits[::-1]))
    piece_flops = 2 * row_count * row_count * width
    bank_frames = bank_frames.reshape(1, slots)
    last_bits = turns[-1]

    def join(kernel, rows, arrays, scratch, name, after=()):
        def run(*refs):
            kernel(*refs[: len(arrays)], *refs[len(arrays) + len(after) :])

        return pl.pallas_call(
            run,
            out_shape=shape(BF16, rows, width),
            in_specs=[pl.BlockSpec(memory_space=pltpu.HBM)] * len(arrays) + [ANY] * len(after),
            out_specs=VMEM,
            scratch_shapes=[*scratch, pltpu.SemaphoreType.DMA((len(arrays),))],
            compiler_params=pltpu.CompilerParams(vmem_limit_bytes=VMEM_LIMIT),
            name=name,
        )(*(pltpu.with_memory_space_constraint(array, pltpu.HBM) for array in arrays), *after)

    joined = join(
        join_kernel,
        2 * row_count + TAIL,
        [memory_index, key_states, value_states],
        [pltpu.VMEM(memory_index.shape, jnp.int32)],
        "join",
    )
    half_width = width // 2
    direct_keys = shift_first(key_states, 1, 1, peers)
    pair = swap(joined, 1, 1, peers)
    held = shape(BF16, slots - 1, 2, frame_len, half_width)
    sums = shape(F32, slots - 1, 2, frame_len, half_width)
    (mine,) = call(functools.partial(split_kernel, peers), [held], [bank_frames, joined, pair], name="split")
    queries = join(join_queries_kernel, 2 * row_count, [query_states, grad_out], [], "join_queries", after=[mine])
    pair_queries = swap(queries, 1, 1, peers)

    bias_rows = -(-(5 * FR_DEV) // 8) * 8
    rows, codes, values_out, keys_out = call(
        functools.partial(plan_kernel, peers, last_bits),
        [shape(F32, heads, bias_rows, row_count), shape(jnp.int32, 8, 128)] + [shape(BF16, row_count, width)] * 2,
        [pair, joined, direct_keys],
        scalars=[bank_frames, memory_index, camera_pose, pose_bias],
        flops=HIDING * piece_flops,
        name="plan",
    )
    outer = [direct_keys, shift_second(keys_out, 1, 1, peers), shift(values_out, 1, 1, peers)]
    even_done = odd_done = 1
    for step, (even_bit, odd_bit) in enumerate(turns):
        got = swap(mine, even_bit, odd_bit, peers)
        if step + 1 < len(turns):
            kernel = functools.partial(step_kernel, peers, even_done, odd_done)
            after = [codes, pair_queries]
            (mine,) = call(kernel, [held], [bank_frames, mine, got], after=after, name="step")
        even_done |= even_bit
        odd_done |= odd_bit

    stats = shape(F32, heads, 8, row_count)
    part, queries_out, cotangent_out = call(
        functools.partial(stats_kernel, peers),
        [stats] + [shape(BF16, row_count, width)] * 2,
        [rows, queries, *outer, pair, joined],
        flops=HIDING * piece_flops,
        name="stats",
    )
    pair_part = swap(part, 1, 1, peers)
    next_queries = shift(queries_out, -1, 2, peers)
    direct_cotangent = shift_first(cotangent_out, -1, 2, peers)
    chosen = shape(BF16, MEM, 2, frame_len, half_width)
    own_mem, pair_mem = call(pick_kernel, [chosen] * 2, [codes, mine, got], name="pick")
    keep, send = call(
        memory_kernel,
        [shape(F32, slots, 2, frame_len, half_width), held],
        [codes, rows, part, pair_part, queries, pair_queries, own_mem, pair_mem],
        flops=HIDING * piece_flops,
        name="memory",
    )
    other_mem = swap(pair_mem, 1, 1, peers)
    pair_sums = shape(F32, 2, row_count, width)
    attended, grad_query, own_terms, stats_all = call(
        functools.partial(rest_kernel, peers),
        [shape(BF16, row_count, width)] * 2 + [pair_sums, stats],
        [rows, part, queries, *outer, pair, joined, own_mem, other_mem],
        after=[send],
        flops=HIDING * piece_flops,
        name="rest",
    )
    passing = [stats_all, direct_cotangent]
    for step, (even_bit, odd_bit) in enumerate(turns[::-1]):
        got = swap(send, even_bit, odd_bit, peers)
        if step + 1 < len(turns):
            keep, send, *passing = call(
                add_kernel,
                [sums, held, stats, shape(BF16, row_count, width)],
                [keep, got, *passing],
                after=[own_terms, next_queries],
                name="add",
            )
    next_stats = lax.ppermute(passing[0], "tm", [(i, i - 1) for i in range(1, peers)])
    relayed_cotangent = shift_second(passing[1], -1, 2, peers)
    (own,) = call(
        functools.partial(next_kernel, peers),
        [pair_sums],
        [rows, next_stats, pair_queries, next_queries, direct_cotangent, relayed_cotangent, joined, own_terms],
        name="next",
    )
    owned_mine, owned_send = call(
        owned_kernel,
        [shape(F32, FR_DEV, 2, frame_len, half_width), shape(BF16, FR_DEV, 2, frame_len, half_width)],
        [codes, keep, got],
        after=[own],
        name="owned",
    )
    owned_got = swap(owned_send, 1, 1, peers)
    grad_key, grad_value = call(
        final_kernel, [shape(BF16, row_count, width)] * 2, [own, owned_mine, owned_got], name="final"
    )
    return (attended, grad_query, grad_key, grad_value)


def solution(mesh):
    rows = P(("traj", "tm"), None)
    in_specs = (rows, rows, rows, rows, P("traj"), P(), rows, P("traj"))
    return jax.shard_map(body, mesh=mesh, in_specs=in_specs, out_specs=(rows,) * 4, check_vma=False)
```

```python
import functools
import math

import jax
import jax.numpy as jnp
from jax import lax
from jax.experimental import pallas as pl
from jax.experimental.pallas import tpu as pltpu
from jax.sharding import PartitionSpec as P

FR_DEV = 2
MEM = 2
DEPTH = 128
TAIL = 16

BLOCKED_LOGIT = -1e30
LOG2E = math.log2(math.e)
FACTOR = 1.0 / math.sqrt(DEPTH)

SMEM = pl.BlockSpec(memory_space=pltpu.SMEM)
VMEM = pl.BlockSpec(memory_space=pltpu.VMEM)
ANY = pl.BlockSpec(memory_space=pl.ANY)
HIDING = 200
VMEM_LIMIT = 16 * 1024 * 1024
BF16, F32 = jnp.bfloat16, jnp.float32


def shape(dtype, *dims):
    return jax.ShapeDtypeStruct(dims, dtype)


def call(kernel, outs, arrays, scalars=(), after=(), flops=0, name=None):
    count = len(scalars) + len(arrays)

    def run(*refs):
        kernel(*refs[:count], *refs[count + len(after) :])

    return pl.pallas_call(
        run,
        out_shape=outs,
        in_specs=[SMEM] * len(scalars) + [VMEM] * len(arrays) + [ANY] * len(after),
        out_specs=[VMEM] * len(outs),
        compiler_params=pltpu.CompilerParams(vmem_limit_bytes=VMEM_LIMIT),
        cost_estimate=pl.CostEstimate(flops=flops, bytes_accessed=0, transcendentals=0) if flops else None,
        name=name,
    )(*scalars, *arrays, *after)


def swap(block, even_bit, odd_bit, peers):
    return lax.ppermute(block, "tm", [(i, i ^ (odd_bit if i & 1 else even_bit)) for i in range(peers)])


def shift(block, by, start, peers):
    pairs = [(i, i + by) for i in range(start, peers, 2) if 0 <= i + by < peers]
    return lax.ppermute(block, "tm", pairs)


def relays_of(by, start, peers):
    pairs = [(i, i + by) for i in range(start, peers, 2) if 0 <= i + by < peers]
    return {(i, j): i ^ 4 for i, j in pairs if peers == 8 and (i ^ j) >> 1 == 3}


def shift_first(block, by, start, peers):
    relays = relays_of(by, start, peers)
    pairs = [(i, i + by) for i in range(start, peers, 2) if 0 <= i + by < peers]
    return lax.ppermute(block, "tm", [(i, relays.get((i, j), j)) for i, j in pairs])


def shift_second(block, by, start, peers):
    pairs = [(relay, j) for (_, j), relay in relays_of(by, start, peers).items()]
    return lax.ppermute(block, "tm", pairs) if pairs else block


def through_relay(by, start, peers):
    me = lax.axis_index("tm")
    return functools.reduce(jnp.logical_or, [me == j for _, j in relays_of(by, start, peers)], me < 0)


def lane_value(row, lane):
    lanes = lax.broadcasted_iota(jnp.int32, row.shape, 1)
    return jnp.max(jnp.where(lanes == lane, row, 0))


def bank_of(bank_ref):
    row = bank_ref[...]
    return [lane_value(row, slot) for slot in range(row.shape[1])]


def dyn_frames(bank, last_frame):
    found = [jnp.int32(0)] * (len(bank) - 2)
    seen = jnp.int32(0)
    for frame in bank:
        free = jnp.logical_and(frame != 0, frame != last_frame)
        for j in range(len(found)):
            found[j] = jnp.where(jnp.logical_and(free, seen == j), frame, found[j])
        seen = seen + free.astype(jnp.int32)
    return found


def place_of(frame, dyns):
    place = jnp.int32(len(dyns))
    for j, dyn in enumerate(dyns):
        place = jnp.where(frame == dyn, j, place)
    return place


def choose(out, take_first, first, second):
    @pl.when(take_first)
    def _():
        out[...] = first[...]

    @pl.when(jnp.logical_not(take_first))
    def _():
        out[...] = second[...]


def has_end(me, done, peers):
    return jnp.logical_or((me & ~done) == 0, (me | done) == peers - 1)


def has_dyn(me, frame, done):
    return ((me ^ (frame // FR_DEV)) & ~done) == 0


def by_role(me, even_value, odd_value):
    return jnp.where((me & 1) == 0, even_value, odd_value)


def join_kernel(index_ref, key_ref, value_ref, joined_ref, index_buf, sems):
    rows = key_ref.shape[0]
    copies = [
        pltpu.make_async_copy(index_ref, index_buf, sems.at[0]),
        pltpu.make_async_copy(key_ref, joined_ref.at[pl.ds(0, rows)], sems.at[1]),
        pltpu.make_async_copy(value_ref, joined_ref.at[pl.ds(rows, rows)], sems.at[2]),
    ]
    for copy in copies:
        copy.start()
    copies[0].wait()
    width = joined_ref.shape[1]
    lane = lax.broadcasted_iota(jnp.int32, (TAIL, width), 1) // DEPTH
    tail = jnp.zeros((TAIL, width), jnp.int32)
    for m in range(MEM):
        tail = jnp.where(lane == m, index_buf[0:1, m : m + 1], tail)
    joined_ref[2 * rows : 2 * rows + TAIL, :] = tail.astype(F32).astype(BF16)
    copies[1].wait()
    copies[2].wait()


def join_queries_kernel(query_ref, cotangent_ref, joined_ref, sems):
    rows = query_ref.shape[0]
    copies = [
        pltpu.make_async_copy(ref, joined_ref.at[pl.ds(j * rows, rows)], sems.at[j])
        for j, ref in enumerate((query_ref, cotangent_ref))
    ]
    for copy in copies:
        copy.start()
    for copy in copies:
        copy.wait()


def pack(fields, width):
    code = jnp.int32(0)
    for j, field in enumerate(fields):
        code = code | (field.astype(jnp.int32) << (j * width))
    return code


def field(code, j, width):
    return (code >> (j * width)) & ((1 << width) - 1)


def code_of(codes_ref, row):
    return jnp.max(codes_ref[row : row + 1, :])


PICK, SUM, OWNED = range(3)
PLACE_BITS = 4
PREV, OWN, MEMORY, NEXT, PAIR = range(5)


def plan_kernel(
    peers,
    last_bits,
    bank_ref,
    index_ref,
    pose_ref,
    bias_ref,
    pair_ref,
    joined_ref,
    direct_keys,
    rows_ref,
    codes_ref,
    values_out,
    keys_out,
):
    me = lax.axis_index("tm")
    last_frame = peers * FR_DEV - 1
    heads, _, row_count = rows_ref.shape
    values_out[...] = joined_ref[row_count : 2 * row_count, :]
    keys_out[...] = direct_keys[...]
    bank = [bank_ref[0, slot] for slot in range(bank_ref.shape[1])]
    tail = pair_ref.shape[0] - TAIL
    pair_ids = []
    for m in range(MEM):
        slot = jnp.max(pair_ref[tail : tail + TAIL, m * DEPTH : (m + 1) * DEPTH].astype(F32)).astype(jnp.int32)
        pair_ids.append(bank_ref[0, slot])
    mem_ids = [bank_ref[0, index_ref[0, m]] for m in range(MEM)]

    own_ids = [me * FR_DEV + j for j in range(FR_DEV)]
    prev_ids = [jnp.maximum(own - FR_DEV, 0) for own in own_ids]
    next_ids = [jnp.minimum(own + FR_DEV, last_frame) for own in own_ids]
    pair_own_ids = [(me ^ 1) * FR_DEV + j for j in range(FR_DEV)]
    pieces = ((prev_ids, own_ids), (own_ids, own_ids), (mem_ids, own_ids), (own_ids, next_ids), (pair_ids, pair_own_ids))
    poses = [([pose_ref[f] for f in key_ids], [pose_ref[f] for f in query_ids]) for key_ids, query_ids in pieces]
    frame_of = lax.broadcasted_iota(jnp.int32, (1, row_count), 1) // (row_count // FR_DEV)
    for head in range(heads):
        for piece, (key_poses, query_poses) in enumerate(poses):
            for j, key_pose in enumerate(key_poses):
                row = jnp.zeros((1, row_count), F32)
                for a, query_pose in enumerate(query_poses):
                    value = bias_ref[head, query_pose, key_pose] * LOG2E
                    if piece == PREV:
                        value = jnp.where(me == 0, BLOCKED_LOGIT, value)
                    row = jnp.where(frame_of == a, value, row)
                rows_ref[head, piece * FR_DEV + j : piece * FR_DEV + j + 1, :] = row

    dyns = dyn_frames(bank, last_frame)
    bit = by_role(me, *last_bits)
    upper = (me & bit) != 0
    picks = []
    for frame in mem_ids + pair_ids:
        source = place_of(frame, dyns)
        local = jnp.where(frame == 0, jnp.logical_not(upper), upper)
        local = jnp.where(source < len(dyns), has_dyn(me, frame, (peers - 1) & ~bit), local)
        picks.append(source * 2 + local.astype(jnp.int32))
    far = jnp.where(upper, 0, last_frame)
    sums = [jnp.where(frame == far, len(dyns) + 1, place_of(frame, dyns)) for frame in mem_ids + pair_ids]
    owned = []
    for group in (me, me ^ 1):
        for j in range(FR_DEV):
            frame = group * FR_DEV + j
            place = place_of(frame, dyns)
            named = jnp.logical_or(place < len(dyns), jnp.logical_or(frame == 0, frame == last_frame))
            owned.append(place * 2 + named.astype(jnp.int32))
    lanes = codes_ref.shape[1]
    for row, code in ((PICK, pack(picks, PLACE_BITS)), (SUM, pack(sums, PLACE_BITS)), (OWNED, pack(owned, PLACE_BITS))):
        codes_ref[row : row + 1, :] = jnp.full((1, lanes), code, jnp.int32)


def split_kernel(peers, bank_ref, mine_ref, pair_ref, out_ref):
    me = lax.axis_index("tm")
    frame_len, half_width = out_ref.shape[2:]
    dyns = dyn_frames(bank_of(bank_ref), peers * FR_DEV - 1)
    places = [(has_dyn(me, dyn, 0), dyn % FR_DEV) for dyn in dyns]
    places.append((has_end(me, 0, peers), jnp.where(me < peers // 2, 0, FR_DEV - 1)))
    for j, (local, frame) in enumerate(places):
        for role in range(2):
            for source, taken in ((mine_ref, local), (pair_ref, jnp.logical_not(local))):

                @pl.when(jnp.logical_and((me & 1) == role, taken))
                def _(source=source, j=j, frame=frame, role=role):
                    for kind in range(2):
                        start = pl.multiple_of((kind * FR_DEV + frame) * frame_len, frame_len)
                        out_ref[j, kind] = source[pl.ds(start, frame_len), role * half_width : (role + 1) * half_width]


def step_kernel(peers, even_done, odd_done, bank_ref, mine_ref, got_ref, out_ref):
    me = lax.axis_index("tm")
    done = by_role(me, even_done, odd_done)
    dyns = dyn_frames(bank_of(bank_ref), peers * FR_DEV - 1)
    flags = [has_dyn(me, dyn, done) for dyn in dyns] + [has_end(me, done, peers)]
    for j, flag in enumerate(flags):
        choose(out_ref.at[j], flag, mine_ref.at[j], got_ref.at[j])


def pick_kernel(codes_ref, mine_ref, got_ref, own_out, pair_out):
    code = code_of(codes_ref, PICK)
    for o, out in enumerate((own_out, pair_out)):
        for m in range(MEM):
            pick = field(code, o * MEM + m, PLACE_BITS)
            source = pick >> 1
            choose(out.at[m], (pick & 1) != 0, mine_ref.at[source], got_ref.at[source])


def dot(a, b, left, right):
    return lax.dot_general(a, b, (((left,), (right,)), ((), ())), preferred_element_type=F32)


def logits_of(keys, query, rows_ref, head, piece):
    frame_len = query.shape[0] // FR_DEV
    raw = dot(keys, query, 1, 1) * (FACTOR * LOG2E)
    parts = []
    for j in range(FR_DEV):
        row = piece * FR_DEV + j
        parts.append(raw[j * frame_len : (j + 1) * frame_len] + rows_ref[head, row : row + 1, :])
    return jnp.concatenate(parts, axis=0)


def joined_parts(joined_ref, cols):
    rows = joined_ref.shape[0] // 2 // DEPTH * DEPTH
    return joined_ref[0:rows, cols], joined_ref[rows : 2 * rows, cols]


def head_cols(head):
    return pl.ds(head * DEPTH, DEPTH)


def part_of(logits, slopes):
    peak = jnp.max(logits, axis=0, keepdims=True)
    exps = jnp.exp2(logits - peak)
    return peak, jnp.sum(exps, axis=0, keepdims=True), jnp.sum(exps * slopes, axis=0, keepdims=True)


def merged(left, right):
    peak = jnp.maximum(left[0], right[0])
    scales = [jnp.exp2(part[0] - peak) for part in (left, right)]
    return peak, *(left[j] * scales[0] + right[j] * scales[1] for j in (1, 2))


def load_part(ref, head):
    return tuple(ref[head, j : j + 1, :] for j in range(3))


def store_part(ref, head, part):
    for j, row in enumerate(part):
        ref[head, j : j + 1, :] = row


def prev_parts(peers, direct_keys, relayed_keys, outer_values, pair_ref, cols):
    even = (lax.axis_index("tm") & 1) == 0
    keys = jnp.where(through_relay(1, 1, peers), relayed_keys[:, cols], direct_keys[:, cols])
    parts = zip((keys, outer_values[:, cols]), joined_parts(pair_ref, cols))
    return tuple(jnp.where(even, outer, pair) for outer, pair in parts)


def stats_kernel(
    peers,
    rows_ref,
    queries_ref,
    direct_keys,
    relayed_keys,
    outer_values,
    pair_ref,
    own_ref,
    part_ref,
    queries_out,
    cotangent_out,
):
    heads = queries_ref.shape[1] // DEPTH
    rows = queries_out.shape[0]
    queries_out[...] = queries_ref[0:rows]
    cotangent_out[...] = queries_ref[rows : 2 * rows]

    def products(head):
        cols = head_cols(head)
        query, cotangent = joined_parts(queries_ref, cols)
        pieces = ((PREV, prev_parts(peers, direct_keys, relayed_keys, outer_values, pair_ref, cols)), (OWN, joined_parts(own_ref, cols)))
        return [
            (logits_of(keys, query, rows_ref, head, piece), dot(values, cotangent, 1, 1))
            for piece, (keys, values) in pieces
        ]

    ahead = products(0)
    for head in range(heads):
        now = ahead
        if head + 1 < heads:
            ahead = products(head + 1)
        store_part(part_ref, head, merged(*(part_of(*piece) for piece in now)))


def rounded(part, logits, slopes):
    peak, total, spread = merged(part, part_of(logits, slopes))
    inverse = 1.0 / total
    stats = peak, inverse, spread * inverse
    return stats, *weights_of(stats, logits, slopes)


def weights_of(stats, logits, slopes):
    peak, inverse, spread = stats
    probs = jnp.exp2(logits - peak) * inverse
    return probs.astype(BF16), (probs * (slopes - spread)).astype(BF16)


def memory_kernel(
    codes_ref, rows_ref, part_ref, pair_part_ref, own_queries, pair_queries, own_mem, pair_mem, keep_ref, send_ref
):
    role = lax.axis_index("tm") & 1
    code = code_of(codes_ref, SUM)
    frame_len, half_width = own_mem.shape[2:]
    half = half_width // DEPTH
    groups = ((own_queries, own_mem, part_ref, MEMORY), (pair_queries, pair_mem, pair_part_ref, PAIR))
    work = [(g, local) for local in range(half) for g in range(len(groups))]
    keep_ref[...] = jnp.zeros(keep_ref.shape, F32)

    def operands(g, local):
        cols = pl.ds(pl.multiple_of((role * half + local) * DEPTH, DEPTH), DEPTH)
        return joined_parts(groups[g][0], cols)

    def products(g, local):
        _, mem, _, piece = groups[g]
        query, cotangent = operands(g, local)
        keys, values = (mem[:, kind, :, head_cols(local)].reshape(MEM * frame_len, DEPTH) for kind in range(2))
        return logits_of(keys, query, rows_ref, role * half + local, piece), dot(values, cotangent, 1, 1)

    def add(g, local, _, weights, dlogits):
        query, cotangent = operands(g, local)
        terms = (dot(dlogits, query, 1, 0) * FACTOR, dot(weights, cotangent, 1, 0))
        for m in range(MEM):
            place = field(code, g * MEM + m, PLACE_BITS)
            for kind, term in enumerate(terms):
                part = term[m * frame_len : (m + 1) * frame_len].astype(BF16).astype(F32)
                keep_ref[place, kind, :, head_cols(local)] += part

    ahead = products(*work[0])
    behind = None
    for j, (g, local) in enumerate(work):
        now = ahead
        if j + 1 < len(work):
            ahead = products(*work[j + 1])
        if behind is not None:
            add(*work[j - 1], *behind)
        behind = rounded(load_part(groups[g][2], role * half + local), *now)
    add(*work[-1], *behind)
    kept = send_ref.shape[0]
    for place in range(kept):
        send_ref[place] = keep_ref[place if place + 1 < kept else kept].astype(BF16)


def next_kernel(
    peers,
    rows_ref,
    stats_ref,
    pair_queries,
    outer_queries,
    direct_cotangent,
    relayed_cotangent,
    own_ref,
    term_ref,
    sum_ref,
):
    even = (lax.axis_index("tm") & 1) == 0
    relayed = through_relay(-1, 2, peers)
    heads = pair_queries.shape[1] // DEPTH

    def operands(head):
        cols = head_cols(head)
        cotangent = jnp.where(relayed, relayed_cotangent[:, cols], direct_cotangent[:, cols])
        outer = outer_queries[:, cols], cotangent
        return [jnp.where(even, a, b) for a, b in zip(joined_parts(pair_queries, cols), outer)]

    def products(head):
        query, cotangent = operands(head)
        keys, values = joined_parts(own_ref, head_cols(head))
        return logits_of(keys, query, rows_ref, head, NEXT), dot(values, cotangent, 1, 1)

    ahead = products(0)
    for head in range(heads):
        now = ahead
        if head + 1 < heads:
            ahead = products(head + 1)
        weights, dlogits = weights_of(load_part(stats_ref, head), *now)
        query, cotangent = operands(head)
        cols = head_cols(head)
        sum_ref[0, :, cols] = term_ref[0, :, cols] + dot(dlogits, query, 1, 0) * FACTOR
        sum_ref[1, :, cols] = term_ref[1, :, cols] + dot(weights, cotangent, 1, 0)


def rest_kernel(
    peers,
    rows_ref,
    part_ref,
    queries_ref,
    direct_keys,
    relayed_keys,
    outer_values,
    pair_ref,
    own_ref,
    own_mem,
    other_mem,
    attended_ref,
    grad_query_ref,
    term_ref,
    stats_ref,
):
    role = lax.axis_index("tm") & 1
    frame_len, half_width = own_mem.shape[2:]
    heads = queries_ref.shape[1] // DEPTH
    half = half_width // DEPTH

    def pieces(head):
        cols = head_cols(head % half)
        prev = prev_parts(peers, direct_keys, relayed_keys, outer_values, pair_ref, head_cols(head))
        memory = [
            jnp.where(role == head // half, own_mem[:, kind, :, cols], other_mem[:, kind, :, cols]).reshape(
                MEM * frame_len, DEPTH
            )
            for kind in range(2)
        ]
        return (PREV, prev), (OWN, joined_parts(own_ref, head_cols(head))), (MEMORY, memory)

    def products(head):
        query, cotangent = joined_parts(queries_ref, head_cols(head))
        return [
            (logits_of(keys, query, rows_ref, head, piece), dot(values, cotangent, 1, 1))
            for piece, (keys, values) in pieces(head)
        ]

    ahead = products(0)
    for head in range(heads):
        now = ahead
        if head + 1 < heads:
            ahead = products(head + 1)
        cols = head_cols(head)
        query, cotangent = joined_parts(queries_ref, cols)
        stats, *last = rounded(load_part(part_ref, head), *now[-1])
        store_part(stats_ref, head, stats)
        rounds = [weights_of(stats, *now[PREV]), weights_of(stats, *now[OWN]), last]
        attended = grad_query = 0.0
        for (piece, (keys, values)), (weights, dlogits) in zip(pieces(head), rounds):
            attended += dot(values, weights, 0, 0)
            grad_query += dot(keys, dlogits, 0, 0)
            if piece == OWN:
                term_ref[0, :, cols] = dot(dlogits, query, 1, 0) * FACTOR
                term_ref[1, :, cols] = dot(weights, cotangent, 1, 0)
        attended_ref[:, cols] = attended.T.astype(BF16)
        grad_query_ref[:, cols] = (grad_query * FACTOR).T.astype(BF16)


def add_kernel(keep_ref, got_ref, out_ref, send_ref):
    value = keep_ref[0 : got_ref.shape[0]] + got_ref[...].astype(F32)
    out_ref[...] = value
    send_ref[...] = value.astype(BF16)


def pass_kernel(in_ref, out_ref):
    out_ref[...] = in_ref[...]


def owned_kernel(codes_ref, keep_ref, got_ref, mine_ref, pair_ref):
    code = code_of(codes_ref, OWNED)
    for o, out in enumerate((mine_ref, pair_ref)):
        for j in range(FR_DEV):
            owned = field(code, o * FR_DEV + j, PLACE_BITS)
            place = owned >> 1
            named = (owned & 1) != 0

            @pl.when(named)
            def _(out=out, j=j, place=place):
                value = keep_ref[place] + got_ref[place].astype(F32)
                out[j] = value.astype(out.dtype)

            @pl.when(jnp.logical_not(named))
            def _(out=out, j=j):
                out[j] = jnp.zeros(out.shape[1:], out.dtype)


def final_kernel(own_ref, mine_ref, got_ref, grad_key_ref, grad_value_ref):
    role = lax.axis_index("tm") & 1
    frame_len, half_width = mine_ref.shape[2:]
    for kind, out in enumerate((grad_key_ref, grad_value_ref)):
        for j in range(FR_DEV):
            rows = pl.ds(j * frame_len, frame_len)
            for half in range(2):
                cols = pl.ds(half * half_width, half_width)
                bank = jnp.where(role == half, mine_ref[j, kind], got_ref[j, kind].astype(F32))
                out[rows, cols] = (own_ref[kind, rows, cols] + bank).astype(BF16)


def body(
    query_states,
    key_states,
    value_states,
    grad_out,
    camera_pose,
    pose_bias,
    memory_index,
    bank_frames,
):
    row_count, width = query_states.shape
    frame_len = row_count // FR_DEV
    heads = pose_bias.shape[0]
    slots = bank_frames.shape[0]
    peers = lax.axis_size("tm")
    bits = [1 << i for i in range(1, peers.bit_length() - 1)]
    turns = list(zip(bits, bits[::-1]))
    piece_flops = 2 * row_count * row_count * width
    bank_frames = bank_frames.reshape(1, slots)
    last_bits = turns[-1]

    def join(kernel, rows, arrays, scratch, name, after=()):
        def run(*refs):
            kernel(*refs[: len(arrays)], *refs[len(arrays) + len(after) :])

        return pl.pallas_call(
            run,
            out_shape=shape(BF16, rows, width),
            in_specs=[pl.BlockSpec(memory_space=pltpu.HBM)] * len(arrays) + [ANY] * len(after),
            out_specs=VMEM,
            scratch_shapes=[*scratch, pltpu.SemaphoreType.DMA((len(arrays),))],
            compiler_params=pltpu.CompilerParams(vmem_limit_bytes=VMEM_LIMIT),
            name=name,
        )(*(pltpu.with_memory_space_constraint(array, pltpu.HBM) for array in arrays), *after)

    joined = join(
        join_kernel,
        2 * row_count + TAIL,
        [memory_index, key_states, value_states],
        [pltpu.VMEM(memory_index.shape, jnp.int32)],
        "join",
    )
    half_width = width // 2
    direct_keys = shift_first(key_states, 1, 1, peers)
    pair = swap(joined, 1, 1, peers)
    held = shape(BF16, slots - 1, 2, frame_len, half_width)
    sums = shape(F32, slots - 1, 2, frame_len, half_width)
    (mine,) = call(functools.partial(split_kernel, peers), [held], [bank_frames, joined, pair], name="split")
    queries = join(join_queries_kernel, 2 * row_count, [query_states, grad_out], [], "join_queries", after=[mine])
    pair_queries = swap(queries, 1, 1, peers)

    bias_rows = -(-(5 * FR_DEV) // 8) * 8
    rows, codes, values_out, keys_out = call(
        functools.partial(plan_kernel, peers, last_bits),
        [shape(F32, heads, bias_rows, row_count), shape(jnp.int32, 8, 128)] + [shape(BF16, row_count, width)] * 2,
        [pair, joined, direct_keys],
        scalars=[bank_frames, memory_index, camera_pose, pose_bias],
        flops=HIDING * piece_flops,
        name="plan",
    )
    outer = [direct_keys, shift_second(keys_out, 1, 1, peers), shift(values_out, 1, 1, peers)]
    even_done = odd_done = 1
    for step, (even_bit, odd_bit) in enumerate(turns):
        got = swap(mine, even_bit, odd_bit, peers)
        if step + 1 < len(turns):
            kernel = functools.partial(step_kernel, peers, even_done, odd_done)
            after = [codes, pair_queries]
            (mine,) = call(kernel, [held], [bank_frames, mine, got], after=after, name="step")
        even_done |= even_bit
        odd_done |= odd_bit

    stats = shape(F32, heads, 8, row_count)
    part, queries_out, cotangent_out = call(
        functools.partial(stats_kernel, peers),
        [stats] + [shape(BF16, row_count, width)] * 2,
        [rows, queries, *outer, pair, joined],
        flops=HIDING * piece_flops,
        name="stats",
    )
    pair_part = swap(part, 1, 1, peers)
    next_queries = shift(queries_out, -1, 2, peers)
    direct_cotangent = shift_first(cotangent_out, -1, 2, peers)
    chosen = shape(BF16, MEM, 2, frame_len, half_width)
    own_mem, pair_mem = call(pick_kernel, [chosen] * 2, [codes, mine, got], name="pick")
    keep, send = call(
        memory_kernel,
        [shape(F32, slots, 2, frame_len, half_width), held],
        [codes, rows, part, pair_part, queries, pair_queries, own_mem, pair_mem],
        flops=HIDING * piece_flops,
        name="memory",
    )
    other_mem = swap(pair_mem, 1, 1, peers)
    pair_sums = shape(F32, 2, row_count, width)
    attended, grad_query, own_terms, stats_all = call(
        functools.partial(rest_kernel, peers),
        [shape(BF16, row_count, width)] * 2 + [pair_sums, stats],
        [rows, part, queries, *outer, pair, joined, own_mem, other_mem],
        after=[send],
        flops=HIDING * piece_flops,
        name="rest",
    )
    next_stats = lax.ppermute(stats_all, "tm", [(i, i - 1) for i in range(1, peers)])
    (passed_on,) = call(
        pass_kernel, [shape(BF16, row_count, width)], [direct_cotangent], after=[own_terms], name="pass_on"
    )
    relayed_cotangent = shift_second(passed_on, -1, 2, peers)
    (own,) = call(
        functools.partial(next_kernel, peers),
        [pair_sums],
        [rows, next_stats, pair_queries, next_queries, direct_cotangent, relayed_cotangent, joined, own_terms],
        flops=HIDING * piece_flops,
        name="next",
    )
    for step, (even_bit, odd_bit) in enumerate(turns[::-1]):
        got = swap(send, even_bit, odd_bit, peers)
        if step + 1 < len(turns):
            after = [own_terms, next_queries]
            keep, send = call(add_kernel, [sums, held], [keep, got], after=after, name="add")
    owned_mine, owned_send = call(
        owned_kernel,
        [shape(F32, FR_DEV, 2, frame_len, half_width), shape(BF16, FR_DEV, 2, frame_len, half_width)],
        [codes, keep, got],
        after=[own],
        name="owned",
    )
    owned_got = swap(owned_send, 1, 1, peers)
    grad_key, grad_value = call(
        final_kernel, [shape(BF16, row_count, width)] * 2, [own, owned_mine, owned_got], name="final"
    )
    return (attended, grad_query, grad_key, grad_value)


def solution(mesh):
    rows = P(("traj", "tm"), None)
    in_specs = (rows, rows, rows, rows, P("traj"), P(), rows, P("traj"))
    return jax.shard_map(body, mesh=mesh, in_specs=in_specs, out_specs=(rows,) * 4, check_vma=False)
```

```python
import functools
import math

import jax
import jax.numpy as jnp
from jax import lax
from jax.experimental import pallas as pl
from jax.experimental.pallas import tpu as pltpu
from jax.sharding import PartitionSpec as P

FR_DEV = 2
MEM = 2
DEPTH = 128
TAIL = 16

BLOCKED_LOGIT = -1e30
LOG2E = math.log2(math.e)
FACTOR = 1.0 / math.sqrt(DEPTH)

SMEM = pl.BlockSpec(memory_space=pltpu.SMEM)
VMEM = pl.BlockSpec(memory_space=pltpu.VMEM)
ANY = pl.BlockSpec(memory_space=pl.ANY)
HIDING = 200
VMEM_LIMIT = 16 * 1024 * 1024
BF16, F32 = jnp.bfloat16, jnp.float32


def shape(dtype, *dims):
    return jax.ShapeDtypeStruct(dims, dtype)


def call(kernel, outs, arrays, scalars=(), after=(), flops=0, name=None):
    count = len(scalars) + len(arrays)

    def run(*refs):
        kernel(*refs[:count], *refs[count + len(after) :])

    return pl.pallas_call(
        run,
        out_shape=outs,
        in_specs=[SMEM] * len(scalars) + [VMEM] * len(arrays) + [ANY] * len(after),
        out_specs=[VMEM] * len(outs),
        compiler_params=pltpu.CompilerParams(vmem_limit_bytes=VMEM_LIMIT),
        cost_estimate=pl.CostEstimate(flops=flops, bytes_accessed=0, transcendentals=0) if flops else None,
        name=name,
    )(*scalars, *arrays, *after)


def swap(block, even_bit, odd_bit, peers):
    return lax.ppermute(block, "tm", [(i, i ^ (odd_bit if i & 1 else even_bit)) for i in range(peers)])


def shift(block, by, start, peers):
    pairs = [(i, i + by) for i in range(start, peers, 2) if 0 <= i + by < peers]
    return lax.ppermute(block, "tm", pairs)


def relays_of(by, start, peers):
    pairs = [(i, i + by) for i in range(start, peers, 2) if 0 <= i + by < peers]
    return {(i, j): i ^ 4 for i, j in pairs if peers == 8 and (i ^ j) >> 1 == 3}


def shift_first(block, by, start, peers):
    relays = relays_of(by, start, peers)
    pairs = [(i, i + by) for i in range(start, peers, 2) if 0 <= i + by < peers]
    return lax.ppermute(block, "tm", [(i, relays.get((i, j), j)) for i, j in pairs])


def shift_straight(block, by, start, peers):
    relays = relays_of(by, start, peers)
    pairs = [(i, i + by) for i in range(start, peers, 2) if 0 <= i + by < peers]
    return lax.ppermute(block, "tm", [pair for pair in pairs if pair not in relays])


def shift_diagonal(block, by, start, peers):
    pairs = list(relays_of(by, start, peers))
    return lax.ppermute(block, "tm", pairs) if pairs else block


def shift_second(block, by, start, peers):
    pairs = [(relay, j) for (_, j), relay in relays_of(by, start, peers).items()]
    return lax.ppermute(block, "tm", pairs) if pairs else block


def through_relay(by, start, peers):
    me = lax.axis_index("tm")
    return functools.reduce(jnp.logical_or, [me == j for _, j in relays_of(by, start, peers)], me < 0)


def lane_value(row, lane):
    lanes = lax.broadcasted_iota(jnp.int32, row.shape, 1)
    return jnp.max(jnp.where(lanes == lane, row, 0))


def bank_of(bank_ref):
    row = bank_ref[...]
    return [lane_value(row, slot) for slot in range(row.shape[1])]


def dyn_frames(bank, last_frame):
    found = [jnp.int32(0)] * (len(bank) - 2)
    seen = jnp.int32(0)
    for frame in bank:
        free = jnp.logical_and(frame != 0, frame != last_frame)
        for j in range(len(found)):
            found[j] = jnp.where(jnp.logical_and(free, seen == j), frame, found[j])
        seen = seen + free.astype(jnp.int32)
    return found


def place_of(frame, dyns):
    place = jnp.int32(len(dyns))
    for j, dyn in enumerate(dyns):
        place = jnp.where(frame == dyn, j, place)
    return place


def choose(out, take_first, first, second):
    @pl.when(take_first)
    def _():
        out[...] = first[...]

    @pl.when(jnp.logical_not(take_first))
    def _():
        out[...] = second[...]


def has_end(me, done, peers):
    return jnp.logical_or((me & ~done) == 0, (me | done) == peers - 1)


def has_dyn(me, frame, done):
    return ((me ^ (frame // FR_DEV)) & ~done) == 0


def by_role(me, even_value, odd_value):
    return jnp.where((me & 1) == 0, even_value, odd_value)


def join_kernel(index_ref, key_ref, value_ref, joined_ref, index_buf, sems):
    rows = key_ref.shape[0]
    copies = [
        pltpu.make_async_copy(index_ref, index_buf, sems.at[0]),
        pltpu.make_async_copy(key_ref, joined_ref.at[pl.ds(0, rows)], sems.at[1]),
        pltpu.make_async_copy(value_ref, joined_ref.at[pl.ds(rows, rows)], sems.at[2]),
    ]
    for copy in copies:
        copy.start()
    copies[0].wait()
    width = joined_ref.shape[1]
    lane = lax.broadcasted_iota(jnp.int32, (TAIL, width), 1) // DEPTH
    tail = jnp.zeros((TAIL, width), jnp.int32)
    for m in range(MEM):
        tail = jnp.where(lane == m, index_buf[0:1, m : m + 1], tail)
    joined_ref[2 * rows : 2 * rows + TAIL, :] = tail.astype(F32).astype(BF16)
    copies[1].wait()
    copies[2].wait()


def join_queries_kernel(query_ref, cotangent_ref, joined_ref, sems):
    rows = query_ref.shape[0]
    copies = [
        pltpu.make_async_copy(ref, joined_ref.at[pl.ds(j * rows, rows)], sems.at[j])
        for j, ref in enumerate((query_ref, cotangent_ref))
    ]
    for copy in copies:
        copy.start()
    for copy in copies:
        copy.wait()


def pack(fields, width):
    code = jnp.int32(0)
    for j, field in enumerate(fields):
        code = code | (field.astype(jnp.int32) << (j * width))
    return code


def field(code, j, width):
    return (code >> (j * width)) & ((1 << width) - 1)


def code_of(codes_ref, row):
    return jnp.max(codes_ref[row : row + 1, :])


PICK, SUM, OWNED = range(3)
PLACE_BITS = 4
PREV, OWN, MEMORY, NEXT, PAIR = range(5)


def plan_kernel(
    peers,
    last_bits,
    bank_ref,
    index_ref,
    pose_ref,
    bias_ref,
    pair_ref,
    joined_ref,
    direct_keys,
    queries_ref,
    rows_ref,
    codes_ref,
    values_out,
    keys_out,
    queries_out,
):
    me = lax.axis_index("tm")
    last_frame = peers * FR_DEV - 1
    heads, _, row_count = rows_ref.shape
    values_out[...] = joined_ref[row_count : 2 * row_count, :]
    keys_out[...] = direct_keys[...]
    queries_out[...] = queries_ref[0:row_count]
    bank = [bank_ref[0, slot] for slot in range(bank_ref.shape[1])]
    tail = pair_ref.shape[0] - TAIL
    pair_ids = []
    for m in range(MEM):
        slot = jnp.max(pair_ref[tail : tail + TAIL, m * DEPTH : (m + 1) * DEPTH].astype(F32)).astype(jnp.int32)
        pair_ids.append(bank_ref[0, slot])
    mem_ids = [bank_ref[0, index_ref[0, m]] for m in range(MEM)]

    own_ids = [me * FR_DEV + j for j in range(FR_DEV)]
    prev_ids = [jnp.maximum(own - FR_DEV, 0) for own in own_ids]
    next_ids = [jnp.minimum(own + FR_DEV, last_frame) for own in own_ids]
    pair_own_ids = [(me ^ 1) * FR_DEV + j for j in range(FR_DEV)]
    pieces = ((prev_ids, own_ids), (own_ids, own_ids), (mem_ids, own_ids), (own_ids, next_ids), (pair_ids, pair_own_ids))
    poses = [([pose_ref[f] for f in key_ids], [pose_ref[f] for f in query_ids]) for key_ids, query_ids in pieces]
    frame_of = lax.broadcasted_iota(jnp.int32, (1, row_count), 1) // (row_count // FR_DEV)
    for head in range(heads):
        for piece, (key_poses, query_poses) in enumerate(poses):
            for j, key_pose in enumerate(key_poses):
                row = jnp.zeros((1, row_count), F32)
                for a, query_pose in enumerate(query_poses):
                    value = bias_ref[head, query_pose, key_pose] * LOG2E
                    if piece == PREV:
                        value = jnp.where(me == 0, BLOCKED_LOGIT, value)
                    row = jnp.where(frame_of == a, value, row)
                rows_ref[head, piece * FR_DEV + j : piece * FR_DEV + j + 1, :] = row

    dyns = dyn_frames(bank, last_frame)
    bit = by_role(me, *last_bits)
    upper = (me & bit) != 0
    picks = []
    for frame in mem_ids + pair_ids:
        source = place_of(frame, dyns)
        local = jnp.where(frame == 0, jnp.logical_not(upper), upper)
        local = jnp.where(source < len(dyns), has_dyn(me, frame, (peers - 1) & ~bit), local)
        picks.append(source * 2 + local.astype(jnp.int32))
    far = jnp.where(upper, 0, last_frame)
    sums = [jnp.where(frame == far, len(dyns) + 1, place_of(frame, dyns)) for frame in mem_ids + pair_ids]
    owned = []
    for group in (me, me ^ 1):
        for j in range(FR_DEV):
            frame = group * FR_DEV + j
            place = place_of(frame, dyns)
            named = jnp.logical_or(place < len(dyns), jnp.logical_or(frame == 0, frame == last_frame))
            owned.append(place * 2 + named.astype(jnp.int32))
    lanes = codes_ref.shape[1]
    for row, code in ((PICK, pack(picks, PLACE_BITS)), (SUM, pack(sums, PLACE_BITS)), (OWNED, pack(owned, PLACE_BITS))):
        codes_ref[row : row + 1, :] = jnp.full((1, lanes), code, jnp.int32)


def split_kernel(peers, bank_ref, mine_ref, pair_ref, out_ref):
    me = lax.axis_index("tm")
    frame_len, half_width = out_ref.shape[2:]
    dyns = dyn_frames(bank_of(bank_ref), peers * FR_DEV - 1)
    places = [(has_dyn(me, dyn, 0), dyn % FR_DEV) for dyn in dyns]
    places.append((has_end(me, 0, peers), jnp.where(me < peers // 2, 0, FR_DEV - 1)))
    for j, (local, frame) in enumerate(places):
        for role in range(2):
            for source, taken in ((mine_ref, local), (pair_ref, jnp.logical_not(local))):

                @pl.when(jnp.logical_and((me & 1) == role, taken))
                def _(source=source, j=j, frame=frame, role=role):
                    for kind in range(2):
                        start = pl.multiple_of((kind * FR_DEV + frame) * frame_len, frame_len)
                        out_ref[j, kind] = source[pl.ds(start, frame_len), role * half_width : (role + 1) * half_width]


def step_kernel(peers, even_done, odd_done, bank_ref, mine_ref, got_ref, out_ref):
    me = lax.axis_index("tm")
    done = by_role(me, even_done, odd_done)
    dyns = dyn_frames(bank_of(bank_ref), peers * FR_DEV - 1)
    flags = [has_dyn(me, dyn, done) for dyn in dyns] + [has_end(me, done, peers)]
    for j, flag in enumerate(flags):
        choose(out_ref.at[j], flag, mine_ref.at[j], got_ref.at[j])


def pick_kernel(codes_ref, mine_ref, got_ref, own_out, pair_out):
    code = code_of(codes_ref, PICK)
    for o, out in enumerate((own_out, pair_out)):
        for m in range(MEM):
            pick = field(code, o * MEM + m, PLACE_BITS)
            source = pick >> 1
            choose(out.at[m], (pick & 1) != 0, mine_ref.at[source], got_ref.at[source])


def dot(a, b, left, right):
    return lax.dot_general(a, b, (((left,), (right,)), ((), ())), preferred_element_type=F32)


def logits_of(keys, query, rows_ref, head, piece):
    frame_len = query.shape[0] // FR_DEV
    raw = dot(keys, query, 1, 1) * (FACTOR * LOG2E)
    parts = []
    for j in range(FR_DEV):
        row = piece * FR_DEV + j
        parts.append(raw[j * frame_len : (j + 1) * frame_len] + rows_ref[head, row : row + 1, :])
    return jnp.concatenate(parts, axis=0)


def joined_parts(joined_ref, cols):
    rows = joined_ref.shape[0] // 2 // DEPTH * DEPTH
    return joined_ref[0:rows, cols], joined_ref[rows : 2 * rows, cols]


def head_cols(head):
    return pl.ds(head * DEPTH, DEPTH)


def part_of(logits, slopes):
    peak = jnp.max(logits, axis=0, keepdims=True)
    exps = jnp.exp2(logits - peak)
    return peak, jnp.sum(exps, axis=0, keepdims=True), jnp.sum(exps * slopes, axis=0, keepdims=True)


def merged(left, right):
    peak = jnp.maximum(left[0], right[0])
    scales = [jnp.exp2(part[0] - peak) for part in (left, right)]
    return peak, *(left[j] * scales[0] + right[j] * scales[1] for j in (1, 2))


def load_part(ref, head):
    return tuple(ref[head, j : j + 1, :] for j in range(3))


def store_part(ref, head, part):
    for j, row in enumerate(part):
        ref[head, j : j + 1, :] = row


def prev_parts(peers, direct_keys, relayed_keys, outer_values, pair_ref, cols):
    even = (lax.axis_index("tm") & 1) == 0
    keys = jnp.where(through_relay(1, 1, peers), relayed_keys[:, cols], direct_keys[:, cols])
    parts = zip((keys, outer_values[:, cols]), joined_parts(pair_ref, cols))
    return tuple(jnp.where(even, outer, pair) for outer, pair in parts)


def stats_kernel(
    peers,
    rows_ref,
    queries_ref,
    direct_keys,
    relayed_keys,
    outer_values,
    pair_ref,
    own_ref,
    part_ref,
    queries_out,
    cotangent_out,
):
    heads = queries_ref.shape[1] // DEPTH
    rows = queries_out.shape[0]
    queries_out[...] = queries_ref[0:rows]
    cotangent_out[...] = queries_ref[rows : 2 * rows]

    def products(head):
        cols = head_cols(head)
        query, cotangent = joined_parts(queries_ref, cols)
        pieces = ((PREV, prev_parts(peers, direct_keys, relayed_keys, outer_values, pair_ref, cols)), (OWN, joined_parts(own_ref, cols)))
        return [
            (logits_of(keys, query, rows_ref, head, piece), dot(values, cotangent, 1, 1))
            for piece, (keys, values) in pieces
        ]

    ahead = products(0)
    for head in range(heads):
        now = ahead
        if head + 1 < heads:
            ahead = products(head + 1)
        store_part(part_ref, head, merged(*(part_of(*piece) for piece in now)))


def rounded(part, logits, slopes):
    peak, total, spread = merged(part, part_of(logits, slopes))
    inverse = 1.0 / total
    stats = peak, inverse, spread * inverse
    return stats, *weights_of(stats, logits, slopes)


def weights_of(stats, logits, slopes):
    peak, inverse, spread = stats
    probs = jnp.exp2(logits - peak) * inverse
    return probs.astype(BF16), (probs * (slopes - spread)).astype(BF16)


def memory_kernel(
    codes_ref, rows_ref, part_ref, pair_part_ref, own_queries, pair_queries, own_mem, pair_mem, keep_ref, send_ref
):
    role = lax.axis_index("tm") & 1
    code = code_of(codes_ref, SUM)
    frame_len, half_width = own_mem.shape[2:]
    half = half_width // DEPTH
    groups = ((own_queries, own_mem, part_ref, MEMORY), (pair_queries, pair_mem, pair_part_ref, PAIR))
    work = [(g, local) for local in range(half) for g in range(len(groups))]
    keep_ref[...] = jnp.zeros(keep_ref.shape, F32)

    def operands(g, local):
        cols = pl.ds(pl.multiple_of((role * half + local) * DEPTH, DEPTH), DEPTH)
        return joined_parts(groups[g][0], cols)

    def products(g, local):
        _, mem, _, piece = groups[g]
        query, cotangent = operands(g, local)
        keys, values = (mem[:, kind, :, head_cols(local)].reshape(MEM * frame_len, DEPTH) for kind in range(2))
        return logits_of(keys, query, rows_ref, role * half + local, piece), dot(values, cotangent, 1, 1)

    def add(g, local, _, weights, dlogits):
        query, cotangent = operands(g, local)
        terms = (dot(dlogits, query, 1, 0) * FACTOR, dot(weights, cotangent, 1, 0))
        for m in range(MEM):
            place = field(code, g * MEM + m, PLACE_BITS)
            for kind, term in enumerate(terms):
                part = term[m * frame_len : (m + 1) * frame_len].astype(BF16).astype(F32)
                keep_ref[place, kind, :, head_cols(local)] += part

    ahead = products(*work[0])
    behind = None
    for j, (g, local) in enumerate(work):
        now = ahead
        if j + 1 < len(work):
            ahead = products(*work[j + 1])
        if behind is not None:
            add(*work[j - 1], *behind)
        behind = rounded(load_part(groups[g][2], role * half + local), *now)
    add(*work[-1], *behind)
    kept = send_ref.shape[0]
    for place in range(kept):
        send_ref[place] = keep_ref[place if place + 1 < kept else kept].astype(BF16)


def next_kernel(
    peers,
    rows_ref,
    stats_ref,
    pair_queries,
    straight_queries,
    diagonal_queries,
    direct_cotangent,
    relayed_cotangent,
    own_ref,
    term_ref,
    sum_ref,
):
    even = (lax.axis_index("tm") & 1) == 0
    relayed = through_relay(-1, 2, peers)
    heads = pair_queries.shape[1] // DEPTH

    def operands(head):
        cols = head_cols(head)
        query = jnp.where(relayed, diagonal_queries[:, cols], straight_queries[:, cols])
        cotangent = jnp.where(relayed, relayed_cotangent[:, cols], direct_cotangent[:, cols])
        outer = query, cotangent
        return [jnp.where(even, a, b) for a, b in zip(joined_parts(pair_queries, cols), outer)]

    def products(head):
        query, cotangent = operands(head)
        keys, values = joined_parts(own_ref, head_cols(head))
        return logits_of(keys, query, rows_ref, head, NEXT), dot(values, cotangent, 1, 1)

    ahead = products(0)
    for head in range(heads):
        now = ahead
        if head + 1 < heads:
            ahead = products(head + 1)
        weights, dlogits = weights_of(load_part(stats_ref, head), *now)
        query, cotangent = operands(head)
        cols = head_cols(head)
        sum_ref[0, :, cols] = term_ref[0, :, cols] + dot(dlogits, query, 1, 0) * FACTOR
        sum_ref[1, :, cols] = term_ref[1, :, cols] + dot(weights, cotangent, 1, 0)


def rest_kernel(
    peers,
    rows_ref,
    part_ref,
    queries_ref,
    direct_keys,
    relayed_keys,
    outer_values,
    pair_ref,
    own_ref,
    own_mem,
    other_mem,
    attended_ref,
    grad_query_ref,
    term_ref,
    stats_ref,
):
    role = lax.axis_index("tm") & 1
    frame_len, half_width = own_mem.shape[2:]
    heads = queries_ref.shape[1] // DEPTH
    half = half_width // DEPTH

    def pieces(head):
        cols = head_cols(head % half)
        prev = prev_parts(peers, direct_keys, relayed_keys, outer_values, pair_ref, head_cols(head))
        memory = [
            jnp.where(role == head // half, own_mem[:, kind, :, cols], other_mem[:, kind, :, cols]).reshape(
                MEM * frame_len, DEPTH
            )
            for kind in range(2)
        ]
        return (PREV, prev), (OWN, joined_parts(own_ref, head_cols(head))), (MEMORY, memory)

    def products(head):
        query, cotangent = joined_parts(queries_ref, head_cols(head))
        return [
            (logits_of(keys, query, rows_ref, head, piece), dot(values, cotangent, 1, 1))
            for piece, (keys, values) in pieces(head)
        ]

    ahead = products(0)
    for head in range(heads):
        now = ahead
        if head + 1 < heads:
            ahead = products(head + 1)
        cols = head_cols(head)
        query, cotangent = joined_parts(queries_ref, cols)
        stats, *last = rounded(load_part(part_ref, head), *now[-1])
        store_part(stats_ref, head, stats)
        rounds = [weights_of(stats, *now[PREV]), weights_of(stats, *now[OWN]), last]
        attended = grad_query = 0.0
        for (piece, (keys, values)), (weights, dlogits) in zip(pieces(head), rounds):
            attended += dot(values, weights, 0, 0)
            grad_query += dot(keys, dlogits, 0, 0)
            if piece == OWN:
                term_ref[0, :, cols] = dot(dlogits, query, 1, 0) * FACTOR
                term_ref[1, :, cols] = dot(weights, cotangent, 1, 0)
        attended_ref[:, cols] = attended.T.astype(BF16)
        grad_query_ref[:, cols] = (grad_query * FACTOR).T.astype(BF16)


def add_kernel(keep_ref, got_ref, out_ref, send_ref):
    value = keep_ref[0 : got_ref.shape[0]] + got_ref[...].astype(F32)
    out_ref[...] = value
    send_ref[...] = value.astype(BF16)


def pass_kernel(in_ref, out_ref):
    out_ref[...] = in_ref[...]


def owned_kernel(codes_ref, keep_ref, got_ref, mine_ref, pair_ref):
    code = code_of(codes_ref, OWNED)
    for o, out in enumerate((mine_ref, pair_ref)):
        for j in range(FR_DEV):
            owned = field(code, o * FR_DEV + j, PLACE_BITS)
            place = owned >> 1
            named = (owned & 1) != 0

            @pl.when(named)
            def _(out=out, j=j, place=place):
                value = keep_ref[place] + got_ref[place].astype(F32)
                out[j] = value.astype(out.dtype)

            @pl.when(jnp.logical_not(named))
            def _(out=out, j=j):
                out[j] = jnp.zeros(out.shape[1:], out.dtype)


def final_kernel(own_ref, mine_ref, got_ref, grad_key_ref, grad_value_ref):
    role = lax.axis_index("tm") & 1
    frame_len, half_width = mine_ref.shape[2:]
    for kind, out in enumerate((grad_key_ref, grad_value_ref)):
        for j in range(FR_DEV):
            rows = pl.ds(j * frame_len, frame_len)
            for half in range(2):
                cols = pl.ds(half * half_width, half_width)
                bank = jnp.where(role == half, mine_ref[j, kind], got_ref[j, kind].astype(F32))
                out[rows, cols] = (own_ref[kind, rows, cols] + bank).astype(BF16)


def body(
    query_states,
    key_states,
    value_states,
    grad_out,
    camera_pose,
    pose_bias,
    memory_index,
    bank_frames,
):
    row_count, width = query_states.shape
    frame_len = row_count // FR_DEV
    heads = pose_bias.shape[0]
    slots = bank_frames.shape[0]
    peers = lax.axis_size("tm")
    bits = [1 << i for i in range(1, peers.bit_length() - 1)]
    turns = list(zip(bits, bits[::-1]))
    piece_flops = 2 * row_count * row_count * width
    bank_frames = bank_frames.reshape(1, slots)
    last_bits = turns[-1]

    def join(kernel, rows, arrays, scratch, name, after=()):
        def run(*refs):
            kernel(*refs[: len(arrays)], *refs[len(arrays) + len(after) :])

        return pl.pallas_call(
            run,
            out_shape=shape(BF16, rows, width),
            in_specs=[pl.BlockSpec(memory_space=pltpu.HBM)] * len(arrays) + [ANY] * len(after),
            out_specs=VMEM,
            scratch_shapes=[*scratch, pltpu.SemaphoreType.DMA((len(arrays),))],
            compiler_params=pltpu.CompilerParams(vmem_limit_bytes=VMEM_LIMIT),
            name=name,
        )(*(pltpu.with_memory_space_constraint(array, pltpu.HBM) for array in arrays), *after)

    joined = join(
        join_kernel,
        2 * row_count + TAIL,
        [memory_index, key_states, value_states],
        [pltpu.VMEM(memory_index.shape, jnp.int32)],
        "join",
    )
    half_width = width // 2
    direct_keys = shift_first(key_states, 1, 1, peers)
    pair = swap(joined, 1, 1, peers)
    held = shape(BF16, slots - 1, 2, frame_len, half_width)
    sums = shape(F32, slots - 1, 2, frame_len, half_width)
    (mine,) = call(functools.partial(split_kernel, peers), [held], [bank_frames, joined, pair], name="split")
    queries = join(join_queries_kernel, 2 * row_count, [query_states, grad_out], [], "join_queries", after=[mine])
    pair_queries = swap(queries, 1, 1, peers)

    bias_rows = -(-(5 * FR_DEV) // 8) * 8
    rows, codes, values_out, keys_out, queries_out = call(
        functools.partial(plan_kernel, peers, last_bits),
        [shape(F32, heads, bias_rows, row_count), shape(jnp.int32, 8, 128)] + [shape(BF16, row_count, width)] * 3,
        [pair, joined, direct_keys, queries],
        scalars=[bank_frames, memory_index, camera_pose, pose_bias],
        flops=HIDING * piece_flops,
        name="plan",
    )
    outer = [direct_keys, shift_second(keys_out, 1, 1, peers), shift(values_out, 1, 1, peers)]
    straight_queries = shift_straight(queries_out, -1, 2, peers)
    even_done = odd_done = 1
    for step, (even_bit, odd_bit) in enumerate(turns):
        got = swap(mine, even_bit, odd_bit, peers)
        if step + 1 < len(turns):
            kernel = functools.partial(step_kernel, peers, even_done, odd_done)
            after = [codes, pair_queries]
            (mine,) = call(kernel, [held], [bank_frames, mine, got], after=after, name="step")
        even_done |= even_bit
        odd_done |= odd_bit

    stats = shape(F32, heads, 8, row_count)
    part, queries_out, cotangent_out = call(
        functools.partial(stats_kernel, peers),
        [stats] + [shape(BF16, row_count, width)] * 2,
        [rows, queries, *outer, pair, joined],
        after=[straight_queries],
        flops=HIDING * piece_flops,
        name="stats",
    )
    pair_part = swap(part, 1, 1, peers)
    diagonal_queries = shift_diagonal(queries_out, -1, 2, peers)
    direct_cotangent = shift_first(cotangent_out, -1, 2, peers)
    chosen = shape(BF16, MEM, 2, frame_len, half_width)
    own_mem, pair_mem = call(pick_kernel, [chosen] * 2, [codes, mine, got], name="pick")
    keep, send = call(
        memory_kernel,
        [shape(F32, slots, 2, frame_len, half_width), held],
        [codes, rows, part, pair_part, queries, pair_queries, own_mem, pair_mem],
        flops=HIDING * piece_flops,
        name="memory",
    )
    other_mem = swap(pair_mem, 1, 1, peers)
    pair_sums = shape(F32, 2, row_count, width)
    attended, grad_query, own_terms, stats_all = call(
        functools.partial(rest_kernel, peers),
        [shape(BF16, row_count, width)] * 2 + [pair_sums, stats],
        [rows, part, queries, *outer, pair, joined, own_mem, other_mem],
        after=[send],
        flops=HIDING * piece_flops,
        name="rest",
    )
    next_stats = lax.ppermute(stats_all, "tm", [(i, i - 1) for i in range(1, peers)])
    (passed_on,) = call(
        pass_kernel, [shape(BF16, row_count, width)], [direct_cotangent], after=[own_terms], name="pass_on"
    )
    relayed_cotangent = shift_second(passed_on, -1, 2, peers)
    (own,) = call(
        functools.partial(next_kernel, peers),
        [pair_sums],
        [rows, next_stats, pair_queries, straight_queries, diagonal_queries, direct_cotangent, relayed_cotangent, joined, own_terms],
        flops=HIDING * piece_flops,
        name="next",
    )
    for step, (even_bit, odd_bit) in enumerate(turns[::-1]):
        got = swap(send, even_bit, odd_bit, peers)
        if step + 1 < len(turns):
            after = [own_terms, diagonal_queries]
            keep, send = call(add_kernel, [sums, held], [keep, got], after=after, name="add")
    owned_mine, owned_send = call(
        owned_kernel,
        [shape(F32, FR_DEV, 2, frame_len, half_width), shape(BF16, FR_DEV, 2, frame_len, half_width)],
        [codes, keep, got],
        after=[own],
        name="owned",
    )
    owned_got = swap(owned_send, 1, 1, peers)
    grad_key, grad_value = call(
        final_kernel, [shape(BF16, row_count, width)] * 2, [own, owned_mine, owned_got], name="final"
    )
    return (attended, grad_query, grad_key, grad_value)


def solution(mesh):
    rows = P(("traj", "tm"), None)
    in_specs = (rows, rows, rows, rows, P("traj"), P(), rows, P("traj"))
    return jax.shard_map(body, mesh=mesh, in_specs=in_specs, out_specs=(rows,) * 4, check_vma=False)
```

```python
import functools
import math

import jax
import jax.numpy as jnp
from jax import lax
from jax.experimental import pallas as pl
from jax.experimental.pallas import tpu as pltpu
from jax.sharding import PartitionSpec as P

FR_DEV = 2
MEM = 2
DEPTH = 128
TAIL = 16

BLOCKED_LOGIT = -1e30
LOG2E = math.log2(math.e)
FACTOR = 1.0 / math.sqrt(DEPTH)

SMEM = pl.BlockSpec(memory_space=pltpu.SMEM)
VMEM = pl.BlockSpec(memory_space=pltpu.VMEM)
ANY = pl.BlockSpec(memory_space=pl.ANY)
HIDING = 200
VMEM_LIMIT = 16 * 1024 * 1024
BF16, F32 = jnp.bfloat16, jnp.float32


def shape(dtype, *dims):
    return jax.ShapeDtypeStruct(dims, dtype)


def call(kernel, outs, arrays, scalars=(), after=(), flops=0, name=None):
    count = len(scalars) + len(arrays)

    def run(*refs):
        kernel(*refs[:count], *refs[count + len(after) :])

    return pl.pallas_call(
        run,
        out_shape=outs,
        in_specs=[SMEM] * len(scalars) + [VMEM] * len(arrays) + [ANY] * len(after),
        out_specs=[VMEM] * len(outs),
        compiler_params=pltpu.CompilerParams(vmem_limit_bytes=VMEM_LIMIT),
        cost_estimate=pl.CostEstimate(flops=flops, bytes_accessed=0, transcendentals=0) if flops else None,
        name=name,
    )(*scalars, *arrays, *after)


def swap(block, even_bit, odd_bit, peers):
    return lax.ppermute(block, "tm", [(i, i ^ (odd_bit if i & 1 else even_bit)) for i in range(peers)])


def shift(block, by, start, peers):
    pairs = [(i, i + by) for i in range(start, peers, 2) if 0 <= i + by < peers]
    return lax.ppermute(block, "tm", pairs)


def relays_of(by, start, peers):
    pairs = [(i, i + by) for i in range(start, peers, 2) if 0 <= i + by < peers]
    return {(i, j): i ^ 4 for i, j in pairs if peers == 8 and (i ^ j) >> 1 == 3}


def shift_first(block, by, start, peers):
    relays = relays_of(by, start, peers)
    pairs = [(i, i + by) for i in range(start, peers, 2) if 0 <= i + by < peers]
    return lax.ppermute(block, "tm", [(i, relays.get((i, j), j)) for i, j in pairs])


def shift_second(block, by, start, peers):
    pairs = [(relay, j) for (_, j), relay in relays_of(by, start, peers).items()]
    return lax.ppermute(block, "tm", pairs) if pairs else block


def through_relay(by, start, peers):
    me = lax.axis_index("tm")
    return functools.reduce(jnp.logical_or, [me == j for _, j in relays_of(by, start, peers)], me < 0)


def lane_value(row, lane):
    lanes = lax.broadcasted_iota(jnp.int32, row.shape, 1)
    return jnp.max(jnp.where(lanes == lane, row, 0))


def bank_of(bank_ref):
    row = bank_ref[...]
    return [lane_value(row, slot) for slot in range(row.shape[1])]


def dyn_frames(bank, last_frame):
    found = [jnp.int32(0)] * (len(bank) - 2)
    seen = jnp.int32(0)
    for frame in bank:
        free = jnp.logical_and(frame != 0, frame != last_frame)
        for j in range(len(found)):
            found[j] = jnp.where(jnp.logical_and(free, seen == j), frame, found[j])
        seen = seen + free.astype(jnp.int32)
    return found


def place_of(frame, dyns):
    place = jnp.int32(len(dyns))
    for j, dyn in enumerate(dyns):
        place = jnp.where(frame == dyn, j, place)
    return place


def choose(out, take_first, first, second):
    @pl.when(take_first)
    def _():
        out[...] = first[...]

    @pl.when(jnp.logical_not(take_first))
    def _():
        out[...] = second[...]


def has_end(me, done, peers):
    return jnp.logical_or((me & ~done) == 0, (me | done) == peers - 1)


def has_dyn(me, frame, done):
    return ((me ^ (frame // FR_DEV)) & ~done) == 0


def by_role(me, even_value, odd_value):
    return jnp.where((me & 1) == 0, even_value, odd_value)


def join_kernel(index_ref, key_ref, value_ref, joined_ref, index_buf, sems):
    rows = key_ref.shape[0]
    copies = [
        pltpu.make_async_copy(index_ref, index_buf, sems.at[0]),
        pltpu.make_async_copy(key_ref, joined_ref.at[pl.ds(0, rows)], sems.at[1]),
        pltpu.make_async_copy(value_ref, joined_ref.at[pl.ds(rows, rows)], sems.at[2]),
    ]
    for copy in copies:
        copy.start()
    copies[0].wait()
    width = joined_ref.shape[1]
    lane = lax.broadcasted_iota(jnp.int32, (TAIL, width), 1) // DEPTH
    tail = jnp.zeros((TAIL, width), jnp.int32)
    for m in range(MEM):
        tail = jnp.where(lane == m, index_buf[0:1, m : m + 1], tail)
    joined_ref[2 * rows : 2 * rows + TAIL, :] = tail.astype(F32).astype(BF16)
    copies[1].wait()
    copies[2].wait()


def join_queries_kernel(query_ref, cotangent_ref, joined_ref, sems):
    rows = query_ref.shape[0]
    copies = [
        pltpu.make_async_copy(ref, joined_ref.at[pl.ds(j * rows, rows)], sems.at[j])
        for j, ref in enumerate((query_ref, cotangent_ref))
    ]
    for copy in copies:
        copy.start()
    for copy in copies:
        copy.wait()


def pack(fields, width):
    code = jnp.int32(0)
    for j, field in enumerate(fields):
        code = code | (field.astype(jnp.int32) << (j * width))
    return code


def field(code, j, width):
    return (code >> (j * width)) & ((1 << width) - 1)


def code_of(codes_ref, row):
    return jnp.max(codes_ref[row : row + 1, :])


PICK, SUM, OWNED = range(3)
PLACE_BITS = 4
PREV, OWN, MEMORY, NEXT, PAIR = range(5)


def plan_kernel(
    peers,
    last_bits,
    bank_ref,
    index_ref,
    pose_ref,
    bias_ref,
    pair_ref,
    joined_ref,
    direct_keys,
    rows_ref,
    codes_ref,
    values_out,
    keys_out,
):
    me = lax.axis_index("tm")
    last_frame = peers * FR_DEV - 1
    heads, _, row_count = rows_ref.shape
    values_out[...] = joined_ref[row_count : 2 * row_count, :]
    keys_out[...] = direct_keys[...]
    bank = [bank_ref[0, slot] for slot in range(bank_ref.shape[1])]
    tail = pair_ref.shape[0] - TAIL
    pair_ids = []
    for m in range(MEM):
        slot = jnp.max(pair_ref[tail : tail + TAIL, m * DEPTH : (m + 1) * DEPTH].astype(F32)).astype(jnp.int32)
        pair_ids.append(bank_ref[0, slot])
    mem_ids = [bank_ref[0, index_ref[0, m]] for m in range(MEM)]

    own_ids = [me * FR_DEV + j for j in range(FR_DEV)]
    prev_ids = [jnp.maximum(own - FR_DEV, 0) for own in own_ids]
    next_ids = [jnp.minimum(own + FR_DEV, last_frame) for own in own_ids]
    pair_own_ids = [(me ^ 1) * FR_DEV + j for j in range(FR_DEV)]
    pieces = ((prev_ids, own_ids), (own_ids, own_ids), (mem_ids, own_ids), (own_ids, next_ids), (pair_ids, pair_own_ids))
    poses = [([pose_ref[f] for f in key_ids], [pose_ref[f] for f in query_ids]) for key_ids, query_ids in pieces]
    frame_of = lax.broadcasted_iota(jnp.int32, (1, row_count), 1) // (row_count // FR_DEV)
    for head in range(heads):
        for piece, (key_poses, query_poses) in enumerate(poses):
            for j, key_pose in enumerate(key_poses):
                row = jnp.zeros((1, row_count), F32)
                for a, query_pose in enumerate(query_poses):
                    value = bias_ref[head, query_pose, key_pose] * LOG2E
                    if piece == PREV:
                        value = jnp.where(me == 0, BLOCKED_LOGIT, value)
                    row = jnp.where(frame_of == a, value, row)
                rows_ref[head, piece * FR_DEV + j : piece * FR_DEV + j + 1, :] = row

    dyns = dyn_frames(bank, last_frame)
    bit = by_role(me, *last_bits)
    upper = (me & bit) != 0
    picks = []
    for frame in mem_ids + pair_ids:
        source = place_of(frame, dyns)
        local = jnp.where(frame == 0, jnp.logical_not(upper), upper)
        local = jnp.where(source < len(dyns), has_dyn(me, frame, (peers - 1) & ~bit), local)
        picks.append(source * 2 + local.astype(jnp.int32))
    far = jnp.where(upper, 0, last_frame)
    sums = [jnp.where(frame == far, len(dyns) + 1, place_of(frame, dyns)) for frame in mem_ids + pair_ids]
    owned = []
    for group in (me, me ^ 1):
        for j in range(FR_DEV):
            frame = group * FR_DEV + j
            place = place_of(frame, dyns)
            named = jnp.logical_or(place < len(dyns), jnp.logical_or(frame == 0, frame == last_frame))
            owned.append(place * 2 + named.astype(jnp.int32))
    lanes = codes_ref.shape[1]
    for row, code in ((PICK, pack(picks, PLACE_BITS)), (SUM, pack(sums, PLACE_BITS)), (OWNED, pack(owned, PLACE_BITS))):
        codes_ref[row : row + 1, :] = jnp.full((1, lanes), code, jnp.int32)


def split_kernel(peers, bank_ref, mine_ref, pair_ref, out_ref):
    me = lax.axis_index("tm")
    frame_len, half_width = out_ref.shape[2:]
    dyns = dyn_frames(bank_of(bank_ref), peers * FR_DEV - 1)
    places = [(has_dyn(me, dyn, 0), dyn % FR_DEV) for dyn in dyns]
    places.append((has_end(me, 0, peers), jnp.where(me < peers // 2, 0, FR_DEV - 1)))
    for j, (local, frame) in enumerate(places):
        for role in range(2):
            for source, taken in ((mine_ref, local), (pair_ref, jnp.logical_not(local))):

                @pl.when(jnp.logical_and((me & 1) == role, taken))
                def _(source=source, j=j, frame=frame, role=role):
                    for kind in range(2):
                        start = pl.multiple_of((kind * FR_DEV + frame) * frame_len, frame_len)
                        out_ref[j, kind] = source[pl.ds(start, frame_len), role * half_width : (role + 1) * half_width]


def step_kernel(peers, even_done, odd_done, bank_ref, mine_ref, got_ref, out_ref):
    me = lax.axis_index("tm")
    done = by_role(me, even_done, odd_done)
    dyns = dyn_frames(bank_of(bank_ref), peers * FR_DEV - 1)
    flags = [has_dyn(me, dyn, done) for dyn in dyns] + [has_end(me, done, peers)]
    for j, flag in enumerate(flags):
        choose(out_ref.at[j], flag, mine_ref.at[j], got_ref.at[j])


def pick_kernel(codes_ref, mine_ref, got_ref, own_out, pair_out):
    code = code_of(codes_ref, PICK)
    for o, out in enumerate((own_out, pair_out)):
        for m in range(MEM):
            pick = field(code, o * MEM + m, PLACE_BITS)
            source = pick >> 1
            choose(out.at[m], (pick & 1) != 0, mine_ref.at[source], got_ref.at[source])


def dot(a, b, left, right):
    return lax.dot_general(a, b, (((left,), (right,)), ((), ())), preferred_element_type=F32)


def logits_of(keys, query, rows_ref, head, piece):
    frame_len = query.shape[0] // FR_DEV
    raw = dot(keys, query, 1, 1) * (FACTOR * LOG2E)
    parts = []
    for j in range(FR_DEV):
        row = piece * FR_DEV + j
        parts.append(raw[j * frame_len : (j + 1) * frame_len] + rows_ref[head, row : row + 1, :])
    return jnp.concatenate(parts, axis=0)


def joined_parts(joined_ref, cols):
    rows = joined_ref.shape[0] // 2 // DEPTH * DEPTH
    return joined_ref[0:rows, cols], joined_ref[rows : 2 * rows, cols]


def head_cols(head):
    return pl.ds(head * DEPTH, DEPTH)


def part_of(logits, slopes):
    peak = jnp.max(logits, axis=0, keepdims=True)
    exps = jnp.exp2(logits - peak)
    return peak, jnp.sum(exps, axis=0, keepdims=True), jnp.sum(exps * slopes, axis=0, keepdims=True)


def merged(left, right):
    peak = jnp.maximum(left[0], right[0])
    scales = [jnp.exp2(part[0] - peak) for part in (left, right)]
    return peak, *(left[j] * scales[0] + right[j] * scales[1] for j in (1, 2))


def load_part(ref, head):
    return tuple(ref[head, j : j + 1, :] for j in range(3))


def store_part(ref, head, part):
    for j, row in enumerate(part):
        ref[head, j : j + 1, :] = row


def prev_parts(peers, direct_keys, relayed_keys, outer_values, pair_ref, cols):
    even = (lax.axis_index("tm") & 1) == 0
    keys = jnp.where(through_relay(1, 1, peers), relayed_keys[:, cols], direct_keys[:, cols])
    parts = zip((keys, outer_values[:, cols]), joined_parts(pair_ref, cols))
    return tuple(jnp.where(even, outer, pair) for outer, pair in parts)


def stats_kernel(
    peers,
    rows_ref,
    queries_ref,
    direct_keys,
    relayed_keys,
    outer_values,
    pair_ref,
    own_ref,
    part_ref,
    queries_out,
):
    heads = queries_ref.shape[1] // DEPTH
    queries_out[...] = queries_ref[...]

    def products(head):
        cols = head_cols(head)
        query, cotangent = joined_parts(queries_ref, cols)
        pieces = ((PREV, prev_parts(peers, direct_keys, relayed_keys, outer_values, pair_ref, cols)), (OWN, joined_parts(own_ref, cols)))
        return [
            (logits_of(keys, query, rows_ref, head, piece), dot(values, cotangent, 1, 1))
            for piece, (keys, values) in pieces
        ]

    ahead = products(0)
    for head in range(heads):
        now = ahead
        if head + 1 < heads:
            ahead = products(head + 1)
        store_part(part_ref, head, merged(*(part_of(*piece) for piece in now)))


def rounded(part, logits, slopes):
    peak, total, spread = merged(part, part_of(logits, slopes))
    inverse = 1.0 / total
    stats = peak, inverse, spread * inverse
    return stats, *weights_of(stats, logits, slopes)


def weights_of(stats, logits, slopes):
    peak, inverse, spread = stats
    probs = jnp.exp2(logits - peak) * inverse
    return probs.astype(BF16), (probs * (slopes - spread)).astype(BF16)


def memory_kernel(
    codes_ref, rows_ref, part_ref, pair_part_ref, own_queries, pair_queries, own_mem, pair_mem, keep_ref, send_ref
):
    role = lax.axis_index("tm") & 1
    code = code_of(codes_ref, SUM)
    frame_len, half_width = own_mem.shape[2:]
    half = half_width // DEPTH
    groups = ((own_queries, own_mem, part_ref, MEMORY), (pair_queries, pair_mem, pair_part_ref, PAIR))
    work = [(g, local) for local in range(half) for g in range(len(groups))]
    keep_ref[...] = jnp.zeros(keep_ref.shape, F32)

    def operands(g, local):
        cols = pl.ds(pl.multiple_of((role * half + local) * DEPTH, DEPTH), DEPTH)
        return joined_parts(groups[g][0], cols)

    def products(g, local):
        _, mem, _, piece = groups[g]
        query, cotangent = operands(g, local)
        keys, values = (mem[:, kind, :, head_cols(local)].reshape(MEM * frame_len, DEPTH) for kind in range(2))
        return logits_of(keys, query, rows_ref, role * half + local, piece), dot(values, cotangent, 1, 1)

    def add(g, local, _, weights, dlogits):
        query, cotangent = operands(g, local)
        terms = (dot(dlogits, query, 1, 0) * FACTOR, dot(weights, cotangent, 1, 0))
        for m in range(MEM):
            place = field(code, g * MEM + m, PLACE_BITS)
            for kind, term in enumerate(terms):
                part = term[m * frame_len : (m + 1) * frame_len].astype(BF16).astype(F32)
                keep_ref[place, kind, :, head_cols(local)] += part

    ahead = products(*work[0])
    behind = None
    for j, (g, local) in enumerate(work):
        now = ahead
        if j + 1 < len(work):
            ahead = products(*work[j + 1])
        if behind is not None:
            add(*work[j - 1], *behind)
        behind = rounded(load_part(groups[g][2], role * half + local), *now)
    add(*work[-1], *behind)
    kept = send_ref.shape[0]
    for place in range(kept):
        send_ref[place] = keep_ref[place if place + 1 < kept else kept].astype(BF16)


def next_kernel(rows_ref, stats_ref, pair_queries, outer_queries, own_ref, term_ref, sum_ref):
    even = (lax.axis_index("tm") & 1) == 0
    heads = pair_queries.shape[1] // DEPTH

    def operands(head):
        cols = head_cols(head)
        both = zip(joined_parts(pair_queries, cols), joined_parts(outer_queries, cols))
        return [jnp.where(even, a, b) for a, b in both]

    def products(head):
        query, cotangent = operands(head)
        keys, values = joined_parts(own_ref, head_cols(head))
        return logits_of(keys, query, rows_ref, head, NEXT), dot(values, cotangent, 1, 1)

    ahead = products(0)
    for head in range(heads):
        now = ahead
        if head + 1 < heads:
            ahead = products(head + 1)
        weights, dlogits = weights_of(load_part(stats_ref, head), *now)
        query, cotangent = operands(head)
        cols = head_cols(head)
        sum_ref[0, :, cols] = term_ref[0, :, cols] + dot(dlogits, query, 1, 0) * FACTOR
        sum_ref[1, :, cols] = term_ref[1, :, cols] + dot(weights, cotangent, 1, 0)


def rest_kernel(
    peers,
    rows_ref,
    part_ref,
    queries_ref,
    direct_keys,
    relayed_keys,
    outer_values,
    pair_ref,
    own_ref,
    own_mem,
    other_mem,
    attended_ref,
    grad_query_ref,
    term_ref,
    stats_ref,
):
    role = lax.axis_index("tm") & 1
    frame_len, half_width = own_mem.shape[2:]
    heads = queries_ref.shape[1] // DEPTH
    half = half_width // DEPTH

    def pieces(head):
        cols = head_cols(head % half)
        prev = prev_parts(peers, direct_keys, relayed_keys, outer_values, pair_ref, head_cols(head))
        memory = [
            jnp.where(role == head // half, own_mem[:, kind, :, cols], other_mem[:, kind, :, cols]).reshape(
                MEM * frame_len, DEPTH
            )
            for kind in range(2)
        ]
        return (PREV, prev), (OWN, joined_parts(own_ref, head_cols(head))), (MEMORY, memory)

    def products(head):
        query, cotangent = joined_parts(queries_ref, head_cols(head))
        return [
            (logits_of(keys, query, rows_ref, head, piece), dot(values, cotangent, 1, 1))
            for piece, (keys, values) in pieces(head)
        ]

    ahead = products(0)
    for head in range(heads):
        now = ahead
        if head + 1 < heads:
            ahead = products(head + 1)
        cols = head_cols(head)
        query, cotangent = joined_parts(queries_ref, cols)
        stats, *last = rounded(load_part(part_ref, head), *now[-1])
        store_part(stats_ref, head, stats)
        rounds = [weights_of(stats, *now[PREV]), weights_of(stats, *now[OWN]), last]
        attended = grad_query = 0.0
        for (piece, (keys, values)), (weights, dlogits) in zip(pieces(head), rounds):
            attended += dot(values, weights, 0, 0)
            grad_query += dot(keys, dlogits, 0, 0)
            if piece == OWN:
                term_ref[0, :, cols] = dot(dlogits, query, 1, 0) * FACTOR
                term_ref[1, :, cols] = dot(weights, cotangent, 1, 0)
        attended_ref[:, cols] = attended.T.astype(BF16)
        grad_query_ref[:, cols] = (grad_query * FACTOR).T.astype(BF16)


def add_kernel(keep_ref, got_ref, out_ref, send_ref):
    value = keep_ref[0 : got_ref.shape[0]] + got_ref[...].astype(F32)
    out_ref[...] = value
    send_ref[...] = value.astype(BF16)


def owned_kernel(codes_ref, keep_ref, got_ref, mine_ref, pair_ref):
    code = code_of(codes_ref, OWNED)
    for o, out in enumerate((mine_ref, pair_ref)):
        for j in range(FR_DEV):
            owned = field(code, o * FR_DEV + j, PLACE_BITS)
            place = owned >> 1
            named = (owned & 1) != 0

            @pl.when(named)
            def _(out=out, j=j, place=place):
                value = keep_ref[place] + got_ref[place].astype(F32)
                out[j] = value.astype(out.dtype)

            @pl.when(jnp.logical_not(named))
            def _(out=out, j=j):
                out[j] = jnp.zeros(out.shape[1:], out.dtype)


def final_kernel(own_ref, mine_ref, got_ref, grad_key_ref, grad_value_ref):
    role = lax.axis_index("tm") & 1
    frame_len, half_width = mine_ref.shape[2:]
    for kind, out in enumerate((grad_key_ref, grad_value_ref)):
        for j in range(FR_DEV):
            rows = pl.ds(j * frame_len, frame_len)
            for half in range(2):
                cols = pl.ds(half * half_width, half_width)
                bank = jnp.where(role == half, mine_ref[j, kind], got_ref[j, kind].astype(F32))
                out[rows, cols] = (own_ref[kind, rows, cols] + bank).astype(BF16)


def body(
    query_states,
    key_states,
    value_states,
    grad_out,
    camera_pose,
    pose_bias,
    memory_index,
    bank_frames,
):
    row_count, width = query_states.shape
    frame_len = row_count // FR_DEV
    heads = pose_bias.shape[0]
    slots = bank_frames.shape[0]
    peers = lax.axis_size("tm")
    bits = [1 << i for i in range(1, peers.bit_length() - 1)]
    turns = list(zip(bits, bits[::-1]))
    piece_flops = 2 * row_count * row_count * width
    bank_frames = bank_frames.reshape(1, slots)
    last_bits = turns[-1]

    def join(kernel, rows, arrays, scratch, name, after=()):
        def run(*refs):
            kernel(*refs[: len(arrays)], *refs[len(arrays) + len(after) :])

        return pl.pallas_call(
            run,
            out_shape=shape(BF16, rows, width),
            in_specs=[pl.BlockSpec(memory_space=pltpu.HBM)] * len(arrays) + [ANY] * len(after),
            out_specs=VMEM,
            scratch_shapes=[*scratch, pltpu.SemaphoreType.DMA((len(arrays),))],
            compiler_params=pltpu.CompilerParams(vmem_limit_bytes=VMEM_LIMIT),
            name=name,
        )(*(pltpu.with_memory_space_constraint(array, pltpu.HBM) for array in arrays), *after)

    joined = join(
        join_kernel,
        2 * row_count + TAIL,
        [memory_index, key_states, value_states],
        [pltpu.VMEM(memory_index.shape, jnp.int32)],
        "join",
    )
    half_width = width // 2
    direct_keys = shift_first(key_states, 1, 1, peers)
    pair = swap(joined, 1, 1, peers)
    held = shape(BF16, slots - 1, 2, frame_len, half_width)
    sums = shape(F32, slots - 1, 2, frame_len, half_width)
    (mine,) = call(functools.partial(split_kernel, peers), [held], [bank_frames, joined, pair], name="split")
    queries = join(join_queries_kernel, 2 * row_count, [query_states, grad_out], [], "join_queries", after=[mine])
    pair_queries = swap(queries, 1, 1, peers)

    bias_rows = -(-(5 * FR_DEV) // 8) * 8
    rows, codes, values_out, keys_out = call(
        functools.partial(plan_kernel, peers, last_bits),
        [shape(F32, heads, bias_rows, row_count), shape(jnp.int32, 8, 128)] + [shape(BF16, row_count, width)] * 2,
        [pair, joined, direct_keys],
        scalars=[bank_frames, memory_index, camera_pose, pose_bias],
        flops=HIDING * piece_flops,
        name="plan",
    )
    outer = [direct_keys, shift_second(keys_out, 1, 1, peers), shift(values_out, 1, 1, peers)]
    even_done = odd_done = 1
    for step, (even_bit, odd_bit) in enumerate(turns):
        got = swap(mine, even_bit, odd_bit, peers)
        if step + 1 < len(turns):
            kernel = functools.partial(step_kernel, peers, even_done, odd_done)
            after = [codes, pair_queries]
            (mine,) = call(kernel, [held], [bank_frames, mine, got], after=after, name="step")
        even_done |= even_bit
        odd_done |= odd_bit

    stats = shape(F32, heads, 8, row_count)
    part, queries_out = call(
        functools.partial(stats_kernel, peers),
        [stats, shape(BF16, 2 * row_count, width)],
        [rows, queries, *outer, pair, joined],
        flops=HIDING * piece_flops,
        name="stats",
    )
    pair_part = swap(part, 1, 1, peers)
    next_queries = shift(queries_out, -1, 2, peers)
    chosen = shape(BF16, MEM, 2, frame_len, half_width)
    own_mem, pair_mem = call(pick_kernel, [chosen] * 2, [codes, mine, got], name="pick")
    keep, send = call(
        memory_kernel,
        [shape(F32, slots, 2, frame_len, half_width), held],
        [codes, rows, part, pair_part, queries, pair_queries, own_mem, pair_mem],
        flops=HIDING * piece_flops,
        name="memory",
    )
    other_mem = swap(pair_mem, 1, 1, peers)
    pair_sums = shape(F32, 2, row_count, width)
    attended, grad_query, own_terms, stats_all = call(
        functools.partial(rest_kernel, peers),
        [shape(BF16, row_count, width)] * 2 + [pair_sums, stats],
        [rows, part, queries, *outer, pair, joined, own_mem, other_mem],
        after=[send],
        flops=HIDING * piece_flops,
        name="rest",
    )
    next_stats = lax.ppermute(stats_all, "tm", [(i, i - 1) for i in range(1, peers)])
    (own,) = call(
        next_kernel,
        [pair_sums],
        [rows, next_stats, pair_queries, next_queries, joined, own_terms],
        flops=HIDING * piece_flops,
        name="next",
    )
    for step, (even_bit, odd_bit) in enumerate(turns[::-1]):
        got = swap(send, even_bit, odd_bit, peers)
        if step + 1 < len(turns):
            after = [own_terms, next_queries]
            keep, send = call(add_kernel, [sums, held], [keep, got], after=after, name="add")
    owned_mine, owned_send = call(
        owned_kernel,
        [shape(F32, FR_DEV, 2, frame_len, half_width), shape(BF16, FR_DEV, 2, frame_len, half_width)],
        [codes, keep, got],
        after=[own],
        name="owned",
    )
    owned_got = swap(owned_send, 1, 1, peers)
    grad_key, grad_value = call(
        final_kernel, [shape(BF16, row_count, width)] * 2, [own, owned_mine, owned_got], name="final"
    )
    return (attended, grad_query, grad_key, grad_value)


def solution(mesh):
    rows = P(("traj", "tm"), None)
    in_specs = (rows, rows, rows, rows, P("traj"), P(), rows, P("traj"))
    return jax.shard_map(body, mesh=mesh, in_specs=in_specs, out_specs=(rows,) * 4, check_vma=False)
```

```python
import functools
import math

import jax
import jax.numpy as jnp
from jax import lax
from jax.experimental import pallas as pl
from jax.experimental.pallas import tpu as pltpu
from jax.sharding import PartitionSpec as P

FR_DEV = 2
MEM = 2
DEPTH = 128
TAIL = 16

BLOCKED_LOGIT = -1e30
LOG2E = math.log2(math.e)
FACTOR = 1.0 / math.sqrt(DEPTH)

SMEM = pl.BlockSpec(memory_space=pltpu.SMEM)
VMEM = pl.BlockSpec(memory_space=pltpu.VMEM)
ANY = pl.BlockSpec(memory_space=pl.ANY)
HIDING = 200
VMEM_LIMIT = 16 * 1024 * 1024
BF16, F32 = jnp.bfloat16, jnp.float32


def shape(dtype, *dims):
    return jax.ShapeDtypeStruct(dims, dtype)


def call(kernel, outs, arrays, scalars=(), after=(), flops=0, name=None):
    count = len(scalars) + len(arrays)

    def run(*refs):
        kernel(*refs[:count], *refs[count + len(after) :])

    return pl.pallas_call(
        run,
        out_shape=outs,
        in_specs=[SMEM] * len(scalars) + [VMEM] * len(arrays) + [ANY] * len(after),
        out_specs=[VMEM] * len(outs),
        compiler_params=pltpu.CompilerParams(vmem_limit_bytes=VMEM_LIMIT),
        cost_estimate=pl.CostEstimate(flops=flops, bytes_accessed=0, transcendentals=0) if flops else None,
        name=name,
    )(*scalars, *arrays, *after)


def swap(block, even_bit, odd_bit, peers):
    return lax.ppermute(block, "tm", [(i, i ^ (odd_bit if i & 1 else even_bit)) for i in range(peers)])


def shift(block, by, start, peers):
    pairs = [(i, i + by) for i in range(start, peers, 2) if 0 <= i + by < peers]
    return lax.ppermute(block, "tm", pairs)


def relays_of(by, start, peers):
    pairs = [(i, i + by) for i in range(start, peers, 2) if 0 <= i + by < peers]
    return {(i, j): i ^ 4 for i, j in pairs if peers == 8 and (i ^ j) >> 1 == 3}


def shift_first(block, by, start, peers):
    relays = relays_of(by, start, peers)
    pairs = [(i, i + by) for i in range(start, peers, 2) if 0 <= i + by < peers]
    return lax.ppermute(block, "tm", [(i, relays.get((i, j), j)) for i, j in pairs])


def shift_second(block, by, start, peers):
    pairs = [(relay, j) for (_, j), relay in relays_of(by, start, peers).items()]
    return lax.ppermute(block, "tm", pairs) if pairs else block


def through_relay(by, start, peers):
    me = lax.axis_index("tm")
    return functools.reduce(jnp.logical_or, [me == j for _, j in relays_of(by, start, peers)], me < 0)


def lane_value(row, lane):
    lanes = lax.broadcasted_iota(jnp.int32, row.shape, 1)
    return jnp.max(jnp.where(lanes == lane, row, 0))


def bank_of(bank_ref):
    row = bank_ref[...]
    return [lane_value(row, slot) for slot in range(row.shape[1])]


def dyn_frames(bank, last_frame):
    found = [jnp.int32(0)] * (len(bank) - 2)
    seen = jnp.int32(0)
    for frame in bank:
        free = jnp.logical_and(frame != 0, frame != last_frame)
        for j in range(len(found)):
            found[j] = jnp.where(jnp.logical_and(free, seen == j), frame, found[j])
        seen = seen + free.astype(jnp.int32)
    return found


def place_of(frame, dyns):
    place = jnp.int32(len(dyns))
    for j, dyn in enumerate(dyns):
        place = jnp.where(frame == dyn, j, place)
    return place


def choose(out, take_first, first, second):
    @pl.when(take_first)
    def _():
        out[...] = first[...]

    @pl.when(jnp.logical_not(take_first))
    def _():
        out[...] = second[...]


def has_end(me, done, peers):
    return jnp.logical_or((me & ~done) == 0, (me | done) == peers - 1)


def has_dyn(me, frame, done):
    return ((me ^ (frame // FR_DEV)) & ~done) == 0


def by_role(me, even_value, odd_value):
    return jnp.where((me & 1) == 0, even_value, odd_value)


def join_kernel(index_ref, key_ref, value_ref, joined_ref, index_buf, sems):
    rows = key_ref.shape[0]
    copies = [
        pltpu.make_async_copy(index_ref, index_buf, sems.at[0]),
        pltpu.make_async_copy(key_ref, joined_ref.at[pl.ds(0, rows)], sems.at[1]),
        pltpu.make_async_copy(value_ref, joined_ref.at[pl.ds(rows, rows)], sems.at[2]),
    ]
    for copy in copies:
        copy.start()
    copies[0].wait()
    width = joined_ref.shape[1]
    lane = lax.broadcasted_iota(jnp.int32, (TAIL, width), 1) // DEPTH
    tail = jnp.zeros((TAIL, width), jnp.int32)
    for m in range(MEM):
        tail = jnp.where(lane == m, index_buf[0:1, m : m + 1], tail)
    joined_ref[2 * rows : 2 * rows + TAIL, :] = tail.astype(F32).astype(BF16)
    copies[1].wait()
    copies[2].wait()


def join_queries_kernel(query_ref, cotangent_ref, joined_ref, sems):
    rows = query_ref.shape[0]
    copies = [
        pltpu.make_async_copy(ref, joined_ref.at[pl.ds(j * rows, rows)], sems.at[j])
        for j, ref in enumerate((query_ref, cotangent_ref))
    ]
    for copy in copies:
        copy.start()
    for copy in copies:
        copy.wait()


def pack(fields, width):
    code = jnp.int32(0)
    for j, field in enumerate(fields):
        code = code | (field.astype(jnp.int32) << (j * width))
    return code


def field(code, j, width):
    return (code >> (j * width)) & ((1 << width) - 1)


def code_of(codes_ref, row):
    return jnp.max(codes_ref[row : row + 1, :])


PICK, SUM, OWNED = range(3)
PLACE_BITS = 4
PREV, OWN, MEMORY, NEXT, PAIR = range(5)


def plan_kernel(
    peers,
    last_bits,
    bank_ref,
    index_ref,
    pose_ref,
    bias_ref,
    pair_ref,
    joined_ref,
    direct_keys,
    rows_ref,
    codes_ref,
    values_out,
    keys_out,
):
    me = lax.axis_index("tm")
    last_frame = peers * FR_DEV - 1
    heads, _, row_count = rows_ref.shape
    values_out[...] = joined_ref[row_count : 2 * row_count, :]
    keys_out[...] = direct_keys[...]
    bank = [bank_ref[0, slot] for slot in range(bank_ref.shape[1])]
    tail = pair_ref.shape[0] - TAIL
    pair_ids = []
    for m in range(MEM):
        slot = jnp.max(pair_ref[tail : tail + TAIL, m * DEPTH : (m + 1) * DEPTH].astype(F32)).astype(jnp.int32)
        pair_ids.append(bank_ref[0, slot])
    mem_ids = [bank_ref[0, index_ref[0, m]] for m in range(MEM)]

    own_ids = [me * FR_DEV + j for j in range(FR_DEV)]
    prev_ids = [jnp.maximum(own - FR_DEV, 0) for own in own_ids]
    next_ids = [jnp.minimum(own + FR_DEV, last_frame) for own in own_ids]
    pair_own_ids = [(me ^ 1) * FR_DEV + j for j in range(FR_DEV)]
    pieces = ((prev_ids, own_ids), (own_ids, own_ids), (mem_ids, own_ids), (own_ids, next_ids), (pair_ids, pair_own_ids))
    poses = [([pose_ref[f] for f in key_ids], [pose_ref[f] for f in query_ids]) for key_ids, query_ids in pieces]
    frame_of = lax.broadcasted_iota(jnp.int32, (1, row_count), 1) // (row_count // FR_DEV)
    for head in range(heads):
        for piece, (key_poses, query_poses) in enumerate(poses):
            for j, key_pose in enumerate(key_poses):
                row = jnp.zeros((1, row_count), F32)
                for a, query_pose in enumerate(query_poses):
                    value = bias_ref[head, query_pose, key_pose] * LOG2E
                    if piece == PREV:
                        value = jnp.where(me == 0, BLOCKED_LOGIT, value)
                    row = jnp.where(frame_of == a, value, row)
                rows_ref[head, piece * FR_DEV + j : piece * FR_DEV + j + 1, :] = row

    dyns = dyn_frames(bank, last_frame)
    bit = by_role(me, *last_bits)
    upper = (me & bit) != 0
    picks = []
    for frame in mem_ids + pair_ids:
        source = place_of(frame, dyns)
        local = jnp.where(frame == 0, jnp.logical_not(upper), upper)
        local = jnp.where(source < len(dyns), has_dyn(me, frame, (peers - 1) & ~bit), local)
        picks.append(source * 2 + local.astype(jnp.int32))
    far = jnp.where(upper, 0, last_frame)
    sums = [jnp.where(frame == far, len(dyns) + 1, place_of(frame, dyns)) for frame in mem_ids + pair_ids]
    owned = []
    for group in (me, me ^ 1):
        for j in range(FR_DEV):
            frame = group * FR_DEV + j
            place = place_of(frame, dyns)
            named = jnp.logical_or(place < len(dyns), jnp.logical_or(frame == 0, frame == last_frame))
            owned.append(place * 2 + named.astype(jnp.int32))
    lanes = codes_ref.shape[1]
    for row, code in ((PICK, pack(picks, PLACE_BITS)), (SUM, pack(sums, PLACE_BITS)), (OWNED, pack(owned, PLACE_BITS))):
        codes_ref[row : row + 1, :] = jnp.full((1, lanes), code, jnp.int32)


def split_kernel(peers, bank_ref, mine_ref, pair_ref, out_ref):
    me = lax.axis_index("tm")
    frame_len, half_width = out_ref.shape[2:]
    dyns = dyn_frames(bank_of(bank_ref), peers * FR_DEV - 1)
    places = [(has_dyn(me, dyn, 0), dyn % FR_DEV) for dyn in dyns]
    places.append((has_end(me, 0, peers), jnp.where(me < peers // 2, 0, FR_DEV - 1)))
    for j, (local, frame) in enumerate(places):
        for role in range(2):
            for source, taken in ((mine_ref, local), (pair_ref, jnp.logical_not(local))):

                @pl.when(jnp.logical_and((me & 1) == role, taken))
                def _(source=source, j=j, frame=frame, role=role):
                    for kind in range(2):
                        start = pl.multiple_of((kind * FR_DEV + frame) * frame_len, frame_len)
                        out_ref[j, kind] = source[pl.ds(start, frame_len), role * half_width : (role + 1) * half_width]


def step_kernel(peers, even_done, odd_done, bank_ref, mine_ref, got_ref, out_ref):
    me = lax.axis_index("tm")
    done = by_role(me, even_done, odd_done)
    dyns = dyn_frames(bank_of(bank_ref), peers * FR_DEV - 1)
    flags = [has_dyn(me, dyn, done) for dyn in dyns] + [has_end(me, done, peers)]
    for j, flag in enumerate(flags):
        choose(out_ref.at[j], flag, mine_ref.at[j], got_ref.at[j])


def pick_kernel(codes_ref, mine_ref, got_ref, own_out, pair_out):
    code = code_of(codes_ref, PICK)
    for o, out in enumerate((own_out, pair_out)):
        for m in range(MEM):
            pick = field(code, o * MEM + m, PLACE_BITS)
            source = pick >> 1
            choose(out.at[m], (pick & 1) != 0, mine_ref.at[source], got_ref.at[source])


def dot(a, b, left, right):
    return lax.dot_general(a, b, (((left,), (right,)), ((), ())), preferred_element_type=F32)


def logits_of(keys, query, rows_ref, head, piece):
    frame_len = query.shape[0] // FR_DEV
    raw = dot(keys, query, 1, 1) * (FACTOR * LOG2E)
    parts = []
    for j in range(FR_DEV):
        row = piece * FR_DEV + j
        parts.append(raw[j * frame_len : (j + 1) * frame_len] + rows_ref[head, row : row + 1, :])
    return jnp.concatenate(parts, axis=0)


def joined_parts(joined_ref, cols):
    rows = joined_ref.shape[0] // 2 // DEPTH * DEPTH
    return joined_ref[0:rows, cols], joined_ref[rows : 2 * rows, cols]


def head_cols(head):
    return pl.ds(head * DEPTH, DEPTH)


def part_of(logits, slopes):
    peak = jnp.max(logits, axis=0, keepdims=True)
    exps = jnp.exp2(logits - peak)
    return peak, jnp.sum(exps, axis=0, keepdims=True), jnp.sum(exps * slopes, axis=0, keepdims=True)


def merged(left, right):
    peak = jnp.maximum(left[0], right[0])
    scales = [jnp.exp2(part[0] - peak) for part in (left, right)]
    return peak, *(left[j] * scales[0] + right[j] * scales[1] for j in (1, 2))


def load_part(ref, head):
    return tuple(ref[head, j : j + 1, :] for j in range(3))


def store_part(ref, head, part):
    for j, row in enumerate(part):
        ref[head, j : j + 1, :] = row


def prev_parts(peers, direct_keys, relayed_keys, outer_values, pair_ref, cols):
    even = (lax.axis_index("tm") & 1) == 0
    keys = jnp.where(through_relay(1, 1, peers), relayed_keys[:, cols], direct_keys[:, cols])
    parts = zip((keys, outer_values[:, cols]), joined_parts(pair_ref, cols))
    return tuple(jnp.where(even, outer, pair) for outer, pair in parts)


def stats_kernel(
    peers,
    rows_ref,
    queries_ref,
    direct_keys,
    relayed_keys,
    outer_values,
    pair_ref,
    own_ref,
    part_ref,
    queries_out,
    cotangent_out,
):
    heads = queries_ref.shape[1] // DEPTH
    rows = queries_out.shape[0]
    queries_out[...] = queries_ref[0:rows]
    cotangent_out[...] = queries_ref[rows : 2 * rows]

    def products(head):
        cols = head_cols(head)
        query, cotangent = joined_parts(queries_ref, cols)
        pieces = ((PREV, prev_parts(peers, direct_keys, relayed_keys, outer_values, pair_ref, cols)), (OWN, joined_parts(own_ref, cols)))
        return [
            (logits_of(keys, query, rows_ref, head, piece), dot(values, cotangent, 1, 1))
            for piece, (keys, values) in pieces
        ]

    ahead = products(0)
    for head in range(heads):
        now = ahead
        if head + 1 < heads:
            ahead = products(head + 1)
        store_part(part_ref, head, merged(*(part_of(*piece) for piece in now)))


def rounded(part, logits, slopes):
    peak, total, spread = merged(part, part_of(logits, slopes))
    inverse = 1.0 / total
    stats = peak, inverse, spread * inverse
    return stats, *weights_of(stats, logits, slopes)


def weights_of(stats, logits, slopes):
    peak, inverse, spread = stats
    probs = jnp.exp2(logits - peak) * inverse
    return probs.astype(BF16), (probs * (slopes - spread)).astype(BF16)


def memory_kernel(
    codes_ref, rows_ref, part_ref, pair_part_ref, own_queries, pair_queries, own_mem, pair_mem, keep_ref, send_ref
):
    role = lax.axis_index("tm") & 1
    code = code_of(codes_ref, SUM)
    frame_len, half_width = own_mem.shape[2:]
    half = half_width // DEPTH
    groups = ((own_queries, own_mem, part_ref, MEMORY), (pair_queries, pair_mem, pair_part_ref, PAIR))
    work = [(g, local) for local in range(half) for g in range(len(groups))]
    keep_ref[...] = jnp.zeros(keep_ref.shape, F32)

    def operands(g, local):
        cols = pl.ds(pl.multiple_of((role * half + local) * DEPTH, DEPTH), DEPTH)
        return joined_parts(groups[g][0], cols)

    def products(g, local):
        _, mem, _, piece = groups[g]
        query, cotangent = operands(g, local)
        keys, values = (mem[:, kind, :, head_cols(local)].reshape(MEM * frame_len, DEPTH) for kind in range(2))
        return logits_of(keys, query, rows_ref, role * half + local, piece), dot(values, cotangent, 1, 1)

    def add(g, local, _, weights, dlogits):
        query, cotangent = operands(g, local)
        terms = (dot(dlogits, query, 1, 0) * FACTOR, dot(weights, cotangent, 1, 0))
        for m in range(MEM):
            place = field(code, g * MEM + m, PLACE_BITS)
            for kind, term in enumerate(terms):
                part = term[m * frame_len : (m + 1) * frame_len].astype(BF16).astype(F32)
                keep_ref[place, kind, :, head_cols(local)] += part

    ahead = products(*work[0])
    behind = None
    for j, (g, local) in enumerate(work):
        now = ahead
        if j + 1 < len(work):
            ahead = products(*work[j + 1])
        if behind is not None:
            add(*work[j - 1], *behind)
        behind = rounded(load_part(groups[g][2], role * half + local), *now)
    add(*work[-1], *behind)
    kept = send_ref.shape[0]
    for place in range(kept):
        send_ref[place] = keep_ref[place if place + 1 < kept else kept].astype(BF16)


def next_kernel(
    peers,
    rows_ref,
    stats_ref,
    pair_queries,
    outer_queries,
    direct_cotangent,
    relayed_cotangent,
    own_ref,
    term_ref,
    sum_ref,
):
    even = (lax.axis_index("tm") & 1) == 0
    relayed = through_relay(-1, 2, peers)
    heads = pair_queries.shape[1] // DEPTH

    def operands(head):
        cols = head_cols(head)
        cotangent = jnp.where(relayed, relayed_cotangent[:, cols], direct_cotangent[:, cols])
        outer = outer_queries[:, cols], cotangent
        return [jnp.where(even, a, b) for a, b in zip(joined_parts(pair_queries, cols), outer)]

    def products(head):
        query, cotangent = operands(head)
        keys, values = joined_parts(own_ref, head_cols(head))
        return logits_of(keys, query, rows_ref, head, NEXT), dot(values, cotangent, 1, 1)

    ahead = products(0)
    for head in range(heads):
        now = ahead
        if head + 1 < heads:
            ahead = products(head + 1)
        weights, dlogits = weights_of(load_part(stats_ref, head), *now)
        query, cotangent = operands(head)
        cols = head_cols(head)
        sum_ref[0, :, cols] = term_ref[0, :, cols] + dot(dlogits, query, 1, 0) * FACTOR
        sum_ref[1, :, cols] = term_ref[1, :, cols] + dot(weights, cotangent, 1, 0)


def memory_parts(own_mem, other_mem, head):
    role = lax.axis_index("tm") & 1
    frame_len, half_width = own_mem.shape[2:]
    half = half_width // DEPTH
    cols = head_cols(head % half)
    return [
        jnp.where(role == head // half, own_mem[:, kind, :, cols], other_mem[:, kind, :, cols]).reshape(
            MEM * frame_len, DEPTH
        )
        for kind in range(2)
    ]


def own_kernel(rows_ref, part_ref, queries_ref, own_ref, own_mem, other_mem, term_ref, stats_ref):
    heads = queries_ref.shape[1] // DEPTH

    def products(head):
        query, cotangent = joined_parts(queries_ref, head_cols(head))
        pieces = ((OWN, joined_parts(own_ref, head_cols(head))), (MEMORY, memory_parts(own_mem, other_mem, head)))
        return [
            (logits_of(keys, query, rows_ref, head, piece), dot(values, cotangent, 1, 1))
            for piece, (keys, values) in pieces
        ]

    ahead = products(0)
    for head in range(heads):
        own, memory = ahead
        if head + 1 < heads:
            ahead = products(head + 1)
        cols = head_cols(head)
        query, cotangent = joined_parts(queries_ref, cols)
        peak, total, spread = merged(load_part(part_ref, head), part_of(*memory))
        inverse = 1.0 / total
        stats = peak, inverse, spread * inverse
        store_part(stats_ref, head, stats)
        weights, dlogits = weights_of(stats, *own)
        term_ref[0, :, cols] = dot(dlogits, query, 1, 0) * FACTOR
        term_ref[1, :, cols] = dot(weights, cotangent, 1, 0)


def attend_kernel(
    peers,
    rows_ref,
    stats_ref,
    queries_ref,
    direct_keys,
    relayed_keys,
    outer_values,
    pair_ref,
    own_ref,
    own_mem,
    other_mem,
    attended_ref,
    grad_query_ref,
    mark_ref,
):
    mark_ref[...] = jnp.zeros(mark_ref.shape, F32)
    heads = queries_ref.shape[1] // DEPTH

    def pieces(head):
        cols = head_cols(head)
        prev = prev_parts(peers, direct_keys, relayed_keys, outer_values, pair_ref, cols)
        return (PREV, prev), (OWN, joined_parts(own_ref, cols)), (MEMORY, memory_parts(own_mem, other_mem, head))

    def products(head):
        query, cotangent = joined_parts(queries_ref, head_cols(head))
        return [
            (logits_of(keys, query, rows_ref, head, piece), dot(values, cotangent, 1, 1))
            for piece, (keys, values) in pieces(head)
        ]

    ahead = products(0)
    for head in range(heads):
        now = ahead
        if head + 1 < heads:
            ahead = products(head + 1)
        cols = head_cols(head)
        stats = load_part(stats_ref, head)
        attended = grad_query = 0.0
        for (_, (keys, values)), piece in zip(pieces(head), now):
            weights, dlogits = weights_of(stats, *piece)
            attended += dot(values, weights, 0, 0)
            grad_query += dot(keys, dlogits, 0, 0)
        attended_ref[:, cols] = attended.T.astype(BF16)
        grad_query_ref[:, cols] = (grad_query * FACTOR).T.astype(BF16)


def add_kernel(keep_ref, got_ref, out_ref, send_ref):
    value = keep_ref[0 : got_ref.shape[0]] + got_ref[...].astype(F32)
    out_ref[...] = value
    send_ref[...] = value.astype(BF16)


def pass_kernel(in_ref, out_ref):
    out_ref[...] = in_ref[...]


def owned_kernel(codes_ref, keep_ref, got_ref, mine_ref, pair_ref):
    code = code_of(codes_ref, OWNED)
    for o, out in enumerate((mine_ref, pair_ref)):
        for j in range(FR_DEV):
            owned = field(code, o * FR_DEV + j, PLACE_BITS)
            place = owned >> 1
            named = (owned & 1) != 0

            @pl.when(named)
            def _(out=out, j=j, place=place):
                value = keep_ref[place] + got_ref[place].astype(F32)
                out[j] = value.astype(out.dtype)

            @pl.when(jnp.logical_not(named))
            def _(out=out, j=j):
                out[j] = jnp.zeros(out.shape[1:], out.dtype)


def final_kernel(own_ref, mine_ref, got_ref, grad_key_ref, grad_value_ref):
    role = lax.axis_index("tm") & 1
    frame_len, half_width = mine_ref.shape[2:]
    for kind, out in enumerate((grad_key_ref, grad_value_ref)):
        for j in range(FR_DEV):
            rows = pl.ds(j * frame_len, frame_len)
            for half in range(2):
                cols = pl.ds(half * half_width, half_width)
                bank = jnp.where(role == half, mine_ref[j, kind], got_ref[j, kind].astype(F32))
                out[rows, cols] = (own_ref[kind, rows, cols] + bank).astype(BF16)


def body(
    query_states,
    key_states,
    value_states,
    grad_out,
    camera_pose,
    pose_bias,
    memory_index,
    bank_frames,
):
    row_count, width = query_states.shape
    frame_len = row_count // FR_DEV
    heads = pose_bias.shape[0]
    slots = bank_frames.shape[0]
    peers = lax.axis_size("tm")
    bits = [1 << i for i in range(1, peers.bit_length() - 1)]
    turns = list(zip(bits, bits[::-1]))
    piece_flops = 2 * row_count * row_count * width
    bank_frames = bank_frames.reshape(1, slots)
    last_bits = turns[-1]

    def join(kernel, rows, arrays, scratch, name, after=()):
        def run(*refs):
            kernel(*refs[: len(arrays)], *refs[len(arrays) + len(after) :])

        return pl.pallas_call(
            run,
            out_shape=shape(BF16, rows, width),
            in_specs=[pl.BlockSpec(memory_space=pltpu.HBM)] * len(arrays) + [ANY] * len(after),
            out_specs=VMEM,
            scratch_shapes=[*scratch, pltpu.SemaphoreType.DMA((len(arrays),))],
            compiler_params=pltpu.CompilerParams(vmem_limit_bytes=VMEM_LIMIT),
            name=name,
        )(*(pltpu.with_memory_space_constraint(array, pltpu.HBM) for array in arrays), *after)

    joined = join(
        join_kernel,
        2 * row_count + TAIL,
        [memory_index, key_states, value_states],
        [pltpu.VMEM(memory_index.shape, jnp.int32)],
        "join",
    )
    half_width = width // 2
    direct_keys = shift_first(key_states, 1, 1, peers)
    pair = swap(joined, 1, 1, peers)
    held = shape(BF16, slots - 1, 2, frame_len, half_width)
    sums = shape(F32, slots - 1, 2, frame_len, half_width)
    (mine,) = call(functools.partial(split_kernel, peers), [held], [bank_frames, joined, pair], name="split")
    queries = join(join_queries_kernel, 2 * row_count, [query_states, grad_out], [], "join_queries", after=[mine])
    pair_queries = swap(queries, 1, 1, peers)

    bias_rows = -(-(5 * FR_DEV) // 8) * 8
    rows, codes, values_out, keys_out = call(
        functools.partial(plan_kernel, peers, last_bits),
        [shape(F32, heads, bias_rows, row_count), shape(jnp.int32, 8, 128)] + [shape(BF16, row_count, width)] * 2,
        [pair, joined, direct_keys],
        scalars=[bank_frames, memory_index, camera_pose, pose_bias],
        flops=HIDING * piece_flops,
        name="plan",
    )
    outer = [direct_keys, shift_second(keys_out, 1, 1, peers), shift(values_out, 1, 1, peers)]
    even_done = odd_done = 1
    for step, (even_bit, odd_bit) in enumerate(turns):
        got = swap(mine, even_bit, odd_bit, peers)
        if step + 1 < len(turns):
            kernel = functools.partial(step_kernel, peers, even_done, odd_done)
            after = [codes, pair_queries]
            (mine,) = call(kernel, [held], [bank_frames, mine, got], after=after, name="step")
        even_done |= even_bit
        odd_done |= odd_bit

    stats = shape(F32, heads, 8, row_count)
    part, queries_out, cotangent_out = call(
        functools.partial(stats_kernel, peers),
        [stats] + [shape(BF16, row_count, width)] * 2,
        [rows, queries, *outer, pair, joined],
        flops=HIDING * piece_flops,
        name="stats",
    )
    pair_part = swap(part, 1, 1, peers)
    next_queries = shift(queries_out, -1, 2, peers)
    direct_cotangent = shift_first(cotangent_out, -1, 2, peers)
    chosen = shape(BF16, MEM, 2, frame_len, half_width)
    own_mem, pair_mem = call(pick_kernel, [chosen] * 2, [codes, mine, got], name="pick")
    keep, send = call(
        memory_kernel,
        [shape(F32, slots, 2, frame_len, half_width), held],
        [codes, rows, part, pair_part, queries, pair_queries, own_mem, pair_mem],
        flops=HIDING * piece_flops,
        name="memory",
    )
    other_mem = swap(pair_mem, 1, 1, peers)
    pair_sums = shape(F32, 2, row_count, width)
    own_terms, stats_all = call(
        own_kernel,
        [pair_sums, stats],
        [rows, part, queries, joined, own_mem, other_mem],
        after=[send],
        flops=HIDING * piece_flops,
        name="own",
    )
    next_stats = lax.ppermute(stats_all, "tm", [(i, i - 1) for i in range(1, peers)])
    (passed_on,) = call(
        pass_kernel, [shape(BF16, row_count, width)], [direct_cotangent], after=[own_terms], name="pass_on"
    )
    relayed_cotangent = shift_second(passed_on, -1, 2, peers)
    (own,) = call(
        functools.partial(next_kernel, peers),
        [pair_sums],
        [rows, next_stats, pair_queries, next_queries, direct_cotangent, relayed_cotangent, joined, own_terms],
        flops=HIDING * piece_flops,
        name="next",
    )
    for step, (even_bit, odd_bit) in enumerate(turns[::-1]):
        got = swap(send, even_bit, odd_bit, peers)
        if step + 1 < len(turns):
            after = [own_terms, next_queries]
            keep, send = call(add_kernel, [sums, held], [keep, got], after=after, name="add")
    attended, grad_query, mark = call(
        functools.partial(attend_kernel, peers),
        [shape(BF16, row_count, width)] * 2 + [shape(F32, 8, 128)],
        [rows, stats_all, queries, *outer, pair, joined, own_mem, other_mem],
        after=[send],
        flops=HIDING * piece_flops,
        name="attend",
    )
    owned_mine, owned_send = call(
        owned_kernel,
        [shape(F32, FR_DEV, 2, frame_len, half_width), shape(BF16, FR_DEV, 2, frame_len, half_width)],
        [codes, keep, got],
        after=[own, mark],
        name="owned",
    )
    owned_got = swap(owned_send, 1, 1, peers)
    grad_key, grad_value = call(
        final_kernel, [shape(BF16, row_count, width)] * 2, [own, owned_mine, owned_got], name="final"
    )
    return (attended, grad_query, grad_key, grad_value)


def solution(mesh):
    rows = P(("traj", "tm"), None)
    in_specs = (rows, rows, rows, rows, P("traj"), P(), rows, P("traj"))
    return jax.shard_map(body, mesh=mesh, in_specs=in_specs, out_specs=(rows,) * 4, check_vma=False)
```

```python
import functools
import math

import jax
import jax.numpy as jnp
from jax import lax
from jax.experimental import pallas as pl
from jax.experimental.pallas import tpu as pltpu
from jax.sharding import PartitionSpec as P

FR_DEV = 2
MEM = 2
DEPTH = 128

BLOCKED_LOGIT = -1e30
LOG2E = math.log2(math.e)
FACTOR = 1.0 / math.sqrt(DEPTH)

SMEM = pl.BlockSpec(memory_space=pltpu.SMEM)
VMEM = pl.BlockSpec(memory_space=pltpu.VMEM)
ANY = pl.BlockSpec(memory_space=pl.ANY)
HIDING = 200
VMEM_LIMIT = 16 * 1024 * 1024
BF16, F32 = jnp.bfloat16, jnp.float32


def shape(dtype, *dims):
    return jax.ShapeDtypeStruct(dims, dtype)


def call(kernel, outs, arrays, scalars=(), after=(), flops=0, name=None):
    count = len(scalars) + len(arrays)

    def run(*refs):
        kernel(*refs[:count], *refs[count + len(after) :])

    return pl.pallas_call(
        run,
        out_shape=outs,
        in_specs=[SMEM] * len(scalars) + [VMEM] * len(arrays) + [ANY] * len(after),
        out_specs=[VMEM] * len(outs),
        compiler_params=pltpu.CompilerParams(vmem_limit_bytes=VMEM_LIMIT),
        cost_estimate=pl.CostEstimate(flops=flops, bytes_accessed=0, transcendentals=0) if flops else None,
        name=name,
    )(*scalars, *arrays, *after)


def swap(block, even_bit, odd_bit, peers):
    return lax.ppermute(block, "tm", [(i, i ^ (odd_bit if i & 1 else even_bit)) for i in range(peers)])


def shift(block, by, start, peers):
    pairs = [(i, i + by) for i in range(start, peers, 2) if 0 <= i + by < peers]
    return lax.ppermute(block, "tm", pairs)


def relays_of(by, start, peers):
    pairs = [(i, i + by) for i in range(start, peers, 2) if 0 <= i + by < peers]
    return {(i, j): i ^ 4 for i, j in pairs if peers == 8 and (i ^ j) >> 1 == 3}


def shift_first(block, by, start, peers):
    relays = relays_of(by, start, peers)
    pairs = [(i, i + by) for i in range(start, peers, 2) if 0 <= i + by < peers]
    return lax.ppermute(block, "tm", [(i, relays.get((i, j), j)) for i, j in pairs])


def shift_second(block, by, start, peers):
    pairs = [(relay, j) for (_, j), relay in relays_of(by, start, peers).items()]
    return lax.ppermute(block, "tm", pairs) if pairs else block


def through_relay(by, start, peers):
    me = lax.axis_index("tm")
    return functools.reduce(jnp.logical_or, [me == j for _, j in relays_of(by, start, peers)], me < 0)


def lane_value(row, lane):
    lanes = lax.broadcasted_iota(jnp.int32, row.shape, 1)
    return jnp.max(jnp.where(lanes == lane, row, 0))


def bank_of(bank_ref):
    row = bank_ref[...]
    return [lane_value(row, slot) for slot in range(row.shape[1])]


def dyn_frames(bank, last_frame):
    found = [jnp.int32(0)] * (len(bank) - 2)
    seen = jnp.int32(0)
    for frame in bank:
        free = jnp.logical_and(frame != 0, frame != last_frame)
        for j in range(len(found)):
            found[j] = jnp.where(jnp.logical_and(free, seen == j), frame, found[j])
        seen = seen + free.astype(jnp.int32)
    return found


def place_of(frame, dyns):
    place = jnp.int32(len(dyns))
    for j, dyn in enumerate(dyns):
        place = jnp.where(frame == dyn, j, place)
    return place


def choose(out, take_first, first, second):
    @pl.when(take_first)
    def _():
        out[...] = first[...]

    @pl.when(jnp.logical_not(take_first))
    def _():
        out[...] = second[...]


def has_end(me, done, peers):
    return jnp.logical_or((me & ~done) == 0, (me | done) == peers - 1)


def has_dyn(me, frame, done):
    return ((me ^ (frame // FR_DEV)) & ~done) == 0


def by_role(me, even_value, odd_value):
    return jnp.where((me & 1) == 0, even_value, odd_value)


def load_kernel(count, *refs):
    arrays, outs, sems = refs[:count], refs[count:-1], refs[-1]
    if len(outs) == 1:
        rows = arrays[0].shape[0]
        outs = [outs[0].at[pl.ds(j * rows, rows)] for j in range(count)]
    copies = [pltpu.make_async_copy(ref, out, sems.at[j]) for j, (ref, out) in enumerate(zip(arrays, outs))]
    for copy in copies:
        copy.start()
    for copy in copies:
        copy.wait()


def pack(fields, width):
    code = jnp.int32(0)
    for j, field in enumerate(fields):
        code = code | (field.astype(jnp.int32) << (j * width))
    return code


def field(code, j, width):
    return (code >> (j * width)) & ((1 << width) - 1)


def code_of(codes_ref, row):
    return jnp.max(codes_ref[row : row + 1, :])


PICK, SUM, OWNED = range(3)
PLACE_BITS = 4
PREV, OWN, MEMORY, NEXT, PAIR = range(5)


def plan_kernel(
    peers,
    last_bits,
    bank_ref,
    index_ref,
    pair_index_ref,
    pose_ref,
    bias_ref,
    value_ref,
    direct_keys,
    rows_ref,
    codes_ref,
    values_out,
    keys_out,
):
    me = lax.axis_index("tm")
    last_frame = peers * FR_DEV - 1
    heads, _, row_count = rows_ref.shape
    values_out[...] = value_ref[...]
    keys_out[...] = direct_keys[...]
    bank = [bank_ref[0, slot] for slot in range(bank_ref.shape[1])]
    pair_ids = [bank_ref[0, pair_index_ref[0, m]] for m in range(MEM)]
    mem_ids = [bank_ref[0, index_ref[0, m]] for m in range(MEM)]

    own_ids = [me * FR_DEV + j for j in range(FR_DEV)]
    prev_ids = [jnp.maximum(own - FR_DEV, 0) for own in own_ids]
    next_ids = [jnp.minimum(own + FR_DEV, last_frame) for own in own_ids]
    pair_own_ids = [(me ^ 1) * FR_DEV + j for j in range(FR_DEV)]
    pieces = ((prev_ids, own_ids), (own_ids, own_ids), (mem_ids, own_ids), (own_ids, next_ids), (pair_ids, pair_own_ids))
    poses = [([pose_ref[f] for f in key_ids], [pose_ref[f] for f in query_ids]) for key_ids, query_ids in pieces]
    frame_of = lax.broadcasted_iota(jnp.int32, (1, row_count), 1) // (row_count // FR_DEV)
    for head in range(heads):
        for piece, (key_poses, query_poses) in enumerate(poses):
            for j, key_pose in enumerate(key_poses):
                row = jnp.zeros((1, row_count), F32)
                for a, query_pose in enumerate(query_poses):
                    value = bias_ref[head, query_pose, key_pose] * LOG2E
                    if piece == PREV:
                        value = jnp.where(me == 0, BLOCKED_LOGIT, value)
                    row = jnp.where(frame_of == a, value, row)
                rows_ref[head, piece * FR_DEV + j : piece * FR_DEV + j + 1, :] = row

    dyns = dyn_frames(bank, last_frame)
    bit = by_role(me, *last_bits)
    upper = (me & bit) != 0
    picks = []
    for frame in mem_ids + pair_ids:
        source = place_of(frame, dyns)
        local = jnp.where(frame == 0, jnp.logical_not(upper), upper)
        local = jnp.where(source < len(dyns), has_dyn(me, frame, (peers - 1) & ~bit), local)
        picks.append(source * 2 + local.astype(jnp.int32))
    far = jnp.where(upper, 0, last_frame)
    sums = [jnp.where(frame == far, len(dyns) + 1, place_of(frame, dyns)) for frame in mem_ids + pair_ids]
    owned = []
    for group in (me, me ^ 1):
        for j in range(FR_DEV):
            frame = group * FR_DEV + j
            place = place_of(frame, dyns)
            named = jnp.logical_or(place < len(dyns), jnp.logical_or(frame == 0, frame == last_frame))
            owned.append(place * 2 + named.astype(jnp.int32))
    lanes = codes_ref.shape[1]
    for row, code in ((PICK, pack(picks, PLACE_BITS)), (SUM, pack(sums, PLACE_BITS)), (OWNED, pack(owned, PLACE_BITS))):
        codes_ref[row : row + 1, :] = jnp.full((1, lanes), code, jnp.int32)


def split_kernel(peers, bank_ref, key_ref, value_ref, pair_keys, pair_values, out_ref):
    me = lax.axis_index("tm")
    frame_len, half_width = out_ref.shape[2:]
    dyns = dyn_frames(bank_of(bank_ref), peers * FR_DEV - 1)
    places = [(has_dyn(me, dyn, 0), dyn % FR_DEV) for dyn in dyns]
    places.append((has_end(me, 0, peers), jnp.where(me < peers // 2, 0, FR_DEV - 1)))
    for j, (local, frame) in enumerate(places):
        for role in range(2):
            for sources, taken in (((key_ref, value_ref), local), ((pair_keys, pair_values), jnp.logical_not(local))):

                @pl.when(jnp.logical_and((me & 1) == role, taken))
                def _(sources=sources, j=j, frame=frame, role=role):
                    part = pl.ds(pl.multiple_of(frame * frame_len, frame_len), frame_len)
                    for kind, source in enumerate(sources):
                        out_ref[j, kind] = source[part, role * half_width : (role + 1) * half_width]


def step_kernel(peers, even_done, odd_done, bank_ref, mine_ref, got_ref, out_ref):
    me = lax.axis_index("tm")
    done = by_role(me, even_done, odd_done)
    dyns = dyn_frames(bank_of(bank_ref), peers * FR_DEV - 1)
    flags = [has_dyn(me, dyn, done) for dyn in dyns] + [has_end(me, done, peers)]
    for j, flag in enumerate(flags):
        choose(out_ref.at[j], flag, mine_ref.at[j], got_ref.at[j])


def pick_kernel(codes_ref, mine_ref, got_ref, own_out, pair_out):
    code = code_of(codes_ref, PICK)
    for o, out in enumerate((own_out, pair_out)):
        for m in range(MEM):
            pick = field(code, o * MEM + m, PLACE_BITS)
            source = pick >> 1
            choose(out.at[m], (pick & 1) != 0, mine_ref.at[source], got_ref.at[source])


def dot(a, b, left, right):
    return lax.dot_general(a, b, (((left,), (right,)), ((), ())), preferred_element_type=F32)


def logits_of(keys, query, rows_ref, head, piece):
    frame_len = query.shape[0] // FR_DEV
    raw = dot(keys, query, 1, 1) * (FACTOR * LOG2E)
    parts = []
    for j in range(FR_DEV):
        row = piece * FR_DEV + j
        parts.append(raw[j * frame_len : (j + 1) * frame_len] + rows_ref[head, row : row + 1, :])
    return jnp.concatenate(parts, axis=0)


def joined_parts(joined_ref, cols):
    rows = joined_ref.shape[0] // 2 // DEPTH * DEPTH
    return joined_ref[0:rows, cols], joined_ref[rows : 2 * rows, cols]


def head_cols(head):
    return pl.ds(head * DEPTH, DEPTH)


def part_of(logits, slopes):
    peak = jnp.max(logits, axis=0, keepdims=True)
    exps = jnp.exp2(logits - peak)
    return peak, jnp.sum(exps, axis=0, keepdims=True), jnp.sum(exps * slopes, axis=0, keepdims=True)


def merged(left, right):
    peak = jnp.maximum(left[0], right[0])
    scales = [jnp.exp2(part[0] - peak) for part in (left, right)]
    return peak, *(left[j] * scales[0] + right[j] * scales[1] for j in (1, 2))


def load_part(ref, head):
    return tuple(ref[head, j : j + 1, :] for j in range(3))


def store_part(ref, head, part):
    for j, row in enumerate(part):
        ref[head, j : j + 1, :] = row


def prev_parts(peers, direct_keys, relayed_keys, outer_values, pair_keys, pair_values, cols):
    even = (lax.axis_index("tm") & 1) == 0
    keys = jnp.where(through_relay(1, 1, peers), relayed_keys[:, cols], direct_keys[:, cols])
    parts = zip((keys, outer_values[:, cols]), (pair_keys[:, cols], pair_values[:, cols]))
    return tuple(jnp.where(even, outer, pair) for outer, pair in parts)


def stats_kernel(
    peers,
    rows_ref,
    queries_ref,
    direct_keys,
    relayed_keys,
    outer_values,
    pair_keys,
    pair_values,
    key_ref,
    value_ref,
    part_ref,
    queries_out,
    cotangent_out,
):
    heads = queries_ref.shape[1] // DEPTH
    rows = queries_out.shape[0]
    queries_out[...] = queries_ref[0:rows]
    cotangent_out[...] = queries_ref[rows : 2 * rows]

    def products(head):
        cols = head_cols(head)
        query, cotangent = joined_parts(queries_ref, cols)
        prev = prev_parts(peers, direct_keys, relayed_keys, outer_values, pair_keys, pair_values, cols)
        pieces = ((PREV, prev), (OWN, (key_ref[:, cols], value_ref[:, cols])))
        return [
            (logits_of(keys, query, rows_ref, head, piece), dot(values, cotangent, 1, 1))
            for piece, (keys, values) in pieces
        ]

    ahead = products(0)
    for head in range(heads):
        now = ahead
        if head + 1 < heads:
            ahead = products(head + 1)
        store_part(part_ref, head, merged(*(part_of(*piece) for piece in now)))


def rounded(part, logits, slopes):
    peak, total, spread = merged(part, part_of(logits, slopes))
    inverse = 1.0 / total
    stats = peak, inverse, spread * inverse
    return stats, *weights_of(stats, logits, slopes)


def weights_of(stats, logits, slopes):
    peak, inverse, spread = stats
    probs = jnp.exp2(logits - peak) * inverse
    return probs.astype(BF16), (probs * (slopes - spread)).astype(BF16)


def memory_kernel(
    codes_ref, rows_ref, part_ref, pair_part_ref, own_queries, pair_queries, own_mem, pair_mem, keep_ref, send_ref
):
    role = lax.axis_index("tm") & 1
    code = code_of(codes_ref, SUM)
    frame_len, half_width = own_mem.shape[2:]
    half = half_width // DEPTH
    groups = ((own_queries, own_mem, part_ref, MEMORY), (pair_queries, pair_mem, pair_part_ref, PAIR))
    work = [(g, local) for local in range(half) for g in range(len(groups))]
    keep_ref[...] = jnp.zeros(keep_ref.shape, F32)

    def operands(g, local):
        cols = pl.ds(pl.multiple_of((role * half + local) * DEPTH, DEPTH), DEPTH)
        return joined_parts(groups[g][0], cols)

    def products(g, local):
        _, mem, _, piece = groups[g]
        query, cotangent = operands(g, local)
        keys, values = (mem[:, kind, :, head_cols(local)].reshape(MEM * frame_len, DEPTH) for kind in range(2))
        return logits_of(keys, query, rows_ref, role * half + local, piece), dot(values, cotangent, 1, 1)

    def add(g, local, _, weights, dlogits):
        query, cotangent = operands(g, local)
        terms = (dot(dlogits, query, 1, 0) * FACTOR, dot(weights, cotangent, 1, 0))
        for m in range(MEM):
            place = field(code, g * MEM + m, PLACE_BITS)
            for kind, term in enumerate(terms):
                part = term[m * frame_len : (m + 1) * frame_len].astype(BF16).astype(F32)
                keep_ref[place, kind, :, head_cols(local)] += part

    ahead = products(*work[0])
    behind = None
    for j, (g, local) in enumerate(work):
        now = ahead
        if j + 1 < len(work):
            ahead = products(*work[j + 1])
        if behind is not None:
            add(*work[j - 1], *behind)
        behind = rounded(load_part(groups[g][2], role * half + local), *now)
    add(*work[-1], *behind)
    kept = send_ref.shape[0]
    for place in range(kept):
        send_ref[place] = keep_ref[place if place + 1 < kept else kept].astype(BF16)


def next_kernel(
    peers,
    rows_ref,
    stats_ref,
    pair_queries,
    outer_queries,
    direct_cotangent,
    relayed_cotangent,
    key_ref,
    value_ref,
    term_ref,
    sum_ref,
):
    even = (lax.axis_index("tm") & 1) == 0
    relayed = through_relay(-1, 2, peers)
    heads = pair_queries.shape[1] // DEPTH

    def operands(head):
        cols = head_cols(head)
        cotangent = jnp.where(relayed, relayed_cotangent[:, cols], direct_cotangent[:, cols])
        outer = outer_queries[:, cols], cotangent
        return [jnp.where(even, a, b) for a, b in zip(joined_parts(pair_queries, cols), outer)]

    def products(head):
        query, cotangent = operands(head)
        keys, values = key_ref[:, head_cols(head)], value_ref[:, head_cols(head)]
        return logits_of(keys, query, rows_ref, head, NEXT), dot(values, cotangent, 1, 1)

    ahead = products(0)
    for head in range(heads):
        now = ahead
        if head + 1 < heads:
            ahead = products(head + 1)
        weights, dlogits = weights_of(load_part(stats_ref, head), *now)
        query, cotangent = operands(head)
        cols = head_cols(head)
        sum_ref[0, :, cols] = term_ref[0, :, cols] + dot(dlogits, query, 1, 0) * FACTOR
        sum_ref[1, :, cols] = term_ref[1, :, cols] + dot(weights, cotangent, 1, 0)


def memory_parts(own_mem, other_mem, head):
    role = lax.axis_index("tm") & 1
    frame_len, half_width = own_mem.shape[2:]
    half = half_width // DEPTH
    cols = head_cols(head % half)
    return [
        jnp.where(role == head // half, own_mem[:, kind, :, cols], other_mem[:, kind, :, cols]).reshape(
            MEM * frame_len, DEPTH
        )
        for kind in range(2)
    ]


def own_kernel(rows_ref, part_ref, queries_ref, key_ref, value_ref, own_mem, other_mem, term_ref, stats_ref):
    heads = queries_ref.shape[1] // DEPTH

    def products(head):
        cols = head_cols(head)
        query, cotangent = joined_parts(queries_ref, cols)
        own = key_ref[:, cols], value_ref[:, cols]
        pieces = ((OWN, own), (MEMORY, memory_parts(own_mem, other_mem, head)))
        return [
            (logits_of(keys, query, rows_ref, head, piece), dot(values, cotangent, 1, 1))
            for piece, (keys, values) in pieces
        ]

    ahead = products(0)
    for head in range(heads):
        own, memory = ahead
        if head + 1 < heads:
            ahead = products(head + 1)
        cols = head_cols(head)
        query, cotangent = joined_parts(queries_ref, cols)
        peak, total, spread = merged(load_part(part_ref, head), part_of(*memory))
        inverse = 1.0 / total
        stats = peak, inverse, spread * inverse
        store_part(stats_ref, head, stats)
        weights, dlogits = weights_of(stats, *own)
        term_ref[0, :, cols] = dot(dlogits, query, 1, 0) * FACTOR
        term_ref[1, :, cols] = dot(weights, cotangent, 1, 0)


def attend_kernel(
    peers,
    rows_ref,
    stats_ref,
    queries_ref,
    direct_keys,
    relayed_keys,
    outer_values,
    pair_keys,
    pair_values,
    key_ref,
    value_ref,
    own_mem,
    other_mem,
    attended_ref,
    grad_query_ref,
    mark_ref,
):
    mark_ref[...] = jnp.zeros(mark_ref.shape, F32)
    heads = queries_ref.shape[1] // DEPTH

    def pieces(head):
        cols = head_cols(head)
        prev = prev_parts(peers, direct_keys, relayed_keys, outer_values, pair_keys, pair_values, cols)
        return (PREV, prev), (OWN, (key_ref[:, cols], value_ref[:, cols])), (MEMORY, memory_parts(own_mem, other_mem, head))

    def products(head):
        query, cotangent = joined_parts(queries_ref, head_cols(head))
        return [
            (logits_of(keys, query, rows_ref, head, piece), dot(values, cotangent, 1, 1))
            for piece, (keys, values) in pieces(head)
        ]

    ahead = products(0)
    for head in range(heads):
        now = ahead
        if head + 1 < heads:
            ahead = products(head + 1)
        cols = head_cols(head)
        stats = load_part(stats_ref, head)
        attended = grad_query = 0.0
        for (_, (keys, values)), piece in zip(pieces(head), now):
            weights, dlogits = weights_of(stats, *piece)
            attended += dot(values, weights, 0, 0)
            grad_query += dot(keys, dlogits, 0, 0)
        attended_ref[:, cols] = attended.T.astype(BF16)
        grad_query_ref[:, cols] = (grad_query * FACTOR).T.astype(BF16)


def add_kernel(keep_ref, got_ref, out_ref, send_ref):
    value = keep_ref[0 : got_ref.shape[0]] + got_ref[...].astype(F32)
    out_ref[...] = value
    send_ref[...] = value.astype(BF16)


def pass_kernel(in_ref, out_ref):
    out_ref[...] = in_ref[...]


def owned_kernel(codes_ref, keep_ref, got_ref, mine_ref, pair_ref):
    code = code_of(codes_ref, OWNED)
    for o, out in enumerate((mine_ref, pair_ref)):
        for j in range(FR_DEV):
            owned = field(code, o * FR_DEV + j, PLACE_BITS)
            place = owned >> 1
            named = (owned & 1) != 0

            @pl.when(named)
            def _(out=out, j=j, place=place):
                value = keep_ref[place] + got_ref[place].astype(F32)
                out[j] = value.astype(out.dtype)

            @pl.when(jnp.logical_not(named))
            def _(out=out, j=j):
                out[j] = jnp.zeros(out.shape[1:], out.dtype)


def final_kernel(own_ref, mine_ref, got_ref, grad_key_ref, grad_value_ref):
    role = lax.axis_index("tm") & 1
    frame_len, half_width = mine_ref.shape[2:]
    for kind, out in enumerate((grad_key_ref, grad_value_ref)):
        for j in range(FR_DEV):
            rows = pl.ds(j * frame_len, frame_len)
            for half in range(2):
                cols = pl.ds(half * half_width, half_width)
                bank = jnp.where(role == half, mine_ref[j, kind], got_ref[j, kind].astype(F32))
                out[rows, cols] = (own_ref[kind, rows, cols] + bank).astype(BF16)


def body(
    query_states,
    key_states,
    value_states,
    grad_out,
    camera_pose,
    pose_bias,
    memory_index,
    bank_frames,
):
    row_count, width = query_states.shape
    frame_len = row_count // FR_DEV
    heads = pose_bias.shape[0]
    slots = bank_frames.shape[0]
    peers = lax.axis_size("tm")
    bits = [1 << i for i in range(1, peers.bit_length() - 1)]
    turns = list(zip(bits, bits[::-1]))
    piece_flops = 2 * row_count * row_count * width
    bank_frames = bank_frames.reshape(1, slots)
    last_bits = turns[-1]

    def load(outs, arrays, name, after=()):
        def run(*refs):
            load_kernel(len(arrays), *refs[: len(arrays)], *refs[len(arrays) + len(after) :])

        return pl.pallas_call(
            run,
            out_shape=outs,
            in_specs=[pl.BlockSpec(memory_space=pltpu.HBM)] * len(arrays) + [ANY] * len(after),
            out_specs=[VMEM] * len(outs),
            scratch_shapes=[pltpu.SemaphoreType.DMA((len(arrays),))],
            compiler_params=pltpu.CompilerParams(vmem_limit_bytes=VMEM_LIMIT),
            name=name,
        )(*(pltpu.with_memory_space_constraint(array, pltpu.HBM) for array in arrays), *after)

    half_width = width // 2
    pair = [swap(array, 1, 1, peers) for array in (key_states, value_states)]
    pair_index = swap(memory_index, 1, 1, peers)
    rows_shape = shape(BF16, row_count, width)
    keys, values, bank = load(
        [rows_shape, rows_shape, shape(jnp.int32, 1, slots)], [key_states, value_states, bank_frames], "load"
    )
    direct_keys = shift_first(keys, 1, 1, peers)
    held = shape(BF16, slots - 1, 2, frame_len, half_width)
    sums = shape(F32, slots - 1, 2, frame_len, half_width)
    (mine,) = call(functools.partial(split_kernel, peers), [held], [bank, keys, values, *pair], name="split")
    (queries,) = load([shape(BF16, 2 * row_count, width)], [query_states, grad_out], "load_queries", after=[mine])
    pair_queries = swap(queries, 1, 1, peers)

    bias_rows = -(-(5 * FR_DEV) // 8) * 8
    rows, codes, values_out, keys_out = call(
        functools.partial(plan_kernel, peers, last_bits),
        [shape(F32, heads, bias_rows, row_count), shape(jnp.int32, 8, 128)] + [shape(BF16, row_count, width)] * 2,
        [values, direct_keys],
        scalars=[bank_frames, memory_index, pair_index, camera_pose, pose_bias],
        flops=HIDING * piece_flops,
        name="plan",
    )
    outer = [direct_keys, shift_second(keys_out, 1, 1, peers), shift(values_out, 1, 1, peers)]
    even_done = odd_done = 1
    for step, (even_bit, odd_bit) in enumerate(turns):
        got = swap(mine, even_bit, odd_bit, peers)
        if step + 1 < len(turns):
            kernel = functools.partial(step_kernel, peers, even_done, odd_done)
            after = [codes, pair_queries]
            (mine,) = call(kernel, [held], [bank, mine, got], after=after, name="step")
        even_done |= even_bit
        odd_done |= odd_bit

    stats = shape(F32, heads, 8, row_count)
    part, queries_out, cotangent_out = call(
        functools.partial(stats_kernel, peers),
        [stats] + [shape(BF16, row_count, width)] * 2,
        [rows, queries, *outer, *pair, keys, values],
        flops=HIDING * piece_flops,
        name="stats",
    )
    pair_part = swap(part, 1, 1, peers)
    next_queries = shift(queries_out, -1, 2, peers)
    direct_cotangent = shift_first(cotangent_out, -1, 2, peers)
    chosen = shape(BF16, MEM, 2, frame_len, half_width)
    own_mem, pair_mem = call(pick_kernel, [chosen] * 2, [codes, mine, got], name="pick")
    keep, send = call(
        memory_kernel,
        [shape(F32, slots, 2, frame_len, half_width), held],
        [codes, rows, part, pair_part, queries, pair_queries, own_mem, pair_mem],
        flops=HIDING * piece_flops,
        name="memory",
    )
    other_mem = swap(pair_mem, 1, 1, peers)
    pair_sums = shape(F32, 2, row_count, width)
    own_terms, stats_all = call(
        own_kernel,
        [pair_sums, stats],
        [rows, part, queries, keys, values, own_mem, other_mem],
        after=[send],
        flops=HIDING * piece_flops,
        name="own",
    )
    next_stats = lax.ppermute(stats_all, "tm", [(i, i - 1) for i in range(1, peers)])
    (passed_on,) = call(
        pass_kernel, [shape(BF16, row_count, width)], [direct_cotangent], after=[own_terms], name="pass_on"
    )
    relayed_cotangent = shift_second(passed_on, -1, 2, peers)
    (own,) = call(
        functools.partial(next_kernel, peers),
        [pair_sums],
        [rows, next_stats, pair_queries, next_queries, direct_cotangent, relayed_cotangent, keys, values, own_terms],
        flops=HIDING * piece_flops,
        name="next",
    )
    for step, (even_bit, odd_bit) in enumerate(turns[::-1]):
        got = swap(send, even_bit, odd_bit, peers)
        if step + 1 < len(turns):
            after = [own_terms, next_queries]
            keep, send = call(add_kernel, [sums, held], [keep, got], after=after, name="add")
    attended, grad_query, mark = call(
        functools.partial(attend_kernel, peers),
        [shape(BF16, row_count, width)] * 2 + [shape(F32, 8, 128)],
        [rows, stats_all, queries, *outer, *pair, keys, values, own_mem, other_mem],
        after=[send],
        flops=HIDING * piece_flops,
        name="attend",
    )
    owned_mine, owned_send = call(
        owned_kernel,
        [shape(F32, FR_DEV, 2, frame_len, half_width), shape(BF16, FR_DEV, 2, frame_len, half_width)],
        [codes, keep, got],
        after=[own, mark],
        name="owned",
    )
    owned_got = swap(owned_send, 1, 1, peers)
    grad_key, grad_value = call(
        final_kernel, [shape(BF16, row_count, width)] * 2, [own, owned_mine, owned_got], name="final"
    )
    return (attended, grad_query, grad_key, grad_value)


def solution(mesh):
    rows = P(("traj", "tm"), None)
    in_specs = (rows, rows, rows, rows, P("traj"), P(), rows, P("traj"))
    return jax.shard_map(body, mesh=mesh, in_specs=in_specs, out_specs=(rows,) * 4, check_vma=False)
```

```python
import functools
import math

import jax
import jax.numpy as jnp
from jax import lax
from jax.experimental import pallas as pl
from jax.experimental.pallas import tpu as pltpu
from jax.sharding import PartitionSpec as P

FR_DEV = 2
MEM = 2
DEPTH = 128

BLOCKED_LOGIT = -1e30
LOG2E = math.log2(math.e)
FACTOR = 1.0 / math.sqrt(DEPTH)

SMEM = pl.BlockSpec(memory_space=pltpu.SMEM)
VMEM = pl.BlockSpec(memory_space=pltpu.VMEM)
ANY = pl.BlockSpec(memory_space=pl.ANY)
HIDING = 200
VMEM_LIMIT = 16 * 1024 * 1024
BF16, F32 = jnp.bfloat16, jnp.float32


def shape(dtype, *dims):
    return jax.ShapeDtypeStruct(dims, dtype)


def call(kernel, outs, arrays, scalars=(), after=(), flops=0, name=None):
    count = len(scalars) + len(arrays)

    def run(*refs):
        kernel(*refs[:count], *refs[count + len(after) :])

    return pl.pallas_call(
        run,
        out_shape=outs,
        in_specs=[SMEM] * len(scalars) + [VMEM] * len(arrays) + [ANY] * len(after),
        out_specs=[VMEM] * len(outs),
        compiler_params=pltpu.CompilerParams(vmem_limit_bytes=VMEM_LIMIT),
        cost_estimate=pl.CostEstimate(flops=flops, bytes_accessed=0, transcendentals=0) if flops else None,
        name=name,
    )(*scalars, *arrays, *after)


def swap(block, even_bit, odd_bit, peers):
    return lax.ppermute(block, "tm", [(i, i ^ (odd_bit if i & 1 else even_bit)) for i in range(peers)])


def shift(block, by, start, peers):
    pairs = [(i, i + by) for i in range(start, peers, 2) if 0 <= i + by < peers]
    return lax.ppermute(block, "tm", pairs)


def relays_of(by, start, peers):
    pairs = [(i, i + by) for i in range(start, peers, 2) if 0 <= i + by < peers]
    return {(i, j): i ^ 4 for i, j in pairs if peers == 8 and (i ^ j) >> 1 == 3}


def shift_first(block, by, start, peers):
    relays = relays_of(by, start, peers)
    pairs = [(i, i + by) for i in range(start, peers, 2) if 0 <= i + by < peers]
    return lax.ppermute(block, "tm", [(i, relays.get((i, j), j)) for i, j in pairs])


def shift_second(block, by, start, peers):
    pairs = [(relay, j) for (_, j), relay in relays_of(by, start, peers).items()]
    return lax.ppermute(block, "tm", pairs) if pairs else block


def through_relay(by, start, peers):
    me = lax.axis_index("tm")
    return functools.reduce(jnp.logical_or, [me == j for _, j in relays_of(by, start, peers)], me < 0)


def lane_value(row, lane):
    lanes = lax.broadcasted_iota(jnp.int32, row.shape, 1)
    return jnp.max(jnp.where(lanes == lane, row, 0))


def bank_of(bank_ref):
    row = bank_ref[...]
    return [lane_value(row, slot) for slot in range(row.shape[1])]


def dyn_frames(bank, last_frame):
    found = [jnp.int32(0)] * (len(bank) - 2)
    seen = jnp.int32(0)
    for frame in bank:
        free = jnp.logical_and(frame != 0, frame != last_frame)
        for j in range(len(found)):
            found[j] = jnp.where(jnp.logical_and(free, seen == j), frame, found[j])
        seen = seen + free.astype(jnp.int32)
    return found


def place_of(frame, dyns):
    place = jnp.int32(len(dyns))
    for j, dyn in enumerate(dyns):
        place = jnp.where(frame == dyn, j, place)
    return place


def choose(out, take_first, first, second):
    @pl.when(take_first)
    def _():
        out[...] = first[...]

    @pl.when(jnp.logical_not(take_first))
    def _():
        out[...] = second[...]


def has_end(me, done, peers):
    return jnp.logical_or((me & ~done) == 0, (me | done) == peers - 1)


def has_dyn(me, frame, done):
    return ((me ^ (frame // FR_DEV)) & ~done) == 0


def by_role(me, even_value, odd_value):
    return jnp.where((me & 1) == 0, even_value, odd_value)


def load_kernel(count, stacked, *refs):
    arrays, outs, sems = refs[:count], refs[count:-1], refs[-1]
    rows = arrays[0].shape[0]
    targets = [outs[0].at[pl.ds(j * rows, rows)] for j in range(stacked)] + list(outs[1 if stacked else 0 :])
    copies = [pltpu.make_async_copy(ref, out, sems.at[j]) for j, (ref, out) in enumerate(zip(arrays, targets))]
    for copy in copies:
        copy.start()
    for copy in copies:
        copy.wait()


def pack(fields, width):
    code = jnp.int32(0)
    for j, field in enumerate(fields):
        code = code | (field.astype(jnp.int32) << (j * width))
    return code


def field(code, j, width):
    return (code >> (j * width)) & ((1 << width) - 1)


def code_of(codes_ref, row):
    return jnp.max(codes_ref[row : row + 1, :])


PICK, SUM, OWNED = range(3)
PLACE_BITS = 4
PREV, OWN, MEMORY, NEXT, PAIR = range(5)


def plan_kernel(
    peers,
    last_bits,
    bank_ref,
    index_ref,
    pair_index_ref,
    pose_ref,
    bias_ref,
    value_ref,
    direct_keys,
    rows_ref,
    codes_ref,
    values_out,
    keys_out,
):
    me = lax.axis_index("tm")
    last_frame = peers * FR_DEV - 1
    heads, _, row_count = rows_ref.shape
    values_out[...] = value_ref[...]
    keys_out[...] = direct_keys[...]
    bank = [bank_ref[0, slot] for slot in range(bank_ref.shape[1])]
    pair_ids = [bank_ref[0, pair_index_ref[0, m]] for m in range(MEM)]
    mem_ids = [bank_ref[0, index_ref[0, m]] for m in range(MEM)]

    own_ids = [me * FR_DEV + j for j in range(FR_DEV)]
    prev_ids = [jnp.maximum(own - FR_DEV, 0) for own in own_ids]
    next_ids = [jnp.minimum(own + FR_DEV, last_frame) for own in own_ids]
    pair_own_ids = [(me ^ 1) * FR_DEV + j for j in range(FR_DEV)]
    pieces = ((prev_ids, own_ids), (own_ids, own_ids), (mem_ids, own_ids), (own_ids, next_ids), (pair_ids, pair_own_ids))
    poses = [([pose_ref[f] for f in key_ids], [pose_ref[f] for f in query_ids]) for key_ids, query_ids in pieces]
    frame_of = lax.broadcasted_iota(jnp.int32, (1, row_count), 1) // (row_count // FR_DEV)
    for head in range(heads):
        for piece, (key_poses, query_poses) in enumerate(poses):
            for j, key_pose in enumerate(key_poses):
                row = jnp.zeros((1, row_count), F32)
                for a, query_pose in enumerate(query_poses):
                    value = bias_ref[head, query_pose, key_pose] * LOG2E
                    if piece == PREV:
                        value = jnp.where(me == 0, BLOCKED_LOGIT, value)
                    row = jnp.where(frame_of == a, value, row)
                rows_ref[head, piece * FR_DEV + j : piece * FR_DEV + j + 1, :] = row

    dyns = dyn_frames(bank, last_frame)
    bit = by_role(me, *last_bits)
    upper = (me & bit) != 0
    picks = []
    for frame in mem_ids + pair_ids:
        source = place_of(frame, dyns)
        local = jnp.where(frame == 0, jnp.logical_not(upper), upper)
        local = jnp.where(source < len(dyns), has_dyn(me, frame, (peers - 1) & ~bit), local)
        picks.append(source * 2 + local.astype(jnp.int32))
    far = jnp.where(upper, 0, last_frame)
    sums = [jnp.where(frame == far, len(dyns) + 1, place_of(frame, dyns)) for frame in mem_ids + pair_ids]
    owned = []
    for group in (me, me ^ 1):
        for j in range(FR_DEV):
            frame = group * FR_DEV + j
            place = place_of(frame, dyns)
            named = jnp.logical_or(place < len(dyns), jnp.logical_or(frame == 0, frame == last_frame))
            owned.append(place * 2 + named.astype(jnp.int32))
    lanes = codes_ref.shape[1]
    for row, code in ((PICK, pack(picks, PLACE_BITS)), (SUM, pack(sums, PLACE_BITS)), (OWNED, pack(owned, PLACE_BITS))):
        codes_ref[row : row + 1, :] = jnp.full((1, lanes), code, jnp.int32)


def split_kernel(peers, bank_ref, key_ref, value_ref, pair_keys, pair_values, out_ref):
    me = lax.axis_index("tm")
    frame_len, half_width = out_ref.shape[2:]
    dyns = dyn_frames(bank_of(bank_ref), peers * FR_DEV - 1)
    places = [(has_dyn(me, dyn, 0), dyn % FR_DEV) for dyn in dyns]
    places.append((has_end(me, 0, peers), jnp.where(me < peers // 2, 0, FR_DEV - 1)))
    for j, (local, frame) in enumerate(places):
        for role in range(2):
            for sources, taken in (((key_ref, value_ref), local), ((pair_keys, pair_values), jnp.logical_not(local))):

                @pl.when(jnp.logical_and((me & 1) == role, taken))
                def _(sources=sources, j=j, frame=frame, role=role):
                    part = pl.ds(pl.multiple_of(frame * frame_len, frame_len), frame_len)
                    for kind, source in enumerate(sources):
                        out_ref[j, kind] = source[part, role * half_width : (role + 1) * half_width]


def step_kernel(peers, even_done, odd_done, bank_ref, mine_ref, got_ref, out_ref):
    me = lax.axis_index("tm")
    done = by_role(me, even_done, odd_done)
    dyns = dyn_frames(bank_of(bank_ref), peers * FR_DEV - 1)
    flags = [has_dyn(me, dyn, done) for dyn in dyns] + [has_end(me, done, peers)]
    for j, flag in enumerate(flags):
        choose(out_ref.at[j], flag, mine_ref.at[j], got_ref.at[j])


def pick_kernel(codes_ref, mine_ref, got_ref, own_out, pair_out):
    code = code_of(codes_ref, PICK)
    for o, out in enumerate((own_out, pair_out)):
        for m in range(MEM):
            pick = field(code, o * MEM + m, PLACE_BITS)
            source = pick >> 1
            choose(out.at[m], (pick & 1) != 0, mine_ref.at[source], got_ref.at[source])


def dot(a, b, left, right):
    return lax.dot_general(a, b, (((left,), (right,)), ((), ())), preferred_element_type=F32)


def logits_of(keys, query, rows_ref, head, piece):
    frame_len = query.shape[0] // FR_DEV
    raw = dot(keys, query, 1, 1) * (FACTOR * LOG2E)
    parts = []
    for j in range(FR_DEV):
        row = piece * FR_DEV + j
        parts.append(raw[j * frame_len : (j + 1) * frame_len] + rows_ref[head, row : row + 1, :])
    return jnp.concatenate(parts, axis=0)


def joined_parts(joined_ref, cols):
    rows = joined_ref.shape[0] // 2 // DEPTH * DEPTH
    return joined_ref[0:rows, cols], joined_ref[rows : 2 * rows, cols]


def head_cols(head):
    return pl.ds(head * DEPTH, DEPTH)


def part_of(logits, slopes):
    peak = jnp.max(logits, axis=0, keepdims=True)
    exps = jnp.exp2(logits - peak)
    return peak, jnp.sum(exps, axis=0, keepdims=True), jnp.sum(exps * slopes, axis=0, keepdims=True)


def merged(left, right):
    peak = jnp.maximum(left[0], right[0])
    scales = [jnp.exp2(part[0] - peak) for part in (left, right)]
    return peak, *(left[j] * scales[0] + right[j] * scales[1] for j in (1, 2))


def load_part(ref, head):
    return tuple(ref[head, j : j + 1, :] for j in range(3))


def store_part(ref, head, part):
    for j, row in enumerate(part):
        ref[head, j : j + 1, :] = row


def prev_parts(peers, direct_keys, relayed_keys, outer_values, pair_keys, pair_values, cols):
    even = (lax.axis_index("tm") & 1) == 0
    keys = jnp.where(through_relay(1, 1, peers), relayed_keys[:, cols], direct_keys[:, cols])
    parts = zip((keys, outer_values[:, cols]), (pair_keys[:, cols], pair_values[:, cols]))
    return tuple(jnp.where(even, outer, pair) for outer, pair in parts)


def stats_kernel(
    peers,
    rows_ref,
    queries_ref,
    direct_keys,
    relayed_keys,
    outer_values,
    pair_keys,
    pair_values,
    key_ref,
    value_ref,
    part_ref,
    queries_out,
    cotangent_out,
):
    heads = queries_ref.shape[1] // DEPTH
    rows = queries_out.shape[0]
    queries_out[...] = queries_ref[0:rows]
    cotangent_out[...] = queries_ref[rows : 2 * rows]

    def products(head):
        cols = head_cols(head)
        query, cotangent = joined_parts(queries_ref, cols)
        prev = prev_parts(peers, direct_keys, relayed_keys, outer_values, pair_keys, pair_values, cols)
        pieces = ((PREV, prev), (OWN, (key_ref[:, cols], value_ref[:, cols])))
        return [
            (logits_of(keys, query, rows_ref, head, piece), dot(values, cotangent, 1, 1))
            for piece, (keys, values) in pieces
        ]

    ahead = products(0)
    for head in range(heads):
        now = ahead
        if head + 1 < heads:
            ahead = products(head + 1)
        store_part(part_ref, head, merged(*(part_of(*piece) for piece in now)))


def rounded(part, logits, slopes):
    peak, total, spread = merged(part, part_of(logits, slopes))
    inverse = 1.0 / total
    stats = peak, inverse, spread * inverse
    return stats, *weights_of(stats, logits, slopes)


def weights_of(stats, logits, slopes):
    peak, inverse, spread = stats
    probs = jnp.exp2(logits - peak) * inverse
    return probs.astype(BF16), (probs * (slopes - spread)).astype(BF16)


def memory_kernel(
    codes_ref, rows_ref, part_ref, pair_part_ref, own_queries, pair_queries, own_mem, pair_mem, keep_ref, send_ref
):
    role = lax.axis_index("tm") & 1
    code = code_of(codes_ref, SUM)
    frame_len, half_width = own_mem.shape[2:]
    half = half_width // DEPTH
    groups = ((own_queries, own_mem, part_ref, MEMORY), (pair_queries, pair_mem, pair_part_ref, PAIR))
    work = [(g, local) for local in range(half) for g in range(len(groups))]
    keep_ref[...] = jnp.zeros(keep_ref.shape, F32)

    def operands(g, local):
        cols = pl.ds(pl.multiple_of((role * half + local) * DEPTH, DEPTH), DEPTH)
        return joined_parts(groups[g][0], cols)

    def products(g, local):
        _, mem, _, piece = groups[g]
        query, cotangent = operands(g, local)
        keys, values = (mem[:, kind, :, head_cols(local)].reshape(MEM * frame_len, DEPTH) for kind in range(2))
        return logits_of(keys, query, rows_ref, role * half + local, piece), dot(values, cotangent, 1, 1)

    def add(g, local, _, weights, dlogits):
        query, cotangent = operands(g, local)
        terms = (dot(dlogits, query, 1, 0) * FACTOR, dot(weights, cotangent, 1, 0))
        for m in range(MEM):
            place = field(code, g * MEM + m, PLACE_BITS)
            for kind, term in enumerate(terms):
                part = term[m * frame_len : (m + 1) * frame_len].astype(BF16).astype(F32)
                keep_ref[place, kind, :, head_cols(local)] += part

    ahead = products(*work[0])
    behind = None
    for j, (g, local) in enumerate(work):
        now = ahead
        if j + 1 < len(work):
            ahead = products(*work[j + 1])
        if behind is not None:
            add(*work[j - 1], *behind)
        behind = rounded(load_part(groups[g][2], role * half + local), *now)
    add(*work[-1], *behind)
    kept = send_ref.shape[0]
    for place in range(kept):
        send_ref[place] = keep_ref[place if place + 1 < kept else kept].astype(BF16)


def next_kernel(
    peers,
    rows_ref,
    stats_ref,
    pair_queries,
    outer_queries,
    direct_cotangent,
    relayed_cotangent,
    key_ref,
    value_ref,
    term_ref,
    sum_ref,
):
    even = (lax.axis_index("tm") & 1) == 0
    relayed = through_relay(-1, 2, peers)
    heads = pair_queries.shape[1] // DEPTH

    def operands(head):
        cols = head_cols(head)
        cotangent = jnp.where(relayed, relayed_cotangent[:, cols], direct_cotangent[:, cols])
        outer = outer_queries[:, cols], cotangent
        return [jnp.where(even, a, b) for a, b in zip(joined_parts(pair_queries, cols), outer)]

    def products(head):
        query, cotangent = operands(head)
        keys, values = key_ref[:, head_cols(head)], value_ref[:, head_cols(head)]
        return logits_of(keys, query, rows_ref, head, NEXT), dot(values, cotangent, 1, 1)

    ahead = products(0)
    for head in range(heads):
        now = ahead
        if head + 1 < heads:
            ahead = products(head + 1)
        weights, dlogits = weights_of(load_part(stats_ref, head), *now)
        query, cotangent = operands(head)
        cols = head_cols(head)
        sum_ref[0, :, cols] = term_ref[0, :, cols] + dot(dlogits, query, 1, 0) * FACTOR
        sum_ref[1, :, cols] = term_ref[1, :, cols] + dot(weights, cotangent, 1, 0)


def memory_parts(own_mem, other_mem, head):
    role = lax.axis_index("tm") & 1
    frame_len, half_width = own_mem.shape[2:]
    half = half_width // DEPTH
    cols = head_cols(head % half)
    return [
        jnp.where(role == head // half, own_mem[:, kind, :, cols], other_mem[:, kind, :, cols]).reshape(
            MEM * frame_len, DEPTH
        )
        for kind in range(2)
    ]


def own_kernel(rows_ref, part_ref, queries_ref, key_ref, value_ref, own_mem, other_mem, term_ref, stats_ref):
    heads = queries_ref.shape[1] // DEPTH

    def products(head):
        cols = head_cols(head)
        query, cotangent = joined_parts(queries_ref, cols)
        own = key_ref[:, cols], value_ref[:, cols]
        pieces = ((OWN, own), (MEMORY, memory_parts(own_mem, other_mem, head)))
        return [
            (logits_of(keys, query, rows_ref, head, piece), dot(values, cotangent, 1, 1))
            for piece, (keys, values) in pieces
        ]

    ahead = products(0)
    for head in range(heads):
        own, memory = ahead
        if head + 1 < heads:
            ahead = products(head + 1)
        cols = head_cols(head)
        query, cotangent = joined_parts(queries_ref, cols)
        peak, total, spread = merged(load_part(part_ref, head), part_of(*memory))
        inverse = 1.0 / total
        stats = peak, inverse, spread * inverse
        store_part(stats_ref, head, stats)
        weights, dlogits = weights_of(stats, *own)
        term_ref[0, :, cols] = dot(dlogits, query, 1, 0) * FACTOR
        term_ref[1, :, cols] = dot(weights, cotangent, 1, 0)


def attend_kernel(
    peers,
    rows_ref,
    stats_ref,
    queries_ref,
    direct_keys,
    relayed_keys,
    outer_values,
    pair_keys,
    pair_values,
    key_ref,
    value_ref,
    own_mem,
    other_mem,
    attended_ref,
    grad_query_ref,
    mark_ref,
):
    mark_ref[...] = jnp.zeros(mark_ref.shape, F32)
    heads = queries_ref.shape[1] // DEPTH

    def pieces(head):
        cols = head_cols(head)
        prev = prev_parts(peers, direct_keys, relayed_keys, outer_values, pair_keys, pair_values, cols)
        return (PREV, prev), (OWN, (key_ref[:, cols], value_ref[:, cols])), (MEMORY, memory_parts(own_mem, other_mem, head))

    def products(head):
        query, cotangent = joined_parts(queries_ref, head_cols(head))
        return [
            (logits_of(keys, query, rows_ref, head, piece), dot(values, cotangent, 1, 1))
            for piece, (keys, values) in pieces(head)
        ]

    ahead = products(0)
    for head in range(heads):
        now = ahead
        if head + 1 < heads:
            ahead = products(head + 1)
        cols = head_cols(head)
        stats = load_part(stats_ref, head)
        attended = grad_query = 0.0
        for (_, (keys, values)), piece in zip(pieces(head), now):
            weights, dlogits = weights_of(stats, *piece)
            attended += dot(values, weights, 0, 0)
            grad_query += dot(keys, dlogits, 0, 0)
        attended_ref[:, cols] = attended.T.astype(BF16)
        grad_query_ref[:, cols] = (grad_query * FACTOR).T.astype(BF16)


def add_kernel(keep_ref, got_ref, out_ref, send_ref):
    value = keep_ref[0 : got_ref.shape[0]] + got_ref[...].astype(F32)
    out_ref[...] = value
    send_ref[...] = value.astype(BF16)


def pass_kernel(in_ref, out_ref):
    out_ref[...] = in_ref[...]


def owned_kernel(codes_ref, keep_ref, got_ref, mine_ref, pair_ref):
    code = code_of(codes_ref, OWNED)
    for o, out in enumerate((mine_ref, pair_ref)):
        for j in range(FR_DEV):
            owned = field(code, o * FR_DEV + j, PLACE_BITS)
            place = owned >> 1
            named = (owned & 1) != 0

            @pl.when(named)
            def _(out=out, j=j, place=place):
                value = keep_ref[place] + got_ref[place].astype(F32)
                out[j] = value.astype(out.dtype)

            @pl.when(jnp.logical_not(named))
            def _(out=out, j=j):
                out[j] = jnp.zeros(out.shape[1:], out.dtype)


def final_kernel(own_ref, mine_ref, got_ref, grad_key_ref, grad_value_ref):
    role = lax.axis_index("tm") & 1
    frame_len, half_width = mine_ref.shape[2:]
    for kind, out in enumerate((grad_key_ref, grad_value_ref)):
        for j in range(FR_DEV):
            rows = pl.ds(j * frame_len, frame_len)
            for half in range(2):
                cols = pl.ds(half * half_width, half_width)
                bank = jnp.where(role == half, mine_ref[j, kind], got_ref[j, kind].astype(F32))
                out[rows, cols] = (own_ref[kind, rows, cols] + bank).astype(BF16)


def body(
    query_states,
    key_states,
    value_states,
    grad_out,
    camera_pose,
    pose_bias,
    memory_index,
    bank_frames,
):
    row_count, width = query_states.shape
    frame_len = row_count // FR_DEV
    heads = pose_bias.shape[0]
    slots = bank_frames.shape[0]
    peers = lax.axis_size("tm")
    bits = [1 << i for i in range(1, peers.bit_length() - 1)]
    turns = list(zip(bits, bits[::-1]))
    piece_flops = 2 * row_count * row_count * width
    bank_frames = bank_frames.reshape(1, slots)
    last_bits = turns[-1]

    def load(outs, arrays, name, stacked=0, after=()):
        def run(*refs):
            load_kernel(len(arrays), stacked, *refs[: len(arrays)], *refs[len(arrays) + len(after) :])

        return pl.pallas_call(
            run,
            out_shape=outs,
            in_specs=[pl.BlockSpec(memory_space=pltpu.HBM)] * len(arrays) + [ANY] * len(after),
            out_specs=[VMEM] * len(outs),
            scratch_shapes=[pltpu.SemaphoreType.DMA((len(arrays),))],
            compiler_params=pltpu.CompilerParams(vmem_limit_bytes=VMEM_LIMIT),
            name=name,
        )(*(pltpu.with_memory_space_constraint(array, pltpu.HBM) for array in arrays), *after)

    half_width = width // 2
    pair = [swap(array, 1, 1, peers) for array in (key_states, value_states)]
    rows_shape = shape(BF16, row_count, width)
    keys, values, bank = load(
        [rows_shape, rows_shape, shape(jnp.int32, 1, slots)], [key_states, value_states, bank_frames], "load"
    )
    direct_keys = shift_first(keys, 1, 1, peers)
    held = shape(BF16, slots - 1, 2, frame_len, half_width)
    sums = shape(F32, slots - 1, 2, frame_len, half_width)
    (mine,) = call(functools.partial(split_kernel, peers), [held], [bank, keys, values, *pair], name="split")
    queries, index = load(
        [shape(BF16, 2 * row_count, width), shape(jnp.int32, 1, MEM)],
        [query_states, grad_out, memory_index],
        "load_queries",
        stacked=2,
        after=[mine],
    )
    pair_index = swap(index, 1, 1, peers)
    pair_queries = swap(queries, 1, 1, peers)

    bias_rows = -(-(5 * FR_DEV) // 8) * 8
    rows, codes, values_out, keys_out = call(
        functools.partial(plan_kernel, peers, last_bits),
        [shape(F32, heads, bias_rows, row_count), shape(jnp.int32, 8, 128)] + [shape(BF16, row_count, width)] * 2,
        [values, direct_keys],
        scalars=[bank_frames, memory_index, pair_index, camera_pose, pose_bias],
        flops=HIDING * piece_flops,
        name="plan",
    )
    outer = [direct_keys, shift_second(keys_out, 1, 1, peers), shift(values_out, 1, 1, peers)]
    even_done = odd_done = 1
    for step, (even_bit, odd_bit) in enumerate(turns):
        got = swap(mine, even_bit, odd_bit, peers)
        if step + 1 < len(turns):
            kernel = functools.partial(step_kernel, peers, even_done, odd_done)
            after = [codes, pair_queries]
            (mine,) = call(kernel, [held], [bank, mine, got], after=after, name="step")
        even_done |= even_bit
        odd_done |= odd_bit

    stats = shape(F32, heads, 8, row_count)
    part, queries_out, cotangent_out = call(
        functools.partial(stats_kernel, peers),
        [stats] + [shape(BF16, row_count, width)] * 2,
        [rows, queries, *outer, *pair, keys, values],
        flops=HIDING * piece_flops,
        name="stats",
    )
    pair_part = swap(part, 1, 1, peers)
    next_queries = shift(queries_out, -1, 2, peers)
    direct_cotangent = shift_first(cotangent_out, -1, 2, peers)
    chosen = shape(BF16, MEM, 2, frame_len, half_width)
    own_mem, pair_mem = call(pick_kernel, [chosen] * 2, [codes, mine, got], name="pick")
    keep, send = call(
        memory_kernel,
        [shape(F32, slots, 2, frame_len, half_width), held],
        [codes, rows, part, pair_part, queries, pair_queries, own_mem, pair_mem],
        flops=HIDING * piece_flops,
        name="memory",
    )
    other_mem = swap(pair_mem, 1, 1, peers)
    pair_sums = shape(F32, 2, row_count, width)
    own_terms, stats_all = call(
        own_kernel,
        [pair_sums, stats],
        [rows, part, queries, keys, values, own_mem, other_mem],
        after=[send],
        flops=HIDING * piece_flops,
        name="own",
    )
    next_stats = lax.ppermute(stats_all, "tm", [(i, i - 1) for i in range(1, peers)])
    (passed_on,) = call(
        pass_kernel, [shape(BF16, row_count, width)], [direct_cotangent], after=[own_terms], name="pass_on"
    )
    relayed_cotangent = shift_second(passed_on, -1, 2, peers)
    (own,) = call(
        functools.partial(next_kernel, peers),
        [pair_sums],
        [rows, next_stats, pair_queries, next_queries, direct_cotangent, relayed_cotangent, keys, values, own_terms],
        flops=HIDING * piece_flops,
        name="next",
    )
    for step, (even_bit, odd_bit) in enumerate(turns[::-1]):
        got = swap(send, even_bit, odd_bit, peers)
        if step + 1 < len(turns):
            after = [own_terms, next_queries]
            keep, send = call(add_kernel, [sums, held], [keep, got], after=after, name="add")
    attended, grad_query, mark = call(
        functools.partial(attend_kernel, peers),
        [shape(BF16, row_count, width)] * 2 + [shape(F32, 8, 128)],
        [rows, stats_all, queries, *outer, *pair, keys, values, own_mem, other_mem],
        after=[send],
        flops=HIDING * piece_flops,
        name="attend",
    )
    owned_mine, owned_send = call(
        owned_kernel,
        [shape(F32, FR_DEV, 2, frame_len, half_width), shape(BF16, FR_DEV, 2, frame_len, half_width)],
        [codes, keep, got],
        after=[own, mark],
        name="owned",
    )
    owned_got = swap(owned_send, 1, 1, peers)
    grad_key, grad_value = call(
        final_kernel, [shape(BF16, row_count, width)] * 2, [own, owned_mine, owned_got], name="final"
    )
    return (attended, grad_query, grad_key, grad_value)


def solution(mesh):
    rows = P(("traj", "tm"), None)
    in_specs = (rows, rows, rows, rows, P("traj"), P(), rows, P("traj"))
    return jax.shard_map(body, mesh=mesh, in_specs=in_specs, out_specs=(rows,) * 4, check_vma=False)
```

```python
import functools
import math

import jax
import jax.numpy as jnp
from jax import lax
from jax.experimental import pallas as pl
from jax.experimental.pallas import tpu as pltpu
from jax.sharding import PartitionSpec as P

FR_DEV = 2
MEM = 2
DEPTH = 128
TAIL = 16

BLOCKED_LOGIT = -1e30
LOG2E = math.log2(math.e)
FACTOR = 1.0 / math.sqrt(DEPTH)

SMEM = pl.BlockSpec(memory_space=pltpu.SMEM)
VMEM = pl.BlockSpec(memory_space=pltpu.VMEM)
ANY = pl.BlockSpec(memory_space=pl.ANY)
HIDING = 200
VMEM_LIMIT = 16 * 1024 * 1024
BF16, F32 = jnp.bfloat16, jnp.float32


def shape(dtype, *dims):
    return jax.ShapeDtypeStruct(dims, dtype)


def call(kernel, outs, arrays, scalars=(), after=(), flops=0, name=None):
    count = len(scalars) + len(arrays)

    def run(*refs):
        kernel(*refs[:count], *refs[count + len(after) :])

    return pl.pallas_call(
        run,
        out_shape=outs,
        in_specs=[SMEM] * len(scalars) + [VMEM] * len(arrays) + [ANY] * len(after),
        out_specs=[VMEM] * len(outs),
        compiler_params=pltpu.CompilerParams(vmem_limit_bytes=VMEM_LIMIT),
        cost_estimate=pl.CostEstimate(flops=flops, bytes_accessed=0, transcendentals=0) if flops else None,
        name=name,
    )(*scalars, *arrays, *after)


def swap(block, even_bit, odd_bit, peers):
    return lax.ppermute(block, "tm", [(i, i ^ (odd_bit if i & 1 else even_bit)) for i in range(peers)])


def shift(block, by, start, peers):
    pairs = [(i, i + by) for i in range(start, peers, 2) if 0 <= i + by < peers]
    return lax.ppermute(block, "tm", pairs)


def relays_of(by, start, peers):
    pairs = [(i, i + by) for i in range(start, peers, 2) if 0 <= i + by < peers]
    return {(i, j): i ^ 4 for i, j in pairs if peers == 8 and (i ^ j) >> 1 == 3}


def shift_first(block, by, start, peers):
    relays = relays_of(by, start, peers)
    pairs = [(i, i + by) for i in range(start, peers, 2) if 0 <= i + by < peers]
    return lax.ppermute(block, "tm", [(i, relays.get((i, j), j)) for i, j in pairs])


def shift_second(block, by, start, peers):
    pairs = [(relay, j) for (_, j), relay in relays_of(by, start, peers).items()]
    return lax.ppermute(block, "tm", pairs) if pairs else block


def through_relay(by, start, peers):
    me = lax.axis_index("tm")
    return functools.reduce(jnp.logical_or, [me == j for _, j in relays_of(by, start, peers)], me < 0)


def lane_value(row, lane):
    lanes = lax.broadcasted_iota(jnp.int32, row.shape, 1)
    return jnp.max(jnp.where(lanes == lane, row, 0))


def bank_of(bank_ref):
    row = bank_ref[...]
    return [lane_value(row, slot) for slot in range(row.shape[1])]


def dyn_frames(bank, last_frame):
    found = [jnp.int32(0)] * (len(bank) - 2)
    seen = jnp.int32(0)
    for frame in bank:
        free = jnp.logical_and(frame != 0, frame != last_frame)
        for j in range(len(found)):
            found[j] = jnp.where(jnp.logical_and(free, seen == j), frame, found[j])
        seen = seen + free.astype(jnp.int32)
    return found


def place_of(frame, dyns):
    place = jnp.int32(len(dyns))
    for j, dyn in enumerate(dyns):
        place = jnp.where(frame == dyn, j, place)
    return place


def choose(out, take_first, first, second):
    @pl.when(take_first)
    def _():
        out[...] = first[...]

    @pl.when(jnp.logical_not(take_first))
    def _():
        out[...] = second[...]


def has_end(me, done, peers):
    return jnp.logical_or((me & ~done) == 0, (me | done) == peers - 1)


def has_dyn(me, frame, done):
    return ((me ^ (frame // FR_DEV)) & ~done) == 0


def by_role(me, even_value, odd_value):
    return jnp.where((me & 1) == 0, even_value, odd_value)


def join_kernel(index_ref, key_ref, value_ref, joined_ref, index_buf, sems):
    rows = key_ref.shape[0]
    copies = [
        pltpu.make_async_copy(index_ref, index_buf, sems.at[0]),
        pltpu.make_async_copy(key_ref, joined_ref.at[pl.ds(0, rows)], sems.at[1]),
        pltpu.make_async_copy(value_ref, joined_ref.at[pl.ds(rows, rows)], sems.at[2]),
    ]
    for copy in copies:
        copy.start()
    copies[0].wait()
    width = joined_ref.shape[1]
    lane = lax.broadcasted_iota(jnp.int32, (TAIL, width), 1) // DEPTH
    tail = jnp.zeros((TAIL, width), jnp.int32)
    for m in range(MEM):
        tail = jnp.where(lane == m, index_buf[0:1, m : m + 1], tail)
    joined_ref[2 * rows : 2 * rows + TAIL, :] = tail.astype(F32).astype(BF16)
    copies[1].wait()
    copies[2].wait()


def join_queries_kernel(query_ref, cotangent_ref, joined_ref, sems):
    rows = query_ref.shape[0]
    copies = [
        pltpu.make_async_copy(ref, joined_ref.at[pl.ds(j * rows, rows)], sems.at[j])
        for j, ref in enumerate((query_ref, cotangent_ref))
    ]
    for copy in copies:
        copy.start()
    for copy in copies:
        copy.wait()


def pack(fields, width):
    code = jnp.int32(0)
    for j, field in enumerate(fields):
        code = code | (field.astype(jnp.int32) << (j * width))
    return code


def field(code, j, width):
    return (code >> (j * width)) & ((1 << width) - 1)


def code_of(codes_ref, row):
    return jnp.max(codes_ref[row : row + 1, :])


PICK, SUM, OWNED = range(3)
PLACE_BITS = 4
PREV, OWN, MEMORY, NEXT, PAIR = range(5)


def plan_kernel(
    peers,
    last_bits,
    bank_ref,
    index_ref,
    pose_ref,
    bias_ref,
    pair_ref,
    rows_ref,
    codes_ref,
):
    me = lax.axis_index("tm")
    last_frame = peers * FR_DEV - 1
    heads, _, row_count = rows_ref.shape
    bank = [bank_ref[0, slot] for slot in range(bank_ref.shape[1])]
    tail = pair_ref.shape[0] - TAIL
    pair_ids = []
    for m in range(MEM):
        slot = jnp.max(pair_ref[tail : tail + TAIL, m * DEPTH : (m + 1) * DEPTH].astype(F32)).astype(jnp.int32)
        pair_ids.append(bank_ref[0, slot])
    mem_ids = [bank_ref[0, index_ref[0, m]] for m in range(MEM)]

    own_ids = [me * FR_DEV + j for j in range(FR_DEV)]
    prev_ids = [jnp.maximum(own - FR_DEV, 0) for own in own_ids]
    next_ids = [jnp.minimum(own + FR_DEV, last_frame) for own in own_ids]
    pair_own_ids = [(me ^ 1) * FR_DEV + j for j in range(FR_DEV)]
    pieces = ((prev_ids, own_ids), (own_ids, own_ids), (mem_ids, own_ids), (own_ids, next_ids), (pair_ids, pair_own_ids))
    poses = [([pose_ref[f] for f in key_ids], [pose_ref[f] for f in query_ids]) for key_ids, query_ids in pieces]
    frame_of = lax.broadcasted_iota(jnp.int32, (1, row_count), 1) // (row_count // FR_DEV)
    for head in range(heads):
        for piece, (key_poses, query_poses) in enumerate(poses):
            for j, key_pose in enumerate(key_poses):
                row = jnp.zeros((1, row_count), F32)
                for a, query_pose in enumerate(query_poses):
                    value = bias_ref[head, query_pose, key_pose] * LOG2E
                    if piece == PREV:
                        value = jnp.where(me == 0, BLOCKED_LOGIT, value)
                    row = jnp.where(frame_of == a, value, row)
                rows_ref[head, piece * FR_DEV + j : piece * FR_DEV + j + 1, :] = row

    dyns = dyn_frames(bank, last_frame)
    bit = by_role(me, *last_bits)
    upper = (me & bit) != 0
    picks = []
    for frame in mem_ids + pair_ids:
        source = place_of(frame, dyns)
        local = jnp.where(frame == 0, jnp.logical_not(upper), upper)
        local = jnp.where(source < len(dyns), has_dyn(me, frame, (peers - 1) & ~bit), local)
        picks.append(source * 2 + local.astype(jnp.int32))
    far = jnp.where(upper, 0, last_frame)
    sums = [jnp.where(frame == far, len(dyns) + 1, place_of(frame, dyns)) for frame in mem_ids + pair_ids]
    owned = []
    for group in (me, me ^ 1):
        for j in range(FR_DEV):
            frame = group * FR_DEV + j
            place = place_of(frame, dyns)
            named = jnp.logical_or(place < len(dyns), jnp.logical_or(frame == 0, frame == last_frame))
            owned.append(place * 2 + named.astype(jnp.int32))
    lanes = codes_ref.shape[1]
    for row, code in ((PICK, pack(picks, PLACE_BITS)), (SUM, pack(sums, PLACE_BITS)), (OWNED, pack(owned, PLACE_BITS))):
        codes_ref[row : row + 1, :] = jnp.full((1, lanes), code, jnp.int32)


def release_kernel(joined_ref, direct_keys, values_out, keys_out):
    rows = values_out.shape[0]
    values_out[...] = joined_ref[rows : 2 * rows, :]
    keys_out[...] = direct_keys[...]


def split_kernel(peers, bank_ref, mine_ref, pair_ref, out_ref):
    me = lax.axis_index("tm")
    frame_len, half_width = out_ref.shape[2:]
    dyns = dyn_frames(bank_of(bank_ref), peers * FR_DEV - 1)
    places = [(has_dyn(me, dyn, 0), dyn % FR_DEV) for dyn in dyns]
    places.append((has_end(me, 0, peers), jnp.where(me < peers // 2, 0, FR_DEV - 1)))
    for j, (local, frame) in enumerate(places):
        for role in range(2):
            for source, taken in ((mine_ref, local), (pair_ref, jnp.logical_not(local))):

                @pl.when(jnp.logical_and((me & 1) == role, taken))
                def _(source=source, j=j, frame=frame, role=role):
                    for kind in range(2):
                        start = pl.multiple_of((kind * FR_DEV + frame) * frame_len, frame_len)
                        out_ref[j, kind] = source[pl.ds(start, frame_len), role * half_width : (role + 1) * half_width]


def step_kernel(peers, even_done, odd_done, bank_ref, mine_ref, got_ref, out_ref):
    me = lax.axis_index("tm")
    done = by_role(me, even_done, odd_done)
    dyns = dyn_frames(bank_of(bank_ref), peers * FR_DEV - 1)
    flags = [has_dyn(me, dyn, done) for dyn in dyns] + [has_end(me, done, peers)]
    for j, flag in enumerate(flags):
        choose(out_ref.at[j], flag, mine_ref.at[j], got_ref.at[j])


def pick_kernel(codes_ref, mine_ref, got_ref, own_out, pair_out):
    code = code_of(codes_ref, PICK)
    for o, out in enumerate((own_out, pair_out)):
        for m in range(MEM):
            pick = field(code, o * MEM + m, PLACE_BITS)
            source = pick >> 1
            choose(out.at[m], (pick & 1) != 0, mine_ref.at[source], got_ref.at[source])


def dot(a, b, left, right):
    return lax.dot_general(a, b, (((left,), (right,)), ((), ())), preferred_element_type=F32)


def logits_of(keys, query, rows_ref, head, piece):
    frame_len = query.shape[0] // FR_DEV
    raw = dot(keys, query, 1, 1) * (FACTOR * LOG2E)
    parts = []
    for j in range(FR_DEV):
        row = piece * FR_DEV + j
        parts.append(raw[j * frame_len : (j + 1) * frame_len] + rows_ref[head, row : row + 1, :])
    return jnp.concatenate(parts, axis=0)


def joined_parts(joined_ref, cols):
    rows = joined_ref.shape[0] // 2 // DEPTH * DEPTH
    return joined_ref[0:rows, cols], joined_ref[rows : 2 * rows, cols]


def head_cols(head):
    return pl.ds(head * DEPTH, DEPTH)


def part_of(logits, slopes):
    peak = jnp.max(logits, axis=0, keepdims=True)
    exps = jnp.exp2(logits - peak)
    return peak, jnp.sum(exps, axis=0, keepdims=True), jnp.sum(exps * slopes, axis=0, keepdims=True)


def merged(left, right):
    peak = jnp.maximum(left[0], right[0])
    scales = [jnp.exp2(part[0] - peak) for part in (left, right)]
    return peak, *(left[j] * scales[0] + right[j] * scales[1] for j in (1, 2))


def load_part(ref, head):
    return tuple(ref[head, j : j + 1, :] for j in range(3))


def store_part(ref, head, part):
    for j, row in enumerate(part):
        ref[head, j : j + 1, :] = row


def prev_parts(peers, direct_keys, relayed_keys, outer_values, pair_ref, cols):
    even = (lax.axis_index("tm") & 1) == 0
    keys = jnp.where(through_relay(1, 1, peers), relayed_keys[:, cols], direct_keys[:, cols])
    parts = zip((keys, outer_values[:, cols]), joined_parts(pair_ref, cols))
    return tuple(jnp.where(even, outer, pair) for outer, pair in parts)


def stats_kernel(
    peers,
    rows_ref,
    queries_ref,
    direct_keys,
    relayed_keys,
    outer_values,
    pair_ref,
    own_ref,
    part_ref,
    queries_out,
    cotangent_out,
):
    heads = queries_ref.shape[1] // DEPTH
    rows = queries_out.shape[0]
    queries_out[...] = queries_ref[0:rows]
    cotangent_out[...] = queries_ref[rows : 2 * rows]

    def products(head):
        cols = head_cols(head)
        query, cotangent = joined_parts(queries_ref, cols)
        pieces = ((PREV, prev_parts(peers, direct_keys, relayed_keys, outer_values, pair_ref, cols)), (OWN, joined_parts(own_ref, cols)))
        return [
            (logits_of(keys, query, rows_ref, head, piece), dot(values, cotangent, 1, 1))
            for piece, (keys, values) in pieces
        ]

    ahead = products(0)
    for head in range(heads):
        now = ahead
        if head + 1 < heads:
            ahead = products(head + 1)
        store_part(part_ref, head, merged(*(part_of(*piece) for piece in now)))


def rounded(part, logits, slopes):
    peak, total, spread = merged(part, part_of(logits, slopes))
    inverse = 1.0 / total
    stats = peak, inverse, spread * inverse
    return stats, *weights_of(stats, logits, slopes)


def weights_of(stats, logits, slopes):
    peak, inverse, spread = stats
    probs = jnp.exp2(logits - peak) * inverse
    return probs.astype(BF16), (probs * (slopes - spread)).astype(BF16)


def memory_kernel(
    codes_ref, rows_ref, part_ref, pair_part_ref, own_queries, pair_queries, own_mem, pair_mem, keep_ref, send_ref
):
    role = lax.axis_index("tm") & 1
    code = code_of(codes_ref, SUM)
    frame_len, half_width = own_mem.shape[2:]
    half = half_width // DEPTH
    groups = ((own_queries, own_mem, part_ref, MEMORY), (pair_queries, pair_mem, pair_part_ref, PAIR))
    work = [(g, local) for local in range(half) for g in range(len(groups))]
    keep_ref[...] = jnp.zeros(keep_ref.shape, F32)

    def operands(g, local):
        cols = pl.ds(pl.multiple_of((role * half + local) * DEPTH, DEPTH), DEPTH)
        return joined_parts(groups[g][0], cols)

    def products(g, local):
        _, mem, _, piece = groups[g]
        query, cotangent = operands(g, local)
        keys, values = (mem[:, kind, :, head_cols(local)].reshape(MEM * frame_len, DEPTH) for kind in range(2))
        return logits_of(keys, query, rows_ref, role * half + local, piece), dot(values, cotangent, 1, 1)

    def add(g, local, _, weights, dlogits):
        query, cotangent = operands(g, local)
        terms = (dot(dlogits, query, 1, 0) * FACTOR, dot(weights, cotangent, 1, 0))
        for m in range(MEM):
            place = field(code, g * MEM + m, PLACE_BITS)
            for kind, term in enumerate(terms):
                part = term[m * frame_len : (m + 1) * frame_len].astype(BF16).astype(F32)
                keep_ref[place, kind, :, head_cols(local)] += part

    ahead = products(*work[0])
    behind = None
    for j, (g, local) in enumerate(work):
        now = ahead
        if j + 1 < len(work):
            ahead = products(*work[j + 1])
        if behind is not None:
            add(*work[j - 1], *behind)
        behind = rounded(load_part(groups[g][2], role * half + local), *now)
    add(*work[-1], *behind)
    kept = send_ref.shape[0]
    for place in range(kept):
        send_ref[place] = keep_ref[place if place + 1 < kept else kept].astype(BF16)


def next_kernel(
    peers,
    rows_ref,
    stats_ref,
    pair_queries,
    outer_queries,
    direct_cotangent,
    relayed_cotangent,
    own_ref,
    term_ref,
    sum_ref,
):
    even = (lax.axis_index("tm") & 1) == 0
    relayed = through_relay(-1, 2, peers)
    heads = pair_queries.shape[1] // DEPTH

    def operands(head):
        cols = head_cols(head)
        cotangent = jnp.where(relayed, relayed_cotangent[:, cols], direct_cotangent[:, cols])
        outer = outer_queries[:, cols], cotangent
        return [jnp.where(even, a, b) for a, b in zip(joined_parts(pair_queries, cols), outer)]

    def products(head):
        query, cotangent = operands(head)
        keys, values = joined_parts(own_ref, head_cols(head))
        return logits_of(keys, query, rows_ref, head, NEXT), dot(values, cotangent, 1, 1)

    ahead = products(0)
    for head in range(heads):
        now = ahead
        if head + 1 < heads:
            ahead = products(head + 1)
        weights, dlogits = weights_of(load_part(stats_ref, head), *now)
        query, cotangent = operands(head)
        cols = head_cols(head)
        sum_ref[0, :, cols] = term_ref[0, :, cols] + dot(dlogits, query, 1, 0) * FACTOR
        sum_ref[1, :, cols] = term_ref[1, :, cols] + dot(weights, cotangent, 1, 0)


def memory_parts(own_mem, other_mem, head):
    role = lax.axis_index("tm") & 1
    frame_len, half_width = own_mem.shape[2:]
    half = half_width // DEPTH
    cols = head_cols(head % half)
    return [
        jnp.where(role == head // half, own_mem[:, kind, :, cols], other_mem[:, kind, :, cols]).reshape(
            MEM * frame_len, DEPTH
        )
        for kind in range(2)
    ]


def own_kernel(rows_ref, part_ref, queries_ref, own_ref, own_mem, other_mem, term_ref, stats_ref):
    heads = queries_ref.shape[1] // DEPTH

    def products(head):
        query, cotangent = joined_parts(queries_ref, head_cols(head))
        pieces = ((OWN, joined_parts(own_ref, head_cols(head))), (MEMORY, memory_parts(own_mem, other_mem, head)))
        return [
            (logits_of(keys, query, rows_ref, head, piece), dot(values, cotangent, 1, 1))
            for piece, (keys, values) in pieces
        ]

    ahead = products(0)
    for head in range(heads):
        own, memory = ahead
        if head + 1 < heads:
            ahead = products(head + 1)
        cols = head_cols(head)
        query, cotangent = joined_parts(queries_ref, cols)
        peak, total, spread = merged(load_part(part_ref, head), part_of(*memory))
        inverse = 1.0 / total
        stats = peak, inverse, spread * inverse
        store_part(stats_ref, head, stats)
        weights, dlogits = weights_of(stats, *own)
        term_ref[0, :, cols] = dot(dlogits, query, 1, 0) * FACTOR
        term_ref[1, :, cols] = dot(weights, cotangent, 1, 0)


def attend_kernel(
    peers,
    rows_ref,
    stats_ref,
    queries_ref,
    direct_keys,
    relayed_keys,
    outer_values,
    pair_ref,
    own_ref,
    own_mem,
    other_mem,
    attended_ref,
    grad_query_ref,
    mark_ref,
):
    mark_ref[...] = jnp.zeros(mark_ref.shape, F32)
    heads = queries_ref.shape[1] // DEPTH

    def pieces(head):
        cols = head_cols(head)
        prev = prev_parts(peers, direct_keys, relayed_keys, outer_values, pair_ref, cols)
        return (PREV, prev), (OWN, joined_parts(own_ref, cols)), (MEMORY, memory_parts(own_mem, other_mem, head))

    def products(head):
        query, cotangent = joined_parts(queries_ref, head_cols(head))
        return [
            (logits_of(keys, query, rows_ref, head, piece), dot(values, cotangent, 1, 1))
            for piece, (keys, values) in pieces(head)
        ]

    ahead = products(0)
    for head in range(heads):
        now = ahead
        if head + 1 < heads:
            ahead = products(head + 1)
        cols = head_cols(head)
        stats = load_part(stats_ref, head)
        attended = grad_query = 0.0
        for (_, (keys, values)), piece in zip(pieces(head), now):
            weights, dlogits = weights_of(stats, *piece)
            attended += dot(values, weights, 0, 0)
            grad_query += dot(keys, dlogits, 0, 0)
        attended_ref[:, cols] = attended.T.astype(BF16)
        grad_query_ref[:, cols] = (grad_query * FACTOR).T.astype(BF16)


def add_kernel(keep_ref, got_ref, out_ref, send_ref):
    value = keep_ref[0 : got_ref.shape[0]] + got_ref[...].astype(F32)
    out_ref[...] = value
    send_ref[...] = value.astype(BF16)


def pass_kernel(in_ref, out_ref):
    out_ref[...] = in_ref[...]


def owned_kernel(codes_ref, keep_ref, got_ref, mine_ref, pair_ref):
    code = code_of(codes_ref, OWNED)
    for o, out in enumerate((mine_ref, pair_ref)):
        for j in range(FR_DEV):
            owned = field(code, o * FR_DEV + j, PLACE_BITS)
            place = owned >> 1
            named = (owned & 1) != 0

            @pl.when(named)
            def _(out=out, j=j, place=place):
                value = keep_ref[place] + got_ref[place].astype(F32)
                out[j] = value.astype(out.dtype)

            @pl.when(jnp.logical_not(named))
            def _(out=out, j=j):
                out[j] = jnp.zeros(out.shape[1:], out.dtype)


def final_kernel(own_ref, mine_ref, got_ref, grad_key_ref, grad_value_ref):
    role = lax.axis_index("tm") & 1
    frame_len, half_width = mine_ref.shape[2:]
    for kind, out in enumerate((grad_key_ref, grad_value_ref)):
        for j in range(FR_DEV):
            rows = pl.ds(j * frame_len, frame_len)
            for half in range(2):
                cols = pl.ds(half * half_width, half_width)
                bank = jnp.where(role == half, mine_ref[j, kind], got_ref[j, kind].astype(F32))
                out[rows, cols] = (own_ref[kind, rows, cols] + bank).astype(BF16)


def body(
    query_states,
    key_states,
    value_states,
    grad_out,
    camera_pose,
    pose_bias,
    memory_index,
    bank_frames,
):
    row_count, width = query_states.shape
    frame_len = row_count // FR_DEV
    heads = pose_bias.shape[0]
    slots = bank_frames.shape[0]
    peers = lax.axis_size("tm")
    bits = [1 << i for i in range(1, peers.bit_length() - 1)]
    turns = list(zip(bits, bits[::-1]))
    piece_flops = 2 * row_count * row_count * width
    bank_frames = bank_frames.reshape(1, slots)
    last_bits = turns[-1]

    def join(kernel, rows, arrays, scratch, name, after=()):
        def run(*refs):
            kernel(*refs[: len(arrays)], *refs[len(arrays) + len(after) :])

        return pl.pallas_call(
            run,
            out_shape=shape(BF16, rows, width),
            in_specs=[pl.BlockSpec(memory_space=pltpu.HBM)] * len(arrays) + [ANY] * len(after),
            out_specs=VMEM,
            scratch_shapes=[*scratch, pltpu.SemaphoreType.DMA((len(arrays),))],
            compiler_params=pltpu.CompilerParams(vmem_limit_bytes=VMEM_LIMIT),
            name=name,
        )(*(pltpu.with_memory_space_constraint(array, pltpu.HBM) for array in arrays), *after)

    joined = join(
        join_kernel,
        2 * row_count + TAIL,
        [memory_index, key_states, value_states],
        [pltpu.VMEM(memory_index.shape, jnp.int32)],
        "join",
    )
    half_width = width // 2
    direct_keys = shift_first(key_states, 1, 1, peers)
    pair = swap(joined, 1, 1, peers)
    held = shape(BF16, slots - 1, 2, frame_len, half_width)
    sums = shape(F32, slots - 1, 2, frame_len, half_width)
    (mine,) = call(functools.partial(split_kernel, peers), [held], [bank_frames, joined, pair], name="split")
    queries = join(join_queries_kernel, 2 * row_count, [query_states, grad_out], [], "join_queries", after=[mine])
    pair_queries = swap(queries, 1, 1, peers)

    bias_rows = -(-(5 * FR_DEV) // 8) * 8
    rows, codes = call(
        functools.partial(plan_kernel, peers, last_bits),
        [shape(F32, heads, bias_rows, row_count), shape(jnp.int32, 8, 128)],
        [pair],
        scalars=[bank_frames, memory_index, camera_pose, pose_bias],
        name="plan",
    )
    values_out, keys_out = call(
        release_kernel,
        [shape(BF16, row_count, width)] * 2,
        [joined, direct_keys],
        after=[codes],
        flops=HIDING * piece_flops,
        name="release",
    )
    outer = [direct_keys, shift_second(keys_out, 1, 1, peers), shift(values_out, 1, 1, peers)]
    even_done = odd_done = 1
    for step, (even_bit, odd_bit) in enumerate(turns):
        got = swap(mine, even_bit, odd_bit, peers)
        if step + 1 < len(turns):
            kernel = functools.partial(step_kernel, peers, even_done, odd_done)
            after = [codes, pair_queries]
            (mine,) = call(kernel, [held], [bank_frames, mine, got], after=after, name="step")
        even_done |= even_bit
        odd_done |= odd_bit

    stats = shape(F32, heads, 8, row_count)
    part, queries_out, cotangent_out = call(
        functools.partial(stats_kernel, peers),
        [stats] + [shape(BF16, row_count, width)] * 2,
        [rows, queries, *outer, pair, joined],
        flops=HIDING * piece_flops,
        name="stats",
    )
    pair_part = swap(part, 1, 1, peers)
    next_queries = shift(queries_out, -1, 2, peers)
    direct_cotangent = shift_first(cotangent_out, -1, 2, peers)
    chosen = shape(BF16, MEM, 2, frame_len, half_width)
    own_mem, pair_mem = call(pick_kernel, [chosen] * 2, [codes, mine, got], name="pick")
    keep, send = call(
        memory_kernel,
        [shape(F32, slots, 2, frame_len, half_width), held],
        [codes, rows, part, pair_part, queries, pair_queries, own_mem, pair_mem],
        flops=HIDING * piece_flops,
        name="memory",
    )
    other_mem = swap(pair_mem, 1, 1, peers)
    pair_sums = shape(F32, 2, row_count, width)
    own_terms, stats_all = call(
        own_kernel,
        [pair_sums, stats],
        [rows, part, queries, joined, own_mem, other_mem],
        after=[send],
        flops=HIDING * piece_flops,
        name="own",
    )
    next_stats = lax.ppermute(stats_all, "tm", [(i, i - 1) for i in range(1, peers)])
    (passed_on,) = call(
        pass_kernel, [shape(BF16, row_count, width)], [direct_cotangent], after=[own_terms], name="pass_on"
    )
    relayed_cotangent = shift_second(passed_on, -1, 2, peers)
    (own,) = call(
        functools.partial(next_kernel, peers),
        [pair_sums],
        [rows, next_stats, pair_queries, next_queries, direct_cotangent, relayed_cotangent, joined, own_terms],
        flops=HIDING * piece_flops,
        name="next",
    )
    for step, (even_bit, odd_bit) in enumerate(turns[::-1]):
        got = swap(send, even_bit, odd_bit, peers)
        if step + 1 < len(turns):
            after = [own_terms, next_queries]
            keep, send = call(add_kernel, [sums, held], [keep, got], after=after, name="add")
    attended, grad_query, mark = call(
        functools.partial(attend_kernel, peers),
        [shape(BF16, row_count, width)] * 2 + [shape(F32, 8, 128)],
        [rows, stats_all, queries, *outer, pair, joined, own_mem, other_mem],
        after=[send],
        flops=HIDING * piece_flops,
        name="attend",
    )
    owned_mine, owned_send = call(
        owned_kernel,
        [shape(F32, FR_DEV, 2, frame_len, half_width), shape(BF16, FR_DEV, 2, frame_len, half_width)],
        [codes, keep, got],
        after=[own, mark],
        name="owned",
    )
    owned_got = swap(owned_send, 1, 1, peers)
    grad_key, grad_value = call(
        final_kernel, [shape(BF16, row_count, width)] * 2, [own, owned_mine, owned_got], name="final"
    )
    return (attended, grad_query, grad_key, grad_value)


def solution(mesh):
    rows = P(("traj", "tm"), None)
    in_specs = (rows, rows, rows, rows, P("traj"), P(), rows, P("traj"))
    return jax.shard_map(body, mesh=mesh, in_specs=in_specs, out_specs=(rows,) * 4, check_vma=False)
```

```python
import functools
import math

import jax
import jax.numpy as jnp
from jax import lax
from jax.experimental import pallas as pl
from jax.experimental.pallas import tpu as pltpu
from jax.sharding import PartitionSpec as P

FR_DEV = 2
MEM = 2
DEPTH = 128

BLOCKED_LOGIT = -1e30
LOG2E = math.log2(math.e)
FACTOR = 1.0 / math.sqrt(DEPTH)

SMEM = pl.BlockSpec(memory_space=pltpu.SMEM)
VMEM = pl.BlockSpec(memory_space=pltpu.VMEM)
ANY = pl.BlockSpec(memory_space=pl.ANY)
HIDING = 200
VMEM_LIMIT = 16 * 1024 * 1024
BF16, F32 = jnp.bfloat16, jnp.float32


def shape(dtype, *dims):
    return jax.ShapeDtypeStruct(dims, dtype)


def call(kernel, outs, arrays, scalars=(), after=(), flops=0, name=None):
    count = len(scalars) + len(arrays)

    def run(*refs):
        kernel(*refs[:count], *refs[count + len(after) :])

    return pl.pallas_call(
        run,
        out_shape=outs,
        in_specs=[SMEM] * len(scalars) + [VMEM] * len(arrays) + [ANY] * len(after),
        out_specs=[VMEM] * len(outs),
        compiler_params=pltpu.CompilerParams(vmem_limit_bytes=VMEM_LIMIT),
        cost_estimate=pl.CostEstimate(flops=flops, bytes_accessed=0, transcendentals=0) if flops else None,
        name=name,
    )(*scalars, *arrays, *after)


def swap(block, even_bit, odd_bit, peers):
    return lax.ppermute(block, "tm", [(i, i ^ (odd_bit if i & 1 else even_bit)) for i in range(peers)])


def shift(block, by, start, peers):
    pairs = [(i, i + by) for i in range(start, peers, 2) if 0 <= i + by < peers]
    return lax.ppermute(block, "tm", pairs)


def relays_of(by, start, peers):
    pairs = [(i, i + by) for i in range(start, peers, 2) if 0 <= i + by < peers]
    return {(i, j): i ^ 4 for i, j in pairs if peers == 8 and (i ^ j) >> 1 == 3}


def shift_first(block, by, start, peers):
    relays = relays_of(by, start, peers)
    pairs = [(i, i + by) for i in range(start, peers, 2) if 0 <= i + by < peers]
    return lax.ppermute(block, "tm", [(i, relays.get((i, j), j)) for i, j in pairs])


def shift_second(block, by, start, peers):
    pairs = [(relay, j) for (_, j), relay in relays_of(by, start, peers).items()]
    return lax.ppermute(block, "tm", pairs) if pairs else block


def through_relay(by, start, peers):
    me = lax.axis_index("tm")
    return functools.reduce(jnp.logical_or, [me == j for _, j in relays_of(by, start, peers)], me < 0)


def lane_value(row, lane):
    lanes = lax.broadcasted_iota(jnp.int32, row.shape, 1)
    return jnp.max(jnp.where(lanes == lane, row, 0))


def bank_of(bank_ref):
    row = bank_ref[...]
    return [lane_value(row, slot) for slot in range(row.shape[1])]


def dyn_frames(bank, last_frame):
    found = [jnp.int32(0)] * (len(bank) - 2)
    seen = jnp.int32(0)
    for frame in bank:
        free = jnp.logical_and(frame != 0, frame != last_frame)
        for j in range(len(found)):
            found[j] = jnp.where(jnp.logical_and(free, seen == j), frame, found[j])
        seen = seen + free.astype(jnp.int32)
    return found


def place_of(frame, dyns):
    place = jnp.int32(len(dyns))
    for j, dyn in enumerate(dyns):
        place = jnp.where(frame == dyn, j, place)
    return place


def choose(out, take_first, first, second):
    @pl.when(take_first)
    def _():
        out[...] = first[...]

    @pl.when(jnp.logical_not(take_first))
    def _():
        out[...] = second[...]


def has_end(me, done, peers):
    return jnp.logical_or((me & ~done) == 0, (me | done) == peers - 1)


def has_dyn(me, frame, done):
    return ((me ^ (frame // FR_DEV)) & ~done) == 0


def by_role(me, even_value, odd_value):
    return jnp.where((me & 1) == 0, even_value, odd_value)


def load_kernel(count, stacked, *refs):
    arrays, outs, sems = refs[:count], refs[count:-1], refs[-1]
    rows = arrays[0].shape[0]
    targets = [outs[0].at[pl.ds(j * rows, rows)] for j in range(stacked)] + list(outs[1 if stacked else 0 :])
    copies = [pltpu.make_async_copy(ref, out, sems.at[j]) for j, (ref, out) in enumerate(zip(arrays, targets))]
    for copy in copies:
        copy.start()
    for copy in copies:
        copy.wait()


def pack(fields, width):
    code = jnp.int32(0)
    for j, field in enumerate(fields):
        code = code | (field.astype(jnp.int32) << (j * width))
    return code


def field(code, j, width):
    return (code >> (j * width)) & ((1 << width) - 1)


def code_of(codes_ref, row):
    return jnp.max(codes_ref[row : row + 1, :])


PICK, SUM, OWNED = range(3)
PLACE_BITS = 4
PREV, OWN, MEMORY, NEXT, PAIR = range(5)


def plan_kernel(
    peers,
    last_bits,
    bank_ref,
    index_ref,
    pair_index_ref,
    pose_ref,
    bias_ref,
    rows_ref,
    codes_ref,
):
    me = lax.axis_index("tm")
    last_frame = peers * FR_DEV - 1
    heads, _, row_count = rows_ref.shape
    bank = [bank_ref[0, slot] for slot in range(bank_ref.shape[1])]
    pair_ids = [bank_ref[0, pair_index_ref[0, m]] for m in range(MEM)]
    mem_ids = [bank_ref[0, index_ref[0, m]] for m in range(MEM)]

    own_ids = [me * FR_DEV + j for j in range(FR_DEV)]
    prev_ids = [jnp.maximum(own - FR_DEV, 0) for own in own_ids]
    next_ids = [jnp.minimum(own + FR_DEV, last_frame) for own in own_ids]
    pair_own_ids = [(me ^ 1) * FR_DEV + j for j in range(FR_DEV)]
    pieces = ((prev_ids, own_ids), (own_ids, own_ids), (mem_ids, own_ids), (own_ids, next_ids), (pair_ids, pair_own_ids))
    poses = [([pose_ref[f] for f in key_ids], [pose_ref[f] for f in query_ids]) for key_ids, query_ids in pieces]
    frame_of = lax.broadcasted_iota(jnp.int32, (1, row_count), 1) // (row_count // FR_DEV)
    for head in range(heads):
        for piece, (key_poses, query_poses) in enumerate(poses):
            for j, key_pose in enumerate(key_poses):
                row = jnp.zeros((1, row_count), F32)
                for a, query_pose in enumerate(query_poses):
                    value = bias_ref[head, query_pose, key_pose] * LOG2E
                    if piece == PREV:
                        value = jnp.where(me == 0, BLOCKED_LOGIT, value)
                    row = jnp.where(frame_of == a, value, row)
                rows_ref[head, piece * FR_DEV + j : piece * FR_DEV + j + 1, :] = row

    dyns = dyn_frames(bank, last_frame)
    bit = by_role(me, *last_bits)
    upper = (me & bit) != 0
    picks = []
    for frame in mem_ids + pair_ids:
        source = place_of(frame, dyns)
        local = jnp.where(frame == 0, jnp.logical_not(upper), upper)
        local = jnp.where(source < len(dyns), has_dyn(me, frame, (peers - 1) & ~bit), local)
        picks.append(source * 2 + local.astype(jnp.int32))
    far = jnp.where(upper, 0, last_frame)
    sums = [jnp.where(frame == far, len(dyns) + 1, place_of(frame, dyns)) for frame in mem_ids + pair_ids]
    owned = []
    for group in (me, me ^ 1):
        for j in range(FR_DEV):
            frame = group * FR_DEV + j
            place = place_of(frame, dyns)
            named = jnp.logical_or(place < len(dyns), jnp.logical_or(frame == 0, frame == last_frame))
            owned.append(place * 2 + named.astype(jnp.int32))
    lanes = codes_ref.shape[1]
    for row, code in ((PICK, pack(picks, PLACE_BITS)), (SUM, pack(sums, PLACE_BITS)), (OWNED, pack(owned, PLACE_BITS))):
        codes_ref[row : row + 1, :] = jnp.full((1, lanes), code, jnp.int32)


def release_kernel(value_ref, direct_keys, values_out, keys_out):
    values_out[...] = value_ref[...]
    keys_out[...] = direct_keys[...]


def split_kernel(peers, bank_ref, key_ref, value_ref, pair_keys, pair_values, out_ref):
    me = lax.axis_index("tm")
    frame_len, half_width = out_ref.shape[2:]
    dyns = dyn_frames(bank_of(bank_ref), peers * FR_DEV - 1)
    places = [(has_dyn(me, dyn, 0), dyn % FR_DEV) for dyn in dyns]
    places.append((has_end(me, 0, peers), jnp.where(me < peers // 2, 0, FR_DEV - 1)))
    for j, (local, frame) in enumerate(places):
        for role in range(2):
            for sources, taken in (((key_ref, value_ref), local), ((pair_keys, pair_values), jnp.logical_not(local))):

                @pl.when(jnp.logical_and((me & 1) == role, taken))
                def _(sources=sources, j=j, frame=frame, role=role):
                    part = pl.ds(pl.multiple_of(frame * frame_len, frame_len), frame_len)
                    for kind, source in enumerate(sources):
                        out_ref[j, kind] = source[part, role * half_width : (role + 1) * half_width]


def step_kernel(peers, even_done, odd_done, bank_ref, mine_ref, got_ref, out_ref):
    me = lax.axis_index("tm")
    done = by_role(me, even_done, odd_done)
    dyns = dyn_frames(bank_of(bank_ref), peers * FR_DEV - 1)
    flags = [has_dyn(me, dyn, done) for dyn in dyns] + [has_end(me, done, peers)]
    for j, flag in enumerate(flags):
        choose(out_ref.at[j], flag, mine_ref.at[j], got_ref.at[j])


def pick_kernel(codes_ref, mine_ref, got_ref, own_out, pair_out):
    code = code_of(codes_ref, PICK)
    for o, out in enumerate((own_out, pair_out)):
        for m in range(MEM):
            pick = field(code, o * MEM + m, PLACE_BITS)
            source = pick >> 1
            choose(out.at[m], (pick & 1) != 0, mine_ref.at[source], got_ref.at[source])


def dot(a, b, left, right):
    return lax.dot_general(a, b, (((left,), (right,)), ((), ())), preferred_element_type=F32)


def logits_of(keys, query, rows_ref, head, piece):
    frame_len = query.shape[0] // FR_DEV
    raw = dot(keys, query, 1, 1) * (FACTOR * LOG2E)
    parts = []
    for j in range(FR_DEV):
        row = piece * FR_DEV + j
        parts.append(raw[j * frame_len : (j + 1) * frame_len] + rows_ref[head, row : row + 1, :])
    return jnp.concatenate(parts, axis=0)


def joined_parts(joined_ref, cols):
    rows = joined_ref.shape[0] // 2 // DEPTH * DEPTH
    return joined_ref[0:rows, cols], joined_ref[rows : 2 * rows, cols]


def head_cols(head):
    return pl.ds(head * DEPTH, DEPTH)


def part_of(logits, slopes):
    peak = jnp.max(logits, axis=0, keepdims=True)
    exps = jnp.exp2(logits - peak)
    return peak, jnp.sum(exps, axis=0, keepdims=True), jnp.sum(exps * slopes, axis=0, keepdims=True)


def merged(left, right):
    peak = jnp.maximum(left[0], right[0])
    scales = [jnp.exp2(part[0] - peak) for part in (left, right)]
    return peak, *(left[j] * scales[0] + right[j] * scales[1] for j in (1, 2))


def load_part(ref, head):
    return tuple(ref[head, j : j + 1, :] for j in range(3))


def store_part(ref, head, part):
    for j, row in enumerate(part):
        ref[head, j : j + 1, :] = row


def prev_parts(peers, direct_keys, relayed_keys, outer_values, pair_keys, pair_values, cols):
    even = (lax.axis_index("tm") & 1) == 0
    keys = jnp.where(through_relay(1, 1, peers), relayed_keys[:, cols], direct_keys[:, cols])
    parts = zip((keys, outer_values[:, cols]), (pair_keys[:, cols], pair_values[:, cols]))
    return tuple(jnp.where(even, outer, pair) for outer, pair in parts)


def stats_kernel(
    peers,
    rows_ref,
    queries_ref,
    direct_keys,
    relayed_keys,
    outer_values,
    pair_keys,
    pair_values,
    key_ref,
    value_ref,
    part_ref,
    queries_out,
    cotangent_out,
):
    heads = queries_ref.shape[1] // DEPTH
    rows = queries_out.shape[0]
    queries_out[...] = queries_ref[0:rows]
    cotangent_out[...] = queries_ref[rows : 2 * rows]

    def products(head):
        cols = head_cols(head)
        query, cotangent = joined_parts(queries_ref, cols)
        prev = prev_parts(peers, direct_keys, relayed_keys, outer_values, pair_keys, pair_values, cols)
        pieces = ((PREV, prev), (OWN, (key_ref[:, cols], value_ref[:, cols])))
        return [
            (logits_of(keys, query, rows_ref, head, piece), dot(values, cotangent, 1, 1))
            for piece, (keys, values) in pieces
        ]

    ahead = products(0)
    for head in range(heads):
        now = ahead
        if head + 1 < heads:
            ahead = products(head + 1)
        store_part(part_ref, head, merged(*(part_of(*piece) for piece in now)))


def rounded(part, logits, slopes):
    peak, total, spread = merged(part, part_of(logits, slopes))
    inverse = 1.0 / total
    stats = peak, inverse, spread * inverse
    return stats, *weights_of(stats, logits, slopes)


def weights_of(stats, logits, slopes):
    peak, inverse, spread = stats
    probs = jnp.exp2(logits - peak) * inverse
    return probs.astype(BF16), (probs * (slopes - spread)).astype(BF16)


def memory_kernel(
    codes_ref, rows_ref, part_ref, pair_part_ref, own_queries, pair_queries, own_mem, pair_mem, keep_ref, send_ref
):
    role = lax.axis_index("tm") & 1
    code = code_of(codes_ref, SUM)
    frame_len, half_width = own_mem.shape[2:]
    half = half_width // DEPTH
    groups = ((own_queries, own_mem, part_ref, MEMORY), (pair_queries, pair_mem, pair_part_ref, PAIR))
    work = [(g, local) for local in range(half) for g in range(len(groups))]
    keep_ref[...] = jnp.zeros(keep_ref.shape, F32)

    def operands(g, local):
        cols = pl.ds(pl.multiple_of((role * half + local) * DEPTH, DEPTH), DEPTH)
        return joined_parts(groups[g][0], cols)

    def products(g, local):
        _, mem, _, piece = groups[g]
        query, cotangent = operands(g, local)
        keys, values = (mem[:, kind, :, head_cols(local)].reshape(MEM * frame_len, DEPTH) for kind in range(2))
        return logits_of(keys, query, rows_ref, role * half + local, piece), dot(values, cotangent, 1, 1)

    def add(g, local, _, weights, dlogits):
        query, cotangent = operands(g, local)
        terms = (dot(dlogits, query, 1, 0) * FACTOR, dot(weights, cotangent, 1, 0))
        for m in range(MEM):
            place = field(code, g * MEM + m, PLACE_BITS)
            for kind, term in enumerate(terms):
                part = term[m * frame_len : (m + 1) * frame_len].astype(BF16).astype(F32)
                keep_ref[place, kind, :, head_cols(local)] += part

    ahead = products(*work[0])
    behind = None
    for j, (g, local) in enumerate(work):
        now = ahead
        if j + 1 < len(work):
            ahead = products(*work[j + 1])
        if behind is not None:
            add(*work[j - 1], *behind)
        behind = rounded(load_part(groups[g][2], role * half + local), *now)
    add(*work[-1], *behind)
    kept = send_ref.shape[0]
    for place in range(kept):
        send_ref[place] = keep_ref[place if place + 1 < kept else kept].astype(BF16)


def next_kernel(
    peers,
    rows_ref,
    stats_ref,
    pair_queries,
    outer_queries,
    direct_cotangent,
    relayed_cotangent,
    key_ref,
    value_ref,
    term_ref,
    sum_ref,
):
    even = (lax.axis_index("tm") & 1) == 0
    relayed = through_relay(-1, 2, peers)
    heads = pair_queries.shape[1] // DEPTH

    def operands(head):
        cols = head_cols(head)
        cotangent = jnp.where(relayed, relayed_cotangent[:, cols], direct_cotangent[:, cols])
        outer = outer_queries[:, cols], cotangent
        return [jnp.where(even, a, b) for a, b in zip(joined_parts(pair_queries, cols), outer)]

    def products(head):
        query, cotangent = operands(head)
        keys, values = key_ref[:, head_cols(head)], value_ref[:, head_cols(head)]
        return logits_of(keys, query, rows_ref, head, NEXT), dot(values, cotangent, 1, 1)

    ahead = products(0)
    for head in range(heads):
        now = ahead
        if head + 1 < heads:
            ahead = products(head + 1)
        weights, dlogits = weights_of(load_part(stats_ref, head), *now)
        query, cotangent = operands(head)
        cols = head_cols(head)
        sum_ref[0, :, cols] = term_ref[0, :, cols] + dot(dlogits, query, 1, 0) * FACTOR
        sum_ref[1, :, cols] = term_ref[1, :, cols] + dot(weights, cotangent, 1, 0)


def memory_parts(own_mem, other_mem, head):
    role = lax.axis_index("tm") & 1
    frame_len, half_width = own_mem.shape[2:]
    half = half_width // DEPTH
    cols = head_cols(head % half)
    return [
        jnp.where(role == head // half, own_mem[:, kind, :, cols], other_mem[:, kind, :, cols]).reshape(
            MEM * frame_len, DEPTH
        )
        for kind in range(2)
    ]


def own_kernel(rows_ref, part_ref, queries_ref, key_ref, value_ref, own_mem, other_mem, term_ref, stats_ref):
    heads = queries_ref.shape[1] // DEPTH

    def products(head):
        cols = head_cols(head)
        query, cotangent = joined_parts(queries_ref, cols)
        own = key_ref[:, cols], value_ref[:, cols]
        pieces = ((OWN, own), (MEMORY, memory_parts(own_mem, other_mem, head)))
        return [
            (logits_of(keys, query, rows_ref, head, piece), dot(values, cotangent, 1, 1))
            for piece, (keys, values) in pieces
        ]

    ahead = products(0)
    for head in range(heads):
        own, memory = ahead
        if head + 1 < heads:
            ahead = products(head + 1)
        cols = head_cols(head)
        query, cotangent = joined_parts(queries_ref, cols)
        peak, total, spread = merged(load_part(part_ref, head), part_of(*memory))
        inverse = 1.0 / total
        stats = peak, inverse, spread * inverse
        store_part(stats_ref, head, stats)
        weights, dlogits = weights_of(stats, *own)
        term_ref[0, :, cols] = dot(dlogits, query, 1, 0) * FACTOR
        term_ref[1, :, cols] = dot(weights, cotangent, 1, 0)


def attend_kernel(
    peers,
    rows_ref,
    stats_ref,
    queries_ref,
    direct_keys,
    relayed_keys,
    outer_values,
    pair_keys,
    pair_values,
    key_ref,
    value_ref,
    own_mem,
    other_mem,
    attended_ref,
    grad_query_ref,
    mark_ref,
):
    mark_ref[...] = jnp.zeros(mark_ref.shape, F32)
    heads = queries_ref.shape[1] // DEPTH

    def pieces(head):
        cols = head_cols(head)
        prev = prev_parts(peers, direct_keys, relayed_keys, outer_values, pair_keys, pair_values, cols)
        return (PREV, prev), (OWN, (key_ref[:, cols], value_ref[:, cols])), (MEMORY, memory_parts(own_mem, other_mem, head))

    def products(head):
        query, cotangent = joined_parts(queries_ref, head_cols(head))
        return [
            (logits_of(keys, query, rows_ref, head, piece), dot(values, cotangent, 1, 1))
            for piece, (keys, values) in pieces(head)
        ]

    ahead = products(0)
    for head in range(heads):
        now = ahead
        if head + 1 < heads:
            ahead = products(head + 1)
        cols = head_cols(head)
        stats = load_part(stats_ref, head)
        attended = grad_query = 0.0
        for (_, (keys, values)), piece in zip(pieces(head), now):
            weights, dlogits = weights_of(stats, *piece)
            attended += dot(values, weights, 0, 0)
            grad_query += dot(keys, dlogits, 0, 0)
        attended_ref[:, cols] = attended.T.astype(BF16)
        grad_query_ref[:, cols] = (grad_query * FACTOR).T.astype(BF16)


def add_kernel(keep_ref, got_ref, out_ref, send_ref):
    value = keep_ref[0 : got_ref.shape[0]] + got_ref[...].astype(F32)
    out_ref[...] = value
    send_ref[...] = value.astype(BF16)


def pass_kernel(in_ref, out_ref):
    out_ref[...] = in_ref[...]


def owned_kernel(codes_ref, keep_ref, got_ref, mine_ref, pair_ref):
    code = code_of(codes_ref, OWNED)
    for o, out in enumerate((mine_ref, pair_ref)):
        for j in range(FR_DEV):
            owned = field(code, o * FR_DEV + j, PLACE_BITS)
            place = owned >> 1
            named = (owned & 1) != 0

            @pl.when(named)
            def _(out=out, j=j, place=place):
                value = keep_ref[place] + got_ref[place].astype(F32)
                out[j] = value.astype(out.dtype)

            @pl.when(jnp.logical_not(named))
            def _(out=out, j=j):
                out[j] = jnp.zeros(out.shape[1:], out.dtype)


def final_kernel(own_ref, mine_ref, got_ref, grad_key_ref, grad_value_ref):
    role = lax.axis_index("tm") & 1
    frame_len, half_width = mine_ref.shape[2:]
    for kind, out in enumerate((grad_key_ref, grad_value_ref)):
        for j in range(FR_DEV):
            rows = pl.ds(j * frame_len, frame_len)
            for half in range(2):
                cols = pl.ds(half * half_width, half_width)
                bank = jnp.where(role == half, mine_ref[j, kind], got_ref[j, kind].astype(F32))
                out[rows, cols] = (own_ref[kind, rows, cols] + bank).astype(BF16)


def body(
    query_states,
    key_states,
    value_states,
    grad_out,
    camera_pose,
    pose_bias,
    memory_index,
    bank_frames,
):
    row_count, width = query_states.shape
    frame_len = row_count // FR_DEV
    heads = pose_bias.shape[0]
    slots = bank_frames.shape[0]
    peers = lax.axis_size("tm")
    bits = [1 << i for i in range(1, peers.bit_length() - 1)]
    turns = list(zip(bits, bits[::-1]))
    piece_flops = 2 * row_count * row_count * width
    bank_frames = bank_frames.reshape(1, slots)
    last_bits = turns[-1]

    def load(outs, arrays, name, stacked=0, after=()):
        def run(*refs):
            load_kernel(len(arrays), stacked, *refs[: len(arrays)], *refs[len(arrays) + len(after) :])

        return pl.pallas_call(
            run,
            out_shape=outs,
            in_specs=[pl.BlockSpec(memory_space=pltpu.HBM)] * len(arrays) + [ANY] * len(after),
            out_specs=[VMEM] * len(outs),
            scratch_shapes=[pltpu.SemaphoreType.DMA((len(arrays),))],
            compiler_params=pltpu.CompilerParams(vmem_limit_bytes=VMEM_LIMIT),
            name=name,
        )(*(pltpu.with_memory_space_constraint(array, pltpu.HBM) for array in arrays), *after)

    half_width = width // 2
    pair = [swap(array, 1, 1, peers) for array in (key_states, value_states)]
    rows_shape = shape(BF16, row_count, width)
    keys, values, bank = load(
        [rows_shape, rows_shape, shape(jnp.int32, 1, slots)], [key_states, value_states, bank_frames], "load"
    )
    direct_keys = shift_first(keys, 1, 1, peers)
    held = shape(BF16, slots - 1, 2, frame_len, half_width)
    sums = shape(F32, slots - 1, 2, frame_len, half_width)
    (mine,) = call(functools.partial(split_kernel, peers), [held], [bank, keys, values, *pair], name="split")
    queries, index = load(
        [shape(BF16, 2 * row_count, width), shape(jnp.int32, 1, MEM)],
        [query_states, grad_out, memory_index],
        "load_queries",
        stacked=2,
        after=[mine],
    )
    pair_index = swap(index, 1, 1, peers)
    pair_queries = swap(queries, 1, 1, peers)

    bias_rows = -(-(5 * FR_DEV) // 8) * 8
    rows, codes = call(
        functools.partial(plan_kernel, peers, last_bits),
        [shape(F32, heads, bias_rows, row_count), shape(jnp.int32, 8, 128)],
        [],
        scalars=[bank_frames, memory_index, pair_index, camera_pose, pose_bias],
        name="plan",
    )
    values_out, keys_out = call(
        release_kernel,
        [rows_shape] * 2,
        [values, direct_keys],
        after=[codes],
        flops=HIDING * piece_flops,
        name="release",
    )
    outer = [direct_keys, shift_second(keys_out, 1, 1, peers), shift(values_out, 1, 1, peers)]
    even_done = odd_done = 1
    for step, (even_bit, odd_bit) in enumerate(turns):
        got = swap(mine, even_bit, odd_bit, peers)
        if step + 1 < len(turns):
            kernel = functools.partial(step_kernel, peers, even_done, odd_done)
            after = [codes, pair_queries]
            (mine,) = call(kernel, [held], [bank, mine, got], after=after, name="step")
        even_done |= even_bit
        odd_done |= odd_bit

    stats = shape(F32, heads, 8, row_count)
    part, queries_out, cotangent_out = call(
        functools.partial(stats_kernel, peers),
        [stats] + [shape(BF16, row_count, width)] * 2,
        [rows, queries, *outer, *pair, keys, values],
        flops=HIDING * piece_flops,
        name="stats",
    )
    pair_part = swap(part, 1, 1, peers)
    next_queries = shift(queries_out, -1, 2, peers)
    direct_cotangent = shift_first(cotangent_out, -1, 2, peers)
    chosen = shape(BF16, MEM, 2, frame_len, half_width)
    own_mem, pair_mem = call(pick_kernel, [chosen] * 2, [codes, mine, got], name="pick")
    keep, send = call(
        memory_kernel,
        [shape(F32, slots, 2, frame_len, half_width), held],
        [codes, rows, part, pair_part, queries, pair_queries, own_mem, pair_mem],
        flops=HIDING * piece_flops,
        name="memory",
    )
    other_mem = swap(pair_mem, 1, 1, peers)
    pair_sums = shape(F32, 2, row_count, width)
    own_terms, stats_all = call(
        own_kernel,
        [pair_sums, stats],
        [rows, part, queries, keys, values, own_mem, other_mem],
        after=[send],
        flops=HIDING * piece_flops,
        name="own",
    )
    next_stats = lax.ppermute(stats_all, "tm", [(i, i - 1) for i in range(1, peers)])
    (passed_on,) = call(
        pass_kernel, [shape(BF16, row_count, width)], [direct_cotangent], after=[own_terms], name="pass_on"
    )
    relayed_cotangent = shift_second(passed_on, -1, 2, peers)
    (own,) = call(
        functools.partial(next_kernel, peers),
        [pair_sums],
        [rows, next_stats, pair_queries, next_queries, direct_cotangent, relayed_cotangent, keys, values, own_terms],
        flops=HIDING * piece_flops,
        name="next",
    )
    for step, (even_bit, odd_bit) in enumerate(turns[::-1]):
        got = swap(send, even_bit, odd_bit, peers)
        if step + 1 < len(turns):
            after = [own_terms, next_queries]
            keep, send = call(add_kernel, [sums, held], [keep, got], after=after, name="add")
    attended, grad_query, mark = call(
        functools.partial(attend_kernel, peers),
        [shape(BF16, row_count, width)] * 2 + [shape(F32, 8, 128)],
        [rows, stats_all, queries, *outer, *pair, keys, values, own_mem, other_mem],
        after=[send],
        flops=HIDING * piece_flops,
        name="attend",
    )
    owned_mine, owned_send = call(
        owned_kernel,
        [shape(F32, FR_DEV, 2, frame_len, half_width), shape(BF16, FR_DEV, 2, frame_len, half_width)],
        [codes, keep, got],
        after=[own, mark],
        name="owned",
    )
    owned_got = swap(owned_send, 1, 1, peers)
    grad_key, grad_value = call(
        final_kernel, [shape(BF16, row_count, width)] * 2, [own, owned_mine, owned_got], name="final"
    )
    return (attended, grad_query, grad_key, grad_value)


def solution(mesh):
    rows = P(("traj", "tm"), None)
    in_specs = (rows, rows, rows, rows, P("traj"), P(), rows, P("traj"))
    return jax.shard_map(body, mesh=mesh, in_specs=in_specs, out_specs=(rows,) * 4, check_vma=False)
```

```python
import functools
import math

import jax
import jax.numpy as jnp
from jax import lax
from jax.experimental import pallas as pl
from jax.experimental.pallas import tpu as pltpu
from jax.sharding import PartitionSpec as P

FR_DEV = 2
MEM = 2
DEPTH = 128
TAIL = 16

BLOCKED_LOGIT = -1e30
LOG2E = math.log2(math.e)
FACTOR = 1.0 / math.sqrt(DEPTH)

SMEM = pl.BlockSpec(memory_space=pltpu.SMEM)
VMEM = pl.BlockSpec(memory_space=pltpu.VMEM)
ANY = pl.BlockSpec(memory_space=pl.ANY)
HIDING = 200
VMEM_LIMIT = 16 * 1024 * 1024
BF16, F32 = jnp.bfloat16, jnp.float32


def shape(dtype, *dims):
    return jax.ShapeDtypeStruct(dims, dtype)


def call(kernel, outs, arrays, scalars=(), after=(), flops=0, name=None):
    count = len(scalars) + len(arrays)

    def run(*refs):
        kernel(*refs[:count], *refs[count + len(after) :])

    return pl.pallas_call(
        run,
        out_shape=outs,
        in_specs=[SMEM] * len(scalars) + [VMEM] * len(arrays) + [ANY] * len(after),
        out_specs=[VMEM] * len(outs),
        compiler_params=pltpu.CompilerParams(vmem_limit_bytes=VMEM_LIMIT),
        cost_estimate=pl.CostEstimate(flops=flops, bytes_accessed=0, transcendentals=0) if flops else None,
        name=name,
    )(*scalars, *arrays, *after)


def swap(block, even_bit, odd_bit, peers):
    return lax.ppermute(block, "tm", [(i, i ^ (odd_bit if i & 1 else even_bit)) for i in range(peers)])


def shift(block, by, start, peers):
    pairs = [(i, i + by) for i in range(start, peers, 2) if 0 <= i + by < peers]
    return lax.ppermute(block, "tm", pairs)


def relays_of(by, start, peers):
    pairs = [(i, i + by) for i in range(start, peers, 2) if 0 <= i + by < peers]
    return {(i, j): i ^ 4 for i, j in pairs if peers == 8 and (i ^ j) >> 1 == 3}


def shift_first(block, by, start, peers):
    relays = relays_of(by, start, peers)
    pairs = [(i, i + by) for i in range(start, peers, 2) if 0 <= i + by < peers]
    return lax.ppermute(block, "tm", [(i, relays.get((i, j), j)) for i, j in pairs])


def shift_second(block, by, start, peers):
    pairs = [(relay, j) for (_, j), relay in relays_of(by, start, peers).items()]
    return lax.ppermute(block, "tm", pairs) if pairs else block


def through_relay(by, start, peers):
    me = lax.axis_index("tm")
    return functools.reduce(jnp.logical_or, [me == j for _, j in relays_of(by, start, peers)], me < 0)


def lane_value(row, lane):
    lanes = lax.broadcasted_iota(jnp.int32, row.shape, 1)
    return jnp.max(jnp.where(lanes == lane, row, 0))


def bank_of(bank_ref):
    row = bank_ref[...]
    return [lane_value(row, slot) for slot in range(row.shape[1])]


def dyn_frames(bank, last_frame):
    found = [jnp.int32(0)] * (len(bank) - 2)
    seen = jnp.int32(0)
    for frame in bank:
        free = jnp.logical_and(frame != 0, frame != last_frame)
        for j in range(len(found)):
            found[j] = jnp.where(jnp.logical_and(free, seen == j), frame, found[j])
        seen = seen + free.astype(jnp.int32)
    return found


def place_of(frame, dyns):
    place = jnp.int32(len(dyns))
    for j, dyn in enumerate(dyns):
        place = jnp.where(frame == dyn, j, place)
    return place


def choose(out, take_first, first, second):
    @pl.when(take_first)
    def _():
        out[...] = first[...]

    @pl.when(jnp.logical_not(take_first))
    def _():
        out[...] = second[...]


def has_end(me, done, peers):
    return jnp.logical_or((me & ~done) == 0, (me | done) == peers - 1)


def has_dyn(me, frame, done):
    return ((me ^ (frame // FR_DEV)) & ~done) == 0


def by_role(me, even_value, odd_value):
    return jnp.where((me & 1) == 0, even_value, odd_value)


def join_kernel(index_ref, key_ref, value_ref, joined_ref, index_buf, sems):
    rows = key_ref.shape[0]
    copies = [
        pltpu.make_async_copy(index_ref, index_buf, sems.at[0]),
        pltpu.make_async_copy(key_ref, joined_ref.at[pl.ds(0, rows)], sems.at[1]),
        pltpu.make_async_copy(value_ref, joined_ref.at[pl.ds(rows, rows)], sems.at[2]),
    ]
    for copy in copies:
        copy.start()
    copies[0].wait()
    width = joined_ref.shape[1]
    lane = lax.broadcasted_iota(jnp.int32, (TAIL, width), 1) // DEPTH
    tail = jnp.zeros((TAIL, width), jnp.int32)
    for m in range(MEM):
        tail = jnp.where(lane == m, index_buf[0:1, m : m + 1], tail)
    joined_ref[2 * rows : 2 * rows + TAIL, :] = tail.astype(F32).astype(BF16)
    copies[1].wait()
    copies[2].wait()


def join_queries_kernel(query_ref, cotangent_ref, joined_ref, sems):
    rows = query_ref.shape[0]
    copies = [
        pltpu.make_async_copy(ref, joined_ref.at[pl.ds(j * rows, rows)], sems.at[j])
        for j, ref in enumerate((query_ref, cotangent_ref))
    ]
    for copy in copies:
        copy.start()
    for copy in copies:
        copy.wait()


def pack(fields, width):
    code = jnp.int32(0)
    for j, field in enumerate(fields):
        code = code | (field.astype(jnp.int32) << (j * width))
    return code


def field(code, j, width):
    return (code >> (j * width)) & ((1 << width) - 1)


def code_of(codes_ref, row):
    return jnp.max(codes_ref[row : row + 1, :])


PICK, SUM, OWNED = range(3)
PLACE_BITS = 4
PREV, OWN, MEMORY, NEXT, PAIR = range(5)


def plan_kernel(
    peers,
    last_bits,
    bank_ref,
    index_ref,
    pose_ref,
    bias_ref,
    pair_ref,
    rows_ref,
    codes_ref,
):
    me = lax.axis_index("tm")
    last_frame = peers * FR_DEV - 1
    heads, _, row_count = rows_ref.shape
    bank = [bank_ref[0, slot] for slot in range(bank_ref.shape[1])]
    tail = pair_ref.shape[0] - TAIL
    pair_ids = []
    for m in range(MEM):
        slot = jnp.max(pair_ref[tail : tail + TAIL, m * DEPTH : (m + 1) * DEPTH].astype(F32)).astype(jnp.int32)
        pair_ids.append(bank_ref[0, slot])
    mem_ids = [bank_ref[0, index_ref[0, m]] for m in range(MEM)]

    own_ids = [me * FR_DEV + j for j in range(FR_DEV)]
    prev_ids = [jnp.maximum(own - FR_DEV, 0) for own in own_ids]
    next_ids = [jnp.minimum(own + FR_DEV, last_frame) for own in own_ids]
    pair_own_ids = [(me ^ 1) * FR_DEV + j for j in range(FR_DEV)]
    pieces = ((prev_ids, own_ids), (own_ids, own_ids), (mem_ids, own_ids), (own_ids, next_ids), (pair_ids, pair_own_ids))
    poses = [([pose_ref[f] for f in key_ids], [pose_ref[f] for f in query_ids]) for key_ids, query_ids in pieces]
    frame_of = lax.broadcasted_iota(jnp.int32, (1, row_count), 1) // (row_count // FR_DEV)
    for head in range(heads):
        for piece, (key_poses, query_poses) in enumerate(poses):
            for j, key_pose in enumerate(key_poses):
                row = jnp.zeros((1, row_count), F32)
                for a, query_pose in enumerate(query_poses):
                    value = bias_ref[head, query_pose, key_pose] * LOG2E
                    if piece == PREV:
                        value = jnp.where(me == 0, BLOCKED_LOGIT, value)
                    row = jnp.where(frame_of == a, value, row)
                rows_ref[head, piece * FR_DEV + j : piece * FR_DEV + j + 1, :] = row

    dyns = dyn_frames(bank, last_frame)
    bit = by_role(me, *last_bits)
    upper = (me & bit) != 0
    picks = []
    for frame in mem_ids + pair_ids:
        source = place_of(frame, dyns)
        local = jnp.where(frame == 0, jnp.logical_not(upper), upper)
        local = jnp.where(source < len(dyns), has_dyn(me, frame, (peers - 1) & ~bit), local)
        picks.append(source * 2 + local.astype(jnp.int32))
    far = jnp.where(upper, 0, last_frame)
    sums = [jnp.where(frame == far, len(dyns) + 1, place_of(frame, dyns)) for frame in mem_ids + pair_ids]
    owned = []
    for group in (me, me ^ 1):
        for j in range(FR_DEV):
            frame = group * FR_DEV + j
            place = place_of(frame, dyns)
            named = jnp.logical_or(place < len(dyns), jnp.logical_or(frame == 0, frame == last_frame))
            owned.append(place * 2 + named.astype(jnp.int32))
    lanes = codes_ref.shape[1]
    for row, code in ((PICK, pack(picks, PLACE_BITS)), (SUM, pack(sums, PLACE_BITS)), (OWNED, pack(owned, PLACE_BITS))):
        codes_ref[row : row + 1, :] = jnp.full((1, lanes), code, jnp.int32)


def release_kernel(joined_ref, direct_keys, values_out, keys_out):
    rows = values_out.shape[0]
    values_out[...] = joined_ref[rows : 2 * rows, :]
    keys_out[...] = direct_keys[...]


def split_kernel(peers, bank_ref, mine_ref, pair_ref, out_ref):
    me = lax.axis_index("tm")
    frame_len, half_width = out_ref.shape[2:]
    dyns = dyn_frames(bank_of(bank_ref), peers * FR_DEV - 1)
    places = [(has_dyn(me, dyn, 0), dyn % FR_DEV) for dyn in dyns]
    places.append((has_end(me, 0, peers), jnp.where(me < peers // 2, 0, FR_DEV - 1)))
    for j, (local, frame) in enumerate(places):
        for role in range(2):
            for source, taken in ((mine_ref, local), (pair_ref, jnp.logical_not(local))):

                @pl.when(jnp.logical_and((me & 1) == role, taken))
                def _(source=source, j=j, frame=frame, role=role):
                    for kind in range(2):
                        start = pl.multiple_of((kind * FR_DEV + frame) * frame_len, frame_len)
                        out_ref[j, kind] = source[pl.ds(start, frame_len), role * half_width : (role + 1) * half_width]


def step_kernel(peers, even_done, odd_done, bank_ref, mine_ref, got_ref, out_ref):
    me = lax.axis_index("tm")
    done = by_role(me, even_done, odd_done)
    dyns = dyn_frames(bank_of(bank_ref), peers * FR_DEV - 1)
    flags = [has_dyn(me, dyn, done) for dyn in dyns] + [has_end(me, done, peers)]
    for j, flag in enumerate(flags):
        choose(out_ref.at[j], flag, mine_ref.at[j], got_ref.at[j])


def pick_kernel(codes_ref, mine_ref, got_ref, own_out, pair_out):
    code = code_of(codes_ref, PICK)
    for o, out in enumerate((own_out, pair_out)):
        for m in range(MEM):
            pick = field(code, o * MEM + m, PLACE_BITS)
            source = pick >> 1
            choose(out.at[m], (pick & 1) != 0, mine_ref.at[source], got_ref.at[source])


def dot(a, b, left, right):
    return lax.dot_general(a, b, (((left,), (right,)), ((), ())), preferred_element_type=F32)


def logits_of(keys, query, rows_ref, head, piece):
    frame_len = query.shape[0] // FR_DEV
    raw = dot(keys, query, 1, 1) * (FACTOR * LOG2E)
    parts = []
    for j in range(FR_DEV):
        row = piece * FR_DEV + j
        parts.append(raw[j * frame_len : (j + 1) * frame_len] + rows_ref[head, row : row + 1, :])
    return jnp.concatenate(parts, axis=0)


def joined_parts(joined_ref, cols):
    rows = joined_ref.shape[0] // 2 // DEPTH * DEPTH
    return joined_ref[0:rows, cols], joined_ref[rows : 2 * rows, cols]


def head_cols(head):
    return pl.ds(head * DEPTH, DEPTH)


def part_of(logits, slopes):
    peak = jnp.max(logits, axis=0, keepdims=True)
    exps = jnp.exp2(logits - peak)
    return peak, jnp.sum(exps, axis=0, keepdims=True), jnp.sum(exps * slopes, axis=0, keepdims=True)


def merged(left, right):
    peak = jnp.maximum(left[0], right[0])
    scales = [jnp.exp2(part[0] - peak) for part in (left, right)]
    return peak, *(left[j] * scales[0] + right[j] * scales[1] for j in (1, 2))


def load_part(ref, head):
    return tuple(ref[head, j : j + 1, :] for j in range(3))


def store_part(ref, head, part):
    for j, row in enumerate(part):
        ref[head, j : j + 1, :] = row


def prev_parts(peers, direct_keys, relayed_keys, outer_values, pair_ref, cols):
    even = (lax.axis_index("tm") & 1) == 0
    keys = jnp.where(through_relay(1, 1, peers), relayed_keys[:, cols], direct_keys[:, cols])
    parts = zip((keys, outer_values[:, cols]), joined_parts(pair_ref, cols))
    return tuple(jnp.where(even, outer, pair) for outer, pair in parts)


def stats_kernel(
    peers,
    rows_ref,
    queries_ref,
    direct_keys,
    outer_values,
    relayed_keys,
    pair_ref,
    own_ref,
    part_ref,
    queries_out,
    cotangent_out,
):
    heads = queries_ref.shape[1] // DEPTH
    rows = queries_out.shape[0]
    queries_out[...] = queries_ref[0:rows]
    cotangent_out[...] = queries_ref[rows : 2 * rows]

    def products(head):
        cols = head_cols(head)
        query, cotangent = joined_parts(queries_ref, cols)
        pieces = ((PREV, prev_parts(peers, direct_keys, relayed_keys, outer_values, pair_ref, cols)), (OWN, joined_parts(own_ref, cols)))
        return [
            (logits_of(keys, query, rows_ref, head, piece), dot(values, cotangent, 1, 1))
            for piece, (keys, values) in pieces
        ]

    ahead = products(0)
    for head in range(heads):
        now = ahead
        if head + 1 < heads:
            ahead = products(head + 1)
        store_part(part_ref, head, merged(*(part_of(*piece) for piece in now)))


def rounded(part, logits, slopes):
    peak, total, spread = merged(part, part_of(logits, slopes))
    inverse = 1.0 / total
    stats = peak, inverse, spread * inverse
    return stats, *weights_of(stats, logits, slopes)


def weights_of(stats, logits, slopes):
    peak, inverse, spread = stats
    probs = jnp.exp2(logits - peak) * inverse
    return probs.astype(BF16), (probs * (slopes - spread)).astype(BF16)


def memory_kernel(
    codes_ref, rows_ref, part_ref, pair_part_ref, own_queries, pair_queries, own_mem, pair_mem, keep_ref, send_ref
):
    role = lax.axis_index("tm") & 1
    code = code_of(codes_ref, SUM)
    frame_len, half_width = own_mem.shape[2:]
    half = half_width // DEPTH
    groups = ((own_queries, own_mem, part_ref, MEMORY), (pair_queries, pair_mem, pair_part_ref, PAIR))
    work = [(g, local) for local in range(half) for g in range(len(groups))]
    keep_ref[...] = jnp.zeros(keep_ref.shape, F32)

    def operands(g, local):
        cols = pl.ds(pl.multiple_of((role * half + local) * DEPTH, DEPTH), DEPTH)
        return joined_parts(groups[g][0], cols)

    def products(g, local):
        _, mem, _, piece = groups[g]
        query, cotangent = operands(g, local)
        keys, values = (mem[:, kind, :, head_cols(local)].reshape(MEM * frame_len, DEPTH) for kind in range(2))
        return logits_of(keys, query, rows_ref, role * half + local, piece), dot(values, cotangent, 1, 1)

    def add(g, local, _, weights, dlogits):
        query, cotangent = operands(g, local)
        terms = (dot(dlogits, query, 1, 0) * FACTOR, dot(weights, cotangent, 1, 0))
        for m in range(MEM):
            place = field(code, g * MEM + m, PLACE_BITS)
            for kind, term in enumerate(terms):
                part = term[m * frame_len : (m + 1) * frame_len].astype(BF16).astype(F32)
                keep_ref[place, kind, :, head_cols(local)] += part

    ahead = products(*work[0])
    behind = None
    for j, (g, local) in enumerate(work):
        now = ahead
        if j + 1 < len(work):
            ahead = products(*work[j + 1])
        if behind is not None:
            add(*work[j - 1], *behind)
        behind = rounded(load_part(groups[g][2], role * half + local), *now)
    add(*work[-1], *behind)
    kept = send_ref.shape[0]
    for place in range(kept):
        send_ref[place] = keep_ref[place if place + 1 < kept else kept].astype(BF16)


def next_kernel(
    peers,
    rows_ref,
    stats_ref,
    pair_queries,
    outer_queries,
    direct_cotangent,
    relayed_cotangent,
    own_ref,
    term_ref,
    sum_ref,
):
    even = (lax.axis_index("tm") & 1) == 0
    relayed = through_relay(-1, 2, peers)
    heads = pair_queries.shape[1] // DEPTH

    def operands(head):
        cols = head_cols(head)
        cotangent = jnp.where(relayed, relayed_cotangent[:, cols], direct_cotangent[:, cols])
        outer = outer_queries[:, cols], cotangent
        return [jnp.where(even, a, b) for a, b in zip(joined_parts(pair_queries, cols), outer)]

    def products(head):
        query, cotangent = operands(head)
        keys, values = joined_parts(own_ref, head_cols(head))
        return logits_of(keys, query, rows_ref, head, NEXT), dot(values, cotangent, 1, 1)

    ahead = products(0)
    for head in range(heads):
        now = ahead
        if head + 1 < heads:
            ahead = products(head + 1)
        weights, dlogits = weights_of(load_part(stats_ref, head), *now)
        query, cotangent = operands(head)
        cols = head_cols(head)
        sum_ref[0, :, cols] = term_ref[0, :, cols] + dot(dlogits, query, 1, 0) * FACTOR
        sum_ref[1, :, cols] = term_ref[1, :, cols] + dot(weights, cotangent, 1, 0)


def memory_parts(own_mem, other_mem, head):
    role = lax.axis_index("tm") & 1
    frame_len, half_width = own_mem.shape[2:]
    half = half_width // DEPTH
    cols = head_cols(head % half)
    return [
        jnp.where(role == head // half, own_mem[:, kind, :, cols], other_mem[:, kind, :, cols]).reshape(
            MEM * frame_len, DEPTH
        )
        for kind in range(2)
    ]


def own_kernel(rows_ref, part_ref, queries_ref, own_ref, own_mem, other_mem, term_ref, stats_ref):
    heads = queries_ref.shape[1] // DEPTH

    def products(head):
        query, cotangent = joined_parts(queries_ref, head_cols(head))
        pieces = ((OWN, joined_parts(own_ref, head_cols(head))), (MEMORY, memory_parts(own_mem, other_mem, head)))
        return [
            (logits_of(keys, query, rows_ref, head, piece), dot(values, cotangent, 1, 1))
            for piece, (keys, values) in pieces
        ]

    ahead = products(0)
    for head in range(heads):
        own, memory = ahead
        if head + 1 < heads:
            ahead = products(head + 1)
        cols = head_cols(head)
        query, cotangent = joined_parts(queries_ref, cols)
        peak, total, spread = merged(load_part(part_ref, head), part_of(*memory))
        inverse = 1.0 / total
        stats = peak, inverse, spread * inverse
        store_part(stats_ref, head, stats)
        weights, dlogits = weights_of(stats, *own)
        term_ref[0, :, cols] = dot(dlogits, query, 1, 0) * FACTOR
        term_ref[1, :, cols] = dot(weights, cotangent, 1, 0)


def attend_kernel(
    peers,
    rows_ref,
    stats_ref,
    queries_ref,
    direct_keys,
    outer_values,
    relayed_keys,
    pair_ref,
    own_ref,
    own_mem,
    other_mem,
    attended_ref,
    grad_query_ref,
    mark_ref,
):
    mark_ref[...] = jnp.zeros(mark_ref.shape, F32)
    heads = queries_ref.shape[1] // DEPTH

    def pieces(head):
        cols = head_cols(head)
        prev = prev_parts(peers, direct_keys, relayed_keys, outer_values, pair_ref, cols)
        return (PREV, prev), (OWN, joined_parts(own_ref, cols)), (MEMORY, memory_parts(own_mem, other_mem, head))

    def products(head):
        query, cotangent = joined_parts(queries_ref, head_cols(head))
        return [
            (logits_of(keys, query, rows_ref, head, piece), dot(values, cotangent, 1, 1))
            for piece, (keys, values) in pieces(head)
        ]

    ahead = products(0)
    for head in range(heads):
        now = ahead
        if head + 1 < heads:
            ahead = products(head + 1)
        cols = head_cols(head)
        stats = load_part(stats_ref, head)
        attended = grad_query = 0.0
        for (_, (keys, values)), piece in zip(pieces(head), now):
            weights, dlogits = weights_of(stats, *piece)
            attended += dot(values, weights, 0, 0)
            grad_query += dot(keys, dlogits, 0, 0)
        attended_ref[:, cols] = attended.T.astype(BF16)
        grad_query_ref[:, cols] = (grad_query * FACTOR).T.astype(BF16)


def add_kernel(keep_ref, got_ref, out_ref, send_ref):
    value = keep_ref[0 : got_ref.shape[0]] + got_ref[...].astype(F32)
    out_ref[...] = value
    send_ref[...] = value.astype(BF16)


def pass_kernel(in_ref, out_ref):
    out_ref[...] = in_ref[...]


def owned_kernel(codes_ref, keep_ref, got_ref, mine_ref, pair_ref):
    code = code_of(codes_ref, OWNED)
    for o, out in enumerate((mine_ref, pair_ref)):
        for j in range(FR_DEV):
            owned = field(code, o * FR_DEV + j, PLACE_BITS)
            place = owned >> 1
            named = (owned & 1) != 0

            @pl.when(named)
            def _(out=out, j=j, place=place):
                value = keep_ref[place] + got_ref[place].astype(F32)
                out[j] = value.astype(out.dtype)

            @pl.when(jnp.logical_not(named))
            def _(out=out, j=j):
                out[j] = jnp.zeros(out.shape[1:], out.dtype)


def final_kernel(own_ref, mine_ref, got_ref, grad_key_ref, grad_value_ref):
    role = lax.axis_index("tm") & 1
    frame_len, half_width = mine_ref.shape[2:]
    for kind, out in enumerate((grad_key_ref, grad_value_ref)):
        for j in range(FR_DEV):
            rows = pl.ds(j * frame_len, frame_len)
            for half in range(2):
                cols = pl.ds(half * half_width, half_width)
                bank = jnp.where(role == half, mine_ref[j, kind], got_ref[j, kind].astype(F32))
                out[rows, cols] = (own_ref[kind, rows, cols] + bank).astype(BF16)


def body(
    query_states,
    key_states,
    value_states,
    grad_out,
    camera_pose,
    pose_bias,
    memory_index,
    bank_frames,
):
    row_count, width = query_states.shape
    frame_len = row_count // FR_DEV
    heads = pose_bias.shape[0]
    slots = bank_frames.shape[0]
    peers = lax.axis_size("tm")
    bits = [1 << i for i in range(1, peers.bit_length() - 1)]
    turns = list(zip(bits, bits[::-1]))
    piece_flops = 2 * row_count * row_count * width
    bank_frames = bank_frames.reshape(1, slots)
    last_bits = turns[-1]

    def join(kernel, rows, arrays, scratch, name, after=()):
        def run(*refs):
            kernel(*refs[: len(arrays)], *refs[len(arrays) + len(after) :])

        return pl.pallas_call(
            run,
            out_shape=shape(BF16, rows, width),
            in_specs=[pl.BlockSpec(memory_space=pltpu.HBM)] * len(arrays) + [ANY] * len(after),
            out_specs=VMEM,
            scratch_shapes=[*scratch, pltpu.SemaphoreType.DMA((len(arrays),))],
            compiler_params=pltpu.CompilerParams(vmem_limit_bytes=VMEM_LIMIT),
            name=name,
        )(*(pltpu.with_memory_space_constraint(array, pltpu.HBM) for array in arrays), *after)

    joined = join(
        join_kernel,
        2 * row_count + TAIL,
        [memory_index, key_states, value_states],
        [pltpu.VMEM(memory_index.shape, jnp.int32)],
        "join",
    )
    half_width = width // 2
    direct_keys = shift_first(key_states, 1, 1, peers)
    pair = swap(joined, 1, 1, peers)
    held = shape(BF16, slots - 1, 2, frame_len, half_width)
    sums = shape(F32, slots - 1, 2, frame_len, half_width)
    (mine,) = call(functools.partial(split_kernel, peers), [held], [bank_frames, joined, pair], name="split")
    queries = join(join_queries_kernel, 2 * row_count, [query_states, grad_out], [], "join_queries", after=[mine])
    pair_queries = swap(queries, 1, 1, peers)

    bias_rows = -(-(5 * FR_DEV) // 8) * 8
    rows, codes = call(
        functools.partial(plan_kernel, peers, last_bits),
        [shape(F32, heads, bias_rows, row_count), shape(jnp.int32, 8, 128)],
        [pair],
        scalars=[bank_frames, memory_index, camera_pose, pose_bias],
        name="plan",
    )
    values_out, keys_out = call(
        release_kernel,
        [shape(BF16, row_count, width)] * 2,
        [joined, direct_keys],
        after=[codes],
        flops=HIDING * piece_flops,
        name="release",
    )
    outer = [direct_keys, shift(values_out, 1, 1, peers), shift_second(keys_out, 1, 1, peers)]
    even_done = odd_done = 1
    for step, (even_bit, odd_bit) in enumerate(turns):
        got = swap(mine, even_bit, odd_bit, peers)
        if step + 1 < len(turns):
            kernel = functools.partial(step_kernel, peers, even_done, odd_done)
            after = [codes, pair_queries]
            (mine,) = call(kernel, [held], [bank_frames, mine, got], after=after, name="step")
        even_done |= even_bit
        odd_done |= odd_bit

    stats = shape(F32, heads, 8, row_count)
    part, queries_out, cotangent_out = call(
        functools.partial(stats_kernel, peers),
        [stats] + [shape(BF16, row_count, width)] * 2,
        [rows, queries, *outer, pair, joined],
        flops=HIDING * piece_flops,
        name="stats",
    )
    pair_part = swap(part, 1, 1, peers)
    next_queries = shift(queries_out, -1, 2, peers)
    direct_cotangent = shift_first(cotangent_out, -1, 2, peers)
    chosen = shape(BF16, MEM, 2, frame_len, half_width)
    own_mem, pair_mem = call(pick_kernel, [chosen] * 2, [codes, mine, got], name="pick")
    keep, send = call(
        memory_kernel,
        [shape(F32, slots, 2, frame_len, half_width), held],
        [codes, rows, part, pair_part, queries, pair_queries, own_mem, pair_mem],
        flops=HIDING * piece_flops,
        name="memory",
    )
    other_mem = swap(pair_mem, 1, 1, peers)
    pair_sums = shape(F32, 2, row_count, width)
    own_terms, stats_all = call(
        own_kernel,
        [pair_sums, stats],
        [rows, part, queries, joined, own_mem, other_mem],
        after=[send],
        flops=HIDING * piece_flops,
        name="own",
    )
    next_stats = lax.ppermute(stats_all, "tm", [(i, i - 1) for i in range(1, peers)])
    (passed_on,) = call(
        pass_kernel, [shape(BF16, row_count, width)], [direct_cotangent], after=[own_terms], name="pass_on"
    )
    relayed_cotangent = shift_second(passed_on, -1, 2, peers)
    (own,) = call(
        functools.partial(next_kernel, peers),
        [pair_sums],
        [rows, next_stats, pair_queries, next_queries, direct_cotangent, relayed_cotangent, joined, own_terms],
        flops=HIDING * piece_flops,
        name="next",
    )
    for step, (even_bit, odd_bit) in enumerate(turns[::-1]):
        got = swap(send, even_bit, odd_bit, peers)
        if step + 1 < len(turns):
            after = [own_terms, next_queries]
            keep, send = call(add_kernel, [sums, held], [keep, got], after=after, name="add")
    attended, grad_query, mark = call(
        functools.partial(attend_kernel, peers),
        [shape(BF16, row_count, width)] * 2 + [shape(F32, 8, 128)],
        [rows, stats_all, queries, *outer, pair, joined, own_mem, other_mem],
        after=[send],
        flops=HIDING * piece_flops,
        name="attend",
    )
    owned_mine, owned_send = call(
        owned_kernel,
        [shape(F32, FR_DEV, 2, frame_len, half_width), shape(BF16, FR_DEV, 2, frame_len, half_width)],
        [codes, keep, got],
        after=[own, mark],
        name="owned",
    )
    owned_got = swap(owned_send, 1, 1, peers)
    grad_key, grad_value = call(
        final_kernel, [shape(BF16, row_count, width)] * 2, [own, owned_mine, owned_got], name="final"
    )
    return (attended, grad_query, grad_key, grad_value)


def solution(mesh):
    rows = P(("traj", "tm"), None)
    in_specs = (rows, rows, rows, rows, P("traj"), P(), rows, P("traj"))
    return jax.shard_map(body, mesh=mesh, in_specs=in_specs, out_specs=(rows,) * 4, check_vma=False)
```

```python
import functools
import math

import jax
import jax.numpy as jnp
from jax import lax
from jax.experimental import pallas as pl
from jax.experimental.pallas import tpu as pltpu
from jax.sharding import PartitionSpec as P

FR_DEV = 2
MEM = 2
DEPTH = 128
TAIL = 16

BLOCKED_LOGIT = -1e30
LOG2E = math.log2(math.e)
FACTOR = 1.0 / math.sqrt(DEPTH)

SMEM = pl.BlockSpec(memory_space=pltpu.SMEM)
VMEM = pl.BlockSpec(memory_space=pltpu.VMEM)
ANY = pl.BlockSpec(memory_space=pl.ANY)
HIDING = 200
VMEM_LIMIT = 16 * 1024 * 1024
BF16, F32 = jnp.bfloat16, jnp.float32


def shape(dtype, *dims):
    return jax.ShapeDtypeStruct(dims, dtype)


def call(kernel, outs, arrays, scalars=(), after=(), flops=0, name=None):
    count = len(scalars) + len(arrays)

    def run(*refs):
        kernel(*refs[:count], *refs[count + len(after) :])

    return pl.pallas_call(
        run,
        out_shape=outs,
        in_specs=[SMEM] * len(scalars) + [VMEM] * len(arrays) + [ANY] * len(after),
        out_specs=[VMEM] * len(outs),
        compiler_params=pltpu.CompilerParams(vmem_limit_bytes=VMEM_LIMIT),
        cost_estimate=pl.CostEstimate(flops=flops, bytes_accessed=0, transcendentals=0) if flops else None,
        name=name,
    )(*scalars, *arrays, *after)


def swap(block, even_bit, odd_bit, peers):
    return lax.ppermute(block, "tm", [(i, i ^ (odd_bit if i & 1 else even_bit)) for i in range(peers)])


def shift(block, by, start, peers):
    pairs = [(i, i + by) for i in range(start, peers, 2) if 0 <= i + by < peers]
    return lax.ppermute(block, "tm", pairs)


def relays_of(by, start, peers):
    pairs = [(i, i + by) for i in range(start, peers, 2) if 0 <= i + by < peers]
    return {(i, j): i ^ 4 for i, j in pairs if peers == 8 and (i ^ j) >> 1 == 3}


def shift_first(block, by, start, peers):
    relays = relays_of(by, start, peers)
    pairs = [(i, i + by) for i in range(start, peers, 2) if 0 <= i + by < peers]
    return lax.ppermute(block, "tm", [(i, relays.get((i, j), j)) for i, j in pairs])


def shift_second(block, by, start, peers):
    pairs = [(relay, j) for (_, j), relay in relays_of(by, start, peers).items()]
    return lax.ppermute(block, "tm", pairs) if pairs else block


def through_relay(by, start, peers):
    me = lax.axis_index("tm")
    return functools.reduce(jnp.logical_or, [me == j for _, j in relays_of(by, start, peers)], me < 0)


def lane_value(row, lane):
    lanes = lax.broadcasted_iota(jnp.int32, row.shape, 1)
    return jnp.max(jnp.where(lanes == lane, row, 0))


def bank_of(bank_ref):
    row = bank_ref[...]
    return [lane_value(row, slot) for slot in range(row.shape[1])]


def dyn_frames(bank, last_frame):
    found = [jnp.int32(0)] * (len(bank) - 2)
    seen = jnp.int32(0)
    for frame in bank:
        free = jnp.logical_and(frame != 0, frame != last_frame)
        for j in range(len(found)):
            found[j] = jnp.where(jnp.logical_and(free, seen == j), frame, found[j])
        seen = seen + free.astype(jnp.int32)
    return found


def place_of(frame, dyns):
    place = jnp.int32(len(dyns))
    for j, dyn in enumerate(dyns):
        place = jnp.where(frame == dyn, j, place)
    return place


def choose(out, take_first, first, second):
    @pl.when(take_first)
    def _():
        out[...] = first[...]

    @pl.when(jnp.logical_not(take_first))
    def _():
        out[...] = second[...]


def has_end(me, done, peers):
    return jnp.logical_or((me & ~done) == 0, (me | done) == peers - 1)


def has_dyn(me, frame, done):
    return ((me ^ (frame // FR_DEV)) & ~done) == 0


def by_role(me, even_value, odd_value):
    return jnp.where((me & 1) == 0, even_value, odd_value)


def join_kernel(index_ref, key_ref, value_ref, joined_ref, index_buf, sems):
    rows = key_ref.shape[0]
    copies = [
        pltpu.make_async_copy(index_ref, index_buf, sems.at[0]),
        pltpu.make_async_copy(key_ref, joined_ref.at[pl.ds(0, rows)], sems.at[1]),
        pltpu.make_async_copy(value_ref, joined_ref.at[pl.ds(rows, rows)], sems.at[2]),
    ]
    for copy in copies:
        copy.start()
    copies[0].wait()
    width = joined_ref.shape[1]
    lane = lax.broadcasted_iota(jnp.int32, (TAIL, width), 1) // DEPTH
    tail = jnp.zeros((TAIL, width), jnp.int32)
    for m in range(MEM):
        tail = jnp.where(lane == m, index_buf[0:1, m : m + 1], tail)
    joined_ref[2 * rows : 2 * rows + TAIL, :] = tail.astype(F32).astype(BF16)
    copies[1].wait()
    copies[2].wait()


def join_queries_kernel(query_ref, cotangent_ref, joined_ref, sems):
    rows = query_ref.shape[0]
    copies = [
        pltpu.make_async_copy(ref, joined_ref.at[pl.ds(j * rows, rows)], sems.at[j])
        for j, ref in enumerate((query_ref, cotangent_ref))
    ]
    for copy in copies:
        copy.start()
    for copy in copies:
        copy.wait()


def pack(fields, width):
    code = jnp.int32(0)
    for j, field in enumerate(fields):
        code = code | (field.astype(jnp.int32) << (j * width))
    return code


def field(code, j, width):
    return (code >> (j * width)) & ((1 << width) - 1)


def code_of(codes_ref, row):
    return jnp.max(codes_ref[row : row + 1, :])


PICK, SUM, OWNED = range(3)
PLACE_BITS = 4
PREV, OWN, MEMORY, NEXT, PAIR = range(5)


def plan_kernel(
    peers,
    last_bits,
    bank_ref,
    index_ref,
    pose_ref,
    bias_ref,
    pair_ref,
    rows_ref,
    codes_ref,
):
    me = lax.axis_index("tm")
    last_frame = peers * FR_DEV - 1
    heads, _, row_count = rows_ref.shape
    bank = [bank_ref[0, slot] for slot in range(bank_ref.shape[1])]
    tail = pair_ref.shape[0] - TAIL
    pair_ids = []
    for m in range(MEM):
        slot = jnp.max(pair_ref[tail : tail + TAIL, m * DEPTH : (m + 1) * DEPTH].astype(F32)).astype(jnp.int32)
        pair_ids.append(bank_ref[0, slot])
    mem_ids = [bank_ref[0, index_ref[0, m]] for m in range(MEM)]

    own_ids = [me * FR_DEV + j for j in range(FR_DEV)]
    prev_ids = [jnp.maximum(own - FR_DEV, 0) for own in own_ids]
    next_ids = [jnp.minimum(own + FR_DEV, last_frame) for own in own_ids]
    pair_own_ids = [(me ^ 1) * FR_DEV + j for j in range(FR_DEV)]
    pieces = ((prev_ids, own_ids), (own_ids, own_ids), (mem_ids, own_ids), (own_ids, next_ids), (pair_ids, pair_own_ids))
    poses = [([pose_ref[f] for f in key_ids], [pose_ref[f] for f in query_ids]) for key_ids, query_ids in pieces]
    frame_of = lax.broadcasted_iota(jnp.int32, (1, row_count), 1) // (row_count // FR_DEV)
    for head in range(heads):
        for piece, (key_poses, query_poses) in enumerate(poses):
            for j, key_pose in enumerate(key_poses):
                row = jnp.zeros((1, row_count), F32)
                for a, query_pose in enumerate(query_poses):
                    value = bias_ref[head, query_pose, key_pose] * LOG2E
                    if piece == PREV:
                        value = jnp.where(me == 0, BLOCKED_LOGIT, value)
                    row = jnp.where(frame_of == a, value, row)
                rows_ref[head, piece * FR_DEV + j : piece * FR_DEV + j + 1, :] = row

    dyns = dyn_frames(bank, last_frame)
    bit = by_role(me, *last_bits)
    upper = (me & bit) != 0
    picks = []
    for frame in mem_ids + pair_ids:
        source = place_of(frame, dyns)
        local = jnp.where(frame == 0, jnp.logical_not(upper), upper)
        local = jnp.where(source < len(dyns), has_dyn(me, frame, (peers - 1) & ~bit), local)
        picks.append(source * 2 + local.astype(jnp.int32))
    far = jnp.where(upper, 0, last_frame)
    sums = [jnp.where(frame == far, len(dyns) + 1, place_of(frame, dyns)) for frame in mem_ids + pair_ids]
    owned = []
    for group in (me, me ^ 1):
        for j in range(FR_DEV):
            frame = group * FR_DEV + j
            place = place_of(frame, dyns)
            named = jnp.logical_or(place < len(dyns), jnp.logical_or(frame == 0, frame == last_frame))
            owned.append(place * 2 + named.astype(jnp.int32))
    lanes = codes_ref.shape[1]
    for row, code in ((PICK, pack(picks, PLACE_BITS)), (SUM, pack(sums, PLACE_BITS)), (OWNED, pack(owned, PLACE_BITS))):
        codes_ref[row : row + 1, :] = jnp.full((1, lanes), code, jnp.int32)


def release_kernel(joined_ref, direct_keys, values_out, keys_out):
    rows = values_out.shape[0]
    values_out[...] = joined_ref[rows : 2 * rows, :]
    keys_out[...] = direct_keys[...]


def split_kernel(peers, bank_ref, mine_ref, pair_ref, out_ref):
    me = lax.axis_index("tm")
    frame_len, half_width = out_ref.shape[2:]
    dyns = dyn_frames(bank_of(bank_ref), peers * FR_DEV - 1)
    places = [(has_dyn(me, dyn, 0), dyn % FR_DEV) for dyn in dyns]
    places.append((has_end(me, 0, peers), jnp.where(me < peers // 2, 0, FR_DEV - 1)))
    for j, (local, frame) in enumerate(places):
        for role in range(2):
            for source, taken in ((mine_ref, local), (pair_ref, jnp.logical_not(local))):

                @pl.when(jnp.logical_and((me & 1) == role, taken))
                def _(source=source, j=j, frame=frame, role=role):
                    for kind in range(2):
                        start = pl.multiple_of((kind * FR_DEV + frame) * frame_len, frame_len)
                        out_ref[j, kind] = source[pl.ds(start, frame_len), role * half_width : (role + 1) * half_width]


def step_kernel(peers, even_done, odd_done, bank_ref, mine_ref, got_ref, out_ref):
    me = lax.axis_index("tm")
    done = by_role(me, even_done, odd_done)
    dyns = dyn_frames(bank_of(bank_ref), peers * FR_DEV - 1)
    flags = [has_dyn(me, dyn, done) for dyn in dyns] + [has_end(me, done, peers)]
    for j, flag in enumerate(flags):
        choose(out_ref.at[j], flag, mine_ref.at[j], got_ref.at[j])


def pick_kernel(codes_ref, mine_ref, got_ref, own_out, pair_out):
    code = code_of(codes_ref, PICK)
    for o, out in enumerate((own_out, pair_out)):
        for m in range(MEM):
            pick = field(code, o * MEM + m, PLACE_BITS)
            source = pick >> 1
            choose(out.at[m], (pick & 1) != 0, mine_ref.at[source], got_ref.at[source])


def dot(a, b, left, right):
    return lax.dot_general(a, b, (((left,), (right,)), ((), ())), preferred_element_type=F32)


def logits_of(keys, query, rows_ref, head, piece):
    frame_len = query.shape[0] // FR_DEV
    raw = dot(keys, query, 1, 1) * (FACTOR * LOG2E)
    parts = []
    for j in range(FR_DEV):
        row = piece * FR_DEV + j
        parts.append(raw[j * frame_len : (j + 1) * frame_len] + rows_ref[head, row : row + 1, :])
    return jnp.concatenate(parts, axis=0)


def joined_parts(joined_ref, cols):
    rows = joined_ref.shape[0] // 2 // DEPTH * DEPTH
    return joined_ref[0:rows, cols], joined_ref[rows : 2 * rows, cols]


def head_cols(head):
    return pl.ds(head * DEPTH, DEPTH)


def part_of(logits, slopes):
    peak = jnp.max(logits, axis=0, keepdims=True)
    exps = jnp.exp2(logits - peak)
    return peak, jnp.sum(exps, axis=0, keepdims=True), jnp.sum(exps * slopes, axis=0, keepdims=True)


def merged(left, right):
    peak = jnp.maximum(left[0], right[0])
    scales = [jnp.exp2(part[0] - peak) for part in (left, right)]
    return peak, *(left[j] * scales[0] + right[j] * scales[1] for j in (1, 2))


def load_part(ref, head):
    return tuple(ref[head, j : j + 1, :] for j in range(3))


def store_part(ref, head, part):
    for j, row in enumerate(part):
        ref[head, j : j + 1, :] = row


def prev_parts(peers, direct_keys, relayed_keys, outer_values, pair_ref, cols):
    even = (lax.axis_index("tm") & 1) == 0
    keys = jnp.where(through_relay(1, 1, peers), relayed_keys[:, cols], direct_keys[:, cols])
    parts = zip((keys, outer_values[:, cols]), joined_parts(pair_ref, cols))
    return tuple(jnp.where(even, outer, pair) for outer, pair in parts)


def stats_kernel(
    peers,
    rows_ref,
    queries_ref,
    direct_keys,
    outer_values,
    relayed_keys,
    pair_ref,
    own_ref,
    part_ref,
    queries_out,
    cotangent_out,
):
    heads = queries_ref.shape[1] // DEPTH
    rows = queries_out.shape[0]
    queries_out[...] = queries_ref[0:rows]
    cotangent_out[...] = queries_ref[rows : 2 * rows]

    def products(head):
        cols = head_cols(head)
        query, cotangent = joined_parts(queries_ref, cols)
        pieces = ((PREV, prev_parts(peers, direct_keys, relayed_keys, outer_values, pair_ref, cols)), (OWN, joined_parts(own_ref, cols)))
        return [
            (logits_of(keys, query, rows_ref, head, piece), dot(values, cotangent, 1, 1))
            for piece, (keys, values) in pieces
        ]

    ahead = products(0)
    for head in range(heads):
        now = ahead
        if head + 1 < heads:
            ahead = products(head + 1)
        store_part(part_ref, head, merged(*(part_of(*piece) for piece in now)))


def rounded(part, logits, slopes):
    peak, total, spread = merged(part, part_of(logits, slopes))
    inverse = 1.0 / total
    stats = peak, inverse, spread * inverse
    return stats, *weights_of(stats, logits, slopes)


def weights_of(stats, logits, slopes):
    peak, inverse, spread = stats
    probs = jnp.exp2(logits - peak) * inverse
    return probs.astype(BF16), (probs * (slopes - spread)).astype(BF16)


def memory_kernel(
    codes_ref, rows_ref, part_ref, pair_part_ref, own_queries, pair_queries, own_mem, pair_mem, keep_ref, send_ref
):
    role = lax.axis_index("tm") & 1
    code = code_of(codes_ref, SUM)
    frame_len, half_width = own_mem.shape[2:]
    half = half_width // DEPTH
    groups = ((own_queries, own_mem, part_ref, MEMORY), (pair_queries, pair_mem, pair_part_ref, PAIR))
    work = [(g, local) for local in range(half) for g in range(len(groups))]
    keep_ref[...] = jnp.zeros(keep_ref.shape, F32)

    def operands(g, local):
        cols = pl.ds(pl.multiple_of((role * half + local) * DEPTH, DEPTH), DEPTH)
        return joined_parts(groups[g][0], cols)

    def products(g, local):
        _, mem, _, piece = groups[g]
        query, cotangent = operands(g, local)
        keys, values = (mem[:, kind, :, head_cols(local)].reshape(MEM * frame_len, DEPTH) for kind in range(2))
        return logits_of(keys, query, rows_ref, role * half + local, piece), dot(values, cotangent, 1, 1)

    def add(g, local, _, weights, dlogits):
        query, cotangent = operands(g, local)
        terms = (dot(dlogits, query, 1, 0) * FACTOR, dot(weights, cotangent, 1, 0))
        for m in range(MEM):
            place = field(code, g * MEM + m, PLACE_BITS)
            for kind, term in enumerate(terms):
                part = term[m * frame_len : (m + 1) * frame_len].astype(BF16).astype(F32)
                keep_ref[place, kind, :, head_cols(local)] += part

    ahead = products(*work[0])
    behind = None
    for j, (g, local) in enumerate(work):
        now = ahead
        if j + 1 < len(work):
            ahead = products(*work[j + 1])
        if behind is not None:
            add(*work[j - 1], *behind)
        behind = rounded(load_part(groups[g][2], role * half + local), *now)
    add(*work[-1], *behind)
    kept = send_ref.shape[0]
    for place in range(kept):
        send_ref[place] = keep_ref[place if place + 1 < kept else kept].astype(BF16)


def next_kernel(
    peers,
    rows_ref,
    stats_ref,
    pair_queries,
    outer_queries,
    direct_cotangent,
    relayed_cotangent,
    own_ref,
    term_ref,
    sum_ref,
):
    even = (lax.axis_index("tm") & 1) == 0
    relayed = through_relay(-1, 2, peers)
    heads = pair_queries.shape[1] // DEPTH

    def operands(head):
        cols = head_cols(head)
        cotangent = jnp.where(relayed, relayed_cotangent[:, cols], direct_cotangent[:, cols])
        outer = outer_queries[:, cols], cotangent
        return [jnp.where(even, a, b) for a, b in zip(joined_parts(pair_queries, cols), outer)]

    def products(head):
        query, cotangent = operands(head)
        keys, values = joined_parts(own_ref, head_cols(head))
        return logits_of(keys, query, rows_ref, head, NEXT), dot(values, cotangent, 1, 1)

    ahead = products(0)
    for head in range(heads):
        now = ahead
        if head + 1 < heads:
            ahead = products(head + 1)
        weights, dlogits = weights_of(load_part(stats_ref, head), *now)
        query, cotangent = operands(head)
        cols = head_cols(head)
        sum_ref[0, :, cols] = term_ref[0, :, cols] + dot(dlogits, query, 1, 0) * FACTOR
        sum_ref[1, :, cols] = term_ref[1, :, cols] + dot(weights, cotangent, 1, 0)


def memory_parts(own_mem, other_mem, head):
    role = lax.axis_index("tm") & 1
    frame_len, half_width = own_mem.shape[2:]
    half = half_width // DEPTH
    cols = head_cols(head % half)
    return [
        jnp.where(role == head // half, own_mem[:, kind, :, cols], other_mem[:, kind, :, cols]).reshape(
            MEM * frame_len, DEPTH
        )
        for kind in range(2)
    ]


def own_kernel(rows_ref, part_ref, queries_ref, own_ref, own_mem, other_mem, term_ref, stats_ref):
    heads = queries_ref.shape[1] // DEPTH

    def products(head):
        query, cotangent = joined_parts(queries_ref, head_cols(head))
        pieces = ((OWN, joined_parts(own_ref, head_cols(head))), (MEMORY, memory_parts(own_mem, other_mem, head)))
        return [
            (logits_of(keys, query, rows_ref, head, piece), dot(values, cotangent, 1, 1))
            for piece, (keys, values) in pieces
        ]

    ahead = products(0)
    for head in range(heads):
        own, memory = ahead
        if head + 1 < heads:
            ahead = products(head + 1)
        cols = head_cols(head)
        query, cotangent = joined_parts(queries_ref, cols)
        peak, total, spread = merged(load_part(part_ref, head), part_of(*memory))
        inverse = 1.0 / total
        stats = peak, inverse, spread * inverse
        store_part(stats_ref, head, stats)
        weights, dlogits = weights_of(stats, *own)
        term_ref[0, :, cols] = dot(dlogits, query, 1, 0) * FACTOR
        term_ref[1, :, cols] = dot(weights, cotangent, 1, 0)


def attend_kernel(
    peers,
    rows_ref,
    stats_ref,
    queries_ref,
    direct_keys,
    outer_values,
    relayed_keys,
    pair_ref,
    own_ref,
    own_mem,
    other_mem,
    attended_ref,
    grad_query_ref,
    mark_ref,
):
    mark_ref[...] = jnp.zeros(mark_ref.shape, F32)
    heads = queries_ref.shape[1] // DEPTH

    def pieces(head):
        cols = head_cols(head)
        prev = prev_parts(peers, direct_keys, relayed_keys, outer_values, pair_ref, cols)
        return (PREV, prev), (OWN, joined_parts(own_ref, cols)), (MEMORY, memory_parts(own_mem, other_mem, head))

    def products(head):
        query, cotangent = joined_parts(queries_ref, head_cols(head))
        return [
            (logits_of(keys, query, rows_ref, head, piece), dot(values, cotangent, 1, 1))
            for piece, (keys, values) in pieces(head)
        ]

    ahead = products(0)
    for head in range(heads):
        now = ahead
        if head + 1 < heads:
            ahead = products(head + 1)
        cols = head_cols(head)
        stats = load_part(stats_ref, head)
        attended = grad_query = 0.0
        for (_, (keys, values)), piece in zip(pieces(head), now):
            weights, dlogits = weights_of(stats, *piece)
            attended += dot(values, weights, 0, 0)
            grad_query += dot(keys, dlogits, 0, 0)
        attended_ref[:, cols] = attended.T.astype(BF16)
        grad_query_ref[:, cols] = (grad_query * FACTOR).T.astype(BF16)


def add_kernel(keep_ref, got_ref, out_ref, send_ref):
    value = keep_ref[0 : got_ref.shape[0]] + got_ref[...].astype(F32)
    out_ref[...] = value
    send_ref[...] = value.astype(BF16)


def pass_kernel(in_ref, out_ref):
    out_ref[...] = in_ref[...]


def owned_kernel(codes_ref, keep_ref, got_ref, mine_ref, pair_ref):
    code = code_of(codes_ref, OWNED)
    for o, out in enumerate((mine_ref, pair_ref)):
        for j in range(FR_DEV):
            owned = field(code, o * FR_DEV + j, PLACE_BITS)
            place = owned >> 1
            named = (owned & 1) != 0

            @pl.when(named)
            def _(out=out, j=j, place=place):
                value = keep_ref[place] + got_ref[place].astype(F32)
                out[j] = value.astype(out.dtype)

            @pl.when(jnp.logical_not(named))
            def _(out=out, j=j):
                out[j] = jnp.zeros(out.shape[1:], out.dtype)


def final_kernel(own_ref, mine_ref, got_ref, grad_key_ref, grad_value_ref, sums, sems):
    role = lax.axis_index("tm") & 1
    frame_len, half_width = mine_ref.shape[2:]
    copies = []
    for kind, out in enumerate((grad_key_ref, grad_value_ref)):
        for j in range(FR_DEV):
            rows = pl.ds(j * frame_len, frame_len)
            for half in range(2):
                cols = pl.ds(half * half_width, half_width)
                bank = jnp.where(role == half, mine_ref[j, kind], got_ref[j, kind].astype(F32))
                sums[kind, rows, cols] = (own_ref[kind, rows, cols] + bank).astype(BF16)
            copies.append(pltpu.make_async_copy(sums.at[kind, rows], out.at[rows], sems.at[kind * FR_DEV + j]))
            copies[-1].start()
    for copy in copies:
        copy.wait()


def body(
    query_states,
    key_states,
    value_states,
    grad_out,
    camera_pose,
    pose_bias,
    memory_index,
    bank_frames,
):
    row_count, width = query_states.shape
    frame_len = row_count // FR_DEV
    heads = pose_bias.shape[0]
    slots = bank_frames.shape[0]
    peers = lax.axis_size("tm")
    bits = [1 << i for i in range(1, peers.bit_length() - 1)]
    turns = list(zip(bits, bits[::-1]))
    piece_flops = 2 * row_count * row_count * width
    bank_frames = bank_frames.reshape(1, slots)
    last_bits = turns[-1]

    def join(kernel, rows, arrays, scratch, name, after=()):
        def run(*refs):
            kernel(*refs[: len(arrays)], *refs[len(arrays) + len(after) :])

        return pl.pallas_call(
            run,
            out_shape=shape(BF16, rows, width),
            in_specs=[pl.BlockSpec(memory_space=pltpu.HBM)] * len(arrays) + [ANY] * len(after),
            out_specs=VMEM,
            scratch_shapes=[*scratch, pltpu.SemaphoreType.DMA((len(arrays),))],
            compiler_params=pltpu.CompilerParams(vmem_limit_bytes=VMEM_LIMIT),
            name=name,
        )(*(pltpu.with_memory_space_constraint(array, pltpu.HBM) for array in arrays), *after)

    joined = join(
        join_kernel,
        2 * row_count + TAIL,
        [memory_index, key_states, value_states],
        [pltpu.VMEM(memory_index.shape, jnp.int32)],
        "join",
    )
    half_width = width // 2
    direct_keys = shift_first(key_states, 1, 1, peers)
    pair = swap(joined, 1, 1, peers)
    held = shape(BF16, slots - 1, 2, frame_len, half_width)
    sums = shape(F32, slots - 1, 2, frame_len, half_width)
    (mine,) = call(functools.partial(split_kernel, peers), [held], [bank_frames, joined, pair], name="split")
    queries = join(join_queries_kernel, 2 * row_count, [query_states, grad_out], [], "join_queries", after=[mine])
    pair_queries = swap(queries, 1, 1, peers)

    bias_rows = -(-(5 * FR_DEV) // 8) * 8
    rows, codes = call(
        functools.partial(plan_kernel, peers, last_bits),
        [shape(F32, heads, bias_rows, row_count), shape(jnp.int32, 8, 128)],
        [pair],
        scalars=[bank_frames, memory_index, camera_pose, pose_bias],
        name="plan",
    )
    values_out, keys_out = call(
        release_kernel,
        [shape(BF16, row_count, width)] * 2,
        [joined, direct_keys],
        after=[codes],
        flops=HIDING * piece_flops,
        name="release",
    )
    outer = [direct_keys, shift(values_out, 1, 1, peers), shift_second(keys_out, 1, 1, peers)]
    even_done = odd_done = 1
    for step, (even_bit, odd_bit) in enumerate(turns):
        got = swap(mine, even_bit, odd_bit, peers)
        if step + 1 < len(turns):
            kernel = functools.partial(step_kernel, peers, even_done, odd_done)
            after = [codes, pair_queries]
            (mine,) = call(kernel, [held], [bank_frames, mine, got], after=after, name="step")
        even_done |= even_bit
        odd_done |= odd_bit

    stats = shape(F32, heads, 8, row_count)
    part, queries_out, cotangent_out = call(
        functools.partial(stats_kernel, peers),
        [stats] + [shape(BF16, row_count, width)] * 2,
        [rows, queries, *outer, pair, joined],
        flops=HIDING * piece_flops,
        name="stats",
    )
    pair_part = swap(part, 1, 1, peers)
    next_queries = shift(queries_out, -1, 2, peers)
    direct_cotangent = shift_first(cotangent_out, -1, 2, peers)
    chosen = shape(BF16, MEM, 2, frame_len, half_width)
    own_mem, pair_mem = call(pick_kernel, [chosen] * 2, [codes, mine, got], name="pick")
    keep, send = call(
        memory_kernel,
        [shape(F32, slots, 2, frame_len, half_width), held],
        [codes, rows, part, pair_part, queries, pair_queries, own_mem, pair_mem],
        flops=HIDING * piece_flops,
        name="memory",
    )
    other_mem = swap(pair_mem, 1, 1, peers)
    pair_sums = shape(F32, 2, row_count, width)
    own_terms, stats_all = call(
        own_kernel,
        [pair_sums, stats],
        [rows, part, queries, joined, own_mem, other_mem],
        after=[send],
        flops=HIDING * piece_flops,
        name="own",
    )
    next_stats = lax.ppermute(stats_all, "tm", [(i, i - 1) for i in range(1, peers)])
    (passed_on,) = call(
        pass_kernel, [shape(BF16, row_count, width)], [direct_cotangent], after=[own_terms], name="pass_on"
    )
    relayed_cotangent = shift_second(passed_on, -1, 2, peers)
    (own,) = call(
        functools.partial(next_kernel, peers),
        [pair_sums],
        [rows, next_stats, pair_queries, next_queries, direct_cotangent, relayed_cotangent, joined, own_terms],
        flops=HIDING * piece_flops,
        name="next",
    )
    for step, (even_bit, odd_bit) in enumerate(turns[::-1]):
        got = swap(send, even_bit, odd_bit, peers)
        if step + 1 < len(turns):
            after = [own_terms, next_queries]
            keep, send = call(add_kernel, [sums, held], [keep, got], after=after, name="add")
    attended, grad_query, mark = call(
        functools.partial(attend_kernel, peers),
        [shape(BF16, row_count, width)] * 2 + [shape(F32, 8, 128)],
        [rows, stats_all, queries, *outer, pair, joined, own_mem, other_mem],
        after=[send],
        flops=HIDING * piece_flops,
        name="attend",
    )
    owned_mine, owned_send = call(
        owned_kernel,
        [shape(F32, FR_DEV, 2, frame_len, half_width), shape(BF16, FR_DEV, 2, frame_len, half_width)],
        [codes, keep, got],
        after=[own, mark],
        name="owned",
    )
    owned_got = swap(owned_send, 1, 1, peers)
    grad_key, grad_value = pl.pallas_call(
        final_kernel,
        out_shape=[shape(BF16, row_count, width)] * 2,
        in_specs=[VMEM] * 3,
        out_specs=[pl.BlockSpec(memory_space=pltpu.HBM)] * 2,
        scratch_shapes=[pltpu.VMEM((2, row_count, width), BF16), pltpu.SemaphoreType.DMA((2 * FR_DEV,))],
        compiler_params=pltpu.CompilerParams(vmem_limit_bytes=VMEM_LIMIT),
        name="final",
    )(own, owned_mine, owned_got)
    return (attended, grad_query, grad_key, grad_value)


def solution(mesh):
    rows = P(("traj", "tm"), None)
    in_specs = (rows, rows, rows, rows, P("traj"), P(), rows, P("traj"))
    return jax.shard_map(body, mesh=mesh, in_specs=in_specs, out_specs=(rows,) * 4, check_vma=False)
```

```python
import functools
import math

import jax
import jax.numpy as jnp
from jax import lax
from jax.experimental import pallas as pl
from jax.experimental.pallas import tpu as pltpu
from jax.sharding import PartitionSpec as P

FR_DEV = 2
MEM = 2
DEPTH = 128
TAIL = 16

BLOCKED_LOGIT = -1e30
LOG2E = math.log2(math.e)
FACTOR = 1.0 / math.sqrt(DEPTH)

SMEM = pl.BlockSpec(memory_space=pltpu.SMEM)
VMEM = pl.BlockSpec(memory_space=pltpu.VMEM)
ANY = pl.BlockSpec(memory_space=pl.ANY)
HIDING = 200
VMEM_LIMIT = 16 * 1024 * 1024
BF16, F32 = jnp.bfloat16, jnp.float32


def shape(dtype, *dims):
    return jax.ShapeDtypeStruct(dims, dtype)


def call(kernel, outs, arrays, scalars=(), after=(), flops=0, name=None):
    count = len(scalars) + len(arrays)

    def run(*refs):
        kernel(*refs[:count], *refs[count + len(after) :])

    return pl.pallas_call(
        run,
        out_shape=outs,
        in_specs=[SMEM] * len(scalars) + [VMEM] * len(arrays) + [ANY] * len(after),
        out_specs=[VMEM] * len(outs),
        compiler_params=pltpu.CompilerParams(vmem_limit_bytes=VMEM_LIMIT),
        cost_estimate=pl.CostEstimate(flops=flops, bytes_accessed=0, transcendentals=0) if flops else None,
        name=name,
    )(*scalars, *arrays, *after)


def swap(block, even_bit, odd_bit, peers):
    return lax.ppermute(block, "tm", [(i, i ^ (odd_bit if i & 1 else even_bit)) for i in range(peers)])


def shift(block, by, start, peers):
    pairs = [(i, i + by) for i in range(start, peers, 2) if 0 <= i + by < peers]
    return lax.ppermute(block, "tm", pairs)


def relays_of(by, start, peers):
    pairs = [(i, i + by) for i in range(start, peers, 2) if 0 <= i + by < peers]
    return {(i, j): i ^ 4 for i, j in pairs if peers == 8 and (i ^ j) >> 1 == 3}


def shift_first(block, by, start, peers):
    relays = relays_of(by, start, peers)
    pairs = [(i, i + by) for i in range(start, peers, 2) if 0 <= i + by < peers]
    return lax.ppermute(block, "tm", [(i, relays.get((i, j), j)) for i, j in pairs])


def shift_second(block, by, start, peers):
    pairs = [(relay, j) for (_, j), relay in relays_of(by, start, peers).items()]
    return lax.ppermute(block, "tm", pairs) if pairs else block


def through_relay(by, start, peers):
    me = lax.axis_index("tm")
    return functools.reduce(jnp.logical_or, [me == j for _, j in relays_of(by, start, peers)], me < 0)


def lane_value(row, lane):
    lanes = lax.broadcasted_iota(jnp.int32, row.shape, 1)
    return jnp.max(jnp.where(lanes == lane, row, 0))


def bank_of(bank_ref):
    row = bank_ref[...]
    return [lane_value(row, slot) for slot in range(row.shape[1])]


def dyn_frames(bank, last_frame):
    found = [jnp.int32(0)] * (len(bank) - 2)
    seen = jnp.int32(0)
    for frame in bank:
        free = jnp.logical_and(frame != 0, frame != last_frame)
        for j in range(len(found)):
            found[j] = jnp.where(jnp.logical_and(free, seen == j), frame, found[j])
        seen = seen + free.astype(jnp.int32)
    return found


def place_of(frame, dyns):
    place = jnp.int32(len(dyns))
    for j, dyn in enumerate(dyns):
        place = jnp.where(frame == dyn, j, place)
    return place


def choose(out, take_first, first, second):
    @pl.when(take_first)
    def _():
        out[...] = first[...]

    @pl.when(jnp.logical_not(take_first))
    def _():
        out[...] = second[...]


def has_end(me, done, peers):
    return jnp.logical_or((me & ~done) == 0, (me | done) == peers - 1)


def has_dyn(me, frame, done):
    return ((me ^ (frame // FR_DEV)) & ~done) == 0


def by_role(me, even_value, odd_value):
    return jnp.where((me & 1) == 0, even_value, odd_value)


def join_kernel(index_ref, key_ref, value_ref, joined_ref, index_buf, sems):
    rows = key_ref.shape[0]
    copies = [
        pltpu.make_async_copy(index_ref, index_buf, sems.at[0]),
        pltpu.make_async_copy(key_ref, joined_ref.at[pl.ds(0, rows)], sems.at[1]),
        pltpu.make_async_copy(value_ref, joined_ref.at[pl.ds(rows, rows)], sems.at[2]),
    ]
    for copy in copies:
        copy.start()
    copies[0].wait()
    width = joined_ref.shape[1]
    lane = lax.broadcasted_iota(jnp.int32, (TAIL, width), 1) // DEPTH
    tail = jnp.zeros((TAIL, width), jnp.int32)
    for m in range(MEM):
        tail = jnp.where(lane == m, index_buf[0:1, m : m + 1], tail)
    joined_ref[2 * rows : 2 * rows + TAIL, :] = tail.astype(F32).astype(BF16)
    copies[1].wait()
    copies[2].wait()


def join_queries_kernel(query_ref, cotangent_ref, joined_ref, sems):
    rows = query_ref.shape[0]
    copies = [
        pltpu.make_async_copy(ref, joined_ref.at[pl.ds(j * rows, rows)], sems.at[j])
        for j, ref in enumerate((query_ref, cotangent_ref))
    ]
    for copy in copies:
        copy.start()
    for copy in copies:
        copy.wait()


def pack(fields, width):
    code = jnp.int32(0)
    for j, field in enumerate(fields):
        code = code | (field.astype(jnp.int32) << (j * width))
    return code


def field(code, j, width):
    return (code >> (j * width)) & ((1 << width) - 1)


def code_of(codes_ref, row):
    return jnp.max(codes_ref[row : row + 1, :])


PICK, SUM, OWNED = range(3)
PLACE_BITS = 4
PREV, OWN, MEMORY, NEXT, PAIR = range(5)


def plan_kernel(
    peers,
    last_bits,
    bank_ref,
    index_ref,
    pose_ref,
    bias_ref,
    pair_ref,
    rows_ref,
    codes_ref,
):
    me = lax.axis_index("tm")
    last_frame = peers * FR_DEV - 1
    heads, _, row_count = rows_ref.shape
    bank = [bank_ref[0, slot] for slot in range(bank_ref.shape[1])]
    tail = pair_ref.shape[0] - TAIL
    pair_ids = []
    for m in range(MEM):
        slot = jnp.max(pair_ref[tail : tail + TAIL, m * DEPTH : (m + 1) * DEPTH].astype(F32)).astype(jnp.int32)
        pair_ids.append(bank_ref[0, slot])
    mem_ids = [bank_ref[0, index_ref[0, m]] for m in range(MEM)]

    own_ids = [me * FR_DEV + j for j in range(FR_DEV)]
    prev_ids = [jnp.maximum(own - FR_DEV, 0) for own in own_ids]
    next_ids = [jnp.minimum(own + FR_DEV, last_frame) for own in own_ids]
    pair_own_ids = [(me ^ 1) * FR_DEV + j for j in range(FR_DEV)]
    pieces = ((prev_ids, own_ids), (own_ids, own_ids), (mem_ids, own_ids), (own_ids, next_ids), (pair_ids, pair_own_ids))
    poses = [([pose_ref[f] for f in key_ids], [pose_ref[f] for f in query_ids]) for key_ids, query_ids in pieces]
    frame_of = lax.broadcasted_iota(jnp.int32, (1, row_count), 1) // (row_count // FR_DEV)
    for head in range(heads):
        for piece, (key_poses, query_poses) in enumerate(poses):
            for j, key_pose in enumerate(key_poses):
                row = jnp.zeros((1, row_count), F32)
                for a, query_pose in enumerate(query_poses):
                    value = bias_ref[head, query_pose, key_pose] * LOG2E
                    if piece == PREV:
                        value = jnp.where(me == 0, BLOCKED_LOGIT, value)
                    row = jnp.where(frame_of == a, value, row)
                rows_ref[head, piece * FR_DEV + j : piece * FR_DEV + j + 1, :] = row

    dyns = dyn_frames(bank, last_frame)
    bit = by_role(me, *last_bits)
    upper = (me & bit) != 0
    picks = []
    for frame in mem_ids + pair_ids:
        source = place_of(frame, dyns)
        local = jnp.where(frame == 0, jnp.logical_not(upper), upper)
        local = jnp.where(source < len(dyns), has_dyn(me, frame, (peers - 1) & ~bit), local)
        picks.append(source * 2 + local.astype(jnp.int32))
    far = jnp.where(upper, 0, last_frame)
    sums = [jnp.where(frame == far, len(dyns) + 1, place_of(frame, dyns)) for frame in mem_ids + pair_ids]
    owned = []
    for group in (me, me ^ 1):
        for j in range(FR_DEV):
            frame = group * FR_DEV + j
            place = place_of(frame, dyns)
            named = jnp.logical_or(place < len(dyns), jnp.logical_or(frame == 0, frame == last_frame))
            owned.append(place * 2 + named.astype(jnp.int32))
    lanes = codes_ref.shape[1]
    for row, code in ((PICK, pack(picks, PLACE_BITS)), (SUM, pack(sums, PLACE_BITS)), (OWNED, pack(owned, PLACE_BITS))):
        codes_ref[row : row + 1, :] = jnp.full((1, lanes), code, jnp.int32)


def release_kernel(joined_ref, direct_keys, values_out, keys_out):
    rows = values_out.shape[0]
    values_out[...] = joined_ref[rows : 2 * rows, :]
    keys_out[...] = direct_keys[...]


def split_kernel(peers, bank_ref, mine_ref, pair_ref, out_ref):
    me = lax.axis_index("tm")
    frame_len, half_width = out_ref.shape[2:]
    dyns = dyn_frames(bank_of(bank_ref), peers * FR_DEV - 1)
    places = [(has_dyn(me, dyn, 0), dyn % FR_DEV) for dyn in dyns]
    places.append((has_end(me, 0, peers), jnp.where(me < peers // 2, 0, FR_DEV - 1)))
    for j, (local, frame) in enumerate(places):
        for role in range(2):
            for source, taken in ((mine_ref, local), (pair_ref, jnp.logical_not(local))):

                @pl.when(jnp.logical_and((me & 1) == role, taken))
                def _(source=source, j=j, frame=frame, role=role):
                    for kind in range(2):
                        start = pl.multiple_of((kind * FR_DEV + frame) * frame_len, frame_len)
                        out_ref[j, kind] = source[pl.ds(start, frame_len), role * half_width : (role + 1) * half_width]


def step_kernel(peers, even_done, odd_done, bank_ref, mine_ref, got_ref, out_ref):
    me = lax.axis_index("tm")
    done = by_role(me, even_done, odd_done)
    dyns = dyn_frames(bank_of(bank_ref), peers * FR_DEV - 1)
    flags = [has_dyn(me, dyn, done) for dyn in dyns] + [has_end(me, done, peers)]
    for j, flag in enumerate(flags):
        choose(out_ref.at[j], flag, mine_ref.at[j], got_ref.at[j])


def pick_kernel(codes_ref, mine_ref, got_ref, own_out, pair_out):
    code = code_of(codes_ref, PICK)
    for o, out in enumerate((own_out, pair_out)):
        for m in range(MEM):
            pick = field(code, o * MEM + m, PLACE_BITS)
            source = pick >> 1
            choose(out.at[m], (pick & 1) != 0, mine_ref.at[source], got_ref.at[source])


def dot(a, b, left, right):
    return lax.dot_general(a, b, (((left,), (right,)), ((), ())), preferred_element_type=F32)


def logits_of(keys, query, rows_ref, head, piece):
    frame_len = query.shape[0] // FR_DEV
    raw = dot(keys, query, 1, 1) * (FACTOR * LOG2E)
    parts = []
    for j in range(FR_DEV):
        row = piece * FR_DEV + j
        parts.append(raw[j * frame_len : (j + 1) * frame_len] + rows_ref[head, row : row + 1, :])
    return jnp.concatenate(parts, axis=0)


def joined_parts(joined_ref, cols):
    rows = joined_ref.shape[0] // 2 // DEPTH * DEPTH
    return joined_ref[0:rows, cols], joined_ref[rows : 2 * rows, cols]


def head_cols(head):
    return pl.ds(head * DEPTH, DEPTH)


def part_of(logits, slopes):
    peak = jnp.max(logits, axis=0, keepdims=True)
    exps = jnp.exp2(logits - peak)
    return peak, jnp.sum(exps, axis=0, keepdims=True), jnp.sum(exps * slopes, axis=0, keepdims=True)


def merged(left, right):
    peak = jnp.maximum(left[0], right[0])
    scales = [jnp.exp2(part[0] - peak) for part in (left, right)]
    return peak, *(left[j] * scales[0] + right[j] * scales[1] for j in (1, 2))


def load_part(ref, head):
    return tuple(ref[head, j : j + 1, :] for j in range(3))


def store_part(ref, head, part):
    for j, row in enumerate(part):
        ref[head, j : j + 1, :] = row


def prev_parts(peers, direct_keys, relayed_keys, outer_values, pair_ref, cols):
    even = (lax.axis_index("tm") & 1) == 0
    keys = jnp.where(through_relay(1, 1, peers), relayed_keys[:, cols], direct_keys[:, cols])
    parts = zip((keys, outer_values[:, cols]), joined_parts(pair_ref, cols))
    return tuple(jnp.where(even, outer, pair) for outer, pair in parts)


def stats_kernel(
    peers,
    rows_ref,
    queries_ref,
    direct_keys,
    outer_values,
    relayed_keys,
    pair_ref,
    own_ref,
    part_ref,
    queries_out,
    cotangent_out,
):
    heads = queries_ref.shape[1] // DEPTH
    rows = queries_out.shape[0]
    queries_out[...] = queries_ref[0:rows]
    cotangent_out[...] = queries_ref[rows : 2 * rows]

    def products(head):
        cols = head_cols(head)
        query, cotangent = joined_parts(queries_ref, cols)
        pieces = ((PREV, prev_parts(peers, direct_keys, relayed_keys, outer_values, pair_ref, cols)), (OWN, joined_parts(own_ref, cols)))
        return [
            (logits_of(keys, query, rows_ref, head, piece), dot(values, cotangent, 1, 1))
            for piece, (keys, values) in pieces
        ]

    ahead = products(0)
    for head in range(heads):
        now = ahead
        if head + 1 < heads:
            ahead = products(head + 1)
        store_part(part_ref, head, merged(*(part_of(*piece) for piece in now)))


def rounded(part, logits, slopes):
    peak, total, spread = merged(part, part_of(logits, slopes))
    inverse = 1.0 / total
    stats = peak, inverse, spread * inverse
    return stats, *weights_of(stats, logits, slopes)


def weights_of(stats, logits, slopes):
    peak, inverse, spread = stats
    probs = jnp.exp2(logits - peak) * inverse
    return probs.astype(BF16), (probs * (slopes - spread)).astype(BF16)


def memory_kernel(
    codes_ref, rows_ref, part_ref, pair_part_ref, own_queries, pair_queries, own_mem, pair_mem, keep_ref, send_ref
):
    role = lax.axis_index("tm") & 1
    code = code_of(codes_ref, SUM)
    frame_len, half_width = own_mem.shape[2:]
    half = half_width // DEPTH
    groups = ((own_queries, own_mem, part_ref, MEMORY), (pair_queries, pair_mem, pair_part_ref, PAIR))
    work = [(g, local) for local in range(half) for g in range(len(groups))]
    keep_ref[...] = jnp.zeros(keep_ref.shape, F32)

    def operands(g, local):
        cols = pl.ds(pl.multiple_of((role * half + local) * DEPTH, DEPTH), DEPTH)
        return joined_parts(groups[g][0], cols)

    def products(g, local):
        _, mem, _, piece = groups[g]
        query, cotangent = operands(g, local)
        keys, values = (mem[:, kind, :, head_cols(local)].reshape(MEM * frame_len, DEPTH) for kind in range(2))
        return logits_of(keys, query, rows_ref, role * half + local, piece), dot(values, cotangent, 1, 1)

    def add(g, local, _, weights, dlogits):
        query, cotangent = operands(g, local)
        terms = (dot(dlogits, query, 1, 0) * FACTOR, dot(weights, cotangent, 1, 0))
        for m in range(MEM):
            place = field(code, g * MEM + m, PLACE_BITS)
            for kind, term in enumerate(terms):
                part = term[m * frame_len : (m + 1) * frame_len].astype(BF16).astype(F32)
                keep_ref[place, kind, :, head_cols(local)] += part

    ahead = products(*work[0])
    behind = None
    for j, (g, local) in enumerate(work):
        now = ahead
        if j + 1 < len(work):
            ahead = products(*work[j + 1])
        if behind is not None:
            add(*work[j - 1], *behind)
        behind = rounded(load_part(groups[g][2], role * half + local), *now)
    add(*work[-1], *behind)
    kept = send_ref.shape[0]
    for place in range(kept):
        send_ref[place] = keep_ref[place if place + 1 < kept else kept].astype(BF16)


def next_kernel(
    peers,
    rows_ref,
    stats_ref,
    pair_queries,
    outer_queries,
    direct_cotangent,
    relayed_cotangent,
    own_ref,
    term_ref,
    sum_ref,
):
    even = (lax.axis_index("tm") & 1) == 0
    relayed = through_relay(-1, 2, peers)
    heads = pair_queries.shape[1] // DEPTH

    def operands(head):
        cols = head_cols(head)
        cotangent = jnp.where(relayed, relayed_cotangent[:, cols], direct_cotangent[:, cols])
        outer = outer_queries[:, cols], cotangent
        return [jnp.where(even, a, b) for a, b in zip(joined_parts(pair_queries, cols), outer)]

    def products(head):
        query, cotangent = operands(head)
        keys, values = joined_parts(own_ref, head_cols(head))
        return logits_of(keys, query, rows_ref, head, NEXT), dot(values, cotangent, 1, 1)

    ahead = products(0)
    for head in range(heads):
        now = ahead
        if head + 1 < heads:
            ahead = products(head + 1)
        weights, dlogits = weights_of(load_part(stats_ref, head), *now)
        query, cotangent = operands(head)
        cols = head_cols(head)
        sum_ref[0, :, cols] = term_ref[0, :, cols] + dot(dlogits, query, 1, 0) * FACTOR
        sum_ref[1, :, cols] = term_ref[1, :, cols] + dot(weights, cotangent, 1, 0)


def memory_parts(own_mem, other_mem, head):
    role = lax.axis_index("tm") & 1
    frame_len, half_width = own_mem.shape[2:]
    half = half_width // DEPTH
    cols = head_cols(head % half)
    return [
        jnp.where(role == head // half, own_mem[:, kind, :, cols], other_mem[:, kind, :, cols]).reshape(
            MEM * frame_len, DEPTH
        )
        for kind in range(2)
    ]


def own_kernel(rows_ref, part_ref, queries_ref, own_ref, own_mem, other_mem, term_ref, stats_ref):
    heads = queries_ref.shape[1] // DEPTH

    def products(head):
        query, cotangent = joined_parts(queries_ref, head_cols(head))
        pieces = ((OWN, joined_parts(own_ref, head_cols(head))), (MEMORY, memory_parts(own_mem, other_mem, head)))
        return [
            (logits_of(keys, query, rows_ref, head, piece), dot(values, cotangent, 1, 1))
            for piece, (keys, values) in pieces
        ]

    ahead = products(0)
    for head in range(heads):
        own, memory = ahead
        if head + 1 < heads:
            ahead = products(head + 1)
        cols = head_cols(head)
        query, cotangent = joined_parts(queries_ref, cols)
        peak, total, spread = merged(load_part(part_ref, head), part_of(*memory))
        inverse = 1.0 / total
        stats = peak, inverse, spread * inverse
        store_part(stats_ref, head, stats)
        weights, dlogits = weights_of(stats, *own)
        term_ref[0, :, cols] = dot(dlogits, query, 1, 0) * FACTOR
        term_ref[1, :, cols] = dot(weights, cotangent, 1, 0)


def attend_kernel(
    peers,
    rows_ref,
    stats_ref,
    queries_ref,
    direct_keys,
    outer_values,
    relayed_keys,
    pair_ref,
    own_ref,
    own_mem,
    other_mem,
    attended_ref,
    grad_query_ref,
    mark_ref,
):
    mark_ref[...] = jnp.zeros(mark_ref.shape, F32)
    heads = queries_ref.shape[1] // DEPTH

    def pieces(head):
        cols = head_cols(head)
        prev = prev_parts(peers, direct_keys, relayed_keys, outer_values, pair_ref, cols)
        return (PREV, prev), (OWN, joined_parts(own_ref, cols)), (MEMORY, memory_parts(own_mem, other_mem, head))

    def products(head):
        query, cotangent = joined_parts(queries_ref, head_cols(head))
        return [
            (logits_of(keys, query, rows_ref, head, piece), dot(values, cotangent, 1, 1))
            for piece, (keys, values) in pieces(head)
        ]

    ahead = products(0)
    for head in range(heads):
        now = ahead
        if head + 1 < heads:
            ahead = products(head + 1)
        cols = head_cols(head)
        stats = load_part(stats_ref, head)
        attended = grad_query = 0.0
        for (_, (keys, values)), piece in zip(pieces(head), now):
            weights, dlogits = weights_of(stats, *piece)
            attended += dot(values, weights, 0, 0)
            grad_query += dot(keys, dlogits, 0, 0)
        attended_ref[:, cols] = attended.T.astype(BF16)
        grad_query_ref[:, cols] = (grad_query * FACTOR).T.astype(BF16)


def add_kernel(keep_ref, got_ref, out_ref, send_ref):
    value = keep_ref[0 : got_ref.shape[0]] + got_ref[...].astype(F32)
    out_ref[...] = value
    send_ref[...] = value.astype(BF16)


def pass_kernel(in_ref, out_ref):
    out_ref[...] = in_ref[...]


def owned_kernel(groups, codes_ref, keep_ref, got_ref, *outs):
    code = code_of(codes_ref, OWNED)
    for o, out in zip(groups, outs):
        for j in range(FR_DEV):
            owned = field(code, o * FR_DEV + j, PLACE_BITS)
            place = owned >> 1
            named = (owned & 1) != 0

            @pl.when(named)
            def _(out=out, j=j, place=place):
                value = keep_ref[place] + got_ref[place].astype(F32)
                out[j] = value.astype(out.dtype)

            @pl.when(jnp.logical_not(named))
            def _(out=out, j=j):
                out[j] = jnp.zeros(out.shape[1:], out.dtype)


def final_kernel(own_ref, mine_ref, got_ref, grad_key_ref, grad_value_ref, sums, sems):
    role = lax.axis_index("tm") & 1
    frame_len, half_width = mine_ref.shape[2:]
    copies = []
    for kind, out in enumerate((grad_key_ref, grad_value_ref)):
        for j in range(FR_DEV):
            rows = pl.ds(j * frame_len, frame_len)
            for half in range(2):
                cols = pl.ds(half * half_width, half_width)
                bank = jnp.where(role == half, mine_ref[j, kind], got_ref[j, kind].astype(F32))
                sums[kind, rows, cols] = (own_ref[kind, rows, cols] + bank).astype(BF16)
            copies.append(pltpu.make_async_copy(sums.at[kind, rows], out.at[rows], sems.at[kind * FR_DEV + j]))
            copies[-1].start()
    for copy in copies:
        copy.wait()


def body(
    query_states,
    key_states,
    value_states,
    grad_out,
    camera_pose,
    pose_bias,
    memory_index,
    bank_frames,
):
    row_count, width = query_states.shape
    frame_len = row_count // FR_DEV
    heads = pose_bias.shape[0]
    slots = bank_frames.shape[0]
    peers = lax.axis_size("tm")
    bits = [1 << i for i in range(1, peers.bit_length() - 1)]
    turns = list(zip(bits, bits[::-1]))
    piece_flops = 2 * row_count * row_count * width
    bank_frames = bank_frames.reshape(1, slots)
    last_bits = turns[-1]

    def join(kernel, rows, arrays, scratch, name, after=()):
        def run(*refs):
            kernel(*refs[: len(arrays)], *refs[len(arrays) + len(after) :])

        return pl.pallas_call(
            run,
            out_shape=shape(BF16, rows, width),
            in_specs=[pl.BlockSpec(memory_space=pltpu.HBM)] * len(arrays) + [ANY] * len(after),
            out_specs=VMEM,
            scratch_shapes=[*scratch, pltpu.SemaphoreType.DMA((len(arrays),))],
            compiler_params=pltpu.CompilerParams(vmem_limit_bytes=VMEM_LIMIT),
            name=name,
        )(*(pltpu.with_memory_space_constraint(array, pltpu.HBM) for array in arrays), *after)

    joined = join(
        join_kernel,
        2 * row_count + TAIL,
        [memory_index, key_states, value_states],
        [pltpu.VMEM(memory_index.shape, jnp.int32)],
        "join",
    )
    half_width = width // 2
    direct_keys = shift_first(key_states, 1, 1, peers)
    pair = swap(joined, 1, 1, peers)
    held = shape(BF16, slots - 1, 2, frame_len, half_width)
    sums = shape(F32, slots - 1, 2, frame_len, half_width)
    (mine,) = call(functools.partial(split_kernel, peers), [held], [bank_frames, joined, pair], name="split")
    queries = join(join_queries_kernel, 2 * row_count, [query_states, grad_out], [], "join_queries", after=[mine])
    pair_queries = swap(queries, 1, 1, peers)

    bias_rows = -(-(5 * FR_DEV) // 8) * 8
    rows, codes = call(
        functools.partial(plan_kernel, peers, last_bits),
        [shape(F32, heads, bias_rows, row_count), shape(jnp.int32, 8, 128)],
        [pair],
        scalars=[bank_frames, memory_index, camera_pose, pose_bias],
        name="plan",
    )
    values_out, keys_out = call(
        release_kernel,
        [shape(BF16, row_count, width)] * 2,
        [joined, direct_keys],
        after=[codes],
        flops=HIDING * piece_flops,
        name="release",
    )
    outer = [direct_keys, shift(values_out, 1, 1, peers), shift_second(keys_out, 1, 1, peers)]
    even_done = odd_done = 1
    for step, (even_bit, odd_bit) in enumerate(turns):
        got = swap(mine, even_bit, odd_bit, peers)
        if step + 1 < len(turns):
            kernel = functools.partial(step_kernel, peers, even_done, odd_done)
            after = [codes, pair_queries]
            (mine,) = call(kernel, [held], [bank_frames, mine, got], after=after, name="step")
        even_done |= even_bit
        odd_done |= odd_bit

    stats = shape(F32, heads, 8, row_count)
    part, queries_out, cotangent_out = call(
        functools.partial(stats_kernel, peers),
        [stats] + [shape(BF16, row_count, width)] * 2,
        [rows, queries, *outer, pair, joined],
        flops=HIDING * piece_flops,
        name="stats",
    )
    pair_part = swap(part, 1, 1, peers)
    next_queries = shift(queries_out, -1, 2, peers)
    direct_cotangent = shift_first(cotangent_out, -1, 2, peers)
    chosen = shape(BF16, MEM, 2, frame_len, half_width)
    own_mem, pair_mem = call(pick_kernel, [chosen] * 2, [codes, mine, got], name="pick")
    keep, send = call(
        memory_kernel,
        [shape(F32, slots, 2, frame_len, half_width), held],
        [codes, rows, part, pair_part, queries, pair_queries, own_mem, pair_mem],
        flops=HIDING * piece_flops,
        name="memory",
    )
    other_mem = swap(pair_mem, 1, 1, peers)
    pair_sums = shape(F32, 2, row_count, width)
    own_terms, stats_all = call(
        own_kernel,
        [pair_sums, stats],
        [rows, part, queries, joined, own_mem, other_mem],
        after=[send],
        flops=HIDING * piece_flops,
        name="own",
    )
    next_stats = lax.ppermute(stats_all, "tm", [(i, i - 1) for i in range(1, peers)])
    (passed_on,) = call(
        pass_kernel, [shape(BF16, row_count, width)], [direct_cotangent], after=[own_terms], name="pass_on"
    )
    relayed_cotangent = shift_second(passed_on, -1, 2, peers)
    (own,) = call(
        functools.partial(next_kernel, peers),
        [pair_sums],
        [rows, next_stats, pair_queries, next_queries, direct_cotangent, relayed_cotangent, joined, own_terms],
        flops=HIDING * piece_flops,
        name="next",
    )
    for step, (even_bit, odd_bit) in enumerate(turns[::-1]):
        got = swap(send, even_bit, odd_bit, peers)
        if step + 1 < len(turns):
            after = [own_terms, next_queries]
            keep, send = call(add_kernel, [sums, held], [keep, got], after=after, name="add")
    attended, grad_query, mark = call(
        functools.partial(attend_kernel, peers),
        [shape(BF16, row_count, width)] * 2 + [shape(F32, 8, 128)],
        [rows, stats_all, queries, *outer, pair, joined, own_mem, other_mem],
        after=[send],
        flops=HIDING * piece_flops,
        name="attend",
    )
    (owned_send,) = call(
        functools.partial(owned_kernel, (1,)),
        [shape(BF16, FR_DEV, 2, frame_len, half_width)],
        [codes, keep, got],
        after=[own, mark],
        name="owned_pair",
    )
    (owned_mine,) = call(
        functools.partial(owned_kernel, (0,)),
        [shape(F32, FR_DEV, 2, frame_len, half_width)],
        [codes, keep, got],
        after=[owned_send],
        name="owned",
    )
    owned_got = swap(owned_send, 1, 1, peers)
    grad_key, grad_value = pl.pallas_call(
        final_kernel,
        out_shape=[shape(BF16, row_count, width)] * 2,
        in_specs=[VMEM] * 3,
        out_specs=[pl.BlockSpec(memory_space=pltpu.HBM)] * 2,
        scratch_shapes=[pltpu.VMEM((2, row_count, width), BF16), pltpu.SemaphoreType.DMA((2 * FR_DEV,))],
        compiler_params=pltpu.CompilerParams(vmem_limit_bytes=VMEM_LIMIT),
        name="final",
    )(own, owned_mine, owned_got)
    return (attended, grad_query, grad_key, grad_value)


def solution(mesh):
    rows = P(("traj", "tm"), None)
    in_specs = (rows, rows, rows, rows, P("traj"), P(), rows, P("traj"))
    return jax.shard_map(body, mesh=mesh, in_specs=in_specs, out_specs=(rows,) * 4, check_vma=False)
```
